32 devices in a mesh: cond: 4 (over x, core), ty: 4 (over z), tx: 2 (over y).
Axes of the slice: x: 2, y: 2, z: 4, core: 2. Of those that a mesh axis runs over, the one named last changes fastest.
Arguments:
- bed: float32 [1024, 2048], P('ty', 'tx'), may hold values from -4 to 4
- land_mask: int32 [1024, 2048], P('ty', 'tx'), may hold values 0 or 1
- cell_class: int32 [1024, 2048], P('ty', 'tx'), may hold values from 0 to 2
- weights: int32 [4], replicated, may hold values from 1 to 8
- cond_params: float32 [4, 4], P('cond'), may hold values from 0.25 to 2
- wave_stress: float32 [4, 2, 1024, 2048], P('cond', None, 'ty', 'tx'), may hold values from -0.6 to 0.6
- hydro_state: float32 [4, 3, 1024, 2048], P('cond', None, 'ty', 'tx'), may hold values from -1.8 to 1.8
Outputs:
- bed_next: float32 [1024, 2048], P('ty', 'tx')
- bed_change: float32 [1024, 2048], P('ty', 'tx')
- hydro_next: float32 [4, 3, 1024, 2048], P('cond', None, 'ty', 'tx')
The draws below stay inside these ranges and needn't reach their ends.
All inputs are finite; a program needn't handle non-finite values. No bound on the sum of `land_mask` on one device may be relied on, other than what follows from the above.
Results may differ from the reference program's by a relative error of at most 0.00002.
Values sent between devices are 32-bit elements; how exact they have to be, the bound alone decides.
No kernel may reach another device: no remote copies, remote signals or barrier semaphores. Data moves between devices by JAX's collectives and lax.ppermute only.
A program may use at most 128 MiB of HBM per device.

```python
import math
import jax
import jax.numpy as jnp

STEPS = 3
CONDS = 4
NR = 1024
NC = 2048


def place_ends(result, own_key, least, high):
    place = [jax.random.randint(jax.random.fold_in(own_key, axis), (), 0, length) for axis, length in enumerate(result.shape)]
    main_axis = result.shape.index(max(result.shape))
    neighbour = place[:main_axis] + [(place[main_axis] + 1) % result.shape[main_axis]] + place[main_axis + 1:]
    return result.at[tuple(place)].set(least).at[tuple(neighbour)].set(high)


def block_levels(key, shape, shards, low, top_value):
    factor_of, own = 1.0, jax.random.fold_in(key, 6)
    for axis_at, parts in shards:
        steps = jnp.exp(jax.random.uniform(jax.random.fold_in(own, axis_at), (parts,), jnp.float32, low / len(shards), top_value / len(shards)))
        factor_of = factor_of * jnp.repeat(steps, shape[axis_at] // parts).reshape([-1 if axis == axis_at else 1 for axis in range(len(shape))])
    return factor_of


def bell_draw(stream_key, dims, width, reach, cuts=(), dtype=jnp.bfloat16):
    gain = block_levels(stream_key, dims, cuts, -0.22, 0.18) if cuts else 1.0
    drawn = jax.random.normal(stream_key, dims, jnp.float32) * width * gain
    return jnp.minimum(jnp.maximum(drawn, -reach), reach).astype(dtype)


def setup_inputs(seed: int = 0) -> dict:
    key_of = jax.random.split(jax.random.key(seed), 8)
    return {
        "bed": bell_draw(key_of[0], (NR, NC), 1.0, 4.0, ((0, 4), (1, 2)), jnp.float32),
        "land_mask": place_ends((jax.random.randint(key_of[1], (NR, NC), 0, 4) < 3).astype(jnp.int32), jax.random.fold_in(key_of[1], 1), 0, 1),
        "cell_class": place_ends(jax.random.randint(key_of[2], (NR, NC), 0, 3), jax.random.fold_in(key_of[2], 1), 0, 2).astype(jnp.int32),
        "weights": place_ends(jax.random.randint(key_of[3], (CONDS,), 1, 9), jax.random.fold_in(key_of[3], 1), 1, 8).astype(jnp.int32),
        "cond_params": jnp.clip(jnp.exp(math.log(2.0) - 2.0794415 * jax.random.uniform(key_of[4], (CONDS, 4), jnp.float32) ** block_levels(key_of[4], (CONDS, 4), ((0, 4),), -0.2, 0.2)), 0.25, 2.0),
        "wave_stress": bell_draw(key_of[5], (CONDS, 2, NR, NC), 0.1, 0.6, ((0, 4), (2, 4), (3, 2)), jnp.float32),
        "hydro_state": bell_draw(key_of[6], (CONDS, 3, NR, NC), 0.3, 1.8, ((0, 4), (2, 4), (3, 2)), jnp.float32),
    }


def east(x):
    return jnp.concatenate([x[:, 1:], jnp.zeros_like(x[:, :1])], axis=1)

def west(x):
    return jnp.concatenate([jnp.zeros_like(x[:, :1]), x[:, :-1]], axis=1)

def south(x):
    return jnp.concatenate([x[1:, :], jnp.zeros_like(x[:1, :])], axis=0)

def north(x):
    return jnp.concatenate([jnp.zeros_like(x[:1, :]), x[:-1, :]], axis=0)

def reference(bed, land_mask, cell_class, weights, cond_params, wave_stress, hydro_state):
    wet = land_mask.astype(jnp.float32)
    depth = wet * (1.0 + 0.5 * jnp.tanh(-bed))
    relax = 0.5 * depth * (cell_class == 1).astype(jnp.float32)
    inflow = depth * (cell_class == 2).astype(jnp.float32)
    face_c = jnp.sqrt(depth * east(depth))
    face_r = jnp.sqrt(depth * south(depth))
    wet_c = face_c / (face_c + 0.1)
    wet_r = face_r / (face_r + 0.1)
    wsum = jnp.sum(weights).astype(jnp.float32)
    total = jnp.zeros(bed.shape, jnp.float32)
    states = []
    for cond in range(CONDS):
        tide = cond_params[cond, 0] - 1.0
        fric = 0.2 * cond_params[cond, 1]
        coef = cond_params[cond, 2]
        flow_in = 0.3 * cond_params[cond, 3]
        level = hydro_state[cond, 0]
        vel_c = hydro_state[cond, 1]
        vel_r = hydro_state[cond, 2]
        stress_c = wave_stress[cond, 0]
        stress_r = wave_stress[cond, 1]
        change = jnp.zeros(bed.shape, jnp.float32)
        for step in range(STEPS):
            vel_c = ((1.0 - fric) * vel_c - 0.3 * (east(level) - level) + stress_c) * wet_c
            vel_r = ((1.0 - fric) * vel_r - 0.3 * (south(level) - level) + stress_r) * wet_r
            flux_c = face_c * vel_c
            flux_r = face_r * vel_r
            level = level - (flux_c - west(flux_c) + flux_r - north(flux_r)) + relax * (tide - level) + flow_in * inflow
            load_c = coef * wet_c * vel_c * jnp.abs(vel_c)
            load_r = coef * wet_r * vel_r * jnp.abs(vel_r)
            change = change - 4.0 * (load_c - west(load_c) + load_r - north(load_r))
        states.append(jnp.stack([level, vel_c, vel_r]))
        total = total + weights[cond].astype(jnp.float32) / wsum * change
    height = bed + total
    col_ids = jnp.arange(NC)[None, :]
    row_ids = jnp.arange(NR)[:, None]
    inside_c = (col_ids < NC - 1).astype(jnp.float32)
    inside_r = (row_ids < NR - 1).astype(jnp.float32)
    slope_c = (east(height) - height) * inside_c
    slope_r = (south(height) - height) * inside_r
    spill_c = 0.25 * (slope_c - jnp.clip(slope_c, -1.0, 1.0))
    spill_r = 0.25 * (slope_r - jnp.clip(slope_r, -1.0, 1.0))
    bed_next = height + spill_c - west(spill_c) + spill_r - north(spill_r)
    return (bed_next, total, jnp.stack(states))
```

```python
import functools

import jax
import jax.numpy as jnp
from jax import lax
from jax.experimental import pallas as pl
from jax.experimental.pallas import tpu as pltpu
from jax.sharding import PartitionSpec as P

STEPS = 3
HALO = STEPS + 1
SUB = 8
LANE = 128
FIELDS = 8
GROUP = HALO * FIELDS
FOLD = LANE // GROUP
ANY = pl.BlockSpec(memory_space=pl.ANY)
VMEM = pl.BlockSpec(memory_space=pltpu.VMEM)
SMEM = pl.BlockSpec(memory_space=pltpu.SMEM)


def rows_of(shape):
    return lax.broadcasted_iota(jnp.int32, shape, 0)


def lanes_of(shape):
    return lax.broadcasted_iota(jnp.int32, shape, 1)


def east(x):
    return pltpu.roll(x, x.shape[1] - 1, 1)


def west(x):
    return pltpu.roll(x, 1, 1)


def south(x, below):
    return pltpu.roll(jnp.where(rows_of(x.shape) == 0, below, x), SUB - 1, 0)


def north(x, above):
    return pltpu.roll(jnp.where(rows_of(x.shape) == SUB - 1, above, x), 1, 0)


def tile_at(index):
    return pl.ds(pl.multiple_of(index * SUB, SUB), SUB)


def pack_kernel(bed, mask, kind, stress, hydro, up, down, side, up_far, down_far, ints, reals, int_side, real_side, sems):
    rows, cols = bed.shape
    at_left = lax.axis_index("tx") == 0
    off = pl.multiple_of(jnp.where(at_left, cols - LANE, 0), LANE)
    sources = [bed, mask, kind] + [stress.at[0, k] for k in range(2)] + [hydro.at[0, k] for k in range(3)]
    slots = [(reals, real_side, 0), (ints, int_side, 0), (ints, int_side, 1)] + [
        (reals, real_side, k) for k in range(1, 6)
    ]
    copies = []
    for f, (src, (edge, strip, k)) in enumerate(zip(sources, slots)):
        copies.append(pltpu.make_async_copy(src.at[pl.ds(0, SUB)], edge.at[0, k], sems.at[f, 0]))
        copies.append(pltpu.make_async_copy(src.at[pl.ds(rows - SUB, SUB)], edge.at[1, k], sems.at[f, 1]))
        copies.append(pltpu.make_async_copy(src.at[:, pl.ds(off, LANE)], strip.at[k], sems.at[f, 2]))
    for copy in copies:
        copy.start()
    for copy in copies:
        copy.wait()

    lift = jnp.where(at_left, HALO, 0)
    low = rows_of((SUB, cols)) < HALO
    lane = lanes_of((SUB, LANE))
    for where, out, far in ((0, up, up_far), (1, down, down_far)):
        corner = jnp.zeros((SUB, LANE), jnp.float32)
        for p in range(FIELDS // 2):
            both = []
            for f in (2 * p, 2 * p + 1):
                edge, _, k = slots[f]
                both.append(edge[where, k].astype(jnp.float32))
            if where == 0:
                pair = jnp.where(low, both[0], pltpu.roll(both[1], HALO, 0))
            else:
                pair = jnp.where(low, pltpu.roll(both[0], HALO, 0), both[1])
            out[pl.ds(p * SUB, SUB), :] = pair
            part = jnp.where(at_left, pair[:, cols - LANE :], pair[:, :LANE])
            part = pltpu.roll(part, lift + p * HALO, 1)
            corner = jnp.where(lane // HALO == p, part, corner)
        far[...] = corner

    span = rows // FOLD

    def fold(i, carry):
        total = jnp.zeros((SUB, LANE), jnp.float32)
        for g in range(FOLD):
            at = pl.ds(pl.multiple_of(g * span + i * SUB, SUB), SUB)
            for f in range(FIELDS):
                _, strip, k = slots[f]
                place = g * FIELDS + f
                part = pltpu.roll(strip[k, at, :].astype(jnp.float32), lift + place * HALO, 1)
                total = jnp.where(lane // HALO == place, part, total)
        side[tile_at(i), :] = total
        return carry

    lax.fori_loop(0, span // SUB, fold, 0)


def pack(bed, mask, kind, stress, hydro):
    rows, cols = bed.shape
    shape = functools.partial(jax.ShapeDtypeStruct, dtype=jnp.float32)
    return pl.pallas_call(
        pack_kernel,
        name="pack_edges",
        out_shape=[
            shape((GROUP, cols)),
            shape((GROUP, cols)),
            shape((rows // FOLD, LANE)),
            shape((SUB, LANE)),
            shape((SUB, LANE)),
        ],
        in_specs=[ANY] * 5,
        out_specs=[VMEM] * 5,
        scratch_shapes=[
            pltpu.VMEM((2, 2, SUB, cols), jnp.int32),
            pltpu.VMEM((2, 6, SUB, cols), jnp.float32),
            pltpu.VMEM((2, rows, LANE), jnp.int32),
            pltpu.VMEM((6, rows, LANE), jnp.float32),
            pltpu.SemaphoreType.DMA((FIELDS, 3)),
        ],
    )(bed, mask, kind, stress, hydro)


CHUNKS = 4


def flow_kernel(
    weights, params, bed, mask, kind, stress, hydro, above, below, side, above_far, below_far,
    hydro_out, send, keep, bed_rim,
    bed_x, mask_x, kind_x, sx_x, sy_x, e0, u0, v0,
    s_x, a_x, b_x, fc_x, fr_x, wc_x, wr_x, e1, u1, v1, e2, u2, v2, qc1, qr1, qc2, qr2,
    e3, u3, v3, change, fr_last, qr_last, rim_cols, in_sems, out_sems,
):
    rows, cols = bed.shape
    blocks = rows // SUB
    wide = cols + LANE
    half = rows // 2
    chunk = rows // CHUNKS
    at_left = lax.axis_index("tx") == 0
    cond = lax.axis_index("cond")
    mine = cond % 2

    sources = [bed, mask, kind] + [stress.at[0, k] for k in range(2)] + [hydro.at[0, k] for k in range(3)]
    fields = [bed_x, mask_x, kind_x, sx_x, sy_x, e0, u0, v0]

    def load(f, c):
        return pltpu.make_async_copy(
            sources[f].at[pl.ds(c * chunk, chunk)],
            fields[f].at[pl.ds(SUB + c * chunk, chunk), pl.ds(0, cols)],
            in_sems.at[f, c],
        )

    for c in range(CHUNKS):
        for f in range(FIELDS):
            load(f, c).start()

    lane = lanes_of((SUB, LANE))
    drop = jnp.where(at_left, 0, HALO)
    valid = jnp.where(at_left, lane, LANE - 1 - lane) < HALO
    halo_lanes = pl.ds(cols, LANE)

    def put(f, at, value):
        if f == 1:
            value = jnp.where(valid, value, 0.0)
        field = fields[f]
        field[at, halo_lanes] = value.astype(field.dtype)

    def place_rows(at, rows_in, far, first):
        corner = far[...]
        for f in range(FIELDS):
            pair = rows_in[pl.ds((f // 2) * SUB, SUB), :]
            part = pltpu.roll(corner, 2 * LANE - drop - (f // 2) * HALO, 1)
            if (f % 2 == 0) != first:
                pair = pltpu.roll(pair, HALO, 0)
                part = pltpu.roll(part, HALO, 0)
            field = fields[f]
            field[at, pl.ds(0, cols)] = pair.astype(field.dtype)
            put(f, at, part)

    place_rows(pl.ds(0, SUB), above, above_far, False)
    place_rows(pl.ds(rows + SUB, SUB), below, below_far, True)
    span = rows // FOLD // SUB

    def unfold(i, carry):
        strip = side[tile_at(i), :]
        for g in range(FOLD):
            at = tile_at(1 + g * span + i)
            for f in range(FIELDS):
                place = g * FIELDS + f
                put(f, at, pltpu.roll(strip, 2 * LANE - drop - place * HALO, 1))
        return carry

    lax.fori_loop(0, span, unfold, 0)

    tide = params[0, 0] - 1.0
    slow = 1.0 - 0.2 * params[0, 1]
    coef = params[0, 2]
    flow_in = 0.3 * params[0, 3]
    total_weight = weights[0]
    for k in range(1, weights.shape[0]):
        total_weight = total_weight + weights[k]
    ones = jnp.ones((SUB, wide), jnp.float32)
    share = weights[cond].astype(jnp.float32) * ones[:1, :LANE] / (total_weight.astype(jnp.float32) * ones[:1, :LANE])
    scale_lane = -4.0 * coef * share

    def prepare(i):
        at = tile_at(i)
        depth = mask_x[at, :].astype(jnp.float32) * (1.0 - 0.5 * jnp.tanh(bed_x[at, :]))
        kinds = kind_x[at, :]
        s_x[at, :] = jnp.sqrt(depth)
        relax = jnp.where(kinds == 1, 0.5 * depth, 0.0)
        a_x[at, :] = 1.0 - relax
        b_x[at, :] = 0.3 * (relax * tide + jnp.where(kinds == 2, flow_in * depth, 0.0))

    def move(i, level, lower, u_in, v_in, fc, fr, wc, wr, n, e_out, u_out, v_out):
        at = tile_at(i)
        u = (slow * u_in[at, :] - (east(level) - level) + sx_x[at, :]) * wc
        v = (slow * v_in[at, :] - (south(level, lower) - level) + sy_x[at, :]) * wr
        flux_c = fc * u
        flux_r = fr * v
        out = a_x[at, :] * level + b_x[at, :] - (flux_c - west(flux_c) + flux_r - north(flux_r, fr_last[n]))
        fr_last[n] = flux_r
        e_out[at, :] = out
        u_out[at, :] = u
        v_out[at, :] = v
        return wc * (u * jnp.abs(u)), wr * (v * jnp.abs(v))

    def step_one(i):
        at, after = tile_at(i), tile_at(i + 1)
        s = s_x[at, :]
        face_c = s * east(s)
        face_r = s * south(s, s_x[after, :])
        wc = face_c / (face_c + 0.1)
        wr = face_r / (face_r + 0.1)
        fc = 0.3 * face_c
        fr = 0.3 * face_r
        fc_x[at, :] = fc
        fr_x[at, :] = fr
        wc_x[at, :] = wc
        wr_x[at, :] = wr
        qc, qr = move(i, 0.3 * e0[at, :], 0.3 * e0[after, :], u0, v0, fc, fr, wc, wr, 0, e1, u1, v1)
        qc1[at, :] = qc
        qr1[at, :] = qr

    def step_two(i):
        at, after = tile_at(i), tile_at(i + 1)
        qc, qr = move(
            i, e1[at, :], e1[after, :], u1, v1, fc_x[at, :], fr_x[at, :], wc_x[at, :], wr_x[at, :], 1, e2, u2, v2
        )
        qc2[at, :] = qc1[at, :] + qc
        qr2[at, :] = qr1[at, :] + qr

    def step_three(i):
        at, after = tile_at(i), tile_at(i + 1)
        qc, qr = move(
            i, e2[at, :], e2[after, :], u2, v2, fc_x[at, :], fr_x[at, :], wc_x[at, :], wr_x[at, :], 2, e3, u3, v3
        )
        qc = qc2[at, :] + qc
        qr = qr2[at, :] + qr
        e3[at, :] = e3[at, :] * (1.0 / 0.3)
        value = (qc - west(qc) + qr - north(qr, qr_last[...])) * jnp.concatenate([scale_lane] * (wide // LANE), axis=1)
        qr_last[...] = qr
        change[at, :] = value[:, :cols]
        rim_cols[at, :] = value[:, cols:]

    last = blocks + 1

    def wave(t):
        fixed = isinstance(t, int)

        def run(stage, i):
            if not fixed or 0 <= i <= last:
                stage(i)

        run(step_three, t - 6)
        run(step_two, t - 4)
        run(step_one, t - 2)
        run(prepare, t)

    fr_last[...] = jnp.zeros_like(fr_last)
    qr_last[...] = jnp.zeros_like(qr_last)
    for ref in (s_x, e0, e1, e2):
        ref[pl.ds((last + 1) * SUB, SUB), :] = jnp.zeros((SUB, wide), jnp.float32)
    wave(0)
    per = chunk // SUB
    for f in range(FIELDS):
        load(f, 0).wait()
    for t in range(1, 7):
        wave(t)

    def step(t, carry):
        for c in range(1, CHUNKS):

            @pl.when(t == c * per + 1)
            def _():
                for f in range(FIELDS):
                    load(f, c).wait()

        wave(t)
        return carry

    lax.fori_loop(7, last + 1, step, 0)
    for t in range(last + 1, last + 7):
        wave(t)

    top = change[pl.ds(0, SUB), :]
    bottom = change[pl.ds((last) * SUB, SUB), :]
    row = rows_of((SUB, cols))
    rim_rows = jnp.where(row == 0, pltpu.roll(top, 1, 0), pltpu.roll(bottom, 1, 0))

    def fold_columns(ref, first):
        def body(g, total):
            part = pltpu.roll(ref[tile_at(g + 1), pl.ds(first, LANE)], 1 + 2 * g, 1)
            return jnp.where(lane // 2 == g, part, total)

        return lax.fori_loop(0, blocks, body, jnp.zeros((SUB, LANE), jnp.float32))

    zeros = jnp.zeros((SUB, cols), jnp.float32)
    first_part = pl.ds(SUB + rows + SUB, SUB)
    second_part = pl.ds(SUB + rows + 2 * SUB, SUB)
    change[first_part, :] = rim_rows
    change[second_part, :] = zeros
    change[second_part, pl.ds(0, LANE)] = fold_columns(rim_cols, 0)
    bed_top = pltpu.roll(bed_x[pl.ds(0, SUB), pl.ds(0, cols)], 1, 0)
    bed_bottom = pltpu.roll(bed_x[pl.ds(last * SUB, SUB), pl.ds(0, cols)], 1, 0)
    bed_rim[0] = jnp.where(row == 0, bed_top, bed_bottom)
    bed_rim[1] = zeros
    bed_rim[1, :, pl.ds(0, LANE)] = fold_columns(bed_x, cols)

    other = 1 - mine
    outs = [
        pltpu.make_async_copy(
            change.at[pl.ds(pl.multiple_of(SUB + other * half, SUB), half)], send.at[pl.ds(0, half)], out_sems.at[0]
        ),
        pltpu.make_async_copy(
            change.at[pl.ds(pl.multiple_of(2 * SUB + rows + other * SUB, SUB), SUB)],
            send.at[pl.ds(half, SUB)],
            out_sems.at[1],
        ),
        pltpu.make_async_copy(
            change.at[pl.ds(pl.multiple_of(SUB + mine * half, SUB), half)], keep.at[pl.ds(0, half)], out_sems.at[2]
        ),
        pltpu.make_async_copy(
            change.at[pl.ds(pl.multiple_of(2 * SUB + rows + mine * SUB, SUB), SUB)],
            keep.at[pl.ds(half, SUB)],
            out_sems.at[3],
        ),
    ] + [
        pltpu.make_async_copy(ref.at[pl.ds(SUB, rows), pl.ds(0, cols)], hydro_out.at[0, k], out_sems.at[4 + k])
        for k, ref in enumerate((e3, u3, v3))
    ]
    for copy in outs:
        copy.start()
    for copy in outs:
        copy.wait()


def flow(weights, params, bed, mask, kind, stress, hydro, halos):
    rows, cols = bed.shape
    wide = cols + LANE
    tall = rows + 3 * SUB
    real = pltpu.VMEM((tall, wide), jnp.float32)
    whole = pltpu.VMEM((tall, wide), jnp.int32)
    shape = functools.partial(jax.ShapeDtypeStruct, dtype=jnp.float32)
    buffers = [real, whole, whole] + [real] * 25 + [
        pltpu.VMEM((rows + 4 * SUB, cols), jnp.float32),
        pltpu.VMEM((STEPS, SUB, wide), jnp.float32),
        pltpu.VMEM((SUB, wide), jnp.float32),
        pltpu.VMEM((tall, LANE), jnp.float32),
    ]
    return pl.pallas_call(
        flow_kernel,
        name="flow_steps",
        out_shape=[
            shape(hydro.shape),
            shape((rows // 2 + SUB, cols)),
            shape((rows // 2 + SUB, cols)),
            shape((2, SUB, cols)),
        ],
        in_specs=[SMEM, SMEM] + [ANY] * 5 + [VMEM] * 5,
        out_specs=[ANY, ANY, ANY, VMEM],
        scratch_shapes=buffers + [pltpu.SemaphoreType.DMA((FIELDS, CHUNKS)), pltpu.SemaphoreType.DMA((7,))],
        compiler_params=pltpu.CompilerParams(vmem_limit_bytes=48 * 2**20),
    )(weights, params, bed, mask, kind, stress, hydro, *halos)


def bed_kernel(bed, own, got, bed_rim, bed_next, bed_change, bed_v, change, rims, z_x, gr_last, next_v, sems):
    rows, cols = bed.shape
    blocks = rows // SUB
    half = rows // 2
    wide = cols + LANE
    mine = lax.axis_index("cond") % 2
    copies = [pltpu.make_async_copy(bed, bed_v, sems.at[0])]
    for k, (part, which) in enumerate(((own, mine), (got, 1 - mine))):
        at = pl.ds(pl.multiple_of(which * half, SUB), half)
        copies.append(pltpu.make_async_copy(part.at[pl.ds(0, half)], change.at[at], sems.at[1 + 2 * k]))
        copies.append(pltpu.make_async_copy(part.at[pl.ds(half, SUB)], rims.at[which], sems.at[2 + 2 * k]))
    for copy in copies:
        copy.start()
    for copy in copies:
        copy.wait()
    out_change = pltpu.make_async_copy(change, bed_change, sems.at[5])
    out_change.start()

    z_rows = rims[0] + bed_rim[0]
    z_cols = rims[1, :, pl.ds(0, LANE)] + bed_rim[1, :, pl.ds(0, LANE)]
    z_x[pl.ds(0, SUB), pl.ds(0, cols)] = pltpu.roll(z_rows, SUB - 1, 0)
    z_x[pl.ds(rows + SUB, SUB), pl.ds(0, cols)] = pltpu.roll(z_rows, SUB - 1, 0)
    zeros = jnp.zeros((SUB, LANE), jnp.float32)
    z_x[pl.ds(0, SUB), pl.ds(cols, LANE)] = zeros
    z_x[pl.ds(rows + SUB, SUB), pl.ds(cols, LANE)] = zeros

    col = lanes_of((SUB, wide))
    last_c = lax.axis_index("tx") == lax.axis_size("tx") - 1
    first_c = lax.axis_index("tx") == 0
    shut_c = (last_c & (col == cols - 1)) | (first_c & (col == wide - 1))
    row = rows_of((SUB, wide))
    last_r = lax.axis_index("ty") == lax.axis_size("ty") - 1
    first_r = lax.axis_index("ty") == 0

    def level(i):
        z_x[tile_at(i + 1), pl.ds(0, cols)] = bed_v[tile_at(i), :] + change[tile_at(i), :]
        z_x[tile_at(i + 1), pl.ds(cols, LANE)] = pltpu.roll(z_cols, 2 * LANE - 1 - 2 * i, 1)

    def spill(slope, shut):
        return jnp.where(shut, 0.0, 0.25 * (slope - jnp.clip(slope, -1.0, 1.0)))

    def faces(i):
        z = z_x[tile_at(i), :]
        shut_r = (last_r & (i == blocks) & (row == SUB - 1)) | (first_r & (i == 0) & (row == SUB - 1))
        return z, spill(south(z, z_x[tile_at(i + 1), :]) - z, shut_r)

    def update(i):
        z, gr = faces(i)
        gc = spill(east(z) - z, shut_c)
        out = z + gc - west(gc) + gr - north(gr, gr_last[...])
        gr_last[...] = gr
        next_v[tile_at(i - 1), :] = out[:, :cols]

    level(0)
    gr_last[...] = faces(0)[1]

    def body(i, carry):
        update(i)
        level(i + 1)
        return carry

    level(1)
    lax.fori_loop(1, blocks - 1, body, 0)
    update(blocks - 1)
    update(blocks)
    out_next = pltpu.make_async_copy(next_v, bed_next, sems.at[6])
    out_next.start()
    out_next.wait()
    out_change.wait()


def update_bed(bed, own, got, bed_rim):
    rows, cols = bed.shape
    wide = cols + LANE
    real = functools.partial(pltpu.VMEM, dtype=jnp.float32)
    return pl.pallas_call(
        bed_kernel,
        name="update_bed",
        out_shape=[jax.ShapeDtypeStruct(bed.shape, jnp.float32)] * 2,
        in_specs=[ANY, ANY, ANY, VMEM],
        out_specs=[ANY, ANY],
        scratch_shapes=[
            real((rows, cols)),
            real((rows, cols)),
            real((2, SUB, cols)),
            real((rows + 2 * SUB, wide)),
            real((SUB, wide)),
            real((rows, cols)),
            pltpu.SemaphoreType.DMA((7,)),
        ],
        compiler_params=pltpu.CompilerParams(vmem_limit_bytes=16 * 2**20),
    )(bed, own, got, bed_rim)


def shards(bed, land_mask, cell_class, weights, cond_params, wave_stress, hydro_state):
    up, down, side, up_far, down_far = pack(bed, land_mask, cell_class, wave_stress, hydro_state)
    ny = lax.axis_size("ty")
    nx = lax.axis_size("tx")
    nc = lax.axis_size("cond")
    go_up = [(i + 1, i) for i in range(ny - 1)]
    go_down = [(i, i + 1) for i in range(ny - 1)]
    far_up = [((i + 1) * nx + j, i * nx + 1 - j) for i in range(ny - 1) for j in range(nx)]
    far_down = [(i * nx + j, (i + 1) * nx + 1 - j) for i in range(ny - 1) for j in range(nx)]
    halos = (
        lax.ppermute(down, "ty", go_down),
        lax.ppermute(up, "ty", go_up),
        lax.ppermute(side, "tx", [(0, 1), (1, 0)]),
        lax.ppermute(down_far, ("ty", "tx"), far_down),
        lax.ppermute(up_far, ("ty", "tx"), far_up),
    )
    hydro_next, send, keep, bed_rim = flow(
        weights, cond_params, bed, land_mask, cell_class, wave_stress, hydro_state, halos
    )
    swap = [(i, i ^ 1) for i in range(nc)]
    part = keep + lax.ppermute(send, "cond", swap)
    reach = 2
    while reach < nc:
        part = part + lax.ppermute(part, "cond", [(i, i ^ reach) for i in range(nc)])
        reach = 2 * reach
    got = lax.ppermute(part, "cond", swap)
    bed_next, bed_change = update_bed(bed, part, got, bed_rim)
    return bed_next, bed_change, hydro_next


def solution(mesh):
    in_specs = (
        P("ty", "tx"),
        P("ty", "tx"),
        P("ty", "tx"),
        P(),
        P("cond", None),
        P("cond", None, "ty", "tx"),
        P("cond", None, "ty", "tx"),
    )
    out_specs = (P("ty", "tx"), P("ty", "tx"), P("cond", None, "ty", "tx"))
    return jax.shard_map(shards, mesh=mesh, in_specs=in_specs, out_specs=out_specs, check_vma=False)
```

```python
import functools

import jax
import jax.numpy as jnp
from jax import lax
from jax.experimental import pallas as pl
from jax.experimental.pallas import tpu as pltpu
from jax.sharding import PartitionSpec as P

STEPS = 3
HALO = STEPS + 1
SUB = 8
LANE = 128
FIELDS = 8
GROUP = HALO * FIELDS
FOLD = LANE // GROUP
LAG = 2
MIB = 2**20
ANY = pl.BlockSpec(memory_space=pl.ANY)
VMEM = pl.BlockSpec(memory_space=pltpu.VMEM)
SMEM = pl.BlockSpec(memory_space=pltpu.SMEM)


def rows_of(shape):
    return lax.broadcasted_iota(jnp.int32, shape, 0)


def lanes_of(shape):
    return lax.broadcasted_iota(jnp.int32, shape, 1)


def east(x):
    return pltpu.roll(x, x.shape[1] - 1, 1)


def west(x):
    return pltpu.roll(x, 1, 1)


def south(x, below):
    return pltpu.roll(jnp.where(rows_of(x.shape) == 0, below, x), SUB - 1, 0)


def north(x, above):
    return pltpu.roll(jnp.where(rows_of(x.shape) == SUB - 1, above, x), 1, 0)


def tile_at(index):
    if isinstance(index, int):
        return pl.ds(index * SUB, SUB)
    return pl.ds(pl.multiple_of(index * SUB, SUB), SUB)


def held(*arrays, space=pltpu.VMEM):
    return [pltpu.with_memory_space_constraint(x, space) for x in arrays]


def pack_kernel(bed, mask, kind, stress, hydro, up, down, side, ints, reals, int_side, real_side, sems):
    rows, cols = bed.shape
    at_left = lax.axis_index("tx") == 0
    off = pl.multiple_of(jnp.where(at_left, cols - LANE, 0), LANE)
    sources = [bed, mask, kind] + [stress.at[0, k] for k in range(2)] + [hydro.at[0, k] for k in range(3)]
    slots = [(reals, real_side, 0), (ints, int_side, 0), (ints, int_side, 1)] + [
        (reals, real_side, k) for k in range(1, 6)
    ]
    strips, edges = [], []
    for f, (src, (edge, strip, k)) in enumerate(zip(sources, slots)):
        strips.append(pltpu.make_async_copy(src.at[:, pl.ds(off, LANE)], strip.at[k], sems.at[f, 2]))
        edges.append(pltpu.make_async_copy(src.at[pl.ds(0, SUB)], edge.at[0, k], sems.at[f, 0]))
        edges.append(pltpu.make_async_copy(src.at[pl.ds(rows - SUB, SUB)], edge.at[1, k], sems.at[f, 1]))
    for copy in strips + edges:
        copy.start()
    for copy in strips:
        copy.wait()

    lift = jnp.where(at_left, HALO, 0)
    lane = lanes_of((SUB, LANE))
    span = rows // FOLD

    def fold(i, carry):
        total = jnp.zeros((SUB, LANE), jnp.float32)
        for g in range(FOLD):
            at = pl.ds(pl.multiple_of(g * span + i * SUB, SUB), SUB)
            for f in range(FIELDS):
                _, strip, k = slots[f]
                place = g * FIELDS + f
                part = pltpu.roll(strip[k, at, :].astype(jnp.float32), lift + place * HALO, 1)
                total = jnp.where(lane // HALO == place, part, total)
        side[tile_at(i), :] = total
        return carry

    lax.fori_loop(0, span // SUB, fold, 0)

    for copy in edges:
        copy.wait()
    low = rows_of((SUB, cols)) < HALO
    for where, out in ((0, up), (1, down)):
        for p in range(FIELDS // 2):
            both = []
            for f in (2 * p, 2 * p + 1):
                edge, _, k = slots[f]
                both.append(edge[where, k].astype(jnp.float32))
            if where == 0:
                pair = jnp.where(low, both[0], pltpu.roll(both[1], HALO, 0))
            else:
                pair = jnp.where(low, pltpu.roll(both[0], HALO, 0), both[1])
            for k in range(cols // LANE):
                out[pl.ds(k * GROUP + p * SUB, SUB), :] = pair[:, k * LANE : (k + 1) * LANE]


def pack(bed, mask, kind, stress, hydro):
    rows, cols = bed.shape
    tall = cols // LANE * GROUP + SUB
    return pl.pallas_call(
        pack_kernel,
        name="pack_edges",
        out_shape=[
            pltpu.VMEM((tall, LANE), jnp.float32),
            pltpu.VMEM((tall, LANE), jnp.float32),
            pltpu.VMEM((rows // FOLD, LANE), jnp.float32),
        ],
        in_specs=[ANY] * 5,
        out_specs=[VMEM] * 3,
        scratch_shapes=[
            pltpu.VMEM((2, 2, SUB, cols), jnp.int32),
            pltpu.VMEM((2, 6, SUB, cols), jnp.float32),
            pltpu.VMEM((2, rows, LANE), jnp.int32),
            pltpu.VMEM((6, rows, LANE), jnp.float32),
            pltpu.SemaphoreType.DMA((FIELDS, 3)),
        ],
        compiler_params=pltpu.CompilerParams(vmem_limit_bytes=4 * MIB),
        cost_estimate=pl.CostEstimate(flops=10**6, bytes_accessed=2 * MIB, transcendentals=0),
    )(*held(bed, mask, kind, stress, hydro, space=pltpu.HBM))


def side_lanes(at_left):
    drop = jnp.where(at_left, 0, HALO)
    lane = lanes_of((SUB, LANE))
    valid = jnp.where(at_left, lane, LANE - 1 - lane) < HALO

    def unfold(strip, place):
        return pltpu.roll(strip, 2 * LANE - drop - place * HALO, 1)

    return unfold, valid


class Sweep:
    NAMES = (
        ["s", "a", "b", "fc", "fr", "wc", "wr", "e1", "u1"]
        + ["v1", "e2", "u2", "v2", "qc1", "qr1", "qc2", "qr2"]
    )

    def __init__(self, count, wide, get, emit, weights, params, refs):
        self.count, self.wide, self.get, self.emit = count, wide, get, emit
        self.__dict__.update(zip(self.NAMES + ["fr_last", "qr_last"], refs))
        cond = lax.axis_index("cond")
        self.tide = params[0, 0] - 1.0
        self.slow = 1.0 - 0.2 * params[0, 1]
        self.flow_in = 0.3 * params[0, 3]
        total = weights[0]
        for k in range(1, weights.shape[0]):
            total = total + weights[k]
        ones = jnp.ones((SUB, LANE), jnp.float32)
        share = weights[cond].astype(jnp.float32) * ones / (total.astype(jnp.float32) * ones)
        self.scale = jnp.concatenate([-4.0 * params[0, 2] * share] * (wide // LANE), axis=1)

    @classmethod
    def scratch(cls, count, wide):
        block = pltpu.VMEM(((count + 1) * SUB, wide), jnp.float32)
        return [block] * len(cls.NAMES) + [
            pltpu.VMEM((STEPS, SUB, wide), jnp.float32),
            pltpu.VMEM((SUB, wide), jnp.float32),
        ]

    def prepare(self, i):
        at = tile_at(i)
        depth = self.get(1, i).astype(jnp.float32) * (1.0 - 0.5 * jnp.tanh(self.get(0, i)))
        kinds = self.get(2, i)
        self.s[at, :] = depth * lax.rsqrt(jnp.maximum(depth, 1e-12))
        relax = jnp.where(kinds == 1, 0.5 * depth, 0.0)
        self.a[at, :] = 1.0 - relax
        self.b[at, :] = 0.3 * (relax * self.tide + jnp.where(kinds == 2, self.flow_in * depth, 0.0))

    def move(self, n, i, level, lower, u, v, fc, fr, wc, wr):
        at = tile_at(i)
        u = (self.slow * u - (east(level) - level) + self.get(3, i)) * wc
        v = (self.slow * v - (south(level, lower) - level) + self.get(4, i)) * wr
        flux_c = fc * u
        flux_r = fr * v
        out = self.a[at, :] * level + self.b[at, :] - (
            flux_c - west(flux_c) + flux_r - north(flux_r, self.fr_last[n])
        )
        self.fr_last[n] = flux_r
        return out, u, v, wc * (u * jnp.abs(u)), wr * (v * jnp.abs(v))

    def step_one(self, i):
        at, after = tile_at(i), tile_at(i + 1)
        s = self.s[at, :]
        face_c = s * east(s)
        face_r = s * south(s, self.s[after, :])
        ratios = []
        for face in (face_c, face_r):
            base = face + 0.1
            inverse = pl.reciprocal(base, approx=True)
            ratios.append(face * (inverse * (2.0 - base * inverse)))
        wc, wr = ratios
        fc = 0.3 * face_c
        fr = 0.3 * face_r
        self.fc[at, :] = fc
        self.fr[at, :] = fr
        self.wc[at, :] = wc
        self.wr[at, :] = wr
        level = 0.3 * self.get(5, i)
        lower = 0.3 * self.get(5, i + 1) if i + 1 < self.count else level
        e, u, v, qc, qr = self.move(0, i, level, lower, self.get(6, i), self.get(7, i), fc, fr, wc, wr)
        self.e1[at, :] = e
        self.u1[at, :] = u
        self.v1[at, :] = v
        self.qc1[at, :] = qc
        self.qr1[at, :] = qr

    def later(self, n, i, e, u, v):
        at, after = tile_at(i), tile_at(i + 1)
        return self.move(
            n, i, e[at, :], e[after, :], u[at, :], v[at, :],
            self.fc[at, :], self.fr[at, :], self.wc[at, :], self.wr[at, :],
        )

    def step_two(self, i):
        at = tile_at(i)
        e, u, v, qc, qr = self.later(1, i, self.e1, self.u1, self.v1)
        self.e2[at, :] = e
        self.u2[at, :] = u
        self.v2[at, :] = v
        self.qc2[at, :] = self.qc1[at, :] + qc
        self.qr2[at, :] = self.qr1[at, :] + qr

    def step_three(self, i):
        at = tile_at(i)
        e, u, v, qc, qr = self.later(2, i, self.e2, self.u2, self.v2)
        qc = self.qc2[at, :] + qc
        qr = self.qr2[at, :] + qr
        change = (qc - west(qc) + qr - north(qr, self.qr_last[...])) * self.scale
        self.qr_last[...] = qr
        self.emit(i, e * (1.0 / 0.3), u, v, change)

    def run(self):
        self.fr_last[...] = jnp.zeros_like(self.fr_last)
        self.qr_last[...] = jnp.zeros_like(self.qr_last)
        for ref in (self.s, self.e1, self.e2):
            ref[tile_at(self.count), :] = jnp.zeros((SUB, self.wide), jnp.float32)
        stages = (self.step_three, self.step_two, self.step_one, self.prepare)
        for t in range(self.count + LAG * STEPS):
            for k, stage in enumerate(stages):
                i = t - LAG * (STEPS - k)
                if 0 <= i < self.count:
                    stage(i)


def raw_reader(bed, mask, kind, stress, hydro, side, unfold, valid):
    rows = bed.shape[0]
    span = rows // FOLD // SUB
    fields = [bed, mask, kind] + [stress.at[0, k] for k in range(2)] + [hydro.at[0, k] for k in range(3)]

    def read(f, block):
        strip = side[tile_at(block % span), :]
        part = unfold(strip, (block // span) * FIELDS + f)
        if f == 1:
            part = jnp.where(valid, part, 0.0)
        main = fields[f][tile_at(block), :]
        return jnp.concatenate([main, part.astype(main.dtype)], axis=1)

    return read


def middle_kernel(weights, params, bed, mask, kind, stress, hydro, side, hydro_out, pay, *refs):
    rows, cols = bed.shape
    quarter = rows // SUB // 4
    wide = cols + LANE
    unfold, valid = side_lanes(lax.axis_index("tx") == 0)
    read = raw_reader(bed, mask, kind, stress, hydro, side, unfold, valid)
    mine = lax.axis_index("cond") % 2
    lane = lanes_of((SUB, LANE))
    rims = [jnp.zeros((SUB, LANE), jnp.float32)] * 2
    first = quarter - 1

    def emit(i, e, u, v, change):
        if not 1 <= i <= 2 * quarter:
            return
        at = tile_at(first + i)
        for k, value in enumerate((e, u, v)):
            hydro_out[0, k, at, :] = value[:, :cols]
        half, g = divmod(i - 1, quarter)
        slot = jnp.where(mine == half, 1, 0)
        for k in range(cols // LANE):
            pay[slot, tile_at(k * quarter + g), :] = change[:, k * LANE : (k + 1) * LANE]
        rims[half] = jnp.where(lane // 2 == g, pltpu.roll(change[:, cols:], 1 + 2 * g, 1), rims[half])
        if g == quarter - 1:
            pay[slot, tile_at(cols // LANE * quarter), :] = rims[half]

    Sweep(2 * quarter + 2, wide, lambda f, i: read(f, first + i), emit, weights, params, refs).run()


def middle(weights, params, raw, side):
    rows, cols = raw[0].shape
    blocks = rows // SUB // 2 + 2
    return pl.pallas_call(
        middle_kernel,
        name="flow_middle",
        out_shape=[
            pltpu.VMEM(raw[4].shape, jnp.float32),
            pltpu.VMEM((2, cols // LANE * rows // 4 + SUB, LANE), jnp.float32),
        ],
        in_specs=[SMEM, SMEM] + [VMEM] * 6,
        out_specs=[VMEM, VMEM],
        scratch_shapes=Sweep.scratch(blocks, cols + LANE),
        compiler_params=pltpu.CompilerParams(vmem_limit_bytes=16 * MIB),
        cost_estimate=pl.CostEstimate(flops=6 * 10**7, bytes_accessed=16 * MIB, transcendentals=0),
    )(weights, params, *held(*raw, side))


def edge_kernel(own, weights, params, bed, mask, kind, stress, hydro, side, above, below, hydro_in, hydro_out, pay, ends_r, ends_i, *refs):
    rows, cols = bed.shape
    blocks = rows // SUB
    quarter = blocks // 4
    wide = cols + LANE
    lanes = cols // LANE
    unfold, valid = side_lanes(lax.axis_index("tx") == 0)
    read = raw_reader(bed, mask, kind, stress, hydro, side, unfold, valid)
    mine = lax.axis_index("cond") % 2
    top = mine == (0 if own else 1)
    first = jnp.where(top, -1, blocks - quarter - 1)
    spots = [(ends_r, 0), (ends_i, 0), (ends_i, 1)] + [(ends_r, k) for k in range(1, 6)]

    inner = jnp.where(top, quarter, blocks - quarter - 1)
    for f in range(FIELDS):
        body = read(f, inner)
        pairs = []
        for ref in (above, below):
            pairs.append([ref[pl.ds(k * GROUP + f // 2 * SUB, SUB), :] for k in range(lanes)])
        if f % 2 == 0:
            pairs[0] = [pltpu.roll(x, HALO, 0) for x in pairs[0]]
        else:
            pairs[1] = [pltpu.roll(x, HALO, 0) for x in pairs[1]]
        corner = jnp.where(
            top,
            unfold(above[pl.ds(lanes * GROUP, SUB), :], (FOLD - 1) * FIELDS + f),
            unfold(below[pl.ds(lanes * GROUP, SUB), :], f),
        )
        if f == 1:
            corner = jnp.where(valid, corner, 0.0)
        outer = jnp.concatenate([jnp.where(top, a, b) for a, b in zip(*pairs)] + [corner], axis=1).astype(body.dtype)
        ref, k = spots[f]
        ref[0, k] = jnp.where(top, outer, body)
        ref[1, k] = jnp.where(top, body, outer)

    def get(f, i):
        if i == 0 or i == quarter + 1:
            ref, k = spots[f]
            return ref[0 if i == 0 else 1, k]
        return read(f, first + i)

    lane = lanes_of((SUB, LANE))
    row = rows_of((SUB, LANE))
    state = {"rim": jnp.zeros((SUB, LANE), jnp.float32)}

    def emit(i, e, u, v, change):
        if i == 0:
            state["row"] = pltpu.roll(change, 1, 0)
            return
        if i == quarter + 1:
            outside = jnp.where(top, state["row"], change)
            total = jnp.zeros((SUB, LANE), jnp.float32)
            for k in range(lanes):
                total = jnp.where(row == k, pltpu.roll(outside[:, k * LANE : (k + 1) * LANE], k, 0) if k else outside[:, :LANE], total)
            pay[tile_at(lanes * quarter + 1), :] = total
            return
        at = tile_at(first + i)
        for k, value in enumerate((e, u, v)):
            hydro_out[0, k, at, :] = value[:, :cols]
        g = i - 1
        for k in range(lanes):
            pay[tile_at(k * quarter + g), :] = change[:, k * LANE : (k + 1) * LANE]
        state["rim"] = jnp.where(lane // 2 == g, pltpu.roll(change[:, cols:], 1 + 2 * g, 1), state["rim"])
        if g == quarter - 1:
            pay[tile_at(lanes * quarter), :] = state["rim"]

    Sweep(quarter + 2, wide, get, emit, weights, params, refs).run()


def edge(own, weights, params, raw, side, above, below, hydro):
    rows, cols = raw[0].shape
    blocks = rows // SUB // 4 + 2
    wide = cols + LANE
    return pl.pallas_call(
        functools.partial(edge_kernel, own),
        name="flow_own" if own else "flow_other",
        out_shape=[
            pltpu.VMEM(hydro.shape, jnp.float32),
            pltpu.VMEM((cols // LANE * rows // 4 + 2 * SUB, LANE), jnp.float32),
        ],
        in_specs=[SMEM, SMEM] + [VMEM] * 9,
        out_specs=[VMEM, VMEM],
        scratch_shapes=[pltpu.VMEM((2, 6, SUB, wide), jnp.float32), pltpu.VMEM((2, 2, SUB, wide), jnp.int32)]
        + Sweep.scratch(blocks, wide),
        input_output_aliases={10: 0},
        compiler_params=pltpu.CompilerParams(vmem_limit_bytes=12 * MIB),
        cost_estimate=pl.CostEstimate(flops=3 * 10**7, bytes_accessed=10 * MIB, transcendentals=0),
    )(weights, params, *held(*raw, side, above, below, hydro))


def bed_kernel(bed, side, above, below, own_m, got_m, own_e, got_e, bed_next, bed_change, change_v, next_v, sems):
    rows, cols = bed.shape
    blocks = rows // SUB
    quarter = blocks // 4
    span = blocks // FOLD
    wide = cols + LANE
    lanes = cols // LANE
    unfold, _ = side_lanes(lax.axis_index("tx") == 0)
    mine = lax.axis_index("cond") % 2

    def merged(q, block):
        half = q // 2
        own, got = (own_e, got_e) if q in (0, 3) else (own_m, got_m)
        at = tile_at(block)
        return jnp.where(mine == half, own[at, :], got[at, :])

    col = lanes_of((SUB, wide))
    last_c = lax.axis_index("tx") == lax.axis_size("tx") - 1
    first_c = lax.axis_index("tx") == 0
    shut_c = (last_c & (col == cols - 1)) | (first_c & (col == wide - 1))
    row = rows_of((SUB, wide))
    last_r = lax.axis_index("ty") == lax.axis_size("ty") - 1
    first_r = lax.axis_index("ty") == 0
    shut_r = row == SUB - 1
    rims = [merged(q, lanes * quarter) for q in range(4)]
    pad = [jnp.zeros((SUB, LANE), jnp.float32)]

    def level(b):
        if b == -1:
            rim = merged(0, lanes * quarter + 1)
            parts = []
            for k in range(lanes):
                z = above[tile_at(k * GROUP // SUB), :] + pltpu.roll(rim, (2 * SUB + HALO - 1 - k) % SUB, 0)
                parts.append(pltpu.roll(z, HALO, 0))
            return jnp.concatenate(parts + pad, axis=1)
        if b == blocks:
            rim = merged(3, lanes * quarter + 1)
            parts = []
            for k in range(lanes):
                parts.append(below[tile_at(k * GROUP // SUB), :] + pltpu.roll(rim, (SUB - k) % SUB, 0))
            return jnp.concatenate(parts + pad, axis=1)
        q, g = divmod(b, quarter)
        change = jnp.concatenate([merged(q, k * quarter + g) for k in range(lanes)], axis=1)
        change_v[tile_at(b), :] = change
        cols_bed = unfold(side[tile_at(b % span), :], b // span * FIELDS)
        cols_change = pltpu.roll(rims[q], LANE - 1 - 2 * g, 1)
        return jnp.concatenate([bed[tile_at(b), :] + change, cols_bed + cols_change], axis=1)

    def spill(slope, shut):
        return jnp.where(shut, 0.0, 0.25 * (slope - jnp.clip(slope, -1.0, 1.0)))

    def south_face(z, lower, b):
        slope = south(z, lower) - z
        if b == -1:
            return spill(slope, first_r & shut_r)
        if b == blocks - 1:
            return spill(slope, last_r & shut_r)
        return 0.25 * (slope - jnp.clip(slope, -1.0, 1.0))

    outs = []

    def send(b):
        parts = 4
        if (b + 1) % (blocks // parts) == 0:
            c = b // (blocks // parts)
            at = pl.ds(c * (rows // parts), rows // parts)
            for k, (src, dst) in enumerate(((change_v, bed_change), (next_v, bed_next))):
                outs.append(pltpu.make_async_copy(src.at[at], dst.at[at], sems.at[k, c]))
                outs[-1].start()

    z = level(-1)
    lower = level(0)
    gr = south_face(z, lower, -1)
    for b in range(blocks):
        z, lower = lower, level(b + 1)
        gr_above, gr = gr, south_face(z, lower, b)
        gc = spill(east(z) - z, shut_c)
        out = z + gc - west(gc) + gr - north(gr, gr_above)
        next_v[tile_at(b), :] = out[:, :cols]
        send(b)
    for copy in outs:
        copy.wait()


def update_bed(bed, side, above, below, own_m, got_m, own_e, got_e):
    rows, cols = bed.shape
    return pl.pallas_call(
        bed_kernel,
        name="update_bed",
        out_shape=[jax.ShapeDtypeStruct(bed.shape, jnp.float32)] * 2,
        in_specs=[VMEM] * 8,
        out_specs=[ANY, ANY],
        scratch_shapes=[
            pltpu.VMEM((rows, cols), jnp.float32),
            pltpu.VMEM((rows, cols), jnp.float32),
            pltpu.SemaphoreType.DMA((2, 4)),
        ],
        compiler_params=pltpu.CompilerParams(vmem_limit_bytes=6 * MIB),
        cost_estimate=pl.CostEstimate(flops=10**7, bytes_accessed=5 * MIB, transcendentals=0),
    )(*held(bed, side, above, below, own_m, got_m, own_e, got_e))


def shards(bed, land_mask, cell_class, weights, cond_params, wave_stress, hydro_state):
    ny = lax.axis_size("ty")
    nc = lax.axis_size("cond")
    raw = (bed, land_mask, cell_class, wave_stress, hydro_state)
    swap = [(i, i ^ 1) for i in range(nc)]

    def over_chips(part):
        reach = 2
        while reach < nc:
            part = part + lax.ppermute(part, "cond", [(i, i ^ reach) for i in range(nc)])
            reach = 2 * reach
        return part

    up, down, side = pack(*raw)
    side = lax.ppermute(side, "tx", [(0, 1), (1, 0)])
    tall = up.shape[0] - SUB
    up = lax.dynamic_update_slice(up, side[:SUB], (tall, 0))
    down = lax.dynamic_update_slice(down, side[-SUB:], (tall, 0))
    above = lax.ppermute(down, "ty", [(i, i + 1) for i in range(ny - 1)])
    below = lax.ppermute(up, "ty", [(i + 1, i) for i in range(ny - 1)])

    hydro, pay_m = middle(weights, cond_params, raw, side)
    got_m = lax.ppermute(pay_m[0], "cond", swap)
    hydro, pay_other = edge(False, weights, cond_params, raw, side, above, below, hydro)
    part_m = pay_m[1] + got_m
    hydro, part_m, pay_other = lax.optimization_barrier((hydro, part_m, pay_other))
    got_e = lax.ppermute(pay_other, "cond", swap)
    own_m = over_chips(part_m)
    hydro, pay_own = edge(True, weights, cond_params, raw, side, above, below, hydro)
    own_e = over_chips(pay_own + got_e)
    other_m = lax.ppermute(own_m, "cond", swap)
    other_e = lax.ppermute(own_e, "cond", swap)
    bed_next, bed_change = update_bed(bed, side, above, below, own_m, other_m, own_e, other_e)
    return bed_next, bed_change, hydro


def solution(mesh):
    in_specs = (
        P("ty", "tx"),
        P("ty", "tx"),
        P("ty", "tx"),
        P(),
        P("cond", None),
        P("cond", None, "ty", "tx"),
        P("cond", None, "ty", "tx"),
    )
    out_specs = (P("ty", "tx"), P("ty", "tx"), P("cond", None, "ty", "tx"))
    return jax.shard_map(shards, mesh=mesh, in_specs=in_specs, out_specs=out_specs, check_vma=False)
```

```python
import functools

import jax
import jax.numpy as jnp
from jax import lax
from jax.experimental import pallas as pl
from jax.experimental.pallas import tpu as pltpu
from jax.sharding import PartitionSpec as P

STEPS = 3
HALO = STEPS + 1
SUB = 8
LANE = 128
FIELDS = 8
GROUP = HALO * FIELDS
FOLD = LANE // GROUP
LAG = 2
MIB = 2**20
ANY = pl.BlockSpec(memory_space=pl.ANY)
VMEM = pl.BlockSpec(memory_space=pltpu.VMEM)
SMEM = pl.BlockSpec(memory_space=pltpu.SMEM)


def rows_of(shape):
    return lax.broadcasted_iota(jnp.int32, shape, 0)


def lanes_of(shape):
    return lax.broadcasted_iota(jnp.int32, shape, 1)


def east(x):
    return pltpu.roll(x, x.shape[1] - 1, 1)


def west(x):
    return pltpu.roll(x, 1, 1)


def south(x, below):
    return pltpu.roll(jnp.where(rows_of(x.shape) == 0, below, x), SUB - 1, 0)


def north(x, above):
    return pltpu.roll(jnp.where(rows_of(x.shape) == SUB - 1, above, x), 1, 0)


def tile_at(index):
    if isinstance(index, int):
        return pl.ds(index * SUB, SUB)
    return pl.ds(pl.multiple_of(index * SUB, SUB), SUB)


def held(*arrays, space=pltpu.VMEM):
    return [pltpu.with_memory_space_constraint(x, space) for x in arrays]


def cost(micros):
    return pl.CostEstimate(flops=int(micros * 10**9), bytes_accessed=0, transcendentals=0)


def raw_fields(bed, mask, kind, stress, hydro):
    return [bed, mask, kind] + [stress.at[0, k] for k in range(2)] + [hydro.at[0, k] for k in range(3)]


SPOTS = [(0, 0), (1, 0), (1, 1)] + [(0, k) for k in range(1, 6)]


def pack_side_kernel(bed, mask, kind, stress, hydro, side, reals, ints, sems):
    rows, cols = bed.shape
    at_left = lax.axis_index("tx") == 0
    off = pl.multiple_of(jnp.where(at_left, cols - LANE, 0), LANE)
    strips = [(reals, ints)[which].at[k] for which, k in SPOTS]
    copies = [
        pltpu.make_async_copy(src.at[:, pl.ds(off, LANE)], strip, sems.at[f])
        for f, (src, strip) in enumerate(zip(raw_fields(bed, mask, kind, stress, hydro), strips))
    ]
    for copy in copies:
        copy.start()
    for copy in copies:
        copy.wait()
    lift = jnp.where(at_left, HALO, 0)
    lane = lanes_of((SUB, LANE))
    span = rows // FOLD // SUB
    for i in range(span):
        total = jnp.zeros((SUB, LANE), jnp.float32)
        for g in range(FOLD):
            for f in range(FIELDS):
                place = g * FIELDS + f
                part = strips[f][tile_at(g * span + i), :].astype(jnp.float32)
                total = jnp.where(lane // HALO == place, pltpu.roll(part, lift + place * HALO, 1), total)
        side[tile_at(i), :] = total


def pack_side(*raw):
    rows, cols = raw[0].shape
    return pl.pallas_call(
        pack_side_kernel,
        name="pack_side",
        out_shape=pltpu.VMEM((rows // FOLD, LANE), jnp.float32),
        in_specs=[ANY] * 5,
        out_specs=VMEM,
        scratch_shapes=[
            pltpu.VMEM((6, rows, LANE), jnp.float32),
            pltpu.VMEM((2, rows, LANE), jnp.int32),
            pltpu.SemaphoreType.DMA((FIELDS,)),
        ],
        compiler_params=pltpu.CompilerParams(vmem_limit_bytes=4 * MIB),
        cost_estimate=cost(2),
    )(*held(*raw, space=pltpu.HBM))


def pack_rows_kernel(bed, mask, kind, stress, hydro, pays, reals, ints, sems):
    rows, cols = bed.shape
    copies = []
    for f, src in enumerate(raw_fields(bed, mask, kind, stress, hydro)):
        which, k = SPOTS[f]
        for end, start in enumerate((0, rows - SUB)):
            copies.append(
                pltpu.make_async_copy(src.at[pl.ds(start, SUB)], (reals, ints)[which].at[end, k], sems.at[f, end])
            )
    for copy in copies:
        copy.start()
    for copy in copies:
        copy.wait()
    low = rows_of((SUB, cols)) < HALO
    odd = lax.axis_index("ty") % 2
    for end in range(2):
        slot = (1 - end + odd) % 2
        for p in range(FIELDS // 2):
            both = []
            for f in (2 * p, 2 * p + 1):
                which, k = SPOTS[f]
                both.append((reals, ints)[which][end, k].astype(jnp.float32))
            both[1 - end] = pltpu.roll(both[1 - end], HALO, 0)
            pair = jnp.where(low, *both)
            for k in range(cols // LANE):
                pays[slot, pl.ds(k * GROUP + p * SUB, SUB), :] = pair[:, k * LANE : (k + 1) * LANE]


def pack_rows(*raw):
    rows, cols = raw[0].shape
    return pl.pallas_call(
        pack_rows_kernel,
        name="pack_rows",
        out_shape=pltpu.VMEM((2, cols // LANE * GROUP, LANE), jnp.float32),
        in_specs=[ANY] * 5,
        out_specs=VMEM,
        scratch_shapes=[
            pltpu.VMEM((2, 6, SUB, cols), jnp.float32),
            pltpu.VMEM((2, 2, SUB, cols), jnp.int32),
            pltpu.SemaphoreType.DMA((FIELDS, 2)),
        ],
        compiler_params=pltpu.CompilerParams(vmem_limit_bytes=4 * MIB),
        cost_estimate=cost(2),
    )(*held(*raw, space=pltpu.HBM))


def side_lanes(at_left):
    drop = jnp.where(at_left, 0, HALO)
    lane = lanes_of((SUB, LANE))
    valid = jnp.where(at_left, lane, LANE - 1 - lane) < HALO

    def unfold(strip, place):
        return pltpu.roll(strip, 2 * LANE - drop - place * HALO, 1)

    return unfold, valid


class Sweep:
    NAMES = (
        ["s", "a", "b", "fc", "fr", "wc", "wr", "e1", "u1"]
        + ["v1", "e2", "u2", "v2", "qc1", "qr1", "qc2", "qr2"]
    )

    def __init__(self, count, wide, get, emit, weights, params, refs):
        self.count, self.wide, self.get, self.emit = count, wide, get, emit
        self.__dict__.update(zip(self.NAMES + ["fr_last", "qr_last"], refs))
        cond = lax.axis_index("cond")
        self.tide = params[0, 0] - 1.0
        self.slow = 1.0 - 0.2 * params[0, 1]
        self.flow_in = 0.3 * params[0, 3]
        total = weights[0]
        for k in range(1, weights.shape[0]):
            total = total + weights[k]
        ones = jnp.ones((SUB, LANE), jnp.float32)
        share = weights[cond].astype(jnp.float32) * ones / (total.astype(jnp.float32) * ones)
        self.scale = jnp.concatenate([-4.0 * params[0, 2] * share] * (wide // LANE), axis=1)

    @classmethod
    def scratch(cls, count, wide):
        block = pltpu.VMEM(((count + 1) * SUB, wide), jnp.float32)
        return [block] * len(cls.NAMES) + [
            pltpu.VMEM((STEPS, SUB, wide), jnp.float32),
            pltpu.VMEM((SUB, wide), jnp.float32),
        ]

    def prepare(self, i):
        at = tile_at(i)
        depth = self.get(1, i).astype(jnp.float32) * (1.0 - 0.5 * jnp.tanh(self.get(0, i)))
        kinds = self.get(2, i)
        self.s[at, :] = depth * lax.rsqrt(jnp.maximum(depth, 1e-12))
        relax = jnp.where(kinds == 1, 0.5 * depth, 0.0)
        self.a[at, :] = 1.0 - relax
        self.b[at, :] = 0.3 * (relax * self.tide + jnp.where(kinds == 2, self.flow_in * depth, 0.0))

    def move(self, n, i, level, lower, u, v, fc, fr, wc, wr):
        at = tile_at(i)
        u = (self.slow * u - (east(level) - level) + self.get(3, i)) * wc
        v = (self.slow * v - (south(level, lower) - level) + self.get(4, i)) * wr
        flux_c = fc * u
        flux_r = fr * v
        out = self.a[at, :] * level + self.b[at, :] - (
            flux_c - west(flux_c) + flux_r - north(flux_r, self.fr_last[n])
        )
        self.fr_last[n] = flux_r
        return out, u, v, wc * (u * jnp.abs(u)), wr * (v * jnp.abs(v))

    def step_one(self, i):
        at, after = tile_at(i), tile_at(i + 1)
        s = self.s[at, :]
        face_c = s * east(s)
        face_r = s * south(s, self.s[after, :])
        ratios = []
        for face in (face_c, face_r):
            base = face + 0.1
            inverse = pl.reciprocal(base, approx=True)
            ratios.append(face * (inverse * (2.0 - base * inverse)))
        wc, wr = ratios
        fc = 0.3 * face_c
        fr = 0.3 * face_r
        self.fc[at, :] = fc
        self.fr[at, :] = fr
        self.wc[at, :] = wc
        self.wr[at, :] = wr
        level = 0.3 * self.get(5, i)
        lower = 0.3 * self.get(5, i + 1) if i + 1 < self.count else level
        e, u, v, qc, qr = self.move(0, i, level, lower, self.get(6, i), self.get(7, i), fc, fr, wc, wr)
        self.e1[at, :] = e
        self.u1[at, :] = u
        self.v1[at, :] = v
        self.qc1[at, :] = qc
        self.qr1[at, :] = qr

    def later(self, n, i, e, u, v):
        at, after = tile_at(i), tile_at(i + 1)
        return self.move(
            n, i, e[at, :], e[after, :], u[at, :], v[at, :],
            self.fc[at, :], self.fr[at, :], self.wc[at, :], self.wr[at, :],
        )

    def step_two(self, i):
        at = tile_at(i)
        e, u, v, qc, qr = self.later(1, i, self.e1, self.u1, self.v1)
        self.e2[at, :] = e
        self.u2[at, :] = u
        self.v2[at, :] = v
        self.qc2[at, :] = self.qc1[at, :] + qc
        self.qr2[at, :] = self.qr1[at, :] + qr

    def step_three(self, i):
        at = tile_at(i)
        e, u, v, qc, qr = self.later(2, i, self.e2, self.u2, self.v2)
        qc = self.qc2[at, :] + qc
        qr = self.qr2[at, :] + qr
        change = (qc - west(qc) + qr - north(qr, self.qr_last[...])) * self.scale
        self.qr_last[...] = qr
        self.emit(i, e * (1.0 / 0.3), u, v, change)

    def run(self):
        self.fr_last[...] = jnp.zeros_like(self.fr_last)
        self.qr_last[...] = jnp.zeros_like(self.qr_last)
        for ref in (self.s, self.e1, self.e2):
            ref[tile_at(self.count), :] = jnp.zeros((SUB, self.wide), jnp.float32)
        stages = (self.step_three, self.step_two, self.step_one, self.prepare)
        for t in range(self.count + LAG * STEPS):
            for k, stage in enumerate(stages):
                i = t - LAG * (STEPS - k)
                if 0 <= i < self.count:
                    stage(i)


def raw_reader(bed, mask, kind, stress, hydro, side, unfold, valid):
    rows = bed.shape[0]
    span = rows // FOLD // SUB
    fields = raw_fields(bed, mask, kind, stress, hydro)

    def read(f, block):
        strip = side[tile_at(block % span), :]
        part = unfold(strip, (block // span) * FIELDS + f)
        if f == 1:
            part = jnp.where(valid, part, 0.0)
        main = fields[f][tile_at(block), :]
        return jnp.concatenate([main, part.astype(main.dtype)], axis=1)

    return read


def middle_kernel(own, weights, params, bed, mask, kind, stress, hydro, side, *refs):
    hydro_out, pay, *refs = refs[1:] if own else refs
    rows, cols = bed.shape
    quarter = rows // SUB // 4
    unfold, valid = side_lanes(lax.axis_index("tx") == 0)
    read = raw_reader(bed, mask, kind, stress, hydro, side, unfold, valid)
    mine = lax.axis_index("cond") % 2
    lower_half = mine == (1 if own else 0)
    first = jnp.where(lower_half, 2 * quarter, quarter) - 1
    emit = quarter_writer(first, quarter, cols, hydro_out, pay)

    def finish(i, e, u, v, change):
        if 1 <= i <= quarter:
            emit(i, e, u, v, change)

    Sweep(quarter + 2, cols + LANE, lambda f, i: read(f, first + i), finish, weights, params, refs).run()


def quarter_writer(first, quarter, cols, hydro_out, pay):
    lane = lanes_of((SUB, LANE))
    lanes = cols // LANE
    rims = [jnp.zeros((SUB, LANE), jnp.float32)]

    def emit(i, e, u, v, change):
        at = tile_at(first + i)
        for k, value in enumerate((e, u, v)):
            hydro_out[0, k, at, :] = value[:, :cols]
        g = i - 1
        for k in range(lanes):
            pay[tile_at(k * quarter + g), :] = change[:, k * LANE : (k + 1) * LANE]
        rims[0] = jnp.where(lane // 2 == g, pltpu.roll(change[:, cols:], 1 + 2 * g, 1), rims[0])
        if g == quarter - 1:
            pay[tile_at(lanes * quarter), :] = rims[0]

    return emit


def middle(own, weights, params, raw, side, hydro=None):
    rows, cols = raw[0].shape
    given = (hydro,) if own else ()
    return pl.pallas_call(
        functools.partial(middle_kernel, own),
        name="middle_own" if own else "middle_other",
        out_shape=[
            pltpu.VMEM(raw[4].shape, jnp.float32),
            pltpu.VMEM((cols // LANE * rows // 4 + SUB, LANE), jnp.float32),
        ],
        in_specs=[SMEM, SMEM] + [VMEM] * (6 + own),
        out_specs=[VMEM, VMEM],
        scratch_shapes=Sweep.scratch(rows // SUB // 4 + 2, cols + LANE),
        input_output_aliases={8: 0} if own else {},
        compiler_params=pltpu.CompilerParams(vmem_limit_bytes=10 * MIB),
        cost_estimate=cost(4),
    )(weights, params, *held(*raw, side, *given))


def edge_kernel(
    own, weights, params, bed, mask, kind, stress, hydro, side, far_a, far_b, hydro_in,
    hydro_out, pay, ends_r, ends_i, *refs,
):
    rows, cols = bed.shape
    blocks = rows // SUB
    quarter = blocks // 4
    wide = cols + LANE
    lanes = cols // LANE
    unfold, valid = side_lanes(lax.axis_index("tx") == 0)
    read = raw_reader(bed, mask, kind, stress, hydro, side, unfold, valid)
    mine = lax.axis_index("cond") % 2
    top = mine == (0 if own else 1)
    from_a = top == (lax.axis_index("ty") % 2 == 1)
    first = jnp.where(top, -1, blocks - quarter - 1)

    inner = jnp.where(top, quarter, blocks - quarter - 1)
    for f in range(FIELDS):
        body = read(f, inner)
        parts = []
        for k in range(lanes):
            at = pl.ds(k * GROUP + f // 2 * SUB, SUB)
            part = jnp.where(from_a, far_a[at, :], far_b[at, :])
            moved = pltpu.roll(part, HALO, 0)
            parts.append(jnp.where(top, moved, part) if f % 2 == 0 else jnp.where(top, part, moved))
        at = pl.ds(lanes * GROUP, SUB)
        corner = jnp.where(from_a, far_a[at, :], far_b[at, :])
        corner = jnp.where(top, unfold(corner, (FOLD - 1) * FIELDS + f), unfold(corner, f))
        if f == 1:
            corner = jnp.where(valid, corner, 0.0)
        outer = jnp.concatenate(parts + [corner], axis=1).astype(body.dtype)
        which, k = SPOTS[f]
        ref = (ends_r, ends_i)[which]
        ref[0, k] = jnp.where(top, outer, body)
        ref[1, k] = jnp.where(top, body, outer)

    def get(f, i):
        if i == 0 or i == quarter + 1:
            which, k = SPOTS[f]
            return (ends_r, ends_i)[which][0 if i == 0 else 1, k]
        return read(f, first + i)

    row = rows_of((SUB, LANE))
    emit = quarter_writer(first, quarter, cols, hydro_out, pay)
    outside = []

    def finish(i, e, u, v, change):
        if i == 0:
            outside.append(pltpu.roll(change, 1, 0))
        elif i == quarter + 1:
            rim = jnp.where(top, outside[0], change)
            total = rim[:, :LANE]
            for k in range(1, lanes):
                total = jnp.where(row == k, pltpu.roll(rim[:, k * LANE : (k + 1) * LANE], k, 0), total)
            pay[tile_at(lanes * quarter + 1), :] = total
        else:
            emit(i, e, u, v, change)

    Sweep(quarter + 2, wide, get, finish, weights, params, refs).run()


def edge(own, weights, params, raw, side, far_a, far_b, hydro):
    rows, cols = raw[0].shape
    wide = cols + LANE
    return pl.pallas_call(
        functools.partial(edge_kernel, own),
        name="edge_own" if own else "edge_other",
        out_shape=[
            pltpu.VMEM(hydro.shape, jnp.float32),
            pltpu.VMEM((cols // LANE * rows // 4 + 2 * SUB, LANE), jnp.float32),
        ],
        in_specs=[SMEM, SMEM] + [VMEM] * 9,
        out_specs=[VMEM, VMEM],
        scratch_shapes=[pltpu.VMEM((2, 6, SUB, wide), jnp.float32), pltpu.VMEM((2, 2, SUB, wide), jnp.int32)]
        + Sweep.scratch(rows // SUB // 4 + 2, wide),
        input_output_aliases={10: 0},
        compiler_params=pltpu.CompilerParams(vmem_limit_bytes=12 * MIB),
        cost_estimate=cost(4),
    )(weights, params, *held(*raw, side, far_a, far_b, hydro))


class Update:
    def __init__(self, bed, side, far_a, far_b, own_m, got_m, own_e, got_e, change_v, next_v):
        self.bed, self.side, self.far_a, self.far_b = bed, side, far_a, far_b
        self.parts = {"m": (own_m, got_m), "e": (own_e, got_e)}
        self.change_v, self.next_v = change_v, next_v
        rows, self.cols = bed.shape
        self.blocks = rows // SUB
        self.quarter = self.blocks // 4
        self.lanes = self.cols // LANE
        self.wide = self.cols + LANE
        self.unfold, _ = side_lanes(lax.axis_index("tx") == 0)
        self.mine = lax.axis_index("cond") % 2
        self.odd = lax.axis_index("ty") % 2 == 1
        col = lanes_of((SUB, self.wide))
        last_c = lax.axis_index("tx") == lax.axis_size("tx") - 1
        first_c = lax.axis_index("tx") == 0
        self.shut_c = (last_c & (col == self.cols - 1)) | (first_c & (col == self.wide - 1))
        self.last_row = rows_of((SUB, self.wide)) == SUB - 1
        self.rims = {}

    def merged(self, q, block):
        own, got = self.parts["e" if q in (0, 3) else "m"]
        at = tile_at(block)
        return jnp.where(self.mine == q // 2, own[at, :], got[at, :])

    def outside(self, q):
        rim = self.merged(q, self.lanes * self.quarter + 1)
        parts = []
        for k in range(self.lanes):
            at = tile_at(k * GROUP // SUB)
            a, b = self.far_a[at, :], self.far_b[at, :]
            if q == 0:
                z = jnp.where(self.odd, a, b) + pltpu.roll(rim, (2 * SUB + HALO - 1 - k) % SUB, 0)
                parts.append(pltpu.roll(z, HALO, 0))
            else:
                parts.append(jnp.where(self.odd, b, a) + pltpu.roll(rim, (SUB - k) % SUB, 0))
        return jnp.concatenate(parts + [jnp.zeros((SUB, LANE), jnp.float32)], axis=1)

    def level(self, b, keep):
        if b == -1:
            return self.outside(0)
        if b == self.blocks:
            return self.outside(3)
        q, g = divmod(b, self.quarter)
        change = jnp.concatenate([self.merged(q, k * self.quarter + g) for k in range(self.lanes)], axis=1)
        if keep:
            self.change_v[tile_at(b), :] = change
        if q not in self.rims:
            self.rims[q] = self.merged(q, self.lanes * self.quarter)
        span = self.blocks // FOLD
        cols_bed = self.unfold(self.side[tile_at(b % span), :], b // span * FIELDS)
        cols_change = pltpu.roll(self.rims[q], LANE - 1 - 2 * g, 1)
        return jnp.concatenate([self.bed[tile_at(b), :] + change, cols_bed + cols_change], axis=1)

    def spill(self, slope):
        return 0.25 * (slope - jnp.clip(slope, -1.0, 1.0))

    def south_face(self, z, lower, b):
        out = self.spill(south(z, lower) - z)
        if b == -1:
            return jnp.where((lax.axis_index("ty") == 0) & self.last_row, 0.0, out)
        if b == self.blocks - 1:
            return jnp.where((lax.axis_index("ty") == lax.axis_size("ty") - 1) & self.last_row, 0.0, out)
        return out

    def run(self, first, stop, keep, after=lambda b: None):
        z = self.level(first - 1, keep)
        lower = self.level(first, keep)
        gr = self.south_face(z, lower, first - 1)
        for b in range(first, stop):
            z, lower = lower, self.level(b + 1, keep)
            gr_above, gr = gr, self.south_face(z, lower, b)
            gc = jnp.where(self.shut_c, 0.0, self.spill(east(z) - z))
            out = z + gc - west(gc) + gr - north(gr, gr_above)
            self.next_v[tile_at(b), :] = out[:, : self.cols]
            after(b)


def bed_middle_kernel(
    bed, side, far_a, far_b, own_m, got_m, hydro, bed_next, bed_change, hydro_out, change_v, next_v, sems
):
    rows = bed.shape[0]
    quarter = rows // SUB // 4
    copies = [pltpu.make_async_copy(hydro, hydro_out, sems.at[0])]
    copies[0].start()
    update = Update(bed, side, far_a, far_b, own_m, got_m, None, None, change_v, next_v)
    update.run(quarter + 1, 3 * quarter - 1, True)
    for src, dst, low, high in (
        (change_v, bed_change, quarter, 3 * quarter),
        (next_v, bed_next, quarter + 1, 3 * quarter - 1),
    ):
        at = pl.ds(low * SUB, (high - low) * SUB)
        copies.append(pltpu.make_async_copy(src.at[at], dst.at[at], sems.at[len(copies)]))
        copies[-1].start()
    for copy in copies:
        copy.wait()


def bed_edge_kernel(
    bed, side, far_a, far_b, own_m, got_m, own_e, got_e, next_in, change_in, bed_next, bed_change,
    change_v, next_v, sems,
):
    rows = bed.shape[0]
    blocks = rows // SUB
    quarter = blocks // 4
    update = Update(bed, side, far_a, far_b, own_m, got_m, own_e, got_e, change_v, next_v)
    copies = []

    def send(src, dst, low, high):
        at = pl.ds(low * SUB, (high - low) * SUB)
        copies.append(pltpu.make_async_copy(src.at[at], dst.at[at], sems.at[len(copies)]))
        copies[-1].start()

    update.run(0, quarter + 1, True)
    send(change_v, bed_change, 0, quarter)
    send(next_v, bed_next, 0, quarter + 1)
    update.run(blocks - quarter - 1, blocks, True)
    send(change_v, bed_change, blocks - quarter, blocks)
    send(next_v, bed_next, blocks - quarter - 1, blocks)
    for copy in copies:
        copy.wait()


def bed_scratch(rows, cols):
    return [
        pltpu.VMEM((rows, cols), jnp.float32),
        pltpu.VMEM((rows, cols), jnp.float32),
        pltpu.SemaphoreType.DMA((4,)),
    ]


def bed_middle(bed, side, far_a, far_b, own_m, got_m, hydro):
    return pl.pallas_call(
        bed_middle_kernel,
        name="bed_middle",
        out_shape=[pltpu.HBM(x.shape, jnp.float32) for x in (bed, bed, hydro)],
        in_specs=[VMEM] * 7,
        out_specs=[ANY] * 3,
        scratch_shapes=bed_scratch(*bed.shape),
        compiler_params=pltpu.CompilerParams(vmem_limit_bytes=6 * MIB),
        cost_estimate=cost(4),
    )(*held(bed, side, far_a, far_b, own_m, got_m, hydro))


def bed_edge(bed, side, far_a, far_b, own_m, got_m, own_e, got_e, bed_next, bed_change):
    return pl.pallas_call(
        bed_edge_kernel,
        name="bed_edge",
        out_shape=[pltpu.HBM(bed.shape, jnp.float32)] * 2,
        in_specs=[VMEM] * 8 + [ANY] * 2,
        out_specs=[ANY] * 2,
        scratch_shapes=bed_scratch(*bed.shape),
        input_output_aliases={8: 0, 9: 1},
        compiler_params=pltpu.CompilerParams(vmem_limit_bytes=6 * MIB),
        cost_estimate=cost(2),
    )(
        *held(bed, side, far_a, far_b, own_m, got_m, own_e, got_e),
        *held(bed_next, bed_change, space=pltpu.HBM),
    )


def shards(bed, land_mask, cell_class, weights, cond_params, wave_stress, hydro_state):
    ny = lax.axis_size("ty")
    nc = lax.axis_size("cond")
    raw = (bed, land_mask, cell_class, wave_stress, hydro_state)
    swap = [(i, i ^ 1) for i in range(nc)]

    def pairs(first):
        return [p for i in range(first, ny - 1, 2) for p in ((i, i + 1), (i + 1, i))]

    def over_chips(part, beside=()):
        reach = 2
        while reach < nc:
            got = lax.ppermute(part, "cond", [(i, i ^ reach) for i in range(nc)])
            got, beside = lax.optimization_barrier((got, beside))
            part = part + got
            reach = 2 * reach
        return part, beside

    side = lax.ppermute(pack_side(*raw), "tx", [(0, 1), (1, 0)])
    pays = pack_rows(*raw)
    odd = lax.axis_index("ty") % 2 == 1
    corners = [side[:SUB], side[-SUB:]]
    far_a = jnp.concatenate([pays[0], jnp.where(odd, corners[0], corners[1])])
    far_b = jnp.concatenate([pays[1], jnp.where(odd, corners[1], corners[0])])
    far_a = lax.ppermute(far_a, "ty", pairs(0))
    far_b = lax.ppermute(far_b, "ty", pairs(1))

    hydro, pay = middle(False, weights, cond_params, raw, side)
    got = lax.ppermute(pay, "cond", swap)
    hydro, pay = middle(True, weights, cond_params, raw, side, hydro)
    part_m = pay + got
    hydro, part_m = lax.optimization_barrier((hydro, part_m))
    hydro, pay = edge(False, weights, cond_params, raw, side, far_a, far_b, hydro)
    got = lax.ppermute(pay, "cond", swap)
    hydro, pay = edge(True, weights, cond_params, raw, side, far_a, far_b, hydro)
    part_e = pay + got
    own_m, (hydro, _) = over_chips(part_m, (hydro, part_e))
    got_m = lax.ppermute(own_m, "cond", swap)
    bed_next, bed_change, hydro = bed_middle(bed, side, far_a, far_b, own_m, got_m, hydro)
    own_e, (bed_next, bed_change) = over_chips(part_e, (bed_next, bed_change))
    got_e = lax.ppermute(own_e, "cond", swap)
    bed_next, bed_change = bed_edge(
        bed, side, far_a, far_b, own_m, got_m, own_e, got_e, bed_next, bed_change
    )
    return bed_next, bed_change, hydro


def solution(mesh):
    in_specs = (
        P("ty", "tx"),
        P("ty", "tx"),
        P("ty", "tx"),
        P(),
        P("cond", None),
        P("cond", None, "ty", "tx"),
        P("cond", None, "ty", "tx"),
    )
    out_specs = (P("ty", "tx"), P("ty", "tx"), P("cond", None, "ty", "tx"))
    return jax.shard_map(shards, mesh=mesh, in_specs=in_specs, out_specs=out_specs, check_vma=False)
```

```python
import functools

import jax
import jax.numpy as jnp
from jax import lax
from jax.experimental import pallas as pl
from jax.experimental.pallas import tpu as pltpu
from jax.sharding import PartitionSpec as P

STEPS = 3
HALO = STEPS + 1
SUB = 8
LANE = 128
FIELDS = 8
GROUP = HALO * FIELDS
FOLD = LANE // GROUP
LAG = 2
MIB = 2**20
ANY = pl.BlockSpec(memory_space=pl.ANY)
VMEM = pl.BlockSpec(memory_space=pltpu.VMEM)
SMEM = pl.BlockSpec(memory_space=pltpu.SMEM)


def rows_of(shape):
    return lax.broadcasted_iota(jnp.int32, shape, 0)


def lanes_of(shape):
    return lax.broadcasted_iota(jnp.int32, shape, 1)


def east(x):
    return pltpu.roll(x, x.shape[1] - 1, 1)


def west(x):
    return pltpu.roll(x, 1, 1)


def south(x, below):
    return pltpu.roll(jnp.where(rows_of(x.shape) == 0, below, x), SUB - 1, 0)


def north(x, above):
    return pltpu.roll(jnp.where(rows_of(x.shape) == SUB - 1, above, x), 1, 0)


def tile_at(index):
    if isinstance(index, int):
        return pl.ds(index * SUB, SUB)
    return pl.ds(pl.multiple_of(index * SUB, SUB), SUB)


def held(*arrays, space=pltpu.VMEM):
    return [pltpu.with_memory_space_constraint(x, space) for x in arrays]


def cost(micros):
    return pl.CostEstimate(flops=int(micros * 10**9), bytes_accessed=0, transcendentals=0)


def raw_fields(bed, mask, kind, stress, hydro):
    return [bed, mask, kind] + [stress.at[0, k] for k in range(2)] + [hydro.at[0, k] for k in range(3)]


SPOTS = [(0, 0), (1, 0), (1, 1)] + [(0, k) for k in range(1, 6)]


def pack_side_kernel(bed, mask, kind, stress, hydro, side, reals, ints, sems):
    rows, cols = bed.shape
    at_left = lax.axis_index("tx") == 0
    off = pl.multiple_of(jnp.where(at_left, cols - LANE, 0), LANE)
    strips = [(reals, ints)[which].at[k] for which, k in SPOTS]
    copies = [
        pltpu.make_async_copy(src.at[:, pl.ds(off, LANE)], strip, sems.at[f])
        for f, (src, strip) in enumerate(zip(raw_fields(bed, mask, kind, stress, hydro), strips))
    ]
    for copy in copies:
        copy.start()
    for copy in copies:
        copy.wait()
    lift = jnp.where(at_left, HALO, 0)
    lane = lanes_of((SUB, LANE))
    span = rows // FOLD // SUB
    for i in range(span):
        total = jnp.zeros((SUB, LANE), jnp.float32)
        for g in range(FOLD):
            for f in range(FIELDS):
                place = g * FIELDS + f
                part = strips[f][tile_at(g * span + i), :].astype(jnp.float32)
                total = jnp.where(lane // HALO == place, pltpu.roll(part, lift + place * HALO, 1), total)
        side[tile_at(i), :] = total


def pack_side(*raw):
    rows, cols = raw[0].shape
    return pl.pallas_call(
        pack_side_kernel,
        name="pack_side",
        out_shape=pltpu.VMEM((rows // FOLD, LANE), jnp.float32),
        in_specs=[ANY] * 5,
        out_specs=VMEM,
        scratch_shapes=[
            pltpu.VMEM((6, rows, LANE), jnp.float32),
            pltpu.VMEM((2, rows, LANE), jnp.int32),
            pltpu.SemaphoreType.DMA((FIELDS,)),
        ],
        compiler_params=pltpu.CompilerParams(vmem_limit_bytes=4 * MIB),
        cost_estimate=cost(2),
    )(*held(*raw, space=pltpu.HBM))


def pack_rows_kernel(bed, mask, kind, stress, hydro, pays, reals, ints, sems):
    rows, cols = bed.shape
    copies = []
    for f, src in enumerate(raw_fields(bed, mask, kind, stress, hydro)):
        which, k = SPOTS[f]
        for end, start in enumerate((0, rows - SUB)):
            copies.append(
                pltpu.make_async_copy(src.at[pl.ds(start, SUB)], (reals, ints)[which].at[end, k], sems.at[f, end])
            )
    for copy in copies:
        copy.start()
    for copy in copies:
        copy.wait()
    low = rows_of((SUB, cols)) < HALO
    odd = lax.axis_index("ty") % 2
    for end in range(2):
        slot = (1 - end + odd) % 2
        for p in range(FIELDS // 2):
            both = []
            for f in (2 * p, 2 * p + 1):
                which, k = SPOTS[f]
                both.append((reals, ints)[which][end, k].astype(jnp.float32))
            both[1 - end] = pltpu.roll(both[1 - end], HALO, 0)
            pair = jnp.where(low, *both)
            for k in range(cols // LANE):
                pays[slot, pl.ds(k * GROUP + p * SUB, SUB), :] = pair[:, k * LANE : (k + 1) * LANE]


def pack_rows(*raw):
    rows, cols = raw[0].shape
    return pl.pallas_call(
        pack_rows_kernel,
        name="pack_rows",
        out_shape=pltpu.VMEM((2, cols // LANE * GROUP, LANE), jnp.float32),
        in_specs=[ANY] * 5,
        out_specs=VMEM,
        scratch_shapes=[
            pltpu.VMEM((2, 6, SUB, cols), jnp.float32),
            pltpu.VMEM((2, 2, SUB, cols), jnp.int32),
            pltpu.SemaphoreType.DMA((FIELDS, 2)),
        ],
        compiler_params=pltpu.CompilerParams(vmem_limit_bytes=4 * MIB),
        cost_estimate=cost(2),
    )(*held(*raw, space=pltpu.HBM))


def side_lanes(at_left):
    drop = jnp.where(at_left, 0, HALO)
    lane = lanes_of((SUB, LANE))
    valid = jnp.where(at_left, lane, LANE - 1 - lane) < HALO

    def unfold(strip, place):
        return pltpu.roll(strip, 2 * LANE - drop - place * HALO, 1)

    return unfold, valid


class Sweep:
    NAMES = (
        ["s", "a", "b", "fc", "fr", "wc", "wr", "e1", "u1"]
        + ["v1", "e2", "u2", "v2", "qc1", "qr1", "qc2", "qr2"]
    )

    def __init__(self, count, wide, get, emit, weights, params, refs):
        self.count, self.wide, self.get, self.emit = count, wide, get, emit
        self.__dict__.update(zip(self.NAMES + ["fr_last", "qr_last"], refs))
        cond = lax.axis_index("cond")
        self.tide = params[0, 0] - 1.0
        self.slow = 1.0 - 0.2 * params[0, 1]
        self.flow_in = 0.3 * params[0, 3]
        total = weights[0]
        for k in range(1, weights.shape[0]):
            total = total + weights[k]
        ones = jnp.ones((SUB, LANE), jnp.float32)
        share = weights[cond].astype(jnp.float32) * ones / (total.astype(jnp.float32) * ones)
        self.scale = jnp.concatenate([-4.0 * params[0, 2] * share] * (wide // LANE), axis=1)

    @classmethod
    def scratch(cls, count, wide):
        block = pltpu.VMEM(((count + 1) * SUB, wide), jnp.float32)
        return [block] * len(cls.NAMES) + [
            pltpu.VMEM((STEPS, SUB, wide), jnp.float32),
            pltpu.VMEM((SUB, wide), jnp.float32),
        ]

    def prepare(self, i):
        at = tile_at(i)
        depth = self.get(1, i).astype(jnp.float32) * (1.0 - 0.5 * jnp.tanh(self.get(0, i)))
        kinds = self.get(2, i)
        self.s[at, :] = depth * lax.rsqrt(jnp.maximum(depth, 1e-12))
        relax = jnp.where(kinds == 1, 0.5 * depth, 0.0)
        self.a[at, :] = 1.0 - relax
        self.b[at, :] = 0.3 * (relax * self.tide + jnp.where(kinds == 2, self.flow_in * depth, 0.0))

    def move(self, n, i, level, lower, u, v, fc, fr, wc, wr):
        at = tile_at(i)
        u = (self.slow * u - (east(level) - level) + self.get(3, i)) * wc
        v = (self.slow * v - (south(level, lower) - level) + self.get(4, i)) * wr
        flux_c = fc * u
        flux_r = fr * v
        out = self.a[at, :] * level + self.b[at, :] - (
            flux_c - west(flux_c) + flux_r - north(flux_r, self.fr_last[n])
        )
        self.fr_last[n] = flux_r
        return out, u, v, wc * (u * jnp.abs(u)), wr * (v * jnp.abs(v))

    def step_one(self, i):
        at, after = tile_at(i), tile_at(i + 1)
        s = self.s[at, :]
        face_c = s * east(s)
        face_r = s * south(s, self.s[after, :])
        ratios = []
        for face in (face_c, face_r):
            base = face + 0.1
            inverse = pl.reciprocal(base, approx=True)
            ratios.append(face * (inverse * (2.0 - base * inverse)))
        wc, wr = ratios
        fc = 0.3 * face_c
        fr = 0.3 * face_r
        self.fc[at, :] = fc
        self.fr[at, :] = fr
        self.wc[at, :] = wc
        self.wr[at, :] = wr
        level = 0.3 * self.get(5, i)
        lower = 0.3 * self.get(5, i + 1) if i + 1 < self.count else level
        e, u, v, qc, qr = self.move(0, i, level, lower, self.get(6, i), self.get(7, i), fc, fr, wc, wr)
        self.e1[at, :] = e
        self.u1[at, :] = u
        self.v1[at, :] = v
        self.qc1[at, :] = qc
        self.qr1[at, :] = qr

    def later(self, n, i, e, u, v):
        at, after = tile_at(i), tile_at(i + 1)
        return self.move(
            n, i, e[at, :], e[after, :], u[at, :], v[at, :],
            self.fc[at, :], self.fr[at, :], self.wc[at, :], self.wr[at, :],
        )

    def step_two(self, i):
        at = tile_at(i)
        e, u, v, qc, qr = self.later(1, i, self.e1, self.u1, self.v1)
        self.e2[at, :] = e
        self.u2[at, :] = u
        self.v2[at, :] = v
        self.qc2[at, :] = self.qc1[at, :] + qc
        self.qr2[at, :] = self.qr1[at, :] + qr

    def step_three(self, i):
        at = tile_at(i)
        e, u, v, qc, qr = self.later(2, i, self.e2, self.u2, self.v2)
        qc = self.qc2[at, :] + qc
        qr = self.qr2[at, :] + qr
        change = (qc - west(qc) + qr - north(qr, self.qr_last[...])) * self.scale
        self.qr_last[...] = qr
        self.emit(i, e * (1.0 / 0.3), u, v, change)

    def run(self):
        self.fr_last[...] = jnp.zeros_like(self.fr_last)
        self.qr_last[...] = jnp.zeros_like(self.qr_last)
        for ref in (self.s, self.e1, self.e2):
            ref[tile_at(self.count), :] = jnp.zeros((SUB, self.wide), jnp.float32)
        stages = (self.step_three, self.step_two, self.step_one, self.prepare)
        for t in range(self.count + LAG * STEPS):
            for k, stage in enumerate(stages):
                i = t - LAG * (STEPS - k)
                if 0 <= i < self.count:
                    stage(i)


def raw_reader(bed, mask, kind, stress, hydro, side, unfold, valid):
    rows = bed.shape[0]
    span = rows // FOLD // SUB
    fields = raw_fields(bed, mask, kind, stress, hydro)

    def read(f, block):
        strip = side[tile_at(block % span), :]
        part = unfold(strip, (block // span) * FIELDS + f)
        if f == 1:
            part = jnp.where(valid, part, 0.0)
        main = fields[f][tile_at(block), :]
        return jnp.concatenate([main, part.astype(main.dtype)], axis=1)

    return read


def middle_kernel(own, weights, params, bed, mask, kind, stress, hydro, side, *refs):
    hydro_out, pay, *refs = refs[1:] if own else refs
    rows, cols = bed.shape
    quarter = rows // SUB // 4
    unfold, valid = side_lanes(lax.axis_index("tx") == 0)
    read = raw_reader(bed, mask, kind, stress, hydro, side, unfold, valid)
    mine = lax.axis_index("cond") % 2
    lower_half = mine == (1 if own else 0)
    first = jnp.where(lower_half, 2 * quarter, quarter) - 1
    emit = quarter_writer(first, quarter, cols, hydro_out, pay)

    def finish(i, e, u, v, change):
        if 1 <= i <= quarter:
            emit(i, e, u, v, change)

    Sweep(quarter + 2, cols + LANE, lambda f, i: read(f, first + i), finish, weights, params, refs).run()


def quarter_writer(first, quarter, cols, hydro_out, pay):
    lane = lanes_of((SUB, LANE))
    lanes = cols // LANE
    rims = [jnp.zeros((SUB, LANE), jnp.float32)]

    def emit(i, e, u, v, change):
        at = tile_at(first + i)
        for k, value in enumerate((e, u, v)):
            hydro_out[0, k, at, :] = value[:, :cols]
        g = i - 1
        for k in range(lanes):
            pay[tile_at(k * quarter + g), :] = change[:, k * LANE : (k + 1) * LANE]
        rims[0] = jnp.where(lane // 2 == g, pltpu.roll(change[:, cols:], 1 + 2 * g, 1), rims[0])
        if g == quarter - 1:
            pay[tile_at(lanes * quarter), :] = rims[0]

    return emit


def middle(own, weights, params, raw, side, hydro=None):
    rows, cols = raw[0].shape
    given = (hydro,) if own else ()
    return pl.pallas_call(
        functools.partial(middle_kernel, own),
        name="middle_own" if own else "middle_other",
        out_shape=[
            pltpu.VMEM(raw[4].shape, jnp.float32),
            pltpu.VMEM((cols // LANE * rows // 4 + SUB, LANE), jnp.float32),
        ],
        in_specs=[SMEM, SMEM] + [VMEM] * (6 + own),
        out_specs=[VMEM, VMEM],
        scratch_shapes=Sweep.scratch(rows // SUB // 4 + 2, cols + LANE),
        input_output_aliases={8: 0} if own else {},
        compiler_params=pltpu.CompilerParams(vmem_limit_bytes=10 * MIB),
        cost_estimate=cost(4),
    )(weights, params, *held(*raw, side, *given))


def edge_kernel(
    own, weights, params, bed, mask, kind, stress, hydro, side, far_a, far_b, hydro_in,
    hydro_out, pay, ends_r, ends_i, *refs,
):
    rows, cols = bed.shape
    blocks = rows // SUB
    quarter = blocks // 4
    wide = cols + LANE
    lanes = cols // LANE
    unfold, valid = side_lanes(lax.axis_index("tx") == 0)
    read = raw_reader(bed, mask, kind, stress, hydro, side, unfold, valid)
    mine = lax.axis_index("cond") % 2
    top = mine == (0 if own else 1)
    from_a = top == (lax.axis_index("ty") % 2 == 1)
    first = jnp.where(top, -1, blocks - quarter - 1)

    inner = jnp.where(top, quarter, blocks - quarter - 1)
    for f in range(FIELDS):
        body = read(f, inner)
        parts = []
        for k in range(lanes):
            at = pl.ds(k * GROUP + f // 2 * SUB, SUB)
            part = jnp.where(from_a, far_a[at, :], far_b[at, :])
            moved = pltpu.roll(part, HALO, 0)
            parts.append(jnp.where(top, moved, part) if f % 2 == 0 else jnp.where(top, part, moved))
        at = pl.ds(lanes * GROUP, SUB)
        corner = jnp.where(from_a, far_a[at, :], far_b[at, :])
        corner = jnp.where(top, unfold(corner, (FOLD - 1) * FIELDS + f), unfold(corner, f))
        if f == 1:
            corner = jnp.where(valid, corner, 0.0)
        outer = jnp.concatenate(parts + [corner], axis=1).astype(body.dtype)
        which, k = SPOTS[f]
        ref = (ends_r, ends_i)[which]
        ref[0, k] = jnp.where(top, outer, body)
        ref[1, k] = jnp.where(top, body, outer)

    def get(f, i):
        if i == 0 or i == quarter + 1:
            which, k = SPOTS[f]
            return (ends_r, ends_i)[which][0 if i == 0 else 1, k]
        return read(f, first + i)

    row = rows_of((SUB, LANE))
    emit = quarter_writer(first, quarter, cols, hydro_out, pay)
    outside = []

    def finish(i, e, u, v, change):
        if i == 0:
            outside.append(pltpu.roll(change, 1, 0))
        elif i == quarter + 1:
            rim = jnp.where(top, outside[0], change)
            total = rim[:, :LANE]
            for k in range(1, lanes):
                total = jnp.where(row == k, pltpu.roll(rim[:, k * LANE : (k + 1) * LANE], k, 0), total)
            pay[tile_at(lanes * quarter + 1), :] = total
        else:
            emit(i, e, u, v, change)

    Sweep(quarter + 2, wide, get, finish, weights, params, refs).run()


def edge(own, weights, params, raw, side, far_a, far_b, hydro):
    rows, cols = raw[0].shape
    wide = cols + LANE
    return pl.pallas_call(
        functools.partial(edge_kernel, own),
        name="edge_own" if own else "edge_other",
        out_shape=[
            pltpu.VMEM(hydro.shape, jnp.float32),
            pltpu.VMEM((cols // LANE * rows // 4 + 2 * SUB, LANE), jnp.float32),
        ],
        in_specs=[SMEM, SMEM] + [VMEM] * 9,
        out_specs=[VMEM, VMEM],
        scratch_shapes=[pltpu.VMEM((2, 6, SUB, wide), jnp.float32), pltpu.VMEM((2, 2, SUB, wide), jnp.int32)]
        + Sweep.scratch(rows // SUB // 4 + 2, wide),
        input_output_aliases={10: 0},
        compiler_params=pltpu.CompilerParams(vmem_limit_bytes=12 * MIB),
        cost_estimate=cost(4),
    )(weights, params, *held(*raw, side, far_a, far_b, hydro))


class Update:
    def __init__(self, bed, side, far_a, far_b, own_m, got_m, own_e, got_e, change_v, next_v):
        self.bed, self.side, self.far_a, self.far_b = bed, side, far_a, far_b
        self.parts = {"m": (own_m, got_m), "e": (own_e, got_e)}
        self.change_v, self.next_v = change_v, next_v
        rows, self.cols = bed.shape
        self.blocks = rows // SUB
        self.quarter = self.blocks // 4
        self.lanes = self.cols // LANE
        self.wide = self.cols + LANE
        self.unfold, _ = side_lanes(lax.axis_index("tx") == 0)
        self.mine = lax.axis_index("cond") % 2
        self.odd = lax.axis_index("ty") % 2 == 1
        col = lanes_of((SUB, self.wide))
        last_c = lax.axis_index("tx") == lax.axis_size("tx") - 1
        first_c = lax.axis_index("tx") == 0
        self.shut_c = (last_c & (col == self.cols - 1)) | (first_c & (col == self.wide - 1))
        self.last_row = rows_of((SUB, self.wide)) == SUB - 1
        self.rims = {}

    def merged(self, q, block):
        own, got = self.parts["e" if q in (0, 3) else "m"]
        at = tile_at(block)
        return jnp.where(self.mine == q // 2, own[at, :], got[at, :])

    def outside(self, q):
        rim = self.merged(q, self.lanes * self.quarter + 1)
        parts = []
        for k in range(self.lanes):
            at = tile_at(k * GROUP // SUB)
            a, b = self.far_a[at, :], self.far_b[at, :]
            if q == 0:
                z = jnp.where(self.odd, a, b) + pltpu.roll(rim, (2 * SUB + HALO - 1 - k) % SUB, 0)
                parts.append(pltpu.roll(z, HALO, 0))
            else:
                parts.append(jnp.where(self.odd, b, a) + pltpu.roll(rim, (SUB - k) % SUB, 0))
        return jnp.concatenate(parts + [jnp.zeros((SUB, LANE), jnp.float32)], axis=1)

    def level(self, b, keep):
        if b == -1:
            return self.outside(0)
        if b == self.blocks:
            return self.outside(3)
        q, g = divmod(b, self.quarter)
        change = jnp.concatenate([self.merged(q, k * self.quarter + g) for k in range(self.lanes)], axis=1)
        if keep:
            self.change_v[tile_at(b), :] = change
        if q not in self.rims:
            self.rims[q] = self.merged(q, self.lanes * self.quarter)
        span = self.blocks // FOLD
        cols_bed = self.unfold(self.side[tile_at(b % span), :], b // span * FIELDS)
        cols_change = pltpu.roll(self.rims[q], LANE - 1 - 2 * g, 1)
        return jnp.concatenate([self.bed[tile_at(b), :] + change, cols_bed + cols_change], axis=1)

    def spill(self, slope):
        return 0.25 * (slope - jnp.clip(slope, -1.0, 1.0))

    def south_face(self, z, lower, b):
        out = self.spill(south(z, lower) - z)
        if b == -1:
            return jnp.where((lax.axis_index("ty") == 0) & self.last_row, 0.0, out)
        if b == self.blocks - 1:
            return jnp.where((lax.axis_index("ty") == lax.axis_size("ty") - 1) & self.last_row, 0.0, out)
        return out

    def run(self, first, stop, keep, after=lambda b: None):
        z = self.level(first - 1, keep)
        lower = self.level(first, keep)
        gr = self.south_face(z, lower, first - 1)
        for b in range(first, stop):
            z, lower = lower, self.level(b + 1, keep)
            gr_above, gr = gr, self.south_face(z, lower, b)
            gc = jnp.where(self.shut_c, 0.0, self.spill(east(z) - z))
            out = z + gc - west(gc) + gr - north(gr, gr_above)
            self.next_v[tile_at(b), :] = out[:, : self.cols]
            after(b)


def bed_middle_kernel(
    bed, side, far_a, far_b, own_m, got_m, hydro, bed_next, bed_change, hydro_out, change_v, next_v, sems
):
    rows = bed.shape[0]
    quarter = rows // SUB // 4
    copies = [pltpu.make_async_copy(hydro, hydro_out, sems.at[0])]
    copies[0].start()
    update = Update(bed, side, far_a, far_b, own_m, got_m, None, None, change_v, next_v)
    update.run(quarter + 1, 3 * quarter - 1, True)
    for src, dst, low, high in (
        (change_v, bed_change, quarter, 3 * quarter),
        (next_v, bed_next, quarter + 1, 3 * quarter - 1),
    ):
        at = pl.ds(low * SUB, (high - low) * SUB)
        copies.append(pltpu.make_async_copy(src.at[at], dst.at[at], sems.at[len(copies)]))
        copies[-1].start()
    for copy in copies:
        copy.wait()


def bed_edge_kernel(
    bed, side, far_a, far_b, own_m, got_m, own_e, got_e, next_in, change_in, bed_next, bed_change,
    change_v, next_v, sems,
):
    rows = bed.shape[0]
    blocks = rows // SUB
    quarter = blocks // 4
    update = Update(bed, side, far_a, far_b, own_m, got_m, own_e, got_e, change_v, next_v)
    copies = []

    def send(src, dst, low, high):
        at = pl.ds(low * SUB, (high - low) * SUB)
        copies.append(pltpu.make_async_copy(src.at[at], dst.at[at], sems.at[len(copies)]))
        copies[-1].start()

    update.run(0, quarter + 1, True)
    send(change_v, bed_change, 0, quarter)
    send(next_v, bed_next, 0, quarter + 1)
    update.run(blocks - quarter - 1, blocks, True)
    send(change_v, bed_change, blocks - quarter, blocks)
    send(next_v, bed_next, blocks - quarter - 1, blocks)
    for copy in copies:
        copy.wait()


def bed_scratch(rows, cols):
    return [
        pltpu.VMEM((rows, cols), jnp.float32),
        pltpu.VMEM((rows, cols), jnp.float32),
        pltpu.SemaphoreType.DMA((4,)),
    ]


def bed_middle(bed, side, far_a, far_b, own_m, got_m, hydro):
    return pl.pallas_call(
        bed_middle_kernel,
        name="bed_middle",
        out_shape=[pltpu.HBM(x.shape, jnp.float32) for x in (bed, bed, hydro)],
        in_specs=[VMEM] * 7,
        out_specs=[ANY] * 3,
        scratch_shapes=bed_scratch(*bed.shape),
        compiler_params=pltpu.CompilerParams(vmem_limit_bytes=6 * MIB),
        cost_estimate=cost(4),
    )(*held(bed, side, far_a, far_b, own_m, got_m, hydro))


def bed_edge(bed, side, far_a, far_b, own_m, got_m, own_e, got_e, bed_next, bed_change):
    return pl.pallas_call(
        bed_edge_kernel,
        name="bed_edge",
        out_shape=[pltpu.HBM(bed.shape, jnp.float32)] * 2,
        in_specs=[VMEM] * 8 + [ANY] * 2,
        out_specs=[ANY] * 2,
        scratch_shapes=bed_scratch(*bed.shape),
        input_output_aliases={8: 0, 9: 1},
        compiler_params=pltpu.CompilerParams(vmem_limit_bytes=6 * MIB),
        cost_estimate=cost(2),
    )(
        *held(bed, side, far_a, far_b, own_m, got_m, own_e, got_e),
        *held(bed_next, bed_change, space=pltpu.HBM),
    )


def shards(bed, land_mask, cell_class, weights, cond_params, wave_stress, hydro_state):
    ny = lax.axis_size("ty")
    nc = lax.axis_size("cond")
    raw = (bed, land_mask, cell_class, wave_stress, hydro_state)
    swap = [(i, i ^ 1) for i in range(nc)]

    def pairs(first):
        return [p for i in range(first, ny - 1, 2) for p in ((i, i + 1), (i + 1, i))]

    def over_chips(part, beside=()):
        reach = 2
        while reach < nc:
            got = lax.ppermute(part, "cond", [(i, i ^ reach) for i in range(nc)])
            got, beside = lax.optimization_barrier((got, beside))
            part = part + got
            reach = 2 * reach
        return part, beside

    side = lax.ppermute(pack_side(*raw), "tx", [(0, 1), (1, 0)])
    pays = pack_rows(*raw)
    odd = lax.axis_index("ty") % 2 == 1
    corners = [side[:SUB], side[-SUB:]]
    far_a = jnp.concatenate([pays[0], jnp.where(odd, corners[0], corners[1])])
    far_b = jnp.concatenate([pays[1], jnp.where(odd, corners[1], corners[0])])
    far_a = lax.ppermute(far_a, "ty", pairs(0))
    hydro, pay = middle(False, weights, cond_params, raw, side)
    hydro, far_b = lax.optimization_barrier((hydro, far_b))
    far_b = lax.ppermute(far_b, "ty", pairs(1))
    got = lax.ppermute(pay, "cond", swap)
    hydro, pay = middle(True, weights, cond_params, raw, side, hydro)
    part_m = pay + got
    hydro, part_m = lax.optimization_barrier((hydro, part_m))
    hydro, pay = edge(False, weights, cond_params, raw, side, far_a, far_b, hydro)
    got = lax.ppermute(pay, "cond", swap)
    hydro, pay = edge(True, weights, cond_params, raw, side, far_a, far_b, hydro)
    own_m, hydro = over_chips(part_m, hydro)
    part_e = pay + got
    got_m = lax.ppermute(own_m, "cond", swap)
    bed_next, bed_change, hydro = bed_middle(bed, side, far_a, far_b, own_m, got_m, hydro)
    own_e, (bed_next, bed_change) = over_chips(part_e, (bed_next, bed_change))
    got_e = lax.ppermute(own_e, "cond", swap)
    bed_next, bed_change = bed_edge(
        bed, side, far_a, far_b, own_m, got_m, own_e, got_e, bed_next, bed_change
    )
    return bed_next, bed_change, hydro


def solution(mesh):
    in_specs = (
        P("ty", "tx"),
        P("ty", "tx"),
        P("ty", "tx"),
        P(),
        P("cond", None),
        P("cond", None, "ty", "tx"),
        P("cond", None, "ty", "tx"),
    )
    out_specs = (P("ty", "tx"), P("ty", "tx"), P("cond", None, "ty", "tx"))
    return jax.shard_map(shards, mesh=mesh, in_specs=in_specs, out_specs=out_specs, check_vma=False)
```

```python
import functools

import jax
import jax.numpy as jnp
from jax import lax
from jax.experimental import pallas as pl
from jax.experimental.pallas import tpu as pltpu
from jax.sharding import PartitionSpec as P

STEPS = 3
HALO = STEPS + 1
SUB = 8
LANE = 128
FIELDS = 8
GROUP = HALO * FIELDS
FOLD = LANE // GROUP
LAG = 2
MIB = 2**20
ANY = pl.BlockSpec(memory_space=pl.ANY)
VMEM = pl.BlockSpec(memory_space=pltpu.VMEM)
SMEM = pl.BlockSpec(memory_space=pltpu.SMEM)


def rows_of(shape):
    return lax.broadcasted_iota(jnp.int32, shape, 0)


def lanes_of(shape):
    return lax.broadcasted_iota(jnp.int32, shape, 1)


def east(x):
    return pltpu.roll(x, x.shape[1] - 1, 1)


def west(x):
    return pltpu.roll(x, 1, 1)


def south(x, below):
    return pltpu.roll(jnp.where(rows_of(x.shape) == 0, below, x), SUB - 1, 0)


def north(x, above):
    return pltpu.roll(jnp.where(rows_of(x.shape) == SUB - 1, above, x), 1, 0)


def tile_at(index):
    if isinstance(index, int):
        return pl.ds(index * SUB, SUB)
    return pl.ds(pl.multiple_of(index * SUB, SUB), SUB)


def held(*arrays, space=pltpu.VMEM):
    return [pltpu.with_memory_space_constraint(x, space) for x in arrays]


def cost(micros):
    return pl.CostEstimate(flops=int(micros * 10**9), bytes_accessed=0, transcendentals=0)


def raw_fields(bed, mask, kind, stress, hydro):
    return [bed, mask, kind] + [stress.at[0, k] for k in range(2)] + [hydro.at[0, k] for k in range(3)]


SPOTS = [(0, 0), (1, 0), (1, 1)] + [(0, k) for k in range(1, 6)]


def pack_side_kernel(bed, mask, kind, stress, hydro, side, reals, ints, sems):
    rows, cols = bed.shape
    at_left = lax.axis_index("tx") == 0
    off = pl.multiple_of(jnp.where(at_left, cols - LANE, 0), LANE)
    strips = [(reals, ints)[which].at[k] for which, k in SPOTS]
    copies = [
        pltpu.make_async_copy(src.at[:, pl.ds(off, LANE)], strip, sems.at[f])
        for f, (src, strip) in enumerate(zip(raw_fields(bed, mask, kind, stress, hydro), strips))
    ]
    for copy in copies:
        copy.start()
    for copy in copies:
        copy.wait()
    lift = jnp.where(at_left, HALO, 0)
    lane = lanes_of((SUB, LANE))
    span = rows // FOLD // SUB
    for i in range(span):
        total = jnp.zeros((SUB, LANE), jnp.float32)
        for g in range(FOLD):
            for f in range(FIELDS):
                place = g * FIELDS + f
                part = strips[f][tile_at(g * span + i), :].astype(jnp.float32)
                total = jnp.where(lane // HALO == place, pltpu.roll(part, lift + place * HALO, 1), total)
        side[tile_at(i), :] = total


def pack_side(*raw):
    rows, cols = raw[0].shape
    return pl.pallas_call(
        pack_side_kernel,
        name="pack_side",
        out_shape=pltpu.VMEM((rows // FOLD, LANE), jnp.float32),
        in_specs=[ANY] * 5,
        out_specs=VMEM,
        scratch_shapes=[
            pltpu.VMEM((6, rows, LANE), jnp.float32),
            pltpu.VMEM((2, rows, LANE), jnp.int32),
            pltpu.SemaphoreType.DMA((FIELDS,)),
        ],
        compiler_params=pltpu.CompilerParams(vmem_limit_bytes=4 * MIB),
        cost_estimate=cost(2),
    )(*held(*raw, space=pltpu.HBM))


def load_kernel(bed, mask, kind, stress, hydro, *refs):
    raw, (pays, reals, ints, edge_sems, load_sems) = refs[:5], refs[5:]
    rows, cols = bed.shape
    sources = raw_fields(bed, mask, kind, stress, hydro)
    edges, loads = [], []
    for f, (src, dst) in enumerate(zip(sources, raw_fields(*raw))):
        which, k = SPOTS[f]
        for end, start in enumerate((0, rows - SUB)):
            edges.append(
                pltpu.make_async_copy(src.at[pl.ds(start, SUB)], (reals, ints)[which].at[end, k], edge_sems.at[f, end])
            )
            at = pl.ds(end * (rows // 2), rows // 2)
            loads.append(pltpu.make_async_copy(src.at[at], dst.at[at], load_sems.at[f, end]))
    for copy in edges + loads:
        copy.start()
    for copy in edges:
        copy.wait()
    low = rows_of((SUB, cols)) < HALO
    odd = lax.axis_index("ty") % 2
    for end in range(2):
        slot = (1 - end + odd) % 2
        for p in range(FIELDS // 2):
            both = []
            for f in (2 * p, 2 * p + 1):
                which, k = SPOTS[f]
                both.append((reals, ints)[which][end, k].astype(jnp.float32))
            both[1 - end] = pltpu.roll(both[1 - end], HALO, 0)
            pair = jnp.where(low, *both)
            for k in range(cols // LANE):
                pays[slot, pl.ds(k * GROUP + p * SUB, SUB), :] = pair[:, k * LANE : (k + 1) * LANE]
    for copy in loads:
        copy.wait()


def load(*raw):
    rows, cols = raw[0].shape
    *held_raw, pays = pl.pallas_call(
        load_kernel,
        name="load",
        out_shape=[pltpu.VMEM(x.shape, x.dtype) for x in raw]
        + [pltpu.VMEM((2, cols // LANE * GROUP, LANE), jnp.float32)],
        in_specs=[ANY] * 5,
        out_specs=[VMEM] * 6,
        scratch_shapes=[
            pltpu.VMEM((2, 6, SUB, cols), jnp.float32),
            pltpu.VMEM((2, 2, SUB, cols), jnp.int32),
            pltpu.SemaphoreType.DMA((FIELDS, 2)),
            pltpu.SemaphoreType.DMA((FIELDS, 2)),
        ],
        compiler_params=pltpu.CompilerParams(vmem_limit_bytes=4 * MIB),
        cost_estimate=cost(4),
    )(*held(*raw, space=pltpu.HBM))
    return held_raw, pays


def side_lanes(at_left):
    drop = jnp.where(at_left, 0, HALO)
    lane = lanes_of((SUB, LANE))
    valid = jnp.where(at_left, lane, LANE - 1 - lane) < HALO

    def unfold(strip, place):
        return pltpu.roll(strip, 2 * LANE - drop - place * HALO, 1)

    return unfold, valid


class Sweep:
    NAMES = (
        ["s", "a", "b", "fc", "fr", "wc", "wr", "e1", "u1"]
        + ["v1", "e2", "u2", "v2", "qc1", "qr1", "qc2", "qr2"]
    )

    def __init__(self, count, wide, get, emit, weights, params, refs):
        self.count, self.wide, self.get, self.emit = count, wide, get, emit
        self.__dict__.update(zip(self.NAMES + ["fr_last", "qr_last"], refs))
        cond = lax.axis_index("cond")
        self.tide = params[0, 0] - 1.0
        self.slow = 1.0 - 0.2 * params[0, 1]
        self.flow_in = 0.3 * params[0, 3]
        total = weights[0]
        for k in range(1, weights.shape[0]):
            total = total + weights[k]
        ones = jnp.ones((SUB, LANE), jnp.float32)
        share = weights[cond].astype(jnp.float32) * ones / (total.astype(jnp.float32) * ones)
        self.scale = jnp.concatenate([-4.0 * params[0, 2] * share] * (wide // LANE), axis=1)

    @classmethod
    def scratch(cls, count, wide):
        block = pltpu.VMEM(((count + 1) * SUB, wide), jnp.float32)
        return [block] * len(cls.NAMES) + [
            pltpu.VMEM((STEPS, SUB, wide), jnp.float32),
            pltpu.VMEM((SUB, wide), jnp.float32),
        ]

    def prepare(self, i):
        at = tile_at(i)
        depth = self.get(1, i).astype(jnp.float32) * (1.0 - 0.5 * jnp.tanh(self.get(0, i)))
        kinds = self.get(2, i)
        self.s[at, :] = depth * lax.rsqrt(jnp.maximum(depth, 1e-12))
        relax = jnp.where(kinds == 1, 0.5 * depth, 0.0)
        self.a[at, :] = 1.0 - relax
        self.b[at, :] = 0.3 * (relax * self.tide + jnp.where(kinds == 2, self.flow_in * depth, 0.0))

    def move(self, n, i, level, lower, u, v, fc, fr, wc, wr):
        at = tile_at(i)
        u = (self.slow * u - (east(level) - level) + self.get(3, i)) * wc
        v = (self.slow * v - (south(level, lower) - level) + self.get(4, i)) * wr
        flux_c = fc * u
        flux_r = fr * v
        out = self.a[at, :] * level + self.b[at, :] - (
            flux_c - west(flux_c) + flux_r - north(flux_r, self.fr_last[n])
        )
        self.fr_last[n] = flux_r
        return out, u, v, u * jnp.abs(u), v * jnp.abs(v)

    def step_one(self, i):
        at, after = tile_at(i), tile_at(i + 1)
        s = self.s[at, :]
        face_c = s * east(s)
        face_r = s * south(s, self.s[after, :])
        ratios = []
        for face in (face_c, face_r):
            base = face + 0.1
            inverse = pl.reciprocal(base, approx=True)
            ratios.append(face * (inverse * (2.0 - base * inverse)))
        wc, wr = ratios
        fc = 0.3 * face_c
        fr = 0.3 * face_r
        self.fc[at, :] = fc
        self.fr[at, :] = fr
        self.wc[at, :] = wc
        self.wr[at, :] = wr
        level = 0.3 * self.get(5, i)
        lower = 0.3 * self.get(5, i + 1) if i + 1 < self.count else level
        e, u, v, qc, qr = self.move(0, i, level, lower, self.get(6, i), self.get(7, i), fc, fr, wc, wr)
        self.e1[at, :] = e
        self.u1[at, :] = u
        self.v1[at, :] = v
        self.qc1[at, :] = qc
        self.qr1[at, :] = qr

    def later(self, n, i, e, u, v):
        at, after = tile_at(i), tile_at(i + 1)
        return self.move(
            n, i, e[at, :], e[after, :], u[at, :], v[at, :],
            self.fc[at, :], self.fr[at, :], self.wc[at, :], self.wr[at, :],
        )

    def step_two(self, i):
        at = tile_at(i)
        e, u, v, qc, qr = self.later(1, i, self.e1, self.u1, self.v1)
        self.e2[at, :] = e
        self.u2[at, :] = u
        self.v2[at, :] = v
        self.qc2[at, :] = self.qc1[at, :] + qc
        self.qr2[at, :] = self.qr1[at, :] + qr

    def step_three(self, i):
        at = tile_at(i)
        e, u, v, qc, qr = self.later(2, i, self.e2, self.u2, self.v2)
        qc = self.wc[at, :] * (self.qc2[at, :] + qc)
        qr = self.wr[at, :] * (self.qr2[at, :] + qr)
        change = (qc - west(qc) + qr - north(qr, self.qr_last[...])) * self.scale
        self.qr_last[...] = qr
        self.emit(i, e * (1.0 / 0.3), u, v, change)

    def run(self):
        self.fr_last[...] = jnp.zeros_like(self.fr_last)
        self.qr_last[...] = jnp.zeros_like(self.qr_last)
        for ref in (self.s, self.e1, self.e2):
            ref[tile_at(self.count), :] = jnp.zeros((SUB, self.wide), jnp.float32)
        stages = (self.step_three, self.step_two, self.step_one, self.prepare)
        for t in range(self.count + LAG * STEPS):
            for k, stage in enumerate(stages):
                i = t - LAG * (STEPS - k)
                if 0 <= i < self.count:
                    stage(i)


def raw_reader(bed, mask, kind, stress, hydro, side, unfold, valid):
    rows = bed.shape[0]
    span = rows // FOLD // SUB
    fields = raw_fields(bed, mask, kind, stress, hydro)

    def read(f, block):
        strip = side[tile_at(block % span), :]
        part = unfold(strip, (block // span) * FIELDS + f)
        if f == 1:
            part = jnp.where(valid, part, 0.0)
        main = fields[f][tile_at(block), :]
        return jnp.concatenate([main, part.astype(main.dtype)], axis=1)

    return read


def middle_kernel(own, weights, params, bed, mask, kind, stress, hydro, side, *refs):
    hydro_out, pay, *refs = refs[1:] if own else refs
    rows, cols = bed.shape
    quarter = rows // SUB // 4
    unfold, valid = side_lanes(lax.axis_index("tx") == 0)
    read = raw_reader(bed, mask, kind, stress, hydro, side, unfold, valid)
    mine = lax.axis_index("cond") % 2
    lower_half = mine == (1 if own else 0)
    first = jnp.where(lower_half, 2 * quarter, quarter) - 1
    emit = quarter_writer(first, quarter, cols, hydro_out, pay)

    def finish(i, e, u, v, change):
        if 1 <= i <= quarter:
            emit(i, e, u, v, change)

    Sweep(quarter + 2, cols + LANE, lambda f, i: read(f, first + i), finish, weights, params, refs).run()


def quarter_writer(first, quarter, cols, hydro_out, pay):
    lane = lanes_of((SUB, LANE))
    lanes = cols // LANE
    rims = [jnp.zeros((SUB, LANE), jnp.float32)]

    def emit(i, e, u, v, change):
        at = tile_at(first + i)
        for k, value in enumerate((e, u, v)):
            hydro_out[0, k, at, :] = value[:, :cols]
        g = i - 1
        for k in range(lanes):
            pay[tile_at(k * quarter + g), :] = change[:, k * LANE : (k + 1) * LANE]
        rims[0] = jnp.where(lane // 2 == g, pltpu.roll(change[:, cols:], 1 + 2 * g, 1), rims[0])
        if g == quarter - 1:
            pay[tile_at(lanes * quarter), :] = rims[0]

    return emit


def middle(own, weights, params, raw, side, hydro=None):
    rows, cols = raw[0].shape
    given = (hydro,) if own else ()
    return pl.pallas_call(
        functools.partial(middle_kernel, own),
        name="middle_own" if own else "middle_other",
        out_shape=[
            pltpu.VMEM(raw[4].shape, jnp.float32),
            pltpu.VMEM((cols // LANE * rows // 4 + SUB, LANE), jnp.float32),
        ],
        in_specs=[SMEM, SMEM] + [VMEM] * (6 + own),
        out_specs=[VMEM, VMEM],
        scratch_shapes=Sweep.scratch(rows // SUB // 4 + 2, cols + LANE),
        input_output_aliases={8: 0} if own else {},
        compiler_params=pltpu.CompilerParams(vmem_limit_bytes=10 * MIB),
        cost_estimate=cost(4),
    )(weights, params, *held(*raw, side, *given))


def edge_kernel(
    own, weights, params, bed, mask, kind, stress, hydro, side, far_a, far_b, hydro_in,
    hydro_out, pay, ends_r, ends_i, *refs,
):
    rows, cols = bed.shape
    blocks = rows // SUB
    quarter = blocks // 4
    wide = cols + LANE
    lanes = cols // LANE
    unfold, valid = side_lanes(lax.axis_index("tx") == 0)
    read = raw_reader(bed, mask, kind, stress, hydro, side, unfold, valid)
    mine = lax.axis_index("cond") % 2
    top = mine == (0 if own else 1)
    from_a = top == (lax.axis_index("ty") % 2 == 1)
    first = jnp.where(top, -1, blocks - quarter - 1)

    inner = jnp.where(top, quarter, blocks - quarter - 1)
    for f in range(FIELDS):
        body = read(f, inner)
        parts = []
        for k in range(lanes):
            at = pl.ds(k * GROUP + f // 2 * SUB, SUB)
            part = jnp.where(from_a, far_a[at, :], far_b[at, :])
            moved = pltpu.roll(part, HALO, 0)
            parts.append(jnp.where(top, moved, part) if f % 2 == 0 else jnp.where(top, part, moved))
        at = pl.ds(lanes * GROUP, SUB)
        corner = jnp.where(from_a, far_a[at, :], far_b[at, :])
        corner = jnp.where(top, unfold(corner, (FOLD - 1) * FIELDS + f), unfold(corner, f))
        if f == 1:
            corner = jnp.where(valid, corner, 0.0)
        outer = jnp.concatenate(parts + [corner], axis=1).astype(body.dtype)
        which, k = SPOTS[f]
        ref = (ends_r, ends_i)[which]
        ref[0, k] = jnp.where(top, outer, body)
        ref[1, k] = jnp.where(top, body, outer)

    def get(f, i):
        if i == 0 or i == quarter + 1:
            which, k = SPOTS[f]
            return (ends_r, ends_i)[which][0 if i == 0 else 1, k]
        return read(f, first + i)

    row = rows_of((SUB, LANE))
    emit = quarter_writer(first, quarter, cols, hydro_out, pay)
    outside = []

    def finish(i, e, u, v, change):
        if i == 0:
            outside.append(pltpu.roll(change, 1, 0))
        elif i == quarter + 1:
            rim = jnp.where(top, outside[0], change)
            total = rim[:, :LANE]
            for k in range(1, lanes):
                total = jnp.where(row == k, pltpu.roll(rim[:, k * LANE : (k + 1) * LANE], k, 0), total)
            pay[tile_at(lanes * quarter + 1), :] = total
        else:
            emit(i, e, u, v, change)

    Sweep(quarter + 2, wide, get, finish, weights, params, refs).run()


def edge(own, weights, params, raw, side, far_a, far_b, hydro):
    rows, cols = raw[0].shape
    wide = cols + LANE
    return pl.pallas_call(
        functools.partial(edge_kernel, own),
        name="edge_own" if own else "edge_other",
        out_shape=[
            pltpu.VMEM(hydro.shape, jnp.float32),
            pltpu.VMEM((cols // LANE * rows // 4 + 2 * SUB, LANE), jnp.float32),
        ],
        in_specs=[SMEM, SMEM] + [VMEM] * 9,
        out_specs=[VMEM, VMEM],
        scratch_shapes=[pltpu.VMEM((2, 6, SUB, wide), jnp.float32), pltpu.VMEM((2, 2, SUB, wide), jnp.int32)]
        + Sweep.scratch(rows // SUB // 4 + 2, wide),
        input_output_aliases={10: 0},
        compiler_params=pltpu.CompilerParams(vmem_limit_bytes=12 * MIB),
        cost_estimate=cost(3),
    )(weights, params, *held(*raw, side, far_a, far_b, hydro))


class Update:
    def __init__(self, bed, side, far_a, far_b, own_m, got_m, own_e, got_e, change_v, next_v):
        self.bed, self.side, self.far_a, self.far_b = bed, side, far_a, far_b
        self.parts = {"m": (own_m, got_m), "e": (own_e, got_e)}
        self.change_v, self.next_v = change_v, next_v
        rows, self.cols = bed.shape
        self.blocks = rows // SUB
        self.quarter = self.blocks // 4
        self.lanes = self.cols // LANE
        self.wide = self.cols + LANE
        self.unfold, _ = side_lanes(lax.axis_index("tx") == 0)
        self.mine = lax.axis_index("cond") % 2
        self.odd = lax.axis_index("ty") % 2 == 1
        col = lanes_of((SUB, self.wide))
        last_c = lax.axis_index("tx") == lax.axis_size("tx") - 1
        first_c = lax.axis_index("tx") == 0
        self.shut_c = (last_c & (col == self.cols - 1)) | (first_c & (col == self.wide - 1))
        self.last_row = rows_of((SUB, self.wide)) == SUB - 1
        self.rims = {}

    def merged(self, q, block):
        own, got = self.parts["e" if q in (0, 3) else "m"]
        at = tile_at(block)
        return jnp.where(self.mine == q // 2, own[at, :], got[at, :])

    def outside(self, q):
        rim = self.merged(q, self.lanes * self.quarter + 1)
        parts = []
        for k in range(self.lanes):
            at = tile_at(k * GROUP // SUB)
            a, b = self.far_a[at, :], self.far_b[at, :]
            if q == 0:
                z = jnp.where(self.odd, a, b) + pltpu.roll(rim, (2 * SUB + HALO - 1 - k) % SUB, 0)
                parts.append(pltpu.roll(z, HALO, 0))
            else:
                parts.append(jnp.where(self.odd, b, a) + pltpu.roll(rim, (SUB - k) % SUB, 0))
        return jnp.concatenate(parts + [jnp.zeros((SUB, LANE), jnp.float32)], axis=1)

    def level(self, b, keep):
        if b == -1:
            return self.outside(0)
        if b == self.blocks:
            return self.outside(3)
        q, g = divmod(b, self.quarter)
        change = jnp.concatenate([self.merged(q, k * self.quarter + g) for k in range(self.lanes)], axis=1)
        if keep:
            self.change_v[tile_at(b), :] = change
        if q not in self.rims:
            self.rims[q] = self.merged(q, self.lanes * self.quarter)
        span = self.blocks // FOLD
        cols_bed = self.unfold(self.side[tile_at(b % span), :], b // span * FIELDS)
        cols_change = pltpu.roll(self.rims[q], LANE - 1 - 2 * g, 1)
        return jnp.concatenate([self.bed[tile_at(b), :] + change, cols_bed + cols_change], axis=1)

    def spill(self, slope):
        return 0.25 * (slope - jnp.clip(slope, -1.0, 1.0))

    def south_face(self, z, lower, b):
        out = self.spill(south(z, lower) - z)
        if b == -1:
            return jnp.where((lax.axis_index("ty") == 0) & self.last_row, 0.0, out)
        if b == self.blocks - 1:
            return jnp.where((lax.axis_index("ty") == lax.axis_size("ty") - 1) & self.last_row, 0.0, out)
        return out

    def run(self, first, stop, keep, after=lambda b: None):
        z = self.level(first - 1, keep)
        lower = self.level(first, keep)
        gr = self.south_face(z, lower, first - 1)
        for b in range(first, stop):
            z, lower = lower, self.level(b + 1, keep)
            gr_above, gr = gr, self.south_face(z, lower, b)
            gc = jnp.where(self.shut_c, 0.0, self.spill(east(z) - z))
            out = z + gc - west(gc) + gr - north(gr, gr_above)
            self.next_v[tile_at(b), :] = out[:, : self.cols]
            after(b)


def bed_middle_kernel(
    bed, side, far_a, far_b, own_m, got_m, hydro, bed_next, bed_change, hydro_out, change_v, next_v, sems
):
    rows = bed.shape[0]
    quarter = rows // SUB // 4
    copies = [pltpu.make_async_copy(hydro, hydro_out, sems.at[0])]
    copies[0].start()
    update = Update(bed, side, far_a, far_b, own_m, got_m, None, None, change_v, next_v)
    update.run(quarter + 1, 3 * quarter - 1, True)
    for src, dst, low, high in (
        (change_v, bed_change, quarter, 3 * quarter),
        (next_v, bed_next, quarter + 1, 3 * quarter - 1),
    ):
        at = pl.ds(low * SUB, (high - low) * SUB)
        copies.append(pltpu.make_async_copy(src.at[at], dst.at[at], sems.at[len(copies)]))
        copies[-1].start()
    for copy in copies:
        copy.wait()


def bed_edge_kernel(
    bed, side, far_a, far_b, own_m, got_m, own_e, got_e, next_in, change_in, bed_next, bed_change,
    change_v, next_v, sems,
):
    rows = bed.shape[0]
    blocks = rows // SUB
    quarter = blocks // 4
    update = Update(bed, side, far_a, far_b, own_m, got_m, own_e, got_e, change_v, next_v)
    copies = []

    def send(src, dst, low, high):
        at = pl.ds(low * SUB, (high - low) * SUB)
        copies.append(pltpu.make_async_copy(src.at[at], dst.at[at], sems.at[len(copies)]))
        copies[-1].start()

    update.run(0, quarter + 1, True)
    send(change_v, bed_change, 0, quarter)
    send(next_v, bed_next, 0, quarter + 1)
    update.run(blocks - quarter - 1, blocks, True)
    send(change_v, bed_change, blocks - quarter, blocks)
    send(next_v, bed_next, blocks - quarter - 1, blocks)
    for copy in copies:
        copy.wait()


def bed_scratch(rows, cols):
    return [
        pltpu.VMEM((rows, cols), jnp.float32),
        pltpu.VMEM((rows, cols), jnp.float32),
        pltpu.SemaphoreType.DMA((4,)),
    ]


def bed_middle(bed, side, far_a, far_b, own_m, got_m, hydro):
    return pl.pallas_call(
        bed_middle_kernel,
        name="bed_middle",
        out_shape=[pltpu.HBM(x.shape, jnp.float32) for x in (bed, bed, hydro)],
        in_specs=[VMEM] * 7,
        out_specs=[ANY] * 3,
        scratch_shapes=bed_scratch(*bed.shape),
        compiler_params=pltpu.CompilerParams(vmem_limit_bytes=6 * MIB),
        cost_estimate=cost(4),
    )(*held(bed, side, far_a, far_b, own_m, got_m, hydro))


def bed_edge(bed, side, far_a, far_b, own_m, got_m, own_e, got_e, bed_next, bed_change):
    return pl.pallas_call(
        bed_edge_kernel,
        name="bed_edge",
        out_shape=[pltpu.HBM(bed.shape, jnp.float32)] * 2,
        in_specs=[VMEM] * 8 + [ANY] * 2,
        out_specs=[ANY] * 2,
        scratch_shapes=bed_scratch(*bed.shape),
        input_output_aliases={8: 0, 9: 1},
        compiler_params=pltpu.CompilerParams(vmem_limit_bytes=6 * MIB),
        cost_estimate=cost(2),
    )(
        *held(bed, side, far_a, far_b, own_m, got_m, own_e, got_e),
        *held(bed_next, bed_change, space=pltpu.HBM),
    )


def shards(bed, land_mask, cell_class, weights, cond_params, wave_stress, hydro_state):
    ny = lax.axis_size("ty")
    nc = lax.axis_size("cond")
    raw = (bed, land_mask, cell_class, wave_stress, hydro_state)
    swap = [(i, i ^ 1) for i in range(nc)]

    def pairs(first):
        return [p for i in range(first, ny - 1, 2) for p in ((i, i + 1), (i + 1, i))]

    def over_chips(part, beside=()):
        reach = 2
        while reach < nc:
            got = lax.ppermute(part, "cond", [(i, i ^ reach) for i in range(nc)])
            got, beside = lax.optimization_barrier((got, beside))
            part = part + got
            reach = 2 * reach
        return part, beside

    side = lax.ppermute(pack_side(*raw), "tx", [(0, 1), (1, 0)])
    raw, pays = load(*raw)
    bed = raw[0]
    odd = lax.axis_index("ty") % 2 == 1
    corners = [side[:SUB], side[-SUB:]]
    far_a = jnp.concatenate([pays[0], jnp.where(odd, corners[0], corners[1])])
    far_b = jnp.concatenate([pays[1], jnp.where(odd, corners[1], corners[0])])
    far_a = lax.ppermute(far_a, "ty", pairs(0))
    hydro, pay = middle(False, weights, cond_params, raw, side)
    hydro, far_b = lax.optimization_barrier((hydro, far_b))
    far_b = lax.ppermute(far_b, "ty", pairs(1))
    got = lax.ppermute(pay, "cond", swap)
    hydro, pay = middle(True, weights, cond_params, raw, side, hydro)
    part_m = pay + got
    hydro, part_m = lax.optimization_barrier((hydro, part_m))
    hydro, pay = edge(False, weights, cond_params, raw, side, far_a, far_b, hydro)
    got = lax.ppermute(pay, "cond", swap)
    hydro, pay = edge(True, weights, cond_params, raw, side, far_a, far_b, hydro)
    own_m, hydro = over_chips(part_m, hydro)
    part_e = pay + got
    own_m, _ = lax.optimization_barrier((own_m, part_e))
    got_m = lax.ppermute(own_m, "cond", swap)
    bed_next, bed_change, hydro = bed_middle(bed, side, far_a, far_b, own_m, got_m, hydro)
    own_e, (bed_next, bed_change) = over_chips(part_e, (bed_next, bed_change))
    got_e = lax.ppermute(own_e, "cond", swap)
    bed_next, bed_change = bed_edge(
        bed, side, far_a, far_b, own_m, got_m, own_e, got_e, bed_next, bed_change
    )
    return bed_next, bed_change, hydro


def solution(mesh):
    in_specs = (
        P("ty", "tx"),
        P("ty", "tx"),
        P("ty", "tx"),
        P(),
        P("cond", None),
        P("cond", None, "ty", "tx"),
        P("cond", None, "ty", "tx"),
    )
    out_specs = (P("ty", "tx"), P("ty", "tx"), P("cond", None, "ty", "tx"))
    return jax.shard_map(shards, mesh=mesh, in_specs=in_specs, out_specs=out_specs, check_vma=False)
```

```python
import functools

import jax
import jax.numpy as jnp
from jax import lax
from jax.experimental import pallas as pl
from jax.experimental.pallas import tpu as pltpu
from jax.sharding import PartitionSpec as P

STEPS = 3
HALO = STEPS + 1
SUB = 8
LANE = 128
FIELDS = 8
GROUP = HALO * FIELDS
FOLD = LANE // GROUP
LAG = 2
MIB = 2**20
ANY = pl.BlockSpec(memory_space=pl.ANY)
VMEM = pl.BlockSpec(memory_space=pltpu.VMEM)
SMEM = pl.BlockSpec(memory_space=pltpu.SMEM)


def rows_of(shape):
    return lax.broadcasted_iota(jnp.int32, shape, 0)


def lanes_of(shape):
    return lax.broadcasted_iota(jnp.int32, shape, 1)


def east(x):
    return pltpu.roll(x, x.shape[1] - 1, 1)


def west(x):
    return pltpu.roll(x, 1, 1)


def south(x, below):
    return pltpu.roll(jnp.where(rows_of(x.shape) == 0, below, x), SUB - 1, 0)


def north(x, above):
    return pltpu.roll(jnp.where(rows_of(x.shape) == SUB - 1, above, x), 1, 0)


def tile_at(index):
    if isinstance(index, int):
        return pl.ds(index * SUB, SUB)
    return pl.ds(pl.multiple_of(index * SUB, SUB), SUB)


def held(*arrays, space=pltpu.VMEM):
    return [pltpu.with_memory_space_constraint(x, space) for x in arrays]


def cost(micros):
    return pl.CostEstimate(flops=int(micros * 10**9), bytes_accessed=0, transcendentals=0)


def raw_fields(bed, mask, kind, stress, hydro):
    return [bed, mask, kind] + [stress.at[0, k] for k in range(2)] + [hydro.at[0, k] for k in range(3)]


SPOTS = [(0, 0), (1, 0), (1, 1)] + [(0, k) for k in range(1, 6)]


def pack_side_kernel(bed, mask, kind, stress, hydro, side, reals, ints, sems):
    rows, cols = bed.shape
    at_left = lax.axis_index("tx") == 0
    off = pl.multiple_of(jnp.where(at_left, cols - LANE, 0), LANE)
    strips = [(reals, ints)[which].at[k] for which, k in SPOTS]
    copies = [
        pltpu.make_async_copy(src.at[:, pl.ds(off, LANE)], strip, sems.at[f])
        for f, (src, strip) in enumerate(zip(raw_fields(bed, mask, kind, stress, hydro), strips))
    ]
    for copy in copies:
        copy.start()
    for copy in copies:
        copy.wait()
    lift = jnp.where(at_left, HALO, 0)
    lane = lanes_of((SUB, LANE))
    span = rows // FOLD // SUB
    for i in range(span):
        total = jnp.zeros((SUB, LANE), jnp.float32)
        for g in range(FOLD):
            for f in range(FIELDS):
                place = g * FIELDS + f
                part = strips[f][tile_at(g * span + i), :].astype(jnp.float32)
                total = jnp.where(lane // HALO == place, pltpu.roll(part, lift + place * HALO, 1), total)
        side[tile_at(i), :] = total


def pack_side(*raw):
    rows, cols = raw[0].shape
    return pl.pallas_call(
        pack_side_kernel,
        name="pack_side",
        out_shape=pltpu.VMEM((rows // FOLD, LANE), jnp.float32),
        in_specs=[ANY] * 5,
        out_specs=VMEM,
        scratch_shapes=[
            pltpu.VMEM((6, rows, LANE), jnp.float32),
            pltpu.VMEM((2, rows, LANE), jnp.int32),
            pltpu.SemaphoreType.DMA((FIELDS,)),
        ],
        compiler_params=pltpu.CompilerParams(vmem_limit_bytes=4 * MIB),
        cost_estimate=cost(2),
    )(*held(*raw, space=pltpu.HBM))


def pack_rows_kernel(bed, mask, kind, stress, hydro, pay_a, pay_b, reals, ints, sems):
    rows, cols = bed.shape
    copies = []
    for f, src in enumerate(raw_fields(bed, mask, kind, stress, hydro)):
        which, k = SPOTS[f]
        for end, start in enumerate((0, rows - SUB)):
            copies.append(
                pltpu.make_async_copy(src.at[pl.ds(start, SUB)], (reals, ints)[which].at[end, k], sems.at[f, end])
            )
    for copy in copies:
        copy.start()
    for copy in copies:
        copy.wait()
    low = rows_of((SUB, cols)) < HALO
    odd = lax.axis_index("ty") % 2 == 1
    for p in range(FIELDS // 2):
        pairs = []
        for end in range(2):
            both = []
            for f in (2 * p, 2 * p + 1):
                which, k = SPOTS[f]
                both.append((reals, ints)[which][end, k].astype(jnp.float32))
            both[1 - end] = pltpu.roll(both[1 - end], HALO, 0)
            pairs.append(jnp.where(low, *both))
        for k in range(cols // LANE):
            at, lanes = pl.ds(k * GROUP + p * SUB, SUB), slice(k * LANE, (k + 1) * LANE)
            top, bottom = pairs[0][:, lanes], pairs[1][:, lanes]
            pay_a[at, :] = jnp.where(odd, top, bottom)
            pay_b[at, :] = jnp.where(odd, bottom, top)


def pack_rows(*raw):
    rows, cols = raw[0].shape
    return pl.pallas_call(
        pack_rows_kernel,
        name="pack_rows",
        out_shape=[pltpu.VMEM((cols // LANE * GROUP + SUB, LANE), jnp.float32)] * 2,
        in_specs=[ANY] * 5,
        out_specs=[VMEM] * 2,
        scratch_shapes=[
            pltpu.VMEM((2, 6, SUB, cols), jnp.float32),
            pltpu.VMEM((2, 2, SUB, cols), jnp.int32),
            pltpu.SemaphoreType.DMA((FIELDS, 2)),
        ],
        compiler_params=pltpu.CompilerParams(vmem_limit_bytes=4 * MIB),
        cost_estimate=cost(2),
    )(*held(*raw, space=pltpu.HBM))


def corner_kernel(side, in_a, in_b, pay_a, pay_b):
    tall = pay_a.shape[0]
    odd = lax.axis_index("ty") % 2 == 1
    top = side[pl.ds(0, SUB), :]
    bottom = side[pl.ds(side.shape[0] - SUB, SUB), :]
    pay_a[pl.ds(tall - SUB, SUB), :] = jnp.where(odd, top, bottom)
    pay_b[pl.ds(tall - SUB, SUB), :] = jnp.where(odd, bottom, top)


def add_corners(side, pay_a, pay_b):
    return pl.pallas_call(
        corner_kernel,
        name="add_corners",
        out_shape=[pltpu.VMEM(pay_a.shape, jnp.float32)] * 2,
        in_specs=[VMEM] * 3,
        out_specs=[VMEM] * 2,
        input_output_aliases={1: 0, 2: 1},
        compiler_params=pltpu.CompilerParams(vmem_limit_bytes=MIB),
        cost_estimate=cost(0.1),
    )(*held(side, pay_a, pay_b))


def side_lanes(at_left):
    drop = jnp.where(at_left, 0, HALO)
    lane = lanes_of((SUB, LANE))
    valid = jnp.where(at_left, lane, LANE - 1 - lane) < HALO

    def unfold(strip, place):
        return pltpu.roll(strip, 2 * LANE - drop - place * HALO, 1)

    return unfold, valid


class Sweep:
    NAMES = (
        ["s", "a", "b", "fc", "fr", "wc", "wr", "e1", "u1"]
        + ["v1", "e2", "u2", "v2", "qc1", "qr1", "qc2", "qr2"]
    )

    def __init__(self, count, wide, get, emit, weights, params, refs):
        self.count, self.wide, self.get, self.emit = count, wide, get, emit
        self.__dict__.update(zip(self.NAMES + ["fr_last", "qr_last"], refs))
        cond = lax.axis_index("cond")
        self.tide = params[0, 0] - 1.0
        self.slow = 1.0 - 0.2 * params[0, 1]
        self.flow_in = 0.3 * params[0, 3]
        total = weights[0]
        for k in range(1, weights.shape[0]):
            total = total + weights[k]
        ones = jnp.ones((SUB, LANE), jnp.float32)
        share = weights[cond].astype(jnp.float32) * ones / (total.astype(jnp.float32) * ones)
        self.scale = jnp.concatenate([-4.0 * params[0, 2] * share] * (wide // LANE), axis=1)

    @classmethod
    def scratch(cls, count, wide):
        block = pltpu.VMEM(((count + 1) * SUB, wide), jnp.float32)
        return [block] * len(cls.NAMES) + [
            pltpu.VMEM((STEPS, SUB, wide), jnp.float32),
            pltpu.VMEM((SUB, wide), jnp.float32),
        ]

    def prepare(self, i):
        at = tile_at(i)
        depth = self.get(1, i).astype(jnp.float32) * (1.0 - 0.5 * jnp.tanh(self.get(0, i)))
        kinds = self.get(2, i)
        self.s[at, :] = depth * lax.rsqrt(jnp.maximum(depth, 1e-12))
        relax = jnp.where(kinds == 1, 0.5 * depth, 0.0)
        self.a[at, :] = 1.0 - relax
        self.b[at, :] = 0.3 * (relax * self.tide + jnp.where(kinds == 2, self.flow_in * depth, 0.0))

    def move(self, n, i, level, lower, u, v, fc, fr, wc, wr):
        at = tile_at(i)
        u = (self.slow * u - (east(level) - level) + self.get(3, i)) * wc
        v = (self.slow * v - (south(level, lower) - level) + self.get(4, i)) * wr
        flux_c = fc * u
        flux_r = fr * v
        out = self.a[at, :] * level + self.b[at, :] - (
            flux_c - west(flux_c) + flux_r - north(flux_r, self.fr_last[n])
        )
        self.fr_last[n] = flux_r
        return out, u, v, u * jnp.abs(u), v * jnp.abs(v)

    def step_one(self, i):
        at, after = tile_at(i), tile_at(i + 1)
        s = self.s[at, :]
        face_c = s * east(s)
        face_r = s * south(s, self.s[after, :])
        ratios = []
        for face in (face_c, face_r):
            base = face + 0.1
            inverse = pl.reciprocal(base, approx=True)
            ratios.append(face * (inverse * (2.0 - base * inverse)))
        wc, wr = ratios
        fc = 0.3 * face_c
        fr = 0.3 * face_r
        self.fc[at, :] = fc
        self.fr[at, :] = fr
        self.wc[at, :] = wc
        self.wr[at, :] = wr
        level = 0.3 * self.get(5, i)
        lower = 0.3 * self.get(5, i + 1) if i + 1 < self.count else level
        e, u, v, qc, qr = self.move(0, i, level, lower, self.get(6, i), self.get(7, i), fc, fr, wc, wr)
        self.e1[at, :] = e
        self.u1[at, :] = u
        self.v1[at, :] = v
        self.qc1[at, :] = qc
        self.qr1[at, :] = qr

    def later(self, n, i, e, u, v):
        at, after = tile_at(i), tile_at(i + 1)
        return self.move(
            n, i, e[at, :], e[after, :], u[at, :], v[at, :],
            self.fc[at, :], self.fr[at, :], self.wc[at, :], self.wr[at, :],
        )

    def step_two(self, i):
        at = tile_at(i)
        e, u, v, qc, qr = self.later(1, i, self.e1, self.u1, self.v1)
        self.e2[at, :] = e
        self.u2[at, :] = u
        self.v2[at, :] = v
        self.qc2[at, :] = self.qc1[at, :] + qc
        self.qr2[at, :] = self.qr1[at, :] + qr

    def step_three(self, i):
        at = tile_at(i)
        e, u, v, qc, qr = self.later(2, i, self.e2, self.u2, self.v2)
        qc = self.wc[at, :] * (self.qc2[at, :] + qc)
        qr = self.wr[at, :] * (self.qr2[at, :] + qr)
        change = (qc - west(qc) + qr - north(qr, self.qr_last[...])) * self.scale
        self.qr_last[...] = qr
        self.emit(i, e * (1.0 / 0.3), u, v, change)

    def run(self):
        self.fr_last[...] = jnp.zeros_like(self.fr_last)
        self.qr_last[...] = jnp.zeros_like(self.qr_last)
        for ref in (self.s, self.e1, self.e2):
            ref[tile_at(self.count), :] = jnp.zeros((SUB, self.wide), jnp.float32)
        stages = (self.step_three, self.step_two, self.step_one, self.prepare)
        for t in range(self.count + LAG * STEPS):
            for k, stage in enumerate(stages):
                i = t - LAG * (STEPS - k)
                if 0 <= i < self.count:
                    stage(i)


def raw_reader(bed, mask, kind, stress, hydro, side, unfold, valid):
    rows = bed.shape[0]
    span = rows // FOLD // SUB
    fields = raw_fields(bed, mask, kind, stress, hydro)

    def read(f, block):
        strip = side[tile_at(block % span), :]
        part = unfold(strip, (block // span) * FIELDS + f)
        if f == 1:
            part = jnp.where(valid, part, 0.0)
        main = fields[f][tile_at(block), :]
        return jnp.concatenate([main, part.astype(main.dtype)], axis=1)

    return read


def middle_kernel(own, weights, params, bed, mask, kind, stress, hydro, side, *refs):
    hydro_out, pay, *refs = refs[1:] if own else refs
    rows, cols = bed.shape
    quarter = rows // SUB // 4
    unfold, valid = side_lanes(lax.axis_index("tx") == 0)
    read = raw_reader(bed, mask, kind, stress, hydro, side, unfold, valid)
    mine = lax.axis_index("cond") % 2
    lower_half = mine == (1 if own else 0)
    first = jnp.where(lower_half, 2 * quarter, quarter) - 1
    emit = quarter_writer(first, quarter, cols, hydro_out, pay)

    def finish(i, e, u, v, change):
        if 1 <= i <= quarter:
            emit(i, e, u, v, change)

    Sweep(quarter + 2, cols + LANE, lambda f, i: read(f, first + i), finish, weights, params, refs).run()


def quarter_writer(first, quarter, cols, hydro_out, pay):
    lane = lanes_of((SUB, LANE))
    lanes = cols // LANE
    rims = [jnp.zeros((SUB, LANE), jnp.float32)]

    def emit(i, e, u, v, change):
        at = tile_at(first + i)
        for k, value in enumerate((e, u, v)):
            hydro_out[0, k, at, :] = value[:, :cols]
        g = i - 1
        for k in range(lanes):
            pay[tile_at(k * quarter + g), :] = change[:, k * LANE : (k + 1) * LANE]
        rims[0] = jnp.where(lane // 2 == g, pltpu.roll(change[:, cols:], 1 + 2 * g, 1), rims[0])
        if g == quarter - 1:
            pay[tile_at(lanes * quarter), :] = rims[0]

    return emit


def middle(own, weights, params, raw, side, hydro=None):
    rows, cols = raw[0].shape
    given = (hydro,) if own else ()
    return pl.pallas_call(
        functools.partial(middle_kernel, own),
        name="middle_own" if own else "middle_other",
        out_shape=[
            pltpu.VMEM(raw[4].shape, jnp.float32),
            pltpu.VMEM((cols // LANE * rows // 4 + SUB, LANE), jnp.float32),
        ],
        in_specs=[SMEM, SMEM] + [VMEM] * (6 + own),
        out_specs=[VMEM, VMEM],
        scratch_shapes=Sweep.scratch(rows // SUB // 4 + 2, cols + LANE),
        input_output_aliases={8: 0} if own else {},
        compiler_params=pltpu.CompilerParams(vmem_limit_bytes=10 * MIB),
        cost_estimate=cost(4),
    )(weights, params, *held(*raw, side, *given))


def edge_kernel(
    own, weights, params, bed, mask, kind, stress, hydro, side, far_a, far_b, hydro_in,
    hydro_out, pay, ends_r, ends_i, *refs,
):
    rows, cols = bed.shape
    blocks = rows // SUB
    quarter = blocks // 4
    wide = cols + LANE
    lanes = cols // LANE
    unfold, valid = side_lanes(lax.axis_index("tx") == 0)
    read = raw_reader(bed, mask, kind, stress, hydro, side, unfold, valid)
    mine = lax.axis_index("cond") % 2
    top = mine == (0 if own else 1)
    from_a = top == (lax.axis_index("ty") % 2 == 1)
    first = jnp.where(top, -1, blocks - quarter - 1)

    inner = jnp.where(top, quarter, blocks - quarter - 1)
    for f in range(FIELDS):
        body = read(f, inner)
        parts = []
        for k in range(lanes):
            at = pl.ds(k * GROUP + f // 2 * SUB, SUB)
            part = jnp.where(from_a, far_a[at, :], far_b[at, :])
            moved = pltpu.roll(part, HALO, 0)
            parts.append(jnp.where(top, moved, part) if f % 2 == 0 else jnp.where(top, part, moved))
        at = pl.ds(lanes * GROUP, SUB)
        corner = jnp.where(from_a, far_a[at, :], far_b[at, :])
        corner = jnp.where(top, unfold(corner, (FOLD - 1) * FIELDS + f), unfold(corner, f))
        if f == 1:
            corner = jnp.where(valid, corner, 0.0)
        outer = jnp.concatenate(parts + [corner], axis=1).astype(body.dtype)
        which, k = SPOTS[f]
        ref = (ends_r, ends_i)[which]
        ref[0, k] = jnp.where(top, outer, body)
        ref[1, k] = jnp.where(top, body, outer)

    def get(f, i):
        if i == 0 or i == quarter + 1:
            which, k = SPOTS[f]
            return (ends_r, ends_i)[which][0 if i == 0 else 1, k]
        return read(f, first + i)

    row = rows_of((SUB, LANE))
    emit = quarter_writer(first, quarter, cols, hydro_out, pay)
    outside = []

    def finish(i, e, u, v, change):
        if i == 0:
            outside.append(pltpu.roll(change, 1, 0))
        elif i == quarter + 1:
            rim = jnp.where(top, outside[0], change)
            total = rim[:, :LANE]
            for k in range(1, lanes):
                total = jnp.where(row == k, pltpu.roll(rim[:, k * LANE : (k + 1) * LANE], k, 0), total)
            pay[tile_at(lanes * quarter + 1), :] = total
        else:
            emit(i, e, u, v, change)

    Sweep(quarter + 2, wide, get, finish, weights, params, refs).run()


def edge(own, weights, params, raw, side, far_a, far_b, hydro):
    rows, cols = raw[0].shape
    wide = cols + LANE
    return pl.pallas_call(
        functools.partial(edge_kernel, own),
        name="edge_own" if own else "edge_other",
        out_shape=[
            pltpu.VMEM(hydro.shape, jnp.float32),
            pltpu.VMEM((cols // LANE * rows // 4 + 2 * SUB, LANE), jnp.float32),
        ],
        in_specs=[SMEM, SMEM] + [VMEM] * 9,
        out_specs=[VMEM, VMEM],
        scratch_shapes=[pltpu.VMEM((2, 6, SUB, wide), jnp.float32), pltpu.VMEM((2, 2, SUB, wide), jnp.int32)]
        + Sweep.scratch(rows // SUB // 4 + 2, wide),
        input_output_aliases={10: 0},
        compiler_params=pltpu.CompilerParams(vmem_limit_bytes=12 * MIB),
        cost_estimate=cost(3),
    )(weights, params, *held(*raw, side, far_a, far_b, hydro))


class Update:
    def __init__(self, bed, side, far_a, far_b, own_m, got_m, own_e, got_e, change_v, next_v):
        self.bed, self.side, self.far_a, self.far_b = bed, side, far_a, far_b
        self.parts = {"m": (own_m, got_m), "e": (own_e, got_e)}
        self.change_v, self.next_v = change_v, next_v
        rows, self.cols = bed.shape
        self.blocks = rows // SUB
        self.quarter = self.blocks // 4
        self.lanes = self.cols // LANE
        self.wide = self.cols + LANE
        self.unfold, _ = side_lanes(lax.axis_index("tx") == 0)
        self.mine = lax.axis_index("cond") % 2
        self.odd = lax.axis_index("ty") % 2 == 1
        col = lanes_of((SUB, self.wide))
        last_c = lax.axis_index("tx") == lax.axis_size("tx") - 1
        first_c = lax.axis_index("tx") == 0
        self.shut_c = (last_c & (col == self.cols - 1)) | (first_c & (col == self.wide - 1))
        self.last_row = rows_of((SUB, self.wide)) == SUB - 1
        self.rims = {}

    def merged(self, q, block):
        own, got = self.parts["e" if q in (0, 3) else "m"]
        at = tile_at(block)
        return jnp.where(self.mine == q // 2, own[at, :], got[at, :])

    def outside(self, q):
        rim = self.merged(q, self.lanes * self.quarter + 1)
        parts = []
        for k in range(self.lanes):
            at = tile_at(k * GROUP // SUB)
            a, b = self.far_a[at, :], self.far_b[at, :]
            if q == 0:
                z = jnp.where(self.odd, a, b) + pltpu.roll(rim, (2 * SUB + HALO - 1 - k) % SUB, 0)
                parts.append(pltpu.roll(z, HALO, 0))
            else:
                parts.append(jnp.where(self.odd, b, a) + pltpu.roll(rim, (SUB - k) % SUB, 0))
        return jnp.concatenate(parts + [jnp.zeros((SUB, LANE), jnp.float32)], axis=1)

    def level(self, b, keep):
        if b == -1:
            return self.outside(0)
        if b == self.blocks:
            return self.outside(3)
        q, g = divmod(b, self.quarter)
        change = jnp.concatenate([self.merged(q, k * self.quarter + g) for k in range(self.lanes)], axis=1)
        if keep:
            self.change_v[tile_at(b), :] = change
        if q not in self.rims:
            self.rims[q] = self.merged(q, self.lanes * self.quarter)
        span = self.blocks // FOLD
        cols_bed = self.unfold(self.side[tile_at(b % span), :], b // span * FIELDS)
        cols_change = pltpu.roll(self.rims[q], LANE - 1 - 2 * g, 1)
        return jnp.concatenate([self.bed[tile_at(b), :] + change, cols_bed + cols_change], axis=1)

    def spill(self, slope):
        return 0.25 * (slope - jnp.clip(slope, -1.0, 1.0))

    def south_face(self, z, lower, b):
        out = self.spill(south(z, lower) - z)
        if b == -1:
            return jnp.where((lax.axis_index("ty") == 0) & self.last_row, 0.0, out)
        if b == self.blocks - 1:
            return jnp.where((lax.axis_index("ty") == lax.axis_size("ty") - 1) & self.last_row, 0.0, out)
        return out

    def run(self, first, stop, keep, after=lambda b: None):
        z = self.level(first - 1, keep)
        lower = self.level(first, keep)
        gr = self.south_face(z, lower, first - 1)
        for b in range(first, stop):
            z, lower = lower, self.level(b + 1, keep)
            gr_above, gr = gr, self.south_face(z, lower, b)
            gc = jnp.where(self.shut_c, 0.0, self.spill(east(z) - z))
            out = z + gc - west(gc) + gr - north(gr, gr_above)
            self.next_v[tile_at(b), :] = out[:, : self.cols]
            after(b)


def bed_middle_kernel(
    bed, side, far_a, far_b, own_m, got_m, hydro, bed_next, bed_change, hydro_out, change_v, next_v, sems
):
    rows = bed.shape[0]
    quarter = rows // SUB // 4
    copies = [pltpu.make_async_copy(hydro, hydro_out, sems.at[0])]
    copies[0].start()
    update = Update(bed, side, far_a, far_b, own_m, got_m, None, None, change_v, next_v)
    update.run(quarter + 1, 3 * quarter - 1, True)
    for src, dst, low, high in (
        (change_v, bed_change, quarter, 3 * quarter),
        (next_v, bed_next, quarter + 1, 3 * quarter - 1),
    ):
        at = pl.ds(low * SUB, (high - low) * SUB)
        copies.append(pltpu.make_async_copy(src.at[at], dst.at[at], sems.at[len(copies)]))
        copies[-1].start()
    for copy in copies:
        copy.wait()


def bed_edge_kernel(
    bed, side, far_a, far_b, own_m, got_m, own_e, got_e, next_in, change_in, bed_next, bed_change,
    change_v, next_v, sems,
):
    rows = bed.shape[0]
    blocks = rows // SUB
    quarter = blocks // 4
    update = Update(bed, side, far_a, far_b, own_m, got_m, own_e, got_e, change_v, next_v)
    copies = []

    def send(src, dst, low, high):
        at = pl.ds(low * SUB, (high - low) * SUB)
        copies.append(pltpu.make_async_copy(src.at[at], dst.at[at], sems.at[len(copies)]))
        copies[-1].start()

    update.run(0, quarter + 1, True)
    send(change_v, bed_change, 0, quarter)
    send(next_v, bed_next, 0, quarter + 1)
    update.run(blocks - quarter - 1, blocks, True)
    send(change_v, bed_change, blocks - quarter, blocks)
    send(next_v, bed_next, blocks - quarter - 1, blocks)
    for copy in copies:
        copy.wait()


def bed_scratch(rows, cols):
    return [
        pltpu.VMEM((rows, cols), jnp.float32),
        pltpu.VMEM((rows, cols), jnp.float32),
        pltpu.SemaphoreType.DMA((4,)),
    ]


def bed_middle(bed, side, far_a, far_b, own_m, got_m, hydro):
    return pl.pallas_call(
        bed_middle_kernel,
        name="bed_middle",
        out_shape=[pltpu.HBM(x.shape, jnp.float32) for x in (bed, bed, hydro)],
        in_specs=[VMEM] * 7,
        out_specs=[ANY] * 3,
        scratch_shapes=bed_scratch(*bed.shape),
        compiler_params=pltpu.CompilerParams(vmem_limit_bytes=6 * MIB),
        cost_estimate=cost(4),
    )(*held(bed, side, far_a, far_b, own_m, got_m, hydro))


def bed_edge(bed, side, far_a, far_b, own_m, got_m, own_e, got_e, bed_next, bed_change):
    return pl.pallas_call(
        bed_edge_kernel,
        name="bed_edge",
        out_shape=[pltpu.HBM(bed.shape, jnp.float32)] * 2,
        in_specs=[VMEM] * 8 + [ANY] * 2,
        out_specs=[ANY] * 2,
        scratch_shapes=bed_scratch(*bed.shape),
        input_output_aliases={8: 0, 9: 1},
        compiler_params=pltpu.CompilerParams(vmem_limit_bytes=6 * MIB),
        cost_estimate=cost(2),
    )(
        *held(bed, side, far_a, far_b, own_m, got_m, own_e, got_e),
        *held(bed_next, bed_change, space=pltpu.HBM),
    )


def shards(bed, land_mask, cell_class, weights, cond_params, wave_stress, hydro_state):
    ny = lax.axis_size("ty")
    nc = lax.axis_size("cond")
    raw = (bed, land_mask, cell_class, wave_stress, hydro_state)
    swap = [(i, i ^ 1) for i in range(nc)]

    def pairs(first):
        return [p for i in range(first, ny - 1, 2) for p in ((i, i + 1), (i + 1, i))]

    def over_chips(part, beside=()):
        reach = 2
        while reach < nc:
            got = lax.ppermute(part, "cond", [(i, i ^ reach) for i in range(nc)])
            got, beside = lax.optimization_barrier((got, beside))
            part = part + got
            reach = 2 * reach
        return part, beside

    side = lax.ppermute(pack_side(*raw), "tx", [(0, 1), (1, 0)])
    far_a, far_b = add_corners(side, *pack_rows(*raw))
    far_a = lax.ppermute(far_a, "ty", pairs(0))
    hydro, pay = middle(False, weights, cond_params, raw, side)
    hydro, far_a, far_b = lax.optimization_barrier((hydro, far_a, far_b))
    far_b = lax.ppermute(far_b, "ty", pairs(1))
    got = lax.ppermute(pay, "cond", swap)
    hydro, pay = middle(True, weights, cond_params, raw, side, hydro)
    part_m = pay + got
    hydro, part_m = lax.optimization_barrier((hydro, part_m))
    hydro, pay = edge(False, weights, cond_params, raw, side, far_a, far_b, hydro)
    got = lax.ppermute(pay, "cond", swap)
    hydro, pay = edge(True, weights, cond_params, raw, side, far_a, far_b, hydro)
    own_m, hydro = over_chips(part_m, hydro)
    part_e = pay + got
    own_m, _ = lax.optimization_barrier((own_m, part_e))
    got_m = lax.ppermute(own_m, "cond", swap)
    bed_next, bed_change, hydro = bed_middle(bed, side, far_a, far_b, own_m, got_m, hydro)
    own_e, (bed_next, bed_change) = over_chips(part_e, (bed_next, bed_change))
    got_e = lax.ppermute(own_e, "cond", swap)
    bed_next, bed_change = bed_edge(
        bed, side, far_a, far_b, own_m, got_m, own_e, got_e, bed_next, bed_change
    )
    return bed_next, bed_change, hydro


def solution(mesh):
    in_specs = (
        P("ty", "tx"),
        P("ty", "tx"),
        P("ty", "tx"),
        P(),
        P("cond", None),
        P("cond", None, "ty", "tx"),
        P("cond", None, "ty", "tx"),
    )
    out_specs = (P("ty", "tx"), P("ty", "tx"), P("cond", None, "ty", "tx"))
    return jax.shard_map(shards, mesh=mesh, in_specs=in_specs, out_specs=out_specs, check_vma=False)
```

```python
import functools

import jax
import jax.numpy as jnp
from jax import lax
from jax.experimental import pallas as pl
from jax.experimental.pallas import tpu as pltpu
from jax.sharding import PartitionSpec as P

STEPS = 3
HALO = STEPS + 1
SUB = 8
LANE = 128
FIELDS = 8
GROUP = HALO * FIELDS
FOLD = LANE // GROUP
LAG = 2
MIB = 2**20
ANY = pl.BlockSpec(memory_space=pl.ANY)
VMEM = pl.BlockSpec(memory_space=pltpu.VMEM)
SMEM = pl.BlockSpec(memory_space=pltpu.SMEM)


def rows_of(shape):
    return lax.broadcasted_iota(jnp.int32, shape, 0)


def lanes_of(shape):
    return lax.broadcasted_iota(jnp.int32, shape, 1)


def east(x):
    return pltpu.roll(x, x.shape[1] - 1, 1)


def west(x):
    return pltpu.roll(x, 1, 1)


def south(x, below):
    return pltpu.roll(jnp.where(rows_of(x.shape) == 0, below, x), SUB - 1, 0)


def north(x, above):
    return pltpu.roll(jnp.where(rows_of(x.shape) == SUB - 1, above, x), 1, 0)


def tile_at(index):
    if isinstance(index, int):
        return pl.ds(index * SUB, SUB)
    return pl.ds(pl.multiple_of(index * SUB, SUB), SUB)


def held(*arrays, space=pltpu.VMEM):
    return [pltpu.with_memory_space_constraint(x, space) for x in arrays]


def cost(micros):
    return pl.CostEstimate(flops=int(micros * 10**9), bytes_accessed=0, transcendentals=0)


def level_terms(params):
    return params[0, 0] - 1.0, 0.3 * params[0, 3]


def coefficients(bed, mask, kind, tide, flow_in):
    depth = mask.astype(jnp.float32) * (1.0 - 0.5 * jnp.tanh(bed))
    root = depth * lax.rsqrt(jnp.maximum(depth, 1e-12))
    relax = jnp.where(kind == 1, 0.5 * depth, 0.0)
    return root, 1.0 - relax, 0.3 * (relax * tide + jnp.where(kind == 2, flow_in * depth, 0.0))


def moving(stress, hydro):
    return [stress.at[0, k] for k in range(2)] + [hydro.at[0, k] for k in range(3)]


def pack_side_kernel(params_in, bed, mask, kind, stress, hydro, side, reals, ints, params, sems):
    rows, cols = bed.shape
    at_left = lax.axis_index("tx") == 0
    off = pl.multiple_of(jnp.where(at_left, cols - LANE, 0), LANE)
    strips = [reals.at[0], ints.at[0], ints.at[1]] + [reals.at[k] for k in range(1, 6)]
    copies = [
        pltpu.make_async_copy(src.at[:, pl.ds(off, LANE)], strip, sems.at[f])
        for f, (src, strip) in enumerate(zip([bed, mask, kind] + moving(stress, hydro), strips))
    ] + [pltpu.make_async_copy(params_in, params, sems.at[FIELDS])]
    for copy in copies:
        copy.start()
    for copy in copies:
        copy.wait()
    tide, flow_in = level_terms(params)
    lift = jnp.where(at_left, HALO, 0)
    lift_bed = jnp.where(at_left, 1, 0)
    lane = lanes_of((SUB, LANE))
    span = rows // FOLD // SUB
    beds = jnp.zeros((SUB, LANE), jnp.float32)
    for i in range(span):
        total = jnp.zeros((SUB, LANE), jnp.float32)
        for g in range(FOLD):
            at = tile_at(g * span + i)
            first = strips[0][at, :]
            fields = list(coefficients(first, strips[1][at, :], strips[2][at, :], tide, flow_in))
            fields += [strip[at, :] for strip in strips[3:]]
            for f, part in enumerate(fields):
                place = g * FIELDS + f
                total = jnp.where(lane // HALO == place, pltpu.roll(part, lift + place * HALO, 1), total)
            block = g * span + i
            beds = jnp.where(lane == block, pltpu.roll(first, lift_bed + block, 1), beds)
        side[tile_at(i), :] = total
    side[tile_at(span), :] = beds


def pack_side(params, *raw):
    rows, cols = raw[0].shape
    return pl.pallas_call(
        pack_side_kernel,
        name="pack_side",
        out_shape=pltpu.VMEM((rows // FOLD + SUB, LANE), jnp.float32),
        in_specs=[ANY] * 6,
        out_specs=VMEM,
        scratch_shapes=[
            pltpu.VMEM((6, rows, LANE), jnp.float32),
            pltpu.VMEM((2, rows, LANE), jnp.int32),
            pltpu.SMEM(params.shape, jnp.float32),
            pltpu.SemaphoreType.DMA((FIELDS + 1,)),
        ],
        compiler_params=pltpu.CompilerParams(vmem_limit_bytes=4 * MIB),
        cost_estimate=cost(2),
    )(*held(params, *raw, space=pltpu.HBM))


PARTS = 4


def prepare_kernel(
    params_in, bed, mask, kind, stress, hydro, bed_v, root, a, b, pay_a, pay_b,
    mask_v, kind_v, ends, params, load_sems, end_sems, params_sem,
):
    rows, cols = bed.shape
    lanes = cols // LANE
    chunk = rows // PARTS
    loads, copies = [], []
    for c in range(PARTS):
        at = pl.ds(c * chunk, chunk)
        loads.append([
            pltpu.make_async_copy(src.at[at], dst.at[at], load_sems.at[f, c])
            for f, (src, dst) in enumerate(((bed, bed_v), (mask, mask_v), (kind, kind_v)))
        ])
    for f, src in enumerate(moving(stress, hydro)):
        for end, start in enumerate((0, rows - SUB)):
            copies.append(pltpu.make_async_copy(src.at[pl.ds(start, SUB)], ends.at[end, f], end_sems.at[f, end]))
    loads[0].append(pltpu.make_async_copy(params_in, params, params_sem))
    for group in loads + [copies]:
        for copy in group:
            copy.start()
    for copy in loads[0]:
        copy.wait()
    tide, flow_in = level_terms(params)
    for c in range(PARTS):
        for copy in loads[c] if c else ():
            copy.wait()
        for i in range(c * chunk // SUB, (c + 1) * chunk // SUB):
            at = tile_at(i)
            root[at, :], a[at, :], b[at, :] = coefficients(bed_v[at, :], mask_v[at, :], kind_v[at, :], tide, flow_in)
    for copy in copies:
        copy.wait()
    low = rows_of((SUB, cols)) < HALO
    odd = lax.axis_index("ty") % 2 == 1

    def edge_rows(f, end):
        if f < 3:
            return (root, a, b)[f][tile_at(0 if end == 0 else rows // SUB - 1), :]
        return ends[end, f - 3]

    for p in range(FIELDS // 2):
        pairs = []
        for end in range(2):
            both = [edge_rows(f, end) for f in (2 * p, 2 * p + 1)]
            both[1 - end] = pltpu.roll(both[1 - end], HALO, 0)
            pairs.append(jnp.where(low, *both))
        for k in range(lanes):
            at, part = pl.ds(k * GROUP + p * SUB, SUB), slice(k * LANE, (k + 1) * LANE)
            top, bottom = pairs[0][:, part], pairs[1][:, part]
            pay_a[at, :] = jnp.where(odd, top, bottom)
            pay_b[at, :] = jnp.where(odd, bottom, top)
    top = fold_row(bed_v[tile_at(0), :])
    bottom = fold_row(pltpu.roll(bed_v[tile_at(rows // SUB - 1), :], 1, 0))
    at = pl.ds(lanes * GROUP + SUB, SUB)
    pay_a[at, :] = jnp.where(odd, top, bottom)
    pay_b[at, :] = jnp.where(odd, bottom, top)


def fold_row(x):
    row = rows_of((SUB, LANE))
    total = x[:, :LANE]
    for k in range(1, x.shape[1] // LANE):
        total = jnp.where(row == k, pltpu.roll(x[:, k * LANE : (k + 1) * LANE], k, 0), total)
    return total


def prepare(params, *raw):
    rows, cols = raw[0].shape
    tile = pltpu.VMEM((rows, cols), jnp.float32)
    return pl.pallas_call(
        prepare_kernel,
        name="prepare",
        out_shape=[tile] * 4 + [pltpu.VMEM((cols // LANE * GROUP + 2 * SUB, LANE), jnp.float32)] * 2,
        in_specs=[ANY] * 6,
        out_specs=[VMEM] * 6,
        scratch_shapes=[
            pltpu.VMEM((rows, cols), jnp.int32),
            pltpu.VMEM((rows, cols), jnp.int32),
            pltpu.VMEM((2, 5, SUB, cols), jnp.float32),
            pltpu.SMEM(params.shape, jnp.float32),
            pltpu.SemaphoreType.DMA((3, PARTS)),
            pltpu.SemaphoreType.DMA((5, 2)),
            pltpu.SemaphoreType.DMA,
        ],
        compiler_params=pltpu.CompilerParams(vmem_limit_bytes=5 * MIB),
        cost_estimate=cost(2),
    )(*held(params, *raw, space=pltpu.HBM))


def corner_kernel(side, in_a, in_b, pay_a, pay_b):
    at = pl.ds(pay_a.shape[0] - 2 * SUB, SUB)
    odd = lax.axis_index("ty") % 2 == 1
    top = side[pl.ds(0, SUB), :]
    bottom = side[pl.ds(side.shape[0] - 2 * SUB, SUB), :]
    pay_a[at, :] = jnp.where(odd, top, bottom)
    pay_b[at, :] = jnp.where(odd, bottom, top)


def add_corners(side, pay_a, pay_b):
    return pl.pallas_call(
        corner_kernel,
        name="add_corners",
        out_shape=[pltpu.VMEM(pay_a.shape, jnp.float32)] * 2,
        in_specs=[VMEM] * 3,
        out_specs=[VMEM] * 2,
        input_output_aliases={1: 0, 2: 1},
        compiler_params=pltpu.CompilerParams(vmem_limit_bytes=MIB),
        cost_estimate=cost(0.1),
    )(*held(side, pay_a, pay_b))


def side_lanes(at_left):
    drop = jnp.where(at_left, 0, HALO)
    lane = lanes_of((SUB, LANE))
    valid = jnp.where(at_left, lane, LANE - 1 - lane) < HALO

    def unfold(strip, place):
        return pltpu.roll(strip, 2 * LANE - drop - place * HALO, 1)

    return unfold, valid


class Sweep:
    NAMES = (
        ["fc", "fr", "wc", "wr", "e1", "u1"]
        + ["v1", "e2", "u2", "v2", "qc1", "qr1", "qc2", "qr2"]
    )

    def __init__(self, count, wide, get, emit, weights, params, refs, trim):
        self.count, self.wide, self.get, self.emit, self.trim = count, wide, get, emit, trim
        self.__dict__.update(zip(self.NAMES + ["fr_last", "qr_last"], refs))
        cond = lax.axis_index("cond")
        self.slow = 1.0 - 0.2 * params[0, 1]
        total = weights[0]
        for k in range(1, weights.shape[0]):
            total = total + weights[k]
        ones = jnp.ones((SUB, LANE), jnp.float32)
        share = weights[cond].astype(jnp.float32) * ones / (total.astype(jnp.float32) * ones)
        self.scale = jnp.concatenate([-4.0 * params[0, 2] * share] * (wide // LANE), axis=1)

    @classmethod
    def scratch(cls, count, wide):
        block = pltpu.VMEM(((count + 1) * SUB, wide), jnp.float32)
        return [block] * len(cls.NAMES) + [
            pltpu.VMEM((STEPS, SUB, wide), jnp.float32),
            pltpu.VMEM((SUB, wide), jnp.float32),
        ]

    def speed_c(self, i, level, u, wc):
        return (self.slow * u - (east(level) - level) + self.get(3, i)) * wc

    def speed_r(self, i, level, lower, v, wr):
        return (self.slow * v - (south(level, lower) - level) + self.get(4, i)) * wr

    def move(self, n, i, level, lower, u, v, fc, fr, wc, wr):
        u = self.speed_c(i, level, u, wc)
        v = self.speed_r(i, level, lower, v, wr)
        flux_c = fc * u
        flux_r = fr * v
        out = self.get(1, i) * level + self.get(2, i) - (
            flux_c - west(flux_c) + flux_r - north(flux_r, self.fr_last[n])
        )
        self.fr_last[n] = flux_r
        return out, u, v

    def step_one(self, i):
        at = tile_at(i)
        s = self.get(0, i)
        level = 0.3 * self.get(5, i)
        inside = i + 1 < self.count
        face_c = s * east(s)
        face_r = s * south(s, self.get(0, i + 1) if inside else s)
        ratios = []
        for face in (face_c, face_r):
            base = face + 0.1
            inverse = pl.reciprocal(base, approx=True)
            ratios.append(face * (inverse * (2.0 - base * inverse)))
        wc, wr = ratios
        fc = 0.3 * face_c
        fr = 0.3 * face_r
        self.fc[at, :] = fc
        self.fr[at, :] = fr
        self.wc[at, :] = wc
        self.wr[at, :] = wr
        lower = 0.3 * self.get(5, i + 1) if inside else level
        e, u, v = self.move(0, i, level, lower, self.get(6, i), self.get(7, i), fc, fr, wc, wr)
        self.e1[at, :] = e
        self.u1[at, :] = u
        self.v1[at, :] = v
        self.qc1[at, :] = u * jnp.abs(u)
        self.qr1[at, :] = v * jnp.abs(v)

    def step_two(self, i):
        at, after = tile_at(i), tile_at(i + 1)
        e, u, v = self.move(
            1, i, self.e1[at, :], self.e1[after, :], self.u1[at, :], self.v1[at, :],
            self.fc[at, :], self.fr[at, :], self.wc[at, :], self.wr[at, :],
        )
        self.e2[at, :] = e
        if self.trim and i == self.count - 1:
            return
        self.u2[at, :] = u
        self.v2[at, :] = v
        self.qc2[at, :] = self.qc1[at, :] + u * jnp.abs(u)
        self.qr2[at, :] = self.qr1[at, :] + v * jnp.abs(v)

    def step_three(self, i):
        at, after = tile_at(i), tile_at(i + 1)
        if self.trim and i == self.count - 1:
            return
        if self.trim and i == 0:
            wr = self.wr[at, :]
            v = self.speed_r(i, self.e2[at, :], self.e2[after, :], self.v2[at, :], wr)
            self.fr_last[2] = self.fr[at, :] * v
            self.qr_last[...] = wr * (self.qr2[at, :] + v * jnp.abs(v))
            return
        wc, wr = self.wc[at, :], self.wr[at, :]
        e, u, v = self.move(
            2, i, self.e2[at, :], self.e2[after, :], self.u2[at, :], self.v2[at, :],
            self.fc[at, :], self.fr[at, :], wc, wr,
        )
        qc = wc * (self.qc2[at, :] + u * jnp.abs(u))
        qr = wr * (self.qr2[at, :] + v * jnp.abs(v))
        change = (qc - west(qc) + qr - north(qr, self.qr_last[...])) * self.scale
        self.qr_last[...] = qr
        self.emit(i, e * (1.0 / 0.3), u, v, change)

    def run(self):
        self.fr_last[...] = jnp.zeros_like(self.fr_last)
        self.qr_last[...] = jnp.zeros_like(self.qr_last)
        for ref in (self.e1, self.e2):
            ref[tile_at(self.count), :] = jnp.zeros((SUB, self.wide), jnp.float32)
        stages = (self.step_three, self.step_two, self.step_one)
        for t in range(self.count + LAG * (STEPS - 1)):
            for k, stage in enumerate(stages):
                i = t - LAG * (STEPS - 1 - k)
                if 0 <= i < self.count:
                    stage(i)


def reader(root, a, b, stress, hydro, side, unfold, valid):
    rows = root.shape[0]
    span = rows // FOLD // SUB
    fields = [root, a, b] + moving(stress, hydro)

    def read(f, block):
        part = unfold(side[tile_at(block % span), :], (block // span) * FIELDS + f)
        if f == 0:
            part = jnp.where(valid, part, 0.0)
        return jnp.concatenate([fields[f][tile_at(block), :], part], axis=1)

    return read


def quarter_writer(first, quarter, cols, hydro_out, pay):
    lane = lanes_of((SUB, LANE))
    lanes = cols // LANE
    rims = [jnp.zeros((SUB, LANE), jnp.float32)]

    def emit(i, e, u, v, change):
        at = tile_at(first + i)
        for k, value in enumerate((e, u, v)):
            hydro_out[0, k, at, :] = value[:, :cols]
        g = i - 1
        for k in range(lanes):
            pay[tile_at(k * quarter + g), :] = change[:, k * LANE : (k + 1) * LANE]
        rims[0] = jnp.where(lane // 2 == g, pltpu.roll(change[:, cols:], 1 + 2 * g, 1), rims[0])
        if g == quarter - 1:
            pay[tile_at(lanes * quarter), :] = rims[0]

    return emit


def middle_kernel(own, weights, params, root, a, b, stress, hydro, side, *refs):
    hydro_out, pay, *refs = refs[1:] if own else refs
    rows, cols = root.shape
    quarter = rows // SUB // 4
    read = reader(root, a, b, stress, hydro, side, *side_lanes(lax.axis_index("tx") == 0))
    mine = lax.axis_index("cond") % 2
    lower_half = mine == (1 if own else 0)
    first = jnp.where(lower_half, 2 * quarter, quarter) - 1
    emit = quarter_writer(first, quarter, cols, hydro_out, pay)
    Sweep(
        quarter + 2, cols + LANE, lambda f, i: read(f, first + i), emit, weights, params, refs, True
    ).run()


def middle(own, weights, params, fields, side, hydro=None):
    rows, cols = fields[0].shape
    given = (hydro,) if own else ()
    return pl.pallas_call(
        functools.partial(middle_kernel, own),
        name="middle_own" if own else "middle_other",
        out_shape=[
            pltpu.VMEM(fields[4].shape, jnp.float32),
            pltpu.VMEM((cols // LANE * rows // 4 + SUB, LANE), jnp.float32),
        ],
        in_specs=[SMEM, SMEM] + [VMEM] * (6 + own),
        out_specs=[VMEM, VMEM],
        scratch_shapes=Sweep.scratch(rows // SUB // 4 + 2, cols + LANE),
        input_output_aliases={8: 0} if own else {},
        compiler_params=pltpu.CompilerParams(vmem_limit_bytes=10 * MIB),
        cost_estimate=cost(4),
    )(weights, params, *held(*fields, side, *given))


def edge_kernel(
    own, weights, params, root, a, b, stress, hydro, side, far_a, far_b, hydro_in,
    hydro_out, pay, ends, *refs,
):
    rows, cols = root.shape
    blocks = rows // SUB
    quarter = blocks // 4
    lanes = cols // LANE
    unfold, valid = side_lanes(lax.axis_index("tx") == 0)
    read = reader(root, a, b, stress, hydro, side, unfold, valid)
    mine = lax.axis_index("cond") % 2
    top = mine == (0 if own else 1)
    from_a = top == (lax.axis_index("ty") % 2 == 1)
    first = jnp.where(top, -1, blocks - quarter - 1)

    inner = jnp.where(top, quarter, blocks - quarter - 1)
    corners = pl.ds(lanes * GROUP, SUB)
    for f in range(FIELDS):
        body = read(f, inner)
        parts = []
        for k in range(lanes):
            at = pl.ds(k * GROUP + f // 2 * SUB, SUB)
            part = jnp.where(from_a, far_a[at, :], far_b[at, :])
            moved = pltpu.roll(part, HALO, 0)
            parts.append(jnp.where(top, moved, part) if f % 2 == 0 else jnp.where(top, part, moved))
        corner = jnp.where(from_a, far_a[corners, :], far_b[corners, :])
        corner = jnp.where(top, unfold(corner, (FOLD - 1) * FIELDS + f), unfold(corner, f))
        if f == 0:
            corner = jnp.where(valid, corner, 0.0)
        outer = jnp.concatenate(parts + [corner], axis=1)
        ends[0, f] = jnp.where(top, outer, body)
        ends[1, f] = jnp.where(top, body, outer)

    def get(f, i):
        if i == 0 or i == quarter + 1:
            return ends[0 if i == 0 else 1, f]
        return read(f, first + i)

    emit = quarter_writer(first, quarter, cols, hydro_out, pay)
    outside = []

    def finish(i, e, u, v, change):
        if i == 0:
            outside.append(pltpu.roll(change[:, :cols], 1, 0))
        elif i == quarter + 1:
            pay[tile_at(lanes * quarter + 1), :] = fold_row(jnp.where(top, outside[0], change[:, :cols]))
        else:
            emit(i, e, u, v, change)

    Sweep(quarter + 2, cols + LANE, get, finish, weights, params, refs, False).run()


def edge(own, weights, params, fields, side, far_a, far_b, hydro):
    rows, cols = fields[0].shape
    wide = cols + LANE
    return pl.pallas_call(
        functools.partial(edge_kernel, own),
        name="edge_own" if own else "edge_other",
        out_shape=[
            pltpu.VMEM(hydro.shape, jnp.float32),
            pltpu.VMEM((cols // LANE * rows // 4 + 2 * SUB, LANE), jnp.float32),
        ],
        in_specs=[SMEM, SMEM] + [VMEM] * 9,
        out_specs=[VMEM, VMEM],
        scratch_shapes=[pltpu.VMEM((2, FIELDS, SUB, wide), jnp.float32)]
        + Sweep.scratch(rows // SUB // 4 + 2, wide),
        input_output_aliases={10: 0},
        compiler_params=pltpu.CompilerParams(vmem_limit_bytes=12 * MIB),
        cost_estimate=cost(3),
    )(weights, params, *held(*fields, side, far_a, far_b, hydro))


class Update:
    def __init__(self, bed, side, far_a, far_b, own_m, got_m, own_e, got_e, change_v, next_v):
        self.bed, self.side, self.far_a, self.far_b = bed, side, far_a, far_b
        self.parts = {"m": (own_m, got_m), "e": (own_e, got_e)}
        self.change_v, self.next_v = change_v, next_v
        rows, self.cols = bed.shape
        self.blocks = rows // SUB
        self.quarter = self.blocks // 4
        self.lanes = self.cols // LANE
        self.wide = self.cols + LANE
        self.side_bed = side[pl.ds(side.shape[0] - SUB, SUB), :]
        self.drop_bed = jnp.where(lax.axis_index("tx") == 0, 0, 1)
        self.mine = lax.axis_index("cond") % 2
        self.odd = lax.axis_index("ty") % 2 == 1
        col = lanes_of((SUB, self.wide))
        last_c = lax.axis_index("tx") == lax.axis_size("tx") - 1
        first_c = lax.axis_index("tx") == 0
        self.shut_c = (last_c & (col == self.cols - 1)) | (first_c & (col == self.wide - 1))
        self.last_row = rows_of((SUB, self.wide)) == SUB - 1
        self.rims = {}

    def merged(self, q, block):
        own, got = self.parts["e" if q in (0, 3) else "m"]
        at = tile_at(block)
        return jnp.where(self.mine == q // 2, own[at, :], got[at, :])

    def outside(self, q):
        at = pl.ds(self.lanes * GROUP + SUB, SUB)
        a, b = self.far_a[at, :], self.far_b[at, :]
        bed = jnp.where(self.odd, a, b) if q == 0 else jnp.where(self.odd, b, a)
        z = bed + self.merged(q, self.lanes * self.quarter + 1)
        target = SUB - 1 if q == 0 else 0
        parts = [pltpu.roll(z, (SUB + target - k) % SUB, 0) if (target - k) % SUB else z for k in range(self.lanes)]
        return jnp.concatenate(parts + [jnp.zeros((SUB, LANE), jnp.float32)], axis=1)

    def level(self, b, keep):
        if b == -1:
            return self.outside(0)
        if b == self.blocks:
            return self.outside(3)
        q, g = divmod(b, self.quarter)
        change = jnp.concatenate([self.merged(q, k * self.quarter + g) for k in range(self.lanes)], axis=1)
        if keep:
            self.change_v[tile_at(b), :] = change
        if q not in self.rims:
            self.rims[q] = self.merged(q, self.lanes * self.quarter)
        cols_bed = pltpu.roll(self.side_bed, 2 * LANE - self.drop_bed - b, 1)
        cols_change = pltpu.roll(self.rims[q], LANE - 1 - 2 * g, 1)
        return jnp.concatenate([self.bed[tile_at(b), :] + change, cols_bed + cols_change], axis=1)

    def spill(self, slope):
        return 0.25 * (slope - jnp.clip(slope, -1.0, 1.0))

    def south_face(self, z, lower, b):
        out = self.spill(south(z, lower) - z)
        if b == -1:
            return jnp.where((lax.axis_index("ty") == 0) & self.last_row, 0.0, out)
        if b == self.blocks - 1:
            return jnp.where((lax.axis_index("ty") == lax.axis_size("ty") - 1) & self.last_row, 0.0, out)
        return out

    def run(self, first, stop, keep, after=lambda b: None):
        z = self.level(first - 1, keep)
        lower = self.level(first, keep)
        gr = self.south_face(z, lower, first - 1)
        for b in range(first, stop):
            z, lower = lower, self.level(b + 1, keep)
            gr_above, gr = gr, self.south_face(z, lower, b)
            gc = jnp.where(self.shut_c, 0.0, self.spill(east(z) - z))
            out = z + gc - west(gc) + gr - north(gr, gr_above)
            self.next_v[tile_at(b), :] = out[:, : self.cols]
            after(b)


def bed_middle_kernel(
    bed, side, far_a, far_b, own_m, got_m, hydro, bed_next, bed_change, hydro_out, change_v, next_v, sems
):
    rows = bed.shape[0]
    quarter = rows // SUB // 4
    copies = [pltpu.make_async_copy(hydro, hydro_out, sems.at[0])]
    copies[0].start()
    update = Update(bed, side, far_a, far_b, own_m, got_m, None, None, change_v, next_v)
    update.run(quarter + 1, 3 * quarter - 1, True)
    for src, dst, low, high in (
        (change_v, bed_change, quarter, 3 * quarter),
        (next_v, bed_next, quarter + 1, 3 * quarter - 1),
    ):
        at = pl.ds(low * SUB, (high - low) * SUB)
        copies.append(pltpu.make_async_copy(src.at[at], dst.at[at], sems.at[len(copies)]))
        copies[-1].start()
    for copy in copies:
        copy.wait()


def bed_edge_kernel(
    bed, side, far_a, far_b, own_m, got_m, own_e, got_e, next_in, change_in, bed_next, bed_change,
    change_v, next_v, sems,
):
    rows = bed.shape[0]
    blocks = rows // SUB
    quarter = blocks // 4
    update = Update(bed, side, far_a, far_b, own_m, got_m, own_e, got_e, change_v, next_v)
    copies = []

    def send(src, dst, low, high):
        at = pl.ds(low * SUB, (high - low) * SUB)
        copies.append(pltpu.make_async_copy(src.at[at], dst.at[at], sems.at[len(copies)]))
        copies[-1].start()

    update.run(0, quarter + 1, True)
    send(change_v, bed_change, 0, quarter)
    send(next_v, bed_next, 0, quarter + 1)
    update.run(blocks - quarter - 1, blocks, True)
    send(change_v, bed_change, blocks - quarter, blocks)
    send(next_v, bed_next, blocks - quarter - 1, blocks)
    for copy in copies:
        copy.wait()


def bed_scratch(rows, cols):
    return [
        pltpu.VMEM((rows, cols), jnp.float32),
        pltpu.VMEM((rows, cols), jnp.float32),
        pltpu.SemaphoreType.DMA((4,)),
    ]


def bed_middle(bed, side, far_a, far_b, own_m, got_m, hydro):
    return pl.pallas_call(
        bed_middle_kernel,
        name="bed_middle",
        out_shape=[pltpu.HBM(x.shape, jnp.float32) for x in (bed, bed, hydro)],
        in_specs=[VMEM] * 7,
        out_specs=[ANY] * 3,
        scratch_shapes=bed_scratch(*bed.shape),
        compiler_params=pltpu.CompilerParams(vmem_limit_bytes=6 * MIB),
        cost_estimate=cost(4),
    )(*held(bed, side, far_a, far_b, own_m, got_m, hydro))


def bed_edge(bed, side, far_a, far_b, own_m, got_m, own_e, got_e, bed_next, bed_change):
    return pl.pallas_call(
        bed_edge_kernel,
        name="bed_edge",
        out_shape=[pltpu.HBM(bed.shape, jnp.float32)] * 2,
        in_specs=[VMEM] * 8 + [ANY] * 2,
        out_specs=[ANY] * 2,
        scratch_shapes=bed_scratch(*bed.shape),
        input_output_aliases={8: 0, 9: 1},
        compiler_params=pltpu.CompilerParams(vmem_limit_bytes=6 * MIB),
        cost_estimate=cost(2),
    )(
        *held(bed, side, far_a, far_b, own_m, got_m, own_e, got_e),
        *held(bed_next, bed_change, space=pltpu.HBM),
    )


def shards(bed, land_mask, cell_class, weights, cond_params, wave_stress, hydro_state):
    ny = lax.axis_size("ty")
    nc = lax.axis_size("cond")
    raw = (bed, land_mask, cell_class, wave_stress, hydro_state)
    swap = [(i, i ^ 1) for i in range(nc)]

    def pairs(first):
        return [p for i in range(first, ny - 1, 2) for p in ((i, i + 1), (i + 1, i))]

    def over_chips(part, beside=()):
        reach = 2
        while reach < nc:
            got = lax.ppermute(part, "cond", [(i, i ^ reach) for i in range(nc)])
            got, beside = lax.optimization_barrier((got, beside))
            part = part + got
            reach = 2 * reach
        return part, beside

    side = lax.ppermute(pack_side(cond_params, *raw), "tx", [(0, 1), (1, 0)])
    bed, *terms, far_a, far_b = prepare(cond_params, *raw)
    fields = (*terms, wave_stress, hydro_state)
    far_a, far_b = add_corners(side, far_a, far_b)
    far_a = lax.ppermute(far_a, "ty", pairs(0))
    hydro, pay = middle(False, weights, cond_params, fields, side)
    hydro, far_a, far_b = lax.optimization_barrier((hydro, far_a, far_b))
    far_b = lax.ppermute(far_b, "ty", pairs(1))
    got = lax.ppermute(pay, "cond", swap)
    hydro, pay = middle(True, weights, cond_params, fields, side, hydro)
    part_m = pay + got
    hydro, part_m = lax.optimization_barrier((hydro, part_m))
    hydro, pay = edge(False, weights, cond_params, fields, side, far_a, far_b, hydro)
    got = lax.ppermute(pay, "cond", swap)
    hydro, pay = edge(True, weights, cond_params, fields, side, far_a, far_b, hydro)
    own_m, hydro = over_chips(part_m, hydro)
    part_e = pay + got
    own_m, _ = lax.optimization_barrier((own_m, part_e))
    got_m = lax.ppermute(own_m, "cond", swap)
    bed_next, bed_change, hydro = bed_middle(bed, side, far_a, far_b, own_m, got_m, hydro)
    own_e, (bed_next, bed_change) = over_chips(part_e, (bed_next, bed_change))
    got_e = lax.ppermute(own_e, "cond", swap)
    bed_next, bed_change = bed_edge(
        bed, side, far_a, far_b, own_m, got_m, own_e, got_e, bed_next, bed_change
    )
    return bed_next, bed_change, hydro


def solution(mesh):
    in_specs = (
        P("ty", "tx"),
        P("ty", "tx"),
        P("ty", "tx"),
        P(),
        P("cond", None),
        P("cond", None, "ty", "tx"),
        P("cond", None, "ty", "tx"),
    )
    out_specs = (P("ty", "tx"), P("ty", "tx"), P("cond", None, "ty", "tx"))
    return jax.shard_map(shards, mesh=mesh, in_specs=in_specs, out_specs=out_specs, check_vma=False)
```

```python
import functools

import jax
import jax.numpy as jnp
from jax import lax
from jax.experimental import pallas as pl
from jax.experimental.pallas import tpu as pltpu
from jax.sharding import PartitionSpec as P

STEPS = 3
HALO = STEPS + 1
SUB = 8
LANE = 128
FIELDS = 8
GROUP = HALO * FIELDS
FOLD = LANE // GROUP
LAG = 2
MIB = 2**20
ANY = pl.BlockSpec(memory_space=pl.ANY)
VMEM = pl.BlockSpec(memory_space=pltpu.VMEM)
SMEM = pl.BlockSpec(memory_space=pltpu.SMEM)


def rows_of(shape):
    return lax.broadcasted_iota(jnp.int32, shape, 0)


def lanes_of(shape):
    return lax.broadcasted_iota(jnp.int32, shape, 1)


def east(x):
    return pltpu.roll(x, x.shape[1] - 1, 1)


def west(x):
    return pltpu.roll(x, 1, 1)


def south(x, below):
    return pltpu.roll(jnp.where(rows_of(x.shape) == 0, below, x), SUB - 1, 0)


def north(x, above):
    return pltpu.roll(jnp.where(rows_of(x.shape) == SUB - 1, above, x), 1, 0)


def tile_at(index):
    if isinstance(index, int):
        return pl.ds(index * SUB, SUB)
    return pl.ds(pl.multiple_of(index * SUB, SUB), SUB)


def held(*arrays, space=pltpu.VMEM):
    return [pltpu.with_memory_space_constraint(x, space) for x in arrays]


def cost(micros):
    return pl.CostEstimate(flops=int(micros * 10**9), bytes_accessed=0, transcendentals=0)


def level_terms(params):
    return params[0, 0] - 1.0, 0.3 * params[0, 3]


def coefficients(bed, mask, kind, tide, flow_in):
    depth = mask.astype(jnp.float32) * (1.0 - 0.5 * jnp.tanh(bed))
    root = depth * lax.rsqrt(jnp.maximum(depth, 1e-12))
    relax = jnp.where(kind == 1, 0.5 * depth, 0.0)
    return root, 1.0 - relax, 0.3 * (relax * tide + jnp.where(kind == 2, flow_in * depth, 0.0))


def moving(stress, hydro):
    return [stress.at[0, k] for k in range(2)] + [hydro.at[0, k] for k in range(3)]


def pack_side_kernel(params_in, bed, mask, kind, stress, hydro, side, reals, ints, params, sems):
    rows, cols = bed.shape
    at_left = lax.axis_index("tx") == 0
    off = pl.multiple_of(jnp.where(at_left, cols - LANE, 0), LANE)
    strips = [reals.at[0], ints.at[0], ints.at[1]] + [reals.at[k] for k in range(1, 6)]
    copies = [
        pltpu.make_async_copy(src.at[:, pl.ds(off, LANE)], strip, sems.at[f])
        for f, (src, strip) in enumerate(zip([bed, mask, kind] + moving(stress, hydro), strips))
    ] + [pltpu.make_async_copy(params_in, params, sems.at[FIELDS])]
    for copy in copies:
        copy.start()
    for copy in copies:
        copy.wait()
    tide, flow_in = level_terms(params)
    lift = jnp.where(at_left, HALO, 0)
    lift_bed = jnp.where(at_left, 1, 0)
    lane = lanes_of((SUB, LANE))
    span = rows // FOLD // SUB
    beds = jnp.zeros((SUB, LANE), jnp.float32)
    for i in range(span):
        total = jnp.zeros((SUB, LANE), jnp.float32)
        for g in range(FOLD):
            at = tile_at(g * span + i)
            first = strips[0][at, :]
            fields = list(coefficients(first, strips[1][at, :], strips[2][at, :], tide, flow_in))
            fields += [strip[at, :] for strip in strips[3:]]
            for f, part in enumerate(fields):
                place = g * FIELDS + f
                total = jnp.where(lane // HALO == place, pltpu.roll(part, lift + place * HALO, 1), total)
            block = g * span + i
            beds = jnp.where(lane == block, pltpu.roll(first, lift_bed + block, 1), beds)
        side[tile_at(i), :] = total
    side[tile_at(span), :] = beds


def pack_side(params, *raw):
    rows, cols = raw[0].shape
    return pl.pallas_call(
        pack_side_kernel,
        name="pack_side",
        out_shape=pltpu.VMEM((rows // FOLD + SUB, LANE), jnp.float32),
        in_specs=[ANY] * 6,
        out_specs=VMEM,
        scratch_shapes=[
            pltpu.VMEM((6, rows, LANE), jnp.float32),
            pltpu.VMEM((2, rows, LANE), jnp.int32),
            pltpu.SMEM(params.shape, jnp.float32),
            pltpu.SemaphoreType.DMA((FIELDS + 1,)),
        ],
        compiler_params=pltpu.CompilerParams(vmem_limit_bytes=4 * MIB),
        cost_estimate=cost(2),
    )(*held(params, *raw, space=pltpu.HBM))


PARTS = 4


def prepare_kernel(
    params_in, bed, mask, kind, stress, hydro, bed_v, root, a, b, pay_a, pay_b,
    mask_v, kind_v, ends, params, load_sems, end_sems, params_sem,
):
    rows, cols = bed.shape
    lanes = cols // LANE
    chunk = rows // PARTS
    loads, copies = [], []
    for c in range(PARTS):
        at = pl.ds(c * chunk, chunk)
        loads.append([
            pltpu.make_async_copy(src.at[at], dst.at[at], load_sems.at[f, c])
            for f, (src, dst) in enumerate(((bed, bed_v), (mask, mask_v), (kind, kind_v)))
        ])
    for f, src in enumerate(moving(stress, hydro)):
        for end, start in enumerate((0, rows - SUB)):
            copies.append(pltpu.make_async_copy(src.at[pl.ds(start, SUB)], ends.at[end, f], end_sems.at[f, end]))
    loads[0].append(pltpu.make_async_copy(params_in, params, params_sem))
    for group in loads + [copies]:
        for copy in group:
            copy.start()
    for copy in loads[0]:
        copy.wait()
    tide, flow_in = level_terms(params)
    for c in range(PARTS):
        for copy in loads[c] if c else ():
            copy.wait()
        for i in range(c * chunk // SUB, (c + 1) * chunk // SUB):
            at = tile_at(i)
            root[at, :], a[at, :], b[at, :] = coefficients(bed_v[at, :], mask_v[at, :], kind_v[at, :], tide, flow_in)
    for copy in copies:
        copy.wait()
    low = rows_of((SUB, cols)) < HALO
    odd = lax.axis_index("ty") % 2 == 1

    def edge_rows(f, end):
        if f < 3:
            return (root, a, b)[f][tile_at(0 if end == 0 else rows // SUB - 1), :]
        return ends[end, f - 3]

    for p in range(FIELDS // 2):
        pairs = []
        for end in range(2):
            both = [edge_rows(f, end) for f in (2 * p, 2 * p + 1)]
            both[1 - end] = pltpu.roll(both[1 - end], HALO, 0)
            pairs.append(jnp.where(low, *both))
        for k in range(lanes):
            at, part = pl.ds(k * GROUP + p * SUB, SUB), slice(k * LANE, (k + 1) * LANE)
            top, bottom = pairs[0][:, part], pairs[1][:, part]
            pay_a[at, :] = jnp.where(odd, top, bottom)
            pay_b[at, :] = jnp.where(odd, bottom, top)
    top = fold_row([bed_v[tile_at(0), lanes_at(k)] for k in range(lanes)])
    bottom = fold_row([pltpu.roll(bed_v[tile_at(rows // SUB - 1), lanes_at(k)], 1, 0) for k in range(lanes)])
    at = pl.ds(lanes * GROUP + SUB, SUB)
    pay_a[at, :] = jnp.where(odd, top, bottom)
    pay_b[at, :] = jnp.where(odd, bottom, top)


def fold_row(x):
    row = rows_of((SUB, LANE))
    total = x[0]
    for k in range(1, len(x)):
        total = jnp.where(row == k, pltpu.roll(x[k], k, 0), total)
    return total


def prepare(params, *raw):
    rows, cols = raw[0].shape
    tile = pltpu.VMEM((rows, cols), jnp.float32)
    return pl.pallas_call(
        prepare_kernel,
        name="prepare",
        out_shape=[tile] * 4 + [pltpu.VMEM((cols // LANE * GROUP + 2 * SUB, LANE), jnp.float32)] * 2,
        in_specs=[ANY] * 6,
        out_specs=[VMEM] * 6,
        scratch_shapes=[
            pltpu.VMEM((rows, cols), jnp.int32),
            pltpu.VMEM((rows, cols), jnp.int32),
            pltpu.VMEM((2, 5, SUB, cols), jnp.float32),
            pltpu.SMEM(params.shape, jnp.float32),
            pltpu.SemaphoreType.DMA((3, PARTS)),
            pltpu.SemaphoreType.DMA((5, 2)),
            pltpu.SemaphoreType.DMA,
        ],
        compiler_params=pltpu.CompilerParams(vmem_limit_bytes=5 * MIB),
        cost_estimate=cost(2),
    )(*held(params, *raw, space=pltpu.HBM))


def corner_kernel(side, in_a, in_b, pay_a, pay_b):
    at = pl.ds(pay_a.shape[0] - 2 * SUB, SUB)
    odd = lax.axis_index("ty") % 2 == 1
    top = side[pl.ds(0, SUB), :]
    bottom = side[pl.ds(side.shape[0] - 2 * SUB, SUB), :]
    pay_a[at, :] = jnp.where(odd, top, bottom)
    pay_b[at, :] = jnp.where(odd, bottom, top)


def add_corners(side, pay_a, pay_b):
    return pl.pallas_call(
        corner_kernel,
        name="add_corners",
        out_shape=[pltpu.VMEM(pay_a.shape, jnp.float32)] * 2,
        in_specs=[VMEM] * 3,
        out_specs=[VMEM] * 2,
        input_output_aliases={1: 0, 2: 1},
        compiler_params=pltpu.CompilerParams(vmem_limit_bytes=MIB),
        cost_estimate=cost(0.1),
    )(*held(side, pay_a, pay_b))


def side_lanes(at_left):
    drop = jnp.where(at_left, 0, HALO)
    lane = lanes_of((SUB, LANE))
    valid = jnp.where(at_left, lane, LANE - 1 - lane) < HALO

    def unfold(strip, place):
        return pltpu.roll(strip, 2 * LANE - drop - place * HALO, 1)

    return unfold, valid


class Sweep:
    NAMES = (
        ["fc", "fr", "wc", "wr", "e1", "u1"]
        + ["v1", "e2", "u2", "v2", "qc1", "qr1", "qc2", "qr2"]
    )

    def __init__(self, count, tiles, get, emit, weights, params, refs, trim):
        self.count, self.tiles, self.get, self.emit, self.trim = count, tiles, get, emit, trim
        self.__dict__.update(zip(self.NAMES + ["fr_last", "qr_last"], refs))
        cond = lax.axis_index("cond")
        self.slow = 1.0 - 0.2 * params[0, 1]
        total = weights[0]
        for k in range(1, weights.shape[0]):
            total = total + weights[k]
        ones = jnp.ones((SUB, LANE), jnp.float32)
        share = weights[cond].astype(jnp.float32) * ones / (total.astype(jnp.float32) * ones)
        self.scale = -4.0 * params[0, 2] * share
        lane, row = lanes_of((SUB, LANE)), rows_of((SUB, LANE))
        self.last_lane, self.first_lane = lane == LANE - 1, lane == 0
        self.last_row, self.first_row = row == SUB - 1, row == 0

    @classmethod
    def scratch(cls, count, tiles):
        block = pltpu.VMEM((tiles, (count + 1) * SUB, LANE), jnp.float32)
        return [block] * len(cls.NAMES) + [
            pltpu.VMEM((STEPS, tiles, SUB, LANE), jnp.float32),
            pltpu.VMEM((tiles, SUB, LANE), jnp.float32),
        ]

    def south(self, x, below):
        return pltpu.roll(jnp.where(self.first_row, below, x), SUB - 1, 0)

    def north(self, x, above):
        return pltpu.roll(jnp.where(self.last_row, above, x), 1, 0)

    def easts(self, values):
        first = value = values(0)
        first_rolled = rolled = pltpu.roll(first, LANE - 1, 1)
        for k in range(self.tiles):
            if k + 1 < self.tiles:
                after = values(k + 1)
                after_rolled = pltpu.roll(after, LANE - 1, 1)
            else:
                after, after_rolled = first, first_rolled
            yield k, value, jnp.where(self.last_lane, after_rolled, rolled)
            value, rolled = after, after_rolled

    def wests(self, values):
        before = pltpu.roll(values[-1], 1, 1)
        for k, value in enumerate(values):
            rolled = pltpu.roll(value, 1, 1)
            yield k, value, jnp.where(self.first_lane, before, rolled)
            before = rolled

    def move(self, n, i, level, lower, speeds, faces, wets, keep):
        flux, part = [], []
        for k, here, right in self.easts(level):
            wc, wr = wets(k)
            fc, fr = faces(k)
            u, v = speeds(k)
            u = (self.slow * u - (right - here) + self.get(3, i, k)) * wc
            v = (self.slow * v - (self.south(here, lower(k)) - here) + self.get(4, i, k)) * wr
            flux_r = fr * v
            part.append(
                self.get(1, i, k) * here + self.get(2, i, k) - flux_r + self.north(flux_r, self.fr_last[n, k])
            )
            self.fr_last[n, k] = flux_r
            flux.append(fc * u)
            keep(k, u, v)
        for k, value, left in self.wests(flux):
            yield k, part[k] - value + left

    def step_one(self, i):
        at = tile_at(i)
        inside = i + 1 < self.count
        for k, s, right in self.easts(lambda k: self.get(0, i, k)):
            below = self.get(0, i + 1, k) if inside else s
            for other, face_ref, wet_ref in ((right, self.fc, self.wc), (self.south(s, below), self.fr, self.wr)):
                face = s * other
                base = face + 0.1
                inverse = pl.reciprocal(base, approx=True)
                wet_ref[k, at, :] = face * (inverse * (2.0 - base * inverse))
                face_ref[k, at, :] = 0.3 * face

        def level(k):
            return 0.3 * self.get(5, i, k)

        def lower(k):
            return 0.3 * self.get(5, i + 1 if inside else i, k)

        def keep(k, u, v):
            self.u1[k, at, :] = u
            self.v1[k, at, :] = v
            self.qc1[k, at, :] = u * jnp.abs(u)
            self.qr1[k, at, :] = v * jnp.abs(v)

        speeds = lambda k: (self.get(6, i, k), self.get(7, i, k))
        for k, e in self.move(0, i, level, lower, speeds, self.faces(at), self.wets(at), keep):
            self.e1[k, at, :] = e

    def faces(self, at):
        return lambda k: (self.fc[k, at, :], self.fr[k, at, :])

    def wets(self, at):
        return lambda k: (self.wc[k, at, :], self.wr[k, at, :])

    def later(self, n, i, e, u, v, keep):
        at, after = tile_at(i), tile_at(i + 1)
        return self.move(
            n, i, lambda k: e[k, at, :], lambda k: e[k, after, :], lambda k: (u[k, at, :], v[k, at, :]),
            self.faces(at), self.wets(at), keep,
        )

    def step_two(self, i):
        at = tile_at(i)
        last = self.trim and i == self.count - 1

        def keep(k, u, v):
            if not last:
                self.u2[k, at, :] = u
                self.v2[k, at, :] = v
                self.qc2[k, at, :] = self.qc1[k, at, :] + u * jnp.abs(u)
                self.qr2[k, at, :] = self.qr1[k, at, :] + v * jnp.abs(v)

        for k, e in self.later(1, i, self.e1, self.u1, self.v1, keep):
            self.e2[k, at, :] = e

    def step_three(self, i):
        at, after = tile_at(i), tile_at(i + 1)
        if self.trim and i == self.count - 1:
            return
        if self.trim and i == 0:
            for k in range(self.tiles):
                here, wr = self.e2[k, at, :], self.wr[k, at, :]
                lower = self.e2[k, after, :]
                v = (self.slow * self.v2[k, at, :] - (self.south(here, lower) - here) + self.get(4, i, k)) * wr
                self.fr_last[2, k] = self.fr[k, at, :] * v
                self.qr_last[k] = wr * (self.qr2[k, at, :] + v * jnp.abs(v))
            return
        qcs, parts = [], []

        def keep(k, u, v):
            wc, wr = self.wets(at)(k)
            self.emit(i, 1, k, u)
            self.emit(i, 2, k, v)
            qr = wr * (self.qr2[k, at, :] + v * jnp.abs(v))
            qcs.append(wc * (self.qc2[k, at, :] + u * jnp.abs(u)))
            parts.append(qr - self.north(qr, self.qr_last[k]))
            self.qr_last[k] = qr

        for k, e in self.later(2, i, self.e2, self.u2, self.v2, keep):
            self.emit(i, 0, k, e * (1.0 / 0.3))
        for k, qc, left in self.wests(qcs):
            self.emit(i, 3, k, (qc - left + parts[k]) * self.scale)

    def run(self):
        self.fr_last[...] = jnp.zeros_like(self.fr_last)
        self.qr_last[...] = jnp.zeros_like(self.qr_last)
        for ref in (self.e1, self.e2):
            ref[:, tile_at(self.count), :] = jnp.zeros((self.tiles, SUB, LANE), jnp.float32)
        stages = (self.step_three, self.step_two, self.step_one)
        for t in range(self.count + LAG * (STEPS - 1)):
            for k, stage in enumerate(stages):
                i = t - LAG * (STEPS - 1 - k)
                if 0 <= i < self.count:
                    stage(i)


def lanes_at(k):
    return slice(k * LANE, (k + 1) * LANE)


def reader(root, a, b, stress, hydro, side, unfold, valid):
    rows, cols = root.shape
    span = rows // FOLD // SUB
    tiles = cols // LANE
    fields = [root, a, b] + moving(stress, hydro)

    def read(f, block, k):
        if k < tiles:
            return fields[f][tile_at(block), lanes_at(k)]
        part = unfold(side[tile_at(block % span), :], (block // span) * FIELDS + f)
        return jnp.where(valid, part, 0.0) if f == 0 else part

    return read


def quarter_writer(first, quarter, cols, hydro_out, pay):
    lane = lanes_of((SUB, LANE))
    tiles = cols // LANE
    rims = [jnp.zeros((SUB, LANE), jnp.float32)]

    def emit(i, what, k, value):
        g = i - 1
        if what < 3:
            if k < tiles:
                hydro_out[0, what, tile_at(first + i), lanes_at(k)] = value
        elif k < tiles:
            pay[tile_at(k * quarter + g), :] = value
        else:
            rims[0] = jnp.where(lane // 2 == g, pltpu.roll(value, 1 + 2 * g, 1), rims[0])
            if g == quarter - 1:
                pay[tile_at(tiles * quarter), :] = rims[0]

    return emit


def middle_kernel(own, weights, params, root, a, b, stress, hydro, side, *refs):
    hydro_out, pay, *refs = refs[1:] if own else refs
    rows, cols = root.shape
    quarter = rows // SUB // 4
    read = reader(root, a, b, stress, hydro, side, *side_lanes(lax.axis_index("tx") == 0))
    mine = lax.axis_index("cond") % 2
    lower_half = mine == (1 if own else 0)
    first = jnp.where(lower_half, 2 * quarter, quarter) - 1
    emit = quarter_writer(first, quarter, cols, hydro_out, pay)
    Sweep(
        quarter + 2, cols // LANE + 1, lambda f, i, k: read(f, first + i, k), emit, weights, params, refs, True
    ).run()


def middle(own, weights, params, fields, side, hydro=None):
    rows, cols = fields[0].shape
    given = (hydro,) if own else ()
    return pl.pallas_call(
        functools.partial(middle_kernel, own),
        name="middle_own" if own else "middle_other",
        out_shape=[
            pltpu.VMEM(fields[4].shape, jnp.float32),
            pltpu.VMEM((cols // LANE * rows // 4 + SUB, LANE), jnp.float32),
        ],
        in_specs=[SMEM, SMEM] + [VMEM] * (6 + own),
        out_specs=[VMEM, VMEM],
        scratch_shapes=Sweep.scratch(rows // SUB // 4 + 2, cols // LANE + 1),
        input_output_aliases={8: 0} if own else {},
        compiler_params=pltpu.CompilerParams(vmem_limit_bytes=10 * MIB),
        cost_estimate=cost(4),
    )(weights, params, *held(*fields, side, *given))


def edge_kernel(
    own, weights, params, root, a, b, stress, hydro, side, far_a, far_b, hydro_in,
    hydro_out, pay, ends, *refs,
):
    rows, cols = root.shape
    blocks = rows // SUB
    quarter = blocks // 4
    lanes = cols // LANE
    unfold, valid = side_lanes(lax.axis_index("tx") == 0)
    read = reader(root, a, b, stress, hydro, side, unfold, valid)
    mine = lax.axis_index("cond") % 2
    top = mine == (0 if own else 1)
    from_a = top == (lax.axis_index("ty") % 2 == 1)
    first = jnp.where(top, -1, blocks - quarter - 1)

    inner = jnp.where(top, quarter, blocks - quarter - 1)
    corners = pl.ds(lanes * GROUP, SUB)
    for f in range(FIELDS):
        for k in range(lanes + 1):
            body = read(f, inner, k)
            if k < lanes:
                at = pl.ds(k * GROUP + f // 2 * SUB, SUB)
                part = jnp.where(from_a, far_a[at, :], far_b[at, :])
                moved = pltpu.roll(part, HALO, 0)
                outer = jnp.where(top, moved, part) if f % 2 == 0 else jnp.where(top, part, moved)
            else:
                corner = jnp.where(from_a, far_a[corners, :], far_b[corners, :])
                outer = jnp.where(top, unfold(corner, (FOLD - 1) * FIELDS + f), unfold(corner, f))
                if f == 0:
                    outer = jnp.where(valid, outer, 0.0)
            ends[0, f, k] = jnp.where(top, outer, body)
            ends[1, f, k] = jnp.where(top, body, outer)

    def get(f, i, k):
        if i == 0 or i == quarter + 1:
            return ends[0 if i == 0 else 1, f, k]
        return read(f, first + i, k)

    emit = quarter_writer(first, quarter, cols, hydro_out, pay)
    outside = {0: [], quarter + 1: []}

    def finish(i, what, k, value):
        if i not in outside:
            emit(i, what, k, value)
        elif what == 3 and k < lanes:
            outside[i].append(value)
            if i and k == lanes - 1:
                rim = [jnp.where(top, pltpu.roll(x, 1, 0), y) for x, y in zip(outside[0], outside[i])]
                pay[tile_at(lanes * quarter + 1), :] = fold_row(rim)

    Sweep(quarter + 2, lanes + 1, get, finish, weights, params, refs, False).run()


def edge(own, weights, params, fields, side, far_a, far_b, hydro):
    rows, cols = fields[0].shape
    return pl.pallas_call(
        functools.partial(edge_kernel, own),
        name="edge_own" if own else "edge_other",
        out_shape=[
            pltpu.VMEM(hydro.shape, jnp.float32),
            pltpu.VMEM((cols // LANE * rows // 4 + 2 * SUB, LANE), jnp.float32),
        ],
        in_specs=[SMEM, SMEM] + [VMEM] * 9,
        out_specs=[VMEM, VMEM],
        scratch_shapes=[pltpu.VMEM((2, FIELDS, cols // LANE + 1, SUB, LANE), jnp.float32)]
        + Sweep.scratch(rows // SUB // 4 + 2, cols // LANE + 1),
        input_output_aliases={10: 0},
        compiler_params=pltpu.CompilerParams(vmem_limit_bytes=12 * MIB),
        cost_estimate=cost(3),
    )(weights, params, *held(*fields, side, far_a, far_b, hydro))


class Update:
    def __init__(self, bed, side, far_a, far_b, own_m, got_m, own_e, got_e, change_v, next_v):
        self.bed, self.side, self.far_a, self.far_b = bed, side, far_a, far_b
        self.parts = {"m": (own_m, got_m), "e": (own_e, got_e)}
        self.change_v, self.next_v = change_v, next_v
        rows, self.cols = bed.shape
        self.blocks = rows // SUB
        self.quarter = self.blocks // 4
        self.lanes = self.cols // LANE
        self.wide = self.cols + LANE
        self.side_bed = side[pl.ds(side.shape[0] - SUB, SUB), :]
        self.drop_bed = jnp.where(lax.axis_index("tx") == 0, 0, 1)
        self.mine = lax.axis_index("cond") % 2
        self.odd = lax.axis_index("ty") % 2 == 1
        col = lanes_of((SUB, self.wide))
        last_c = lax.axis_index("tx") == lax.axis_size("tx") - 1
        first_c = lax.axis_index("tx") == 0
        self.shut_c = (last_c & (col == self.cols - 1)) | (first_c & (col == self.wide - 1))
        self.last_row = rows_of((SUB, self.wide)) == SUB - 1
        self.rims = {}

    def merged(self, q, block):
        own, got = self.parts["e" if q in (0, 3) else "m"]
        at = tile_at(block)
        return jnp.where(self.mine == q // 2, own[at, :], got[at, :])

    def outside(self, q):
        at = pl.ds(self.lanes * GROUP + SUB, SUB)
        a, b = self.far_a[at, :], self.far_b[at, :]
        bed = jnp.where(self.odd, a, b) if q == 0 else jnp.where(self.odd, b, a)
        z = bed + self.merged(q, self.lanes * self.quarter + 1)
        target = SUB - 1 if q == 0 else 0
        parts = [pltpu.roll(z, (SUB + target - k) % SUB, 0) if (target - k) % SUB else z for k in range(self.lanes)]
        return jnp.concatenate(parts + [jnp.zeros((SUB, LANE), jnp.float32)], axis=1)

    def level(self, b, keep):
        if b == -1:
            return self.outside(0)
        if b == self.blocks:
            return self.outside(3)
        q, g = divmod(b, self.quarter)
        change = jnp.concatenate([self.merged(q, k * self.quarter + g) for k in range(self.lanes)], axis=1)
        if keep:
            self.change_v[tile_at(b), :] = change
        if q not in self.rims:
            self.rims[q] = self.merged(q, self.lanes * self.quarter)
        cols_bed = pltpu.roll(self.side_bed, 2 * LANE - self.drop_bed - b, 1)
        cols_change = pltpu.roll(self.rims[q], LANE - 1 - 2 * g, 1)
        return jnp.concatenate([self.bed[tile_at(b), :] + change, cols_bed + cols_change], axis=1)

    def spill(self, slope):
        return 0.25 * (slope - jnp.clip(slope, -1.0, 1.0))

    def south_face(self, z, lower, b):
        out = self.spill(south(z, lower) - z)
        if b == -1:
            return jnp.where((lax.axis_index("ty") == 0) & self.last_row, 0.0, out)
        if b == self.blocks - 1:
            return jnp.where((lax.axis_index("ty") == lax.axis_size("ty") - 1) & self.last_row, 0.0, out)
        return out

    def run(self, first, stop, keep, after=lambda b: None):
        z = self.level(first - 1, keep)
        lower = self.level(first, keep)
        gr = self.south_face(z, lower, first - 1)
        for b in range(first, stop):
            z, lower = lower, self.level(b + 1, keep)
            gr_above, gr = gr, self.south_face(z, lower, b)
            gc = jnp.where(self.shut_c, 0.0, self.spill(east(z) - z))
            out = z + gc - west(gc) + gr - north(gr, gr_above)
            self.next_v[tile_at(b), :] = out[:, : self.cols]
            after(b)


def bed_middle_kernel(
    bed, side, far_a, far_b, own_m, got_m, hydro, bed_next, bed_change, hydro_out, change_v, next_v, sems
):
    rows = bed.shape[0]
    quarter = rows // SUB // 4
    copies = [pltpu.make_async_copy(hydro, hydro_out, sems.at[0])]
    copies[0].start()
    update = Update(bed, side, far_a, far_b, own_m, got_m, None, None, change_v, next_v)
    update.run(quarter + 1, 3 * quarter - 1, True)
    for src, dst, low, high in (
        (change_v, bed_change, quarter, 3 * quarter),
        (next_v, bed_next, quarter + 1, 3 * quarter - 1),
    ):
        at = pl.ds(low * SUB, (high - low) * SUB)
        copies.append(pltpu.make_async_copy(src.at[at], dst.at[at], sems.at[len(copies)]))
        copies[-1].start()
    for copy in copies:
        copy.wait()


def bed_edge_kernel(
    bed, side, far_a, far_b, own_m, got_m, own_e, got_e, next_in, change_in, bed_next, bed_change,
    change_v, next_v, sems,
):
    rows = bed.shape[0]
    blocks = rows // SUB
    quarter = blocks // 4
    update = Update(bed, side, far_a, far_b, own_m, got_m, own_e, got_e, change_v, next_v)
    copies = []

    def send(src, dst, low, high):
        at = pl.ds(low * SUB, (high - low) * SUB)
        copies.append(pltpu.make_async_copy(src.at[at], dst.at[at], sems.at[len(copies)]))
        copies[-1].start()

    update.run(0, quarter + 1, True)
    send(change_v, bed_change, 0, quarter)
    send(next_v, bed_next, 0, quarter + 1)
    update.run(blocks - quarter - 1, blocks, True)
    send(change_v, bed_change, blocks - quarter, blocks)
    send(next_v, bed_next, blocks - quarter - 1, blocks)
    for copy in copies:
        copy.wait()


def bed_scratch(rows, cols):
    return [
        pltpu.VMEM((rows, cols), jnp.float32),
        pltpu.VMEM((rows, cols), jnp.float32),
        pltpu.SemaphoreType.DMA((4,)),
    ]


def bed_middle(bed, side, far_a, far_b, own_m, got_m, hydro):
    return pl.pallas_call(
        bed_middle_kernel,
        name="bed_middle",
        out_shape=[pltpu.HBM(x.shape, jnp.float32) for x in (bed, bed, hydro)],
        in_specs=[VMEM] * 7,
        out_specs=[ANY] * 3,
        scratch_shapes=bed_scratch(*bed.shape),
        compiler_params=pltpu.CompilerParams(vmem_limit_bytes=6 * MIB),
        cost_estimate=cost(4),
    )(*held(bed, side, far_a, far_b, own_m, got_m, hydro))


def bed_edge(bed, side, far_a, far_b, own_m, got_m, own_e, got_e, bed_next, bed_change):
    return pl.pallas_call(
        bed_edge_kernel,
        name="bed_edge",
        out_shape=[pltpu.HBM(bed.shape, jnp.float32)] * 2,
        in_specs=[VMEM] * 8 + [ANY] * 2,
        out_specs=[ANY] * 2,
        scratch_shapes=bed_scratch(*bed.shape),
        input_output_aliases={8: 0, 9: 1},
        compiler_params=pltpu.CompilerParams(vmem_limit_bytes=6 * MIB),
        cost_estimate=cost(2),
    )(
        *held(bed, side, far_a, far_b, own_m, got_m, own_e, got_e),
        *held(bed_next, bed_change, space=pltpu.HBM),
    )


def shards(bed, land_mask, cell_class, weights, cond_params, wave_stress, hydro_state):
    ny = lax.axis_size("ty")
    nc = lax.axis_size("cond")
    raw = (bed, land_mask, cell_class, wave_stress, hydro_state)
    swap = [(i, i ^ 1) for i in range(nc)]

    def pairs(first):
        return [p for i in range(first, ny - 1, 2) for p in ((i, i + 1), (i + 1, i))]

    def over_chips(part, beside=()):
        reach = 2
        while reach < nc:
            got = lax.ppermute(part, "cond", [(i, i ^ reach) for i in range(nc)])
            got, beside = lax.optimization_barrier((got, beside))
            part = part + got
            reach = 2 * reach
        return part, beside

    side = lax.ppermute(pack_side(cond_params, *raw), "tx", [(0, 1), (1, 0)])
    bed, *terms, far_a, far_b = prepare(cond_params, *raw)
    fields = (*terms, wave_stress, hydro_state)
    far_a, far_b = add_corners(side, far_a, far_b)
    far_a = lax.ppermute(far_a, "ty", pairs(0))
    hydro, pay = middle(False, weights, cond_params, fields, side)
    hydro, far_a, far_b = lax.optimization_barrier((hydro, far_a, far_b))
    far_b = lax.ppermute(far_b, "ty", pairs(1))
    got = lax.ppermute(pay, "cond", swap)
    hydro, pay = middle(True, weights, cond_params, fields, side, hydro)
    part_m = pay + got
    hydro, part_m = lax.optimization_barrier((hydro, part_m))
    hydro, pay = edge(False, weights, cond_params, fields, side, far_a, far_b, hydro)
    got = lax.ppermute(pay, "cond", swap)
    hydro, pay = edge(True, weights, cond_params, fields, side, far_a, far_b, hydro)
    own_m, hydro = over_chips(part_m, hydro)
    part_e = pay + got
    own_m, _ = lax.optimization_barrier((own_m, part_e))
    got_m = lax.ppermute(own_m, "cond", swap)
    bed_next, bed_change, hydro = bed_middle(bed, side, far_a, far_b, own_m, got_m, hydro)
    own_e, (bed_next, bed_change) = over_chips(part_e, (bed_next, bed_change))
    got_e = lax.ppermute(own_e, "cond", swap)
    bed_next, bed_change = bed_edge(
        bed, side, far_a, far_b, own_m, got_m, own_e, got_e, bed_next, bed_change
    )
    return bed_next, bed_change, hydro


def solution(mesh):
    in_specs = (
        P("ty", "tx"),
        P("ty", "tx"),
        P("ty", "tx"),
        P(),
        P("cond", None),
        P("cond", None, "ty", "tx"),
        P("cond", None, "ty", "tx"),
    )
    out_specs = (P("ty", "tx"), P("ty", "tx"), P("cond", None, "ty", "tx"))
    return jax.shard_map(shards, mesh=mesh, in_specs=in_specs, out_specs=out_specs, check_vma=False)
```

```python
import functools

import jax
import jax.numpy as jnp
from jax import lax
from jax.experimental import pallas as pl
from jax.experimental.pallas import tpu as pltpu
from jax.sharding import PartitionSpec as P

HALO = 4
SUB = 8
LANE = 128
FIELDS = 8
GROUP = HALO * FIELDS
FOLD = LANE // GROUP
MIB = 2**20
ANY = pl.BlockSpec(memory_space=pl.ANY)
VMEM = pl.BlockSpec(memory_space=pltpu.VMEM)
SMEM = pl.BlockSpec(memory_space=pltpu.SMEM)


def rows_of(shape):
    return lax.broadcasted_iota(jnp.int32, shape, 0)


def lanes_of(shape):
    return lax.broadcasted_iota(jnp.int32, shape, 1)


def east(x):
    return pltpu.roll(x, x.shape[1] - 1, 1)


def west(x):
    return pltpu.roll(x, 1, 1)


def south(x, below):
    return pltpu.roll(jnp.where(rows_of(x.shape) == 0, below, x), SUB - 1, 0)


def north(x, above):
    return pltpu.roll(jnp.where(rows_of(x.shape) == SUB - 1, above, x), 1, 0)


def tile_at(index):
    if isinstance(index, int):
        return pl.ds(index * SUB, SUB)
    return pl.ds(pl.multiple_of(index * SUB, SUB), SUB)


def lanes_at(k):
    return slice(k * LANE, (k + 1) * LANE)


def held(*arrays, space=pltpu.VMEM):
    return [pltpu.with_memory_space_constraint(x, space) for x in arrays]


def cost(micros):
    return pl.CostEstimate(flops=int(micros * 10**9), bytes_accessed=0, transcendentals=0)


def level_terms(params):
    return params[0, 0] - 1.0, 0.3 * params[0, 3]


def coefficients(bed, mask, kind, tide, flow_in):
    depth = mask.astype(jnp.float32) * (1.0 - 0.5 * jnp.tanh(bed))
    root = depth * lax.rsqrt(jnp.maximum(depth, 1e-12))
    relax = jnp.where(kind == 1, 0.5 * depth, 0.0)
    return root, 1.0 - relax, 0.3 * (relax * tide + jnp.where(kind == 2, flow_in * depth, 0.0))


def moving(stress, hydro):
    return [stress.at[0, k] for k in range(2)] + [hydro.at[0, k] for k in range(3)]


def pack_side_kernel(params_in, bed, mask, kind, stress, hydro, side, reals, ints, params, sems):
    rows, cols = bed.shape
    at_left = lax.axis_index("tx") == 0
    off = pl.multiple_of(jnp.where(at_left, cols - LANE, 0), LANE)
    strips = [reals.at[0], ints.at[0], ints.at[1]] + [reals.at[k] for k in range(1, 6)]
    copies = [
        pltpu.make_async_copy(src.at[:, pl.ds(off, LANE)], strip, sems.at[f])
        for f, (src, strip) in enumerate(zip([bed, mask, kind] + moving(stress, hydro), strips))
    ] + [pltpu.make_async_copy(params_in, params, sems.at[FIELDS])]
    for copy in copies:
        copy.start()
    for copy in copies:
        copy.wait()
    tide, flow_in = level_terms(params)
    lift = jnp.where(at_left, HALO, 0)
    lift_bed = jnp.where(at_left, 1, 0)
    lane = lanes_of((SUB, LANE))
    span = rows // FOLD // SUB
    beds = jnp.zeros((SUB, LANE), jnp.float32)
    for i in range(span):
        total = jnp.zeros((SUB, LANE), jnp.float32)
        for g in range(FOLD):
            at = tile_at(g * span + i)
            first = strips[0][at, :]
            fields = list(coefficients(first, strips[1][at, :], strips[2][at, :], tide, flow_in))
            fields += [strip[at, :] for strip in strips[3:]]
            for f, part in enumerate(fields):
                place = g * FIELDS + f
                total = jnp.where(lane // HALO == place, pltpu.roll(part, lift + place * HALO, 1), total)
            block = g * span + i
            beds = jnp.where(lane == block, pltpu.roll(first, lift_bed + block, 1), beds)
        side[tile_at(i), :] = total
    side[tile_at(span), :] = beds


def pack_side(params, *raw):
    rows, cols = raw[0].shape
    return pl.pallas_call(
        pack_side_kernel,
        name="pack_side",
        out_shape=pltpu.VMEM((rows // FOLD + SUB, LANE), jnp.float32),
        in_specs=[ANY] * 6,
        out_specs=VMEM,
        scratch_shapes=[
            pltpu.VMEM((6, rows, LANE), jnp.float32),
            pltpu.VMEM((2, rows, LANE), jnp.int32),
            pltpu.SMEM(params.shape, jnp.float32),
            pltpu.SemaphoreType.DMA((FIELDS + 1,)),
        ],
        compiler_params=pltpu.CompilerParams(vmem_limit_bytes=4 * MIB),
        cost_estimate=cost(2),
    )(*held(params, *raw, space=pltpu.HBM))


PARTS = 4


def prepare_kernel(
    params_in, bed, mask, kind, stress, hydro, bed_v, root, a, b, pay_a, pay_b,
    mask_v, kind_v, ends, params, load_sems, end_sems, params_sem,
):
    rows, cols = bed.shape
    lanes = cols // LANE
    chunk = rows // PARTS
    loads, copies = [], []
    for c in range(PARTS):
        at = pl.ds(c * chunk, chunk)
        loads.append([
            pltpu.make_async_copy(src.at[at], dst.at[at], load_sems.at[f, c])
            for f, (src, dst) in enumerate(((bed, bed_v), (mask, mask_v), (kind, kind_v)))
        ])
    for f, src in enumerate(moving(stress, hydro)):
        for end, start in enumerate((0, rows - SUB)):
            copies.append(pltpu.make_async_copy(src.at[pl.ds(start, SUB)], ends.at[end, f], end_sems.at[f, end]))
    loads[0].append(pltpu.make_async_copy(params_in, params, params_sem))
    for group in loads + [copies]:
        for copy in group:
            copy.start()
    for copy in loads[0]:
        copy.wait()
    tide, flow_in = level_terms(params)
    for c in range(PARTS):
        for copy in loads[c] if c else ():
            copy.wait()
        for i in range(c * chunk // SUB, (c + 1) * chunk // SUB):
            at = tile_at(i)
            values = coefficients(bed_v[at, :], mask_v[at, :], kind_v[at, :], tide, flow_in)
            for ref, value in zip((root, a, b), values):
                for k in range(lanes):
                    ref[k, at, :] = value[:, lanes_at(k)]
    for copy in copies:
        copy.wait()
    low = rows_of((SUB, cols)) < HALO
    odd = lax.axis_index("ty") % 2 == 1

    def edge_rows(f, end):
        if f < 3:
            at = tile_at(0 if end == 0 else rows // SUB - 1)
            return jnp.concatenate([(root, a, b)[f][k, at, :] for k in range(lanes)], axis=1)
        return ends[end, f - 3]

    for p in range(FIELDS // 2):
        pairs = []
        for end in range(2):
            both = [edge_rows(f, end) for f in (2 * p, 2 * p + 1)]
            both[1 - end] = pltpu.roll(both[1 - end], HALO, 0)
            pairs.append(jnp.where(low, *both))
        for k in range(lanes):
            at, part = pl.ds(k * GROUP + p * SUB, SUB), slice(k * LANE, (k + 1) * LANE)
            top, bottom = pairs[0][:, part], pairs[1][:, part]
            pay_a[at, :] = jnp.where(odd, top, bottom)
            pay_b[at, :] = jnp.where(odd, bottom, top)
    top = fold_row([bed_v[tile_at(0), lanes_at(k)] for k in range(lanes)])
    bottom = fold_row([pltpu.roll(bed_v[tile_at(rows // SUB - 1), lanes_at(k)], 1, 0) for k in range(lanes)])
    at = pl.ds(lanes * GROUP + SUB, SUB)
    pay_a[at, :] = jnp.where(odd, top, bottom)
    pay_b[at, :] = jnp.where(odd, bottom, top)


def fold_row(x):
    row = rows_of((SUB, LANE))
    total = x[0]
    for k in range(1, len(x)):
        total = jnp.where(row == k, pltpu.roll(x[k], k, 0), total)
    return total


def prepare(params, *raw):
    rows, cols = raw[0].shape
    tile = pltpu.VMEM((rows, cols), jnp.float32)
    planes = pltpu.VMEM((cols // LANE, rows, LANE), jnp.float32)
    return pl.pallas_call(
        prepare_kernel,
        name="prepare",
        out_shape=[tile] + [planes] * 3 + [pltpu.VMEM((cols // LANE * GROUP + 2 * SUB, LANE), jnp.float32)] * 2,
        in_specs=[ANY] * 6,
        out_specs=[VMEM] * 6,
        scratch_shapes=[
            pltpu.VMEM((rows, cols), jnp.int32),
            pltpu.VMEM((rows, cols), jnp.int32),
            pltpu.VMEM((2, 5, SUB, cols), jnp.float32),
            pltpu.SMEM(params.shape, jnp.float32),
            pltpu.SemaphoreType.DMA((3, PARTS)),
            pltpu.SemaphoreType.DMA((5, 2)),
            pltpu.SemaphoreType.DMA,
        ],
        compiler_params=pltpu.CompilerParams(vmem_limit_bytes=5 * MIB),
        cost_estimate=cost(2),
    )(*held(params, *raw, space=pltpu.HBM))


def corner_kernel(side, in_a, in_b, pay_a, pay_b):
    at = pl.ds(pay_a.shape[0] - 2 * SUB, SUB)
    odd = lax.axis_index("ty") % 2 == 1
    top = side[pl.ds(0, SUB), :]
    bottom = side[pl.ds(side.shape[0] - 2 * SUB, SUB), :]
    pay_a[at, :] = jnp.where(odd, top, bottom)
    pay_b[at, :] = jnp.where(odd, bottom, top)


def add_corners(side, pay_a, pay_b):
    return pl.pallas_call(
        corner_kernel,
        name="add_corners",
        out_shape=[pltpu.VMEM(pay_a.shape, jnp.float32)] * 2,
        in_specs=[VMEM] * 3,
        out_specs=[VMEM] * 2,
        input_output_aliases={1: 0, 2: 1},
        compiler_params=pltpu.CompilerParams(vmem_limit_bytes=MIB),
        cost_estimate=cost(0.1),
    )(*held(side, pay_a, pay_b))


def side_lanes(at_left):
    drop = jnp.where(at_left, 0, HALO)
    lane = lanes_of((SUB, LANE))
    valid = jnp.where(at_left, lane, LANE - 1 - lane) < HALO

    def unfold(strip, place):
        return pltpu.roll(strip, 2 * LANE - drop - place * HALO, 1)

    return unfold, valid


class Sweep:
    NAMES = (
        ["s", "e0", "fc", "fr", "wc", "wr", "e1", "u1", "v1"]
        + ["e2", "u2", "v2", "qc1", "qr1", "qc2", "qr2", "flux", "load"]
    )

    def __init__(self, count, tiles, get, weights, params, refs):
        self.count, self.tiles, self.get = count, tiles, get
        self.__dict__.update(zip(self.NAMES + ["results"], refs))
        cond = lax.axis_index("cond")
        self.slow = 1.0 - 0.2 * params[0, 1]
        total = weights[0]
        for k in range(1, weights.shape[0]):
            total = total + weights[k]
        ones = jnp.ones((SUB, LANE), jnp.float32)
        share = weights[cond].astype(jnp.float32) * ones / (total.astype(jnp.float32) * ones)
        self.scale = jnp.concatenate([-4.0 * params[0, 2] * share] * tiles, axis=1)

    @classmethod
    def scratch(cls, count, tiles):
        block = pltpu.VMEM((count * SUB, tiles * LANE), jnp.float32)
        return [block] * len(cls.NAMES) + [pltpu.VMEM((4, tiles, count * SUB, LANE), jnp.float32)]

    def below(self, ref, j):
        if j + 1 < self.count:
            return ref[tile_at(j + 1), :]
        return pltpu.roll(ref[tile_at(0), :], SUB - 1, 0)

    def above(self, ref, j):
        if j > 0:
            return ref[tile_at(j - 1), :]
        return pltpu.roll(ref[tile_at(self.count - 1), :], 1, 0)

    def put(self, what, j, value):
        for k in range(self.tiles):
            self.results[what, k, pl.ds(j, SUB, stride=self.count), :] = value[:, lanes_at(k)]

    def step(self, e, u, v, after):
        rest = []
        for j in range(self.count):
            at = tile_at(j)
            level = e[at, :]
            new_u = (self.slow * u(j) - (east(level) - level) + self.get(3, j)) * self.wc[at, :]
            new_v = (self.slow * v(j) - (self.below(e, j) - level) + self.get(4, j)) * self.wr[at, :]
            flux_c = self.fc[at, :] * new_u
            flux_r = self.fr[at, :] * new_v
            self.flux[at, :] = flux_r
            part = self.get(1, j) * level + self.get(2, j) - (flux_c - west(flux_c) + flux_r)
            if j == 0:
                rest.append(part)
            after(j, new_u, new_v)
            if j:
                yield j, part + self.above(self.flux, j)
        yield 0, rest[0] + self.above(self.flux, 0)

    def run(self):
        for j in range(self.count):
            at = tile_at(j)
            self.s[at, :] = self.get(0, j)
            self.e0[at, :] = 0.3 * self.get(5, j)
        for j in range(self.count):
            at = tile_at(j)
            s = self.s[at, :]
            for other, face_ref, wet_ref in (
                (east(s), self.fc, self.wc),
                (self.below(self.s, j), self.fr, self.wr),
            ):
                face = s * other
                base = face + 0.1
                inverse = pl.reciprocal(base, approx=True)
                wet_ref[at, :] = face * (inverse * (2.0 - base * inverse))
                face_ref[at, :] = 0.3 * face

        def first(j, u, v):
            at = tile_at(j)
            self.u1[at, :] = u
            self.v1[at, :] = v
            self.qc1[at, :] = u * jnp.abs(u)
            self.qr1[at, :] = v * jnp.abs(v)

        for j, e in self.step(self.e0, lambda j: self.get(6, j), lambda j: self.get(7, j), first):
            self.e1[tile_at(j), :] = e

        def second(j, u, v):
            at = tile_at(j)
            self.u2[at, :] = u
            self.v2[at, :] = v
            self.qc2[at, :] = self.qc1[at, :] + u * jnp.abs(u)
            self.qr2[at, :] = self.qr1[at, :] + v * jnp.abs(v)

        u, v = self.u1, self.v1
        for j, e in self.step(self.e1, lambda j: u[tile_at(j), :], lambda j: v[tile_at(j), :], second):
            self.e2[tile_at(j), :] = e

        rest = []

        def third(j, u, v):
            at = tile_at(j)
            self.put(1, j, u)
            self.put(2, j, v)
            qc = self.wc[at, :] * (self.qc2[at, :] + u * jnp.abs(u))
            qr = self.wr[at, :] * (self.qr2[at, :] + v * jnp.abs(v))
            self.load[at, :] = qr
            part = qc - west(qc) + qr
            if j == 0:
                rest.append(part)
            else:
                self.put(3, j, (part - self.above(self.load, j)) * self.scale)

        u2, v2 = self.u2, self.v2
        for j, e in self.step(self.e2, lambda j: u2[tile_at(j), :], lambda j: v2[tile_at(j), :], third):
            self.put(0, j, e * (1.0 / 0.3))
        self.put(3, 0, (rest[0] - self.above(self.load, 0)) * self.scale)
        return self.results


class Region:
    def __init__(self, fields, side, stage, first, quarter):
        self.fields, self.side, self.stage, self.first = fields, side, stage, first
        self.count = quarter + 2
        _, rows, _ = fields[0].shape
        self.span = rows // FOLD // SUB
        self.tiles = fields[0].shape[0]
        self.unfold, self.valid = side_lanes(lax.axis_index("tx") == 0)

    def main(self, f, block, k):
        if f < 3:
            return self.fields[f][k, tile_at(block), :]
        return self.fields[f][tile_at(block), lanes_at(k)]

    def lanes(self, f, block):
        part = self.unfold(self.side[tile_at(block % self.span), :], (block // self.span) * FIELDS + f)
        return jnp.where(self.valid, part, 0.0) if f == 0 else part

    def fill(self, spots, direct):
        for i in spots:
            for f in range(FIELDS):
                for k in range(self.tiles):
                    if not (direct and f < 3):
                        self.stage[f, k, tile_at(i), :] = self.main(f, self.first + i, k)
                self.stage[f, self.tiles, tile_at(i), :] = self.lanes(f, self.first + i)

    def get(self, direct):
        start = pl.multiple_of(self.first * SUB, SUB)

        def get(f, j):
            parts = []
            for k in range(self.tiles + 1):
                if direct and f < 3 and k < self.tiles:
                    parts.append(self.fields[f][k, pl.ds(start + j, SUB, stride=self.count), :])
                else:
                    parts.append(self.stage[f, k, pl.ds(j, SUB, stride=self.count), :])
            return jnp.concatenate(parts, axis=1)

        return get

    def write(self, results, hydro_out, pay):
        lane = lanes_of((SUB, LANE))
        quarter = self.count - 2
        rim = jnp.zeros((SUB, LANE), jnp.float32)
        for g in range(quarter):
            for k in range(self.tiles):
                for what in range(3):
                    hydro_out[0, what, tile_at(self.first + g + 1), lanes_at(k)] = results[what, k, tile_at(g + 1), :]
                pay[tile_at(k * quarter + g), :] = results[3, k, tile_at(g + 1), :]
            rim = jnp.where(lane // 2 == g, pltpu.roll(results[3, self.tiles, tile_at(g + 1), :], 1 + 2 * g, 1), rim)
        pay[tile_at(self.tiles * quarter), :] = rim


def middle_kernel(own, weights, params, root, a, b, stress, hydro, side, *refs):
    hydro_out, pay, stage, *refs = refs[1:] if own else refs
    tiles, rows, _ = root.shape
    quarter = rows // SUB // 4
    mine = lax.axis_index("cond") % 2
    lower_half = mine == (1 if own else 0)
    first = jnp.where(lower_half, 2 * quarter, quarter) - 1
    region = Region([root, a, b] + moving(stress, hydro), side, stage, first, quarter)
    region.fill(range(quarter + 2), True)
    results = Sweep(quarter + 2, tiles + 1, region.get(True), weights, params, refs).run()
    region.write(results, hydro_out, pay)


def flow_scratch(rows, tiles):
    count = rows // SUB // 4 + 2
    return [pltpu.VMEM((FIELDS, tiles + 1, count * SUB, LANE), jnp.float32)] + Sweep.scratch(count, tiles + 1)


def middle(own, weights, params, fields, side, hydro=None):
    tiles, rows, _ = fields[0].shape
    given = (hydro,) if own else ()
    return pl.pallas_call(
        functools.partial(middle_kernel, own),
        name="middle_own" if own else "middle_other",
        out_shape=[
            pltpu.VMEM(fields[4].shape, jnp.float32),
            pltpu.VMEM((tiles * rows // 4 + SUB, LANE), jnp.float32),
        ],
        in_specs=[SMEM, SMEM] + [VMEM] * (6 + own),
        out_specs=[VMEM, VMEM],
        scratch_shapes=flow_scratch(rows, tiles),
        input_output_aliases={8: 0} if own else {},
        compiler_params=pltpu.CompilerParams(vmem_limit_bytes=16 * MIB),
        cost_estimate=cost(4),
    )(weights, params, *held(*fields, side, *given))


def edge_kernel(
    own, weights, params, root, a, b, stress, hydro, side, far_a, far_b, hydro_in,
    hydro_out, pay, stage, *refs,
):
    tiles, rows, _ = root.shape
    blocks = rows // SUB
    quarter = blocks // 4
    mine = lax.axis_index("cond") % 2
    top = mine == (0 if own else 1)
    from_a = top == (lax.axis_index("ty") % 2 == 1)
    first = jnp.where(top, -1, blocks - quarter - 1)
    region = Region([root, a, b] + moving(stress, hydro), side, stage, first, quarter)
    region.fill(range(1, quarter + 1), False)

    inner = jnp.where(top, quarter, blocks - quarter - 1)
    corners = pl.ds(tiles * GROUP, SUB)
    for f in range(FIELDS):
        for k in range(tiles + 1):
            if k < tiles:
                body = region.main(f, inner, k)
                at = pl.ds(k * GROUP + f // 2 * SUB, SUB)
                part = jnp.where(from_a, far_a[at, :], far_b[at, :])
                moved = pltpu.roll(part, HALO, 0)
                outer = jnp.where(top, moved, part) if f % 2 == 0 else jnp.where(top, part, moved)
            else:
                body = region.lanes(f, inner)
                corner = jnp.where(from_a, far_a[corners, :], far_b[corners, :])
                outer = region.unfold(corner, jnp.where(top, (FOLD - 1) * FIELDS, 0) + f)
                if f == 0:
                    outer = jnp.where(region.valid, outer, 0.0)
            stage[f, k, tile_at(0), :] = jnp.where(top, outer, body)
            stage[f, k, tile_at(quarter + 1), :] = jnp.where(top, body, outer)

    results = Sweep(quarter + 2, tiles + 1, region.get(False), weights, params, refs).run()
    region.write(results, hydro_out, pay)
    rim = [
        jnp.where(top, pltpu.roll(results[3, k, tile_at(0), :], 1, 0), results[3, k, tile_at(quarter + 1), :])
        for k in range(tiles)
    ]
    pay[tile_at(tiles * quarter + 1), :] = fold_row(rim)


def edge(own, weights, params, fields, side, far_a, far_b, hydro):
    tiles, rows, _ = fields[0].shape
    return pl.pallas_call(
        functools.partial(edge_kernel, own),
        name="edge_own" if own else "edge_other",
        out_shape=[
            pltpu.VMEM(hydro.shape, jnp.float32),
            pltpu.VMEM((tiles * rows // 4 + 2 * SUB, LANE), jnp.float32),
        ],
        in_specs=[SMEM, SMEM] + [VMEM] * 9,
        out_specs=[VMEM, VMEM],
        scratch_shapes=flow_scratch(rows, tiles),
        input_output_aliases={10: 0},
        compiler_params=pltpu.CompilerParams(vmem_limit_bytes=16 * MIB),
        cost_estimate=cost(3),
    )(weights, params, *held(*fields, side, far_a, far_b, hydro))


class Update:
    def __init__(self, bed, side, far_a, far_b, own_m, got_m, own_e, got_e, change_v, next_v):
        self.bed, self.side, self.far_a, self.far_b = bed, side, far_a, far_b
        self.parts = {"m": (own_m, got_m), "e": (own_e, got_e)}
        self.change_v, self.next_v = change_v, next_v
        rows, self.cols = bed.shape
        self.blocks = rows // SUB
        self.quarter = self.blocks // 4
        self.lanes = self.cols // LANE
        self.wide = self.cols + LANE
        self.side_bed = side[pl.ds(side.shape[0] - SUB, SUB), :]
        self.drop_bed = jnp.where(lax.axis_index("tx") == 0, 0, 1)
        self.mine = lax.axis_index("cond") % 2
        self.odd = lax.axis_index("ty") % 2 == 1
        col = lanes_of((SUB, self.wide))
        last_c = lax.axis_index("tx") == lax.axis_size("tx") - 1
        first_c = lax.axis_index("tx") == 0
        self.shut_c = (last_c & (col == self.cols - 1)) | (first_c & (col == self.wide - 1))
        self.last_row = rows_of((SUB, self.wide)) == SUB - 1
        self.rims = {}

    def merged(self, q, block):
        own, got = self.parts["e" if q in (0, 3) else "m"]
        at = tile_at(block)
        return jnp.where(self.mine == q // 2, own[at, :], got[at, :])

    def outside(self, q):
        at = pl.ds(self.lanes * GROUP + SUB, SUB)
        a, b = self.far_a[at, :], self.far_b[at, :]
        bed = jnp.where(self.odd, a, b) if q == 0 else jnp.where(self.odd, b, a)
        z = bed + self.merged(q, self.lanes * self.quarter + 1)
        target = SUB - 1 if q == 0 else 0
        parts = [pltpu.roll(z, (SUB + target - k) % SUB, 0) if (target - k) % SUB else z for k in range(self.lanes)]
        return jnp.concatenate(parts + [jnp.zeros((SUB, LANE), jnp.float32)], axis=1)

    def level(self, b, keep):
        if b == -1:
            return self.outside(0)
        if b == self.blocks:
            return self.outside(3)
        q, g = divmod(b, self.quarter)
        change = jnp.concatenate([self.merged(q, k * self.quarter + g) for k in range(self.lanes)], axis=1)
        if keep:
            self.change_v[tile_at(b), :] = change
        if q not in self.rims:
            self.rims[q] = self.merged(q, self.lanes * self.quarter)
        cols_bed = pltpu.roll(self.side_bed, 2 * LANE - self.drop_bed - b, 1)
        cols_change = pltpu.roll(self.rims[q], LANE - 1 - 2 * g, 1)
        return jnp.concatenate([self.bed[tile_at(b), :] + change, cols_bed + cols_change], axis=1)

    def spill(self, slope):
        return 0.25 * (slope - jnp.clip(slope, -1.0, 1.0))

    def south_face(self, z, lower, b):
        out = self.spill(south(z, lower) - z)
        if b == -1:
            return jnp.where((lax.axis_index("ty") == 0) & self.last_row, 0.0, out)
        if b == self.blocks - 1:
            return jnp.where((lax.axis_index("ty") == lax.axis_size("ty") - 1) & self.last_row, 0.0, out)
        return out

    def run(self, first, stop, keep, after=lambda b: None):
        z = self.level(first - 1, keep)
        lower = self.level(first, keep)
        gr = self.south_face(z, lower, first - 1)
        for b in range(first, stop):
            z, lower = lower, self.level(b + 1, keep)
            gr_above, gr = gr, self.south_face(z, lower, b)
            gc = jnp.where(self.shut_c, 0.0, self.spill(east(z) - z))
            out = z + gc - west(gc) + gr - north(gr, gr_above)
            self.next_v[tile_at(b), :] = out[:, : self.cols]
            after(b)


def bed_middle_kernel(
    bed, side, far_a, far_b, own_m, got_m, hydro, bed_next, bed_change, hydro_out, change_v, next_v, sems
):
    rows = bed.shape[0]
    quarter = rows // SUB // 4
    copies = [pltpu.make_async_copy(hydro, hydro_out, sems.at[0])]
    copies[0].start()
    update = Update(bed, side, far_a, far_b, own_m, got_m, None, None, change_v, next_v)
    update.run(quarter + 1, 3 * quarter - 1, True)
    for src, dst, low, high in (
        (change_v, bed_change, quarter, 3 * quarter),
        (next_v, bed_next, quarter + 1, 3 * quarter - 1),
    ):
        at = pl.ds(low * SUB, (high - low) * SUB)
        copies.append(pltpu.make_async_copy(src.at[at], dst.at[at], sems.at[len(copies)]))
        copies[-1].start()
    for copy in copies:
        copy.wait()


def bed_edge_kernel(
    bed, side, far_a, far_b, own_m, got_m, own_e, got_e, next_in, change_in, bed_next, bed_change,
    change_v, next_v, sems,
):
    rows = bed.shape[0]
    blocks = rows // SUB
    quarter = blocks // 4
    update = Update(bed, side, far_a, far_b, own_m, got_m, own_e, got_e, change_v, next_v)
    copies = []

    def send(src, dst, low, high):
        at = pl.ds(low * SUB, (high - low) * SUB)
        copies.append(pltpu.make_async_copy(src.at[at], dst.at[at], sems.at[len(copies)]))
        copies[-1].start()

    update.run(0, quarter + 1, True)
    send(change_v, bed_change, 0, quarter)
    send(next_v, bed_next, 0, quarter + 1)
    update.run(blocks - quarter - 1, blocks, True)
    send(change_v, bed_change, blocks - quarter, blocks)
    send(next_v, bed_next, blocks - quarter - 1, blocks)
    for copy in copies:
        copy.wait()


def bed_scratch(rows, cols):
    return [
        pltpu.VMEM((rows, cols), jnp.float32),
        pltpu.VMEM((rows, cols), jnp.float32),
        pltpu.SemaphoreType.DMA((4,)),
    ]


def bed_middle(bed, side, far_a, far_b, own_m, got_m, hydro):
    return pl.pallas_call(
        bed_middle_kernel,
        name="bed_middle",
        out_shape=[pltpu.HBM(x.shape, jnp.float32) for x in (bed, bed, hydro)],
        in_specs=[VMEM] * 7,
        out_specs=[ANY] * 3,
        scratch_shapes=bed_scratch(*bed.shape),
        compiler_params=pltpu.CompilerParams(vmem_limit_bytes=6 * MIB),
        cost_estimate=cost(4),
    )(*held(bed, side, far_a, far_b, own_m, got_m, hydro))


def bed_edge(bed, side, far_a, far_b, own_m, got_m, own_e, got_e, bed_next, bed_change):
    return pl.pallas_call(
        bed_edge_kernel,
        name="bed_edge",
        out_shape=[pltpu.HBM(bed.shape, jnp.float32)] * 2,
        in_specs=[VMEM] * 8 + [ANY] * 2,
        out_specs=[ANY] * 2,
        scratch_shapes=bed_scratch(*bed.shape),
        input_output_aliases={8: 0, 9: 1},
        compiler_params=pltpu.CompilerParams(vmem_limit_bytes=6 * MIB),
        cost_estimate=cost(2),
    )(
        *held(bed, side, far_a, far_b, own_m, got_m, own_e, got_e),
        *held(bed_next, bed_change, space=pltpu.HBM),
    )


def shards(bed, land_mask, cell_class, weights, cond_params, wave_stress, hydro_state):
    ny = lax.axis_size("ty")
    nc = lax.axis_size("cond")
    raw = (bed, land_mask, cell_class, wave_stress, hydro_state)
    swap = [(i, i ^ 1) for i in range(nc)]

    def pairs(first):
        return [p for i in range(first, ny - 1, 2) for p in ((i, i + 1), (i + 1, i))]

    def over_chips(part, beside=()):
        reach = 2
        while reach < nc:
            got = lax.ppermute(part, "cond", [(i, i ^ reach) for i in range(nc)])
            got, beside = lax.optimization_barrier((got, beside))
            part = part + got
            reach = 2 * reach
        return part, beside

    side = lax.ppermute(pack_side(cond_params, *raw), "tx", [(0, 1), (1, 0)])
    bed, *terms, far_a, far_b = prepare(cond_params, *raw)
    fields = (*terms, wave_stress, hydro_state)
    far_a, far_b = add_corners(side, far_a, far_b)
    far_a = lax.ppermute(far_a, "ty", pairs(0))
    hydro, pay = middle(False, weights, cond_params, fields, side)
    hydro, far_a, far_b = lax.optimization_barrier((hydro, far_a, far_b))
    far_b = lax.ppermute(far_b, "ty", pairs(1))
    got = lax.ppermute(pay, "cond", swap)
    hydro, pay = middle(True, weights, cond_params, fields, side, hydro)
    part_m = pay + got
    hydro, part_m = lax.optimization_barrier((hydro, part_m))
    hydro, pay = edge(False, weights, cond_params, fields, side, far_a, far_b, hydro)
    got = lax.ppermute(pay, "cond", swap)
    hydro, pay = edge(True, weights, cond_params, fields, side, far_a, far_b, hydro)
    own_m, hydro = over_chips(part_m, hydro)
    part_e = pay + got
    own_m, _ = lax.optimization_barrier((own_m, part_e))
    got_m = lax.ppermute(own_m, "cond", swap)
    bed_next, bed_change, hydro = bed_middle(bed, side, far_a, far_b, own_m, got_m, hydro)
    own_e, (bed_next, bed_change) = over_chips(part_e, (bed_next, bed_change))
    got_e = lax.ppermute(own_e, "cond", swap)
    bed_next, bed_change = bed_edge(
        bed, side, far_a, far_b, own_m, got_m, own_e, got_e, bed_next, bed_change
    )
    return bed_next, bed_change, hydro


def solution(mesh):
    in_specs = (
        P("ty", "tx"),
        P("ty", "tx"),
        P("ty", "tx"),
        P(),
        P("cond", None),
        P("cond", None, "ty", "tx"),
        P("cond", None, "ty", "tx"),
    )
    out_specs = (P("ty", "tx"), P("ty", "tx"), P("cond", None, "ty", "tx"))
    return jax.shard_map(shards, mesh=mesh, in_specs=in_specs, out_specs=out_specs, check_vma=False)
```

```python
import functools

import jax
import jax.numpy as jnp
from jax import lax
from jax.experimental import pallas as pl
from jax.experimental.pallas import tpu as pltpu
from jax.sharding import PartitionSpec as P

STEPS = 3
HALO = STEPS + 1
SUB = 8
LANE = 128
FIELDS = 8
GROUP = HALO * FIELDS
FOLD = LANE // GROUP
LAG = 2
MIB = 2**20
ANY = pl.BlockSpec(memory_space=pl.ANY)
VMEM = pl.BlockSpec(memory_space=pltpu.VMEM)
SMEM = pl.BlockSpec(memory_space=pltpu.SMEM)


def rows_of(shape):
    return lax.broadcasted_iota(jnp.int32, shape, 0)


def lanes_of(shape):
    return lax.broadcasted_iota(jnp.int32, shape, 1)


def east(x):
    return pltpu.roll(x, x.shape[1] - 1, 1)


def west(x):
    return pltpu.roll(x, 1, 1)


def south(x, below):
    return pltpu.roll(jnp.where(rows_of(x.shape) == 0, below, x), SUB - 1, 0)


def north(x, above):
    return pltpu.roll(jnp.where(rows_of(x.shape) == SUB - 1, above, x), 1, 0)


def tile_at(index):
    if isinstance(index, int):
        return pl.ds(index * SUB, SUB)
    return pl.ds(pl.multiple_of(index * SUB, SUB), SUB)


def held(*arrays, space=pltpu.VMEM):
    return [pltpu.with_memory_space_constraint(x, space) for x in arrays]


MIDDLE, EDGE_FIRST, EDGE_SECOND = 5, 3, 3


def cost(micros):
    return pl.CostEstimate(flops=int(micros * 10**9), bytes_accessed=0, transcendentals=0)


def level_terms(params):
    return params[0, 0] - 1.0, 0.3 * params[0, 3]


def coefficients(bed, mask, kind, tide, flow_in):
    depth = mask.astype(jnp.float32) * (1.0 - 0.5 * jnp.tanh(bed))
    root = depth * lax.rsqrt(jnp.maximum(depth, 1e-12))
    relax = jnp.where(kind == 1, 0.5 * depth, 0.0)
    return root, 1.0 - relax, 0.3 * (relax * tide + jnp.where(kind == 2, flow_in * depth, 0.0))


def moving(stress, hydro):
    return [stress.at[0, k] for k in range(2)] + [hydro.at[0, k] for k in range(3)]


def pack_side_kernel(params_in, bed, mask, kind, stress, hydro, side, reals, ints, params, sems):
    rows, cols = bed.shape
    at_left = lax.axis_index("tx") == 0
    off = pl.multiple_of(jnp.where(at_left, cols - LANE, 0), LANE)
    strips = [reals.at[0], ints.at[0], ints.at[1]] + [reals.at[k] for k in range(1, 6)]
    copies = [
        pltpu.make_async_copy(src.at[:, pl.ds(off, LANE)], strip, sems.at[f])
        for f, (src, strip) in enumerate(zip([bed, mask, kind] + moving(stress, hydro), strips))
    ] + [pltpu.make_async_copy(params_in, params, sems.at[FIELDS])]
    for copy in copies:
        copy.start()
    for copy in copies:
        copy.wait()
    tide, flow_in = level_terms(params)
    lift = jnp.where(at_left, HALO, 0)
    lift_bed = jnp.where(at_left, 1, 0)
    lane = lanes_of((SUB, LANE))
    span = rows // FOLD // SUB
    beds = jnp.zeros((SUB, LANE), jnp.float32)
    for i in range(span):
        total = jnp.zeros((SUB, LANE), jnp.float32)
        for g in range(FOLD):
            at = tile_at(g * span + i)
            first = strips[0][at, :]
            fields = list(coefficients(first, strips[1][at, :], strips[2][at, :], tide, flow_in))
            fields += [strip[at, :] for strip in strips[3:]]
            for f, part in enumerate(fields):
                place = g * FIELDS + f
                total = jnp.where(lane // HALO == place, pltpu.roll(part, lift + place * HALO, 1), total)
            block = g * span + i
            beds = jnp.where(lane == block, pltpu.roll(first, lift_bed + block, 1), beds)
        side[tile_at(i), :] = total
    side[tile_at(span), :] = beds


def pack_side(params, *raw):
    rows, cols = raw[0].shape
    return pl.pallas_call(
        pack_side_kernel,
        name="pack_side",
        out_shape=pltpu.VMEM((rows // FOLD + SUB, LANE), jnp.float32),
        in_specs=[ANY] * 6,
        out_specs=VMEM,
        scratch_shapes=[
            pltpu.VMEM((6, rows, LANE), jnp.float32),
            pltpu.VMEM((2, rows, LANE), jnp.int32),
            pltpu.SMEM(params.shape, jnp.float32),
            pltpu.SemaphoreType.DMA((FIELDS + 1,)),
        ],
        compiler_params=pltpu.CompilerParams(vmem_limit_bytes=4 * MIB),
        cost_estimate=cost(2),
    )(*held(params, *raw, space=pltpu.HBM))


PARTS = 4


def prepare_kernel(
    params_in, bed, mask, kind, stress, hydro, bed_v, root, a, b, pay_a, pay_b,
    mask_v, kind_v, ends, params, load_sems, end_sems, params_sem,
):
    rows, cols = bed.shape
    lanes = cols // LANE
    chunk = rows // PARTS
    loads, copies = [], []
    for c in range(PARTS):
        at = pl.ds(c * chunk, chunk)
        loads.append([
            pltpu.make_async_copy(src.at[at], dst.at[at], load_sems.at[f, c])
            for f, (src, dst) in enumerate(((bed, bed_v), (mask, mask_v), (kind, kind_v)))
        ])
    for f, src in enumerate(moving(stress, hydro)):
        for end, start in enumerate((0, rows - SUB)):
            copies.append(pltpu.make_async_copy(src.at[pl.ds(start, SUB)], ends.at[end, f], end_sems.at[f, end]))
    loads[0].append(pltpu.make_async_copy(params_in, params, params_sem))
    for group in loads + [copies]:
        for copy in group:
            copy.start()
    for copy in loads[0]:
        copy.wait()
    tide, flow_in = level_terms(params)
    for c in range(PARTS):
        for copy in loads[c] if c else ():
            copy.wait()
        for i in range(c * chunk // SUB, (c + 1) * chunk // SUB):
            at = tile_at(i)
            root[at, :], a[at, :], b[at, :] = coefficients(bed_v[at, :], mask_v[at, :], kind_v[at, :], tide, flow_in)
    for copy in copies:
        copy.wait()
    low = rows_of((SUB, cols)) < HALO
    odd = lax.axis_index("ty") % 2 == 1

    def edge_rows(f, end):
        if f < 3:
            return (root, a, b)[f][tile_at(0 if end == 0 else rows // SUB - 1), :]
        return ends[end, f - 3]

    for p in range(FIELDS // 2):
        pairs = []
        for end in range(2):
            both = [edge_rows(f, end) for f in (2 * p, 2 * p + 1)]
            both[1 - end] = pltpu.roll(both[1 - end], HALO, 0)
            pairs.append(jnp.where(low, *both))
        for k in range(lanes):
            at, part = pl.ds(k * GROUP + p * SUB, SUB), slice(k * LANE, (k + 1) * LANE)
            top, bottom = pairs[0][:, part], pairs[1][:, part]
            pay_a[at, :] = jnp.where(odd, top, bottom)
            pay_b[at, :] = jnp.where(odd, bottom, top)
    parts = [slice(k * LANE, (k + 1) * LANE) for k in range(lanes)]
    top = fold_row([bed_v[tile_at(0), part] for part in parts])
    bottom = fold_row([pltpu.roll(bed_v[tile_at(rows // SUB - 1), part], 1, 0) for part in parts])
    at = pl.ds(lanes * GROUP + SUB, SUB)
    pay_a[at, :] = jnp.where(odd, top, bottom)
    pay_b[at, :] = jnp.where(odd, bottom, top)


def fold_row(x):
    row = rows_of((SUB, LANE))
    total = x[0]
    for k in range(1, len(x)):
        total = jnp.where(row == k, pltpu.roll(x[k], k, 0), total)
    return total


def prepare(params, *raw):
    rows, cols = raw[0].shape
    tile = pltpu.VMEM((rows, cols), jnp.float32)
    return pl.pallas_call(
        prepare_kernel,
        name="prepare",
        out_shape=[tile] * 4 + [pltpu.VMEM((cols // LANE * GROUP + 2 * SUB, LANE), jnp.float32)] * 2,
        in_specs=[ANY] * 6,
        out_specs=[VMEM] * 6,
        scratch_shapes=[
            pltpu.VMEM((rows, cols), jnp.int32),
            pltpu.VMEM((rows, cols), jnp.int32),
            pltpu.VMEM((2, 5, SUB, cols), jnp.float32),
            pltpu.SMEM(params.shape, jnp.float32),
            pltpu.SemaphoreType.DMA((3, PARTS)),
            pltpu.SemaphoreType.DMA((5, 2)),
            pltpu.SemaphoreType.DMA,
        ],
        compiler_params=pltpu.CompilerParams(vmem_limit_bytes=5 * MIB),
        cost_estimate=cost(2),
    )(*held(params, *raw, space=pltpu.HBM))


def corner_kernel(side, in_a, in_b, pay_a, pay_b):
    at = pl.ds(pay_a.shape[0] - 2 * SUB, SUB)
    odd = lax.axis_index("ty") % 2 == 1
    top = side[pl.ds(0, SUB), :]
    bottom = side[pl.ds(side.shape[0] - 2 * SUB, SUB), :]
    pay_a[at, :] = jnp.where(odd, top, bottom)
    pay_b[at, :] = jnp.where(odd, bottom, top)


def add_corners(side, pay_a, pay_b):
    return pl.pallas_call(
        corner_kernel,
        name="add_corners",
        out_shape=[pltpu.VMEM(pay_a.shape, jnp.float32)] * 2,
        in_specs=[VMEM] * 3,
        out_specs=[VMEM] * 2,
        input_output_aliases={1: 0, 2: 1},
        compiler_params=pltpu.CompilerParams(vmem_limit_bytes=MIB),
        cost_estimate=cost(0.1),
    )(*held(side, pay_a, pay_b))


def side_lanes(at_left):
    drop = jnp.where(at_left, 0, HALO)
    lane = lanes_of((SUB, LANE))
    valid = jnp.where(at_left, lane, LANE - 1 - lane) < HALO

    def unfold(strip, place):
        return pltpu.roll(strip, 2 * LANE - drop - place * HALO, 1)

    return unfold, valid


class Sweep:
    NAMES = (
        ["fc", "fr", "wc", "wr", "e1", "u1"]
        + ["v1", "e2", "u2", "v2"]
    )

    def __init__(self, count, wide, get, emit, weights, params, refs, trim):
        self.count, self.wide, self.get, self.emit, self.trim = count, wide, get, emit, trim
        self.__dict__.update(zip(self.NAMES + ["fr_last", "qr_last"], refs))
        cond = lax.axis_index("cond")
        self.slow = 1.0 - 0.2 * params[0, 1]
        total = weights[0]
        for k in range(1, weights.shape[0]):
            total = total + weights[k]
        ones = jnp.ones((SUB, LANE), jnp.float32)
        share = weights[cond].astype(jnp.float32) * ones / (total.astype(jnp.float32) * ones)
        self.scale = jnp.concatenate([-4.0 * params[0, 2] * share] * (wide // LANE), axis=1)

    @classmethod
    def scratch(cls, count, wide):
        block = pltpu.VMEM(((count + 1) * SUB, wide), jnp.float32)
        return [block] * len(cls.NAMES) + [
            pltpu.VMEM((STEPS, SUB, wide), jnp.float32),
            pltpu.VMEM((SUB, wide), jnp.float32),
        ]

    def speed_c(self, i, level, u, wc):
        return (self.slow * u - (east(level) - level) + self.get(3, i)) * wc

    def speed_r(self, i, level, lower, v, wr):
        return (self.slow * v - (south(level, lower) - level) + self.get(4, i)) * wr

    def move(self, n, i, level, lower, u, v, fc, fr, wc, wr):
        u = self.speed_c(i, level, u, wc)
        v = self.speed_r(i, level, lower, v, wr)
        flux_c = fc * u
        flux_r = fr * v
        out = self.get(1, i) * level + self.get(2, i) - (
            flux_c - west(flux_c) + flux_r - north(flux_r, self.fr_last[n])
        )
        self.fr_last[n] = flux_r
        return out, u, v

    def step_one(self, i):
        at = tile_at(i)
        s = self.get(0, i)
        level = 0.3 * self.get(5, i)
        inside = i + 1 < self.count
        face_c = s * east(s)
        face_r = s * south(s, self.get(0, i + 1) if inside else s)
        ratios = []
        for face in (face_c, face_r):
            base = face + 0.1
            inverse = pl.reciprocal(base, approx=True)
            ratios.append(face * (inverse * (2.0 - base * inverse)))
        wc, wr = ratios
        fc = 0.3 * face_c
        fr = 0.3 * face_r
        self.fc[at, :] = fc
        self.fr[at, :] = fr
        self.wc[at, :] = wc
        self.wr[at, :] = wr
        lower = 0.3 * self.get(5, i + 1) if inside else level
        e, u, v = self.move(0, i, level, lower, self.get(6, i), self.get(7, i), fc, fr, wc, wr)
        self.e1[at, :] = e
        self.u1[at, :] = u
        self.v1[at, :] = v

    def step_two(self, i):
        at, after = tile_at(i), tile_at(i + 1)
        e, u, v = self.move(
            1, i, self.e1[at, :], self.e1[after, :], self.u1[at, :], self.v1[at, :],
            self.fc[at, :], self.fr[at, :], self.wc[at, :], self.wr[at, :],
        )
        self.e2[at, :] = e
        self.u2[at, :] = u
        self.v2[at, :] = v

    def transport(self, *speeds):
        total = speeds[0] * jnp.abs(speeds[0])
        for speed in speeds[1:]:
            total = total + speed * jnp.abs(speed)
        return total

    def step_three(self, i):
        at, after = tile_at(i), tile_at(i + 1)
        if self.trim and i == self.count - 1:
            return
        if self.trim and i == 0:
            wr = self.wr[at, :]
            v = self.speed_r(i, self.e2[at, :], self.e2[after, :], self.v2[at, :], wr)
            self.fr_last[2] = self.fr[at, :] * v
            self.qr_last[...] = wr * self.transport(self.v1[at, :], self.v2[at, :], v)
            return
        wc, wr = self.wc[at, :], self.wr[at, :]
        u2, v2 = self.u2[at, :], self.v2[at, :]
        e, u, v = self.move(
            2, i, self.e2[at, :], self.e2[after, :], u2, v2, self.fc[at, :], self.fr[at, :], wc, wr
        )
        qc = wc * self.transport(self.u1[at, :], u2, u)
        qr = wr * self.transport(self.v1[at, :], v2, v)
        change = (qc - west(qc) + qr - north(qr, self.qr_last[...])) * self.scale
        self.qr_last[...] = qr
        self.emit(i, e * (1.0 / 0.3), u, v, change)

    def run(self):
        self.fr_last[...] = jnp.zeros_like(self.fr_last)
        self.qr_last[...] = jnp.zeros_like(self.qr_last)
        for ref in (self.e1, self.e2):
            ref[tile_at(self.count), :] = jnp.zeros((SUB, self.wide), jnp.float32)
        stages = (self.step_three, self.step_two, self.step_one)
        for t in range(self.count + LAG * (STEPS - 1)):
            for k, stage in enumerate(stages):
                i = t - LAG * (STEPS - 1 - k)
                if 0 <= i < self.count:
                    stage(i)


def reader(root, a, b, stress, hydro, side, unfold, valid):
    rows = root.shape[0]
    span = rows // FOLD // SUB
    fields = [root, a, b] + moving(stress, hydro)

    def read(f, block):
        part = unfold(side[tile_at(block % span), :], (block // span) * FIELDS + f)
        if f == 0:
            part = jnp.where(valid, part, 0.0)
        return jnp.concatenate([fields[f][tile_at(block), :], part], axis=1)

    return read


def chunk_writer(first, count, cols, hydro_out, pay):
    lane = lanes_of((SUB, LANE))
    lanes = cols // LANE
    half = count // 2
    mine = lax.axis_index("cond") % 2
    rims = [jnp.zeros((SUB, LANE), jnp.float32)] * 2

    def emit(i, e, u, v, change):
        at = tile_at(first + i)
        for k, value in enumerate((e, u, v)):
            hydro_out[0, k, at, :] = value[:, :cols]
        which, g = divmod(i - 1, half)
        slot = jnp.where(mine == which, 1, 0)
        for k in range(lanes):
            pay[slot, tile_at(k * half + g), :] = change[:, k * LANE : (k + 1) * LANE]
        rims[which] = jnp.where(lane // 2 == g, pltpu.roll(change[:, cols:], 1 + 2 * g, 1), rims[which])
        if g == half - 1:
            pay[slot, tile_at(lanes * half), :] = rims[which]

    return emit


def middle_kernel(weights, params, root, a, b, stress, hydro, side, hydro_out, pay, *refs):
    rows, cols = root.shape
    blocks = rows // SUB
    read = reader(root, a, b, stress, hydro, side, *side_lanes(lax.axis_index("tx") == 0))
    first = blocks // 4 - 1
    write = chunk_writer(first, blocks // 2, cols, hydro_out, pay)
    Sweep(
        blocks // 2 + 2, cols + LANE, lambda f, i: read(f, first + i), write, weights, params, refs, True
    ).run()


def middle(weights, params, fields, side):
    rows, cols = fields[0].shape
    return pl.pallas_call(
        middle_kernel,
        name="middle",
        out_shape=[
            pltpu.VMEM(fields[4].shape, jnp.float32),
            pltpu.VMEM((2, cols // LANE * rows // 4 + SUB, LANE), jnp.float32),
        ],
        in_specs=[SMEM, SMEM] + [VMEM] * 6,
        out_specs=[VMEM, VMEM],
        scratch_shapes=Sweep.scratch(rows // SUB // 2 + 2, cols + LANE),
        compiler_params=pltpu.CompilerParams(vmem_limit_bytes=12 * MIB),
        cost_estimate=cost(MIDDLE),
    )(weights, params, *held(*fields, side))


def edge_kernel(
    second, weights, params, root, a, b, stress, hydro, side, far, hydro_in, hydro_out, pay, ends, *refs
):
    rows, cols = root.shape
    blocks = rows // SUB
    quarter = blocks // 4
    lanes = cols // LANE
    unfold, valid = side_lanes(lax.axis_index("tx") == 0)
    read = reader(root, a, b, stress, hydro, side, unfold, valid)
    top = lax.axis_index("ty") % 2 == (0 if second else 1)
    first = jnp.where(top, -1, blocks - quarter - 1)

    inner = jnp.where(top, quarter, blocks - quarter - 1)
    corners = pl.ds(lanes * GROUP, SUB)
    for f in range(FIELDS):
        body = read(f, inner)
        parts = []
        for k in range(lanes):
            part = far[pl.ds(k * GROUP + f // 2 * SUB, SUB), :]
            moved = pltpu.roll(part, HALO, 0)
            parts.append(jnp.where(top, moved, part) if f % 2 == 0 else jnp.where(top, part, moved))
        corner = unfold(far[corners, :], jnp.where(top, (FOLD - 1) * FIELDS, 0) + f)
        if f == 0:
            corner = jnp.where(valid, corner, 0.0)
        outer = jnp.concatenate(parts + [corner], axis=1)
        ends[0, f] = jnp.where(top, outer, body)
        ends[1, f] = jnp.where(top, body, outer)

    def get(f, i):
        if i == 0 or i == quarter + 1:
            return ends[0 if i == 0 else 1, f]
        return read(f, first + i)

    write = chunk_writer(first, quarter, cols, hydro_out, pay)
    outside = []

    def finish(i, e, u, v, change):
        if i == 0:
            outside.append(pltpu.roll(change[:, :cols], 1, 0))
        elif i == quarter + 1:
            rim = jnp.where(top, outside[0], change[:, :cols])
            rim = fold_row([rim[:, k * LANE : (k + 1) * LANE] for k in range(lanes)])
            for slot in range(2):
                pay[slot, tile_at(lanes * quarter // 2 + 1), :] = rim
        else:
            write(i, e, u, v, change)

    Sweep(quarter + 2, cols + LANE, get, finish, weights, params, refs, False).run()


def edge(second, weights, params, fields, side, far, hydro):
    rows, cols = fields[0].shape
    wide = cols + LANE
    return pl.pallas_call(
        functools.partial(edge_kernel, second),
        name="edge_second" if second else "edge_first",
        out_shape=[
            pltpu.VMEM(hydro.shape, jnp.float32),
            pltpu.VMEM((2, cols // LANE * rows // 8 + 2 * SUB, LANE), jnp.float32),
        ],
        in_specs=[SMEM, SMEM] + [VMEM] * 8,
        out_specs=[VMEM, VMEM],
        scratch_shapes=[pltpu.VMEM((2, FIELDS, SUB, wide), jnp.float32)]
        + Sweep.scratch(rows // SUB // 4 + 2, wide),
        input_output_aliases={9: 0},
        compiler_params=pltpu.CompilerParams(vmem_limit_bytes=12 * MIB),
        cost_estimate=cost(EDGE_SECOND if second else EDGE_FIRST),
    )(weights, params, *held(*fields, side, far, hydro))


class Update:
    def __init__(self, odd, bed, side, far_a, far_b, middle, first, second, change_v, next_v):
        self.bed, self.side = bed, side
        self.far = (far_a, far_b) if odd else (far_b, far_a)
        self.parts = [first if odd else second, middle, second if odd else first]
        self.change_v, self.next_v = change_v, next_v
        rows, self.cols = bed.shape
        self.blocks = rows // SUB
        self.quarter = self.blocks // 4
        self.lanes = self.cols // LANE
        self.wide = self.cols + LANE
        self.side_bed = side[pl.ds(side.shape[0] - SUB, SUB), :]
        self.drop_bed = jnp.where(lax.axis_index("tx") == 0, 0, 1)
        self.mine = lax.axis_index("cond") % 2
        col = lanes_of((SUB, self.wide))
        last_c = lax.axis_index("tx") == lax.axis_size("tx") - 1
        first_c = lax.axis_index("tx") == 0
        self.shut_c = (last_c & (col == self.cols - 1)) | (first_c & (col == self.wide - 1))
        self.last_row = rows_of((SUB, self.wide)) == SUB - 1
        self.rims = {}

    def merged(self, chunk, half, block):
        own, got = self.parts[chunk]
        at = tile_at(block)
        return jnp.where(self.mine == half, own[at, :], got[at, :])

    def outside(self, chunk):
        bed = self.far[0 if chunk == 0 else 1][pl.ds(self.lanes * GROUP + SUB, SUB), :]
        z = bed + self.merged(chunk, 0, self.lanes * self.quarter // 2 + 1)
        target = SUB - 1 if chunk == 0 else 0
        parts = [pltpu.roll(z, (SUB + target - k) % SUB, 0) if (target - k) % SUB else z for k in range(self.lanes)]
        return jnp.concatenate(parts + [jnp.zeros((SUB, LANE), jnp.float32)], axis=1)

    def level(self, b, keep):
        if b == -1:
            return self.outside(0)
        if b == self.blocks:
            return self.outside(2)
        q = b // self.quarter
        chunk = (0, 1, 1, 2)[q]
        start, count = ((0, self.quarter), (self.quarter, 2 * self.quarter), (3 * self.quarter, self.quarter))[chunk]
        half, g = divmod(b - start, count // 2)
        change = jnp.concatenate(
            [self.merged(chunk, half, k * (count // 2) + g) for k in range(self.lanes)], axis=1
        )
        if keep(q):
            self.change_v[tile_at(b), :] = change
        if (chunk, half) not in self.rims:
            self.rims[chunk, half] = self.merged(chunk, half, self.lanes * count // 2)
        cols_bed = pltpu.roll(self.side_bed, 2 * LANE - self.drop_bed - b, 1)
        cols_change = pltpu.roll(self.rims[chunk, half], LANE - 1 - 2 * g, 1)
        return jnp.concatenate([self.bed[tile_at(b), :] + change, cols_bed + cols_change], axis=1)

    def spill(self, slope):
        return 0.25 * (slope - jnp.clip(slope, -1.0, 1.0))

    def south_face(self, z, lower, b):
        out = self.spill(south(z, lower) - z)
        if b == -1:
            return jnp.where((lax.axis_index("ty") == 0) & self.last_row, 0.0, out)
        if b == self.blocks - 1:
            return jnp.where((lax.axis_index("ty") == lax.axis_size("ty") - 1) & self.last_row, 0.0, out)
        return out

    def run(self, first, stop, keep):
        z = self.level(first - 1, keep)
        lower = self.level(first, keep)
        gr = self.south_face(z, lower, first - 1)
        for b in range(first, stop):
            z, lower = lower, self.level(b + 1, keep)
            gr_above, gr = gr, self.south_face(z, lower, b)
            gc = jnp.where(self.shut_c, 0.0, self.spill(east(z) - z))
            out = z + gc - west(gc) + gr - north(gr, gr_above)
            self.next_v[tile_at(b), :] = out[:, : self.cols]


def by_row(run):
    odd = lax.axis_index("ty") % 2 == 1
    pl.when(odd)(lambda: run(True))
    pl.when(jnp.logical_not(odd))(lambda: run(False))


def send_rows(copies, sems):
    started = []
    for n, (src, dst, low, high) in enumerate(copies):
        at = pl.ds(low * SUB, (high - low) * SUB)
        started.append(pltpu.make_async_copy(src.at[at], dst.at[at], sems.at[n]))
        started[-1].start()
    for copy in started:
        copy.wait()


def bed_early_kernel(
    bed, side, far_a, far_b, own_m, got_m, own_a, got_a, hydro, bed_next, bed_change, hydro_out,
    change_v, next_v, sems,
):
    blocks = bed.shape[0] // SUB
    quarter = blocks // 4
    state = pltpu.make_async_copy(hydro, hydro_out, sems.at[2])
    state.start()

    def run(odd):
        update = Update(
            odd, bed, side, far_a, far_b, (own_m, got_m), (own_a, got_a), None, change_v, next_v
        )
        rows = (0, 3 * quarter - 1) if odd else (quarter + 1, blocks)
        changes = (0, 3 * quarter) if odd else (quarter, blocks)
        update.run(*rows, lambda q: True)
        send_rows([(change_v, bed_change, *changes), (next_v, bed_next, *rows)], sems)

    by_row(run)
    state.wait()


def bed_late_kernel(
    bed, side, far_a, far_b, own_m, got_m, own_b, got_b, next_in, change_in, bed_next, bed_change,
    change_v, next_v, sems,
):
    blocks = bed.shape[0] // SUB
    quarter = blocks // 4

    def run(odd):
        update = Update(
            odd, bed, side, far_a, far_b, (own_m, got_m), None, (own_b, got_b), change_v, next_v
        )
        rows = (3 * quarter - 1, blocks) if odd else (0, quarter + 1)
        changes = (3 * quarter, blocks) if odd else (0, quarter)
        update.run(*rows, lambda q: q in (0, 3))
        send_rows([(change_v, bed_change, *changes), (next_v, bed_next, *rows)], sems)

    by_row(run)


def bed_scratch(rows, cols):
    return [
        pltpu.VMEM((rows, cols), jnp.float32),
        pltpu.VMEM((rows, cols), jnp.float32),
        pltpu.SemaphoreType.DMA((3,)),
    ]


def bed_early(bed, side, far_a, far_b, merged_m, merged_a, hydro):
    return pl.pallas_call(
        bed_early_kernel,
        name="bed_early",
        out_shape=[pltpu.HBM(x.shape, jnp.float32) for x in (bed, bed, hydro)],
        in_specs=[VMEM] * 9,
        out_specs=[ANY] * 3,
        scratch_shapes=bed_scratch(*bed.shape),
        compiler_params=pltpu.CompilerParams(vmem_limit_bytes=6 * MIB),
        cost_estimate=cost(4),
    )(*held(bed, side, far_a, far_b, *merged_m, *merged_a, hydro))


def bed_late(bed, side, far_a, far_b, merged_m, merged_b, bed_next, bed_change):
    return pl.pallas_call(
        bed_late_kernel,
        name="bed_late",
        out_shape=[pltpu.HBM(bed.shape, jnp.float32)] * 2,
        in_specs=[VMEM] * 8 + [ANY] * 2,
        out_specs=[ANY] * 2,
        scratch_shapes=bed_scratch(*bed.shape),
        input_output_aliases={8: 0, 9: 1},
        compiler_params=pltpu.CompilerParams(vmem_limit_bytes=6 * MIB),
        cost_estimate=cost(2),
    )(
        *held(bed, side, far_a, far_b, *merged_m, *merged_b),
        *held(bed_next, bed_change, space=pltpu.HBM),
    )


def shards(bed, land_mask, cell_class, weights, cond_params, wave_stress, hydro_state):
    ny = lax.axis_size("ty")
    nc = lax.axis_size("cond")
    raw = (bed, land_mask, cell_class, wave_stress, hydro_state)
    swap = [(i, i ^ 1) for i in range(nc)]

    def pairs(first):
        return [p for i in range(first, ny - 1, 2) for p in ((i, i + 1), (i + 1, i))]

    def over_chips(part, beside=()):
        reach = 2
        while reach < nc:
            got = lax.ppermute(part, "cond", [(i, i ^ reach) for i in range(nc)])
            got, beside = lax.optimization_barrier((got, beside))
            part = part + got
            reach = 2 * reach
        return part, beside

    side = lax.ppermute(pack_side(cond_params, *raw), "tx", [(0, 1), (1, 0)])
    bed, *terms, far_a, far_b = prepare(cond_params, *raw)
    fields = (*terms, wave_stress, hydro_state)
    far_a, far_b = add_corners(side, far_a, far_b)
    far_a = lax.ppermute(far_a, "ty", pairs(0))
    hydro, pay_m = middle(weights, cond_params, fields, side)
    hydro, pay_m, far_a, far_b = lax.optimization_barrier((hydro, pay_m, far_a, far_b))
    got_m = lax.ppermute(pay_m[0], "cond", swap)
    far_b = lax.ppermute(far_b, "ty", pairs(1))
    part_m = pay_m[1] + got_m
    hydro, part_m = lax.optimization_barrier((hydro, part_m))
    hydro, pay_a = edge(False, weights, cond_params, fields, side, far_a, hydro)
    got_a = lax.ppermute(pay_a[0], "cond", swap)
    hydro, pay_b = edge(True, weights, cond_params, fields, side, far_b, hydro)
    own_m, hydro = over_chips(part_m, hydro)
    own_m, got_a = lax.optimization_barrier((own_m, got_a))
    part_a = pay_a[1] + got_a
    got_b = lax.ppermute(pay_b[0], "cond", swap)
    part_b = pay_b[1] + got_b
    merged_m = (own_m, lax.ppermute(own_m, "cond", swap))
    own_a, _ = over_chips(part_a, part_b)
    merged_a = (own_a, lax.ppermute(own_a, "cond", swap))
    bed_next, bed_change, hydro = bed_early(bed, side, far_a, far_b, merged_m, merged_a, hydro)
    own_b, (bed_next, bed_change) = over_chips(part_b, (bed_next, bed_change))
    merged_b = (own_b, lax.ppermute(own_b, "cond", swap))
    bed_next, bed_change = bed_late(bed, side, far_a, far_b, merged_m, merged_b, bed_next, bed_change)
    return bed_next, bed_change, hydro


def solution(mesh):
    in_specs = (
        P("ty", "tx"),
        P("ty", "tx"),
        P("ty", "tx"),
        P(),
        P("cond", None),
        P("cond", None, "ty", "tx"),
        P("cond", None, "ty", "tx"),
    )
    out_specs = (P("ty", "tx"), P("ty", "tx"), P("cond", None, "ty", "tx"))
    return jax.shard_map(shards, mesh=mesh, in_specs=in_specs, out_specs=out_specs, check_vma=False)
```

```python
import functools

import jax
import jax.numpy as jnp
from jax import lax
from jax.experimental import pallas as pl
from jax.experimental.pallas import tpu as pltpu
from jax.sharding import PartitionSpec as P

STEPS = 3
HALO = STEPS + 1
SUB = 8
LANE = 128
FIELDS = 8
GROUP = HALO * FIELDS
FOLD = LANE // GROUP
LAG = 2
MIB = 2**20
ANY = pl.BlockSpec(memory_space=pl.ANY)
VMEM = pl.BlockSpec(memory_space=pltpu.VMEM)
SMEM = pl.BlockSpec(memory_space=pltpu.SMEM)


def rows_of(shape):
    return lax.broadcasted_iota(jnp.int32, shape, 0)


def lanes_of(shape):
    return lax.broadcasted_iota(jnp.int32, shape, 1)


def east(x):
    return pltpu.roll(x, x.shape[1] - 1, 1)


def west(x):
    return pltpu.roll(x, 1, 1)


def south(x, below):
    return pltpu.roll(jnp.where(rows_of(x.shape) == 0, below, x), SUB - 1, 0)


def north(x, above):
    return pltpu.roll(jnp.where(rows_of(x.shape) == SUB - 1, above, x), 1, 0)


def tile_at(index):
    if isinstance(index, int):
        return pl.ds(index * SUB, SUB)
    return pl.ds(pl.multiple_of(index * SUB, SUB), SUB)


def held(*arrays, space=pltpu.VMEM):
    return [pltpu.with_memory_space_constraint(x, space) for x in arrays]


def cost(micros):
    return pl.CostEstimate(flops=int(micros * 10**9), bytes_accessed=0, transcendentals=0)


def level_terms(params):
    return params[0, 0] - 1.0, 0.3 * params[0, 3]


def coefficients(bed, mask, kind, tide, flow_in):
    depth = mask.astype(jnp.float32) * (1.0 - 0.5 * jnp.tanh(bed))
    root = depth * lax.rsqrt(jnp.maximum(depth, 1e-12))
    relax = jnp.where(kind == 1, 0.5 * depth, 0.0)
    return root, 1.0 - relax, 0.3 * (relax * tide + jnp.where(kind == 2, flow_in * depth, 0.0))


def moving(stress, hydro):
    return [stress.at[0, k] for k in range(2)] + [hydro.at[0, k] for k in range(3)]


def pack_side_kernel(params_in, bed, mask, kind, stress, hydro, side, reals, ints, params, sems):
    rows, cols = bed.shape
    at_left = lax.axis_index("tx") == 0
    off = pl.multiple_of(jnp.where(at_left, cols - LANE, 0), LANE)
    strips = [reals.at[0], ints.at[0], ints.at[1]] + [reals.at[k] for k in range(1, 6)]
    copies = [
        pltpu.make_async_copy(src.at[:, pl.ds(off, LANE)], strip, sems.at[f])
        for f, (src, strip) in enumerate(zip([bed, mask, kind] + moving(stress, hydro), strips))
    ] + [pltpu.make_async_copy(params_in, params, sems.at[FIELDS])]
    for copy in copies:
        copy.start()
    for copy in copies:
        copy.wait()
    tide, flow_in = level_terms(params)
    lift = jnp.where(at_left, HALO, 0)
    lift_bed = jnp.where(at_left, 1, 0)
    lane = lanes_of((SUB, LANE))
    span = rows // FOLD // SUB
    beds = jnp.zeros((SUB, LANE), jnp.float32)
    for i in range(span):
        total = jnp.zeros((SUB, LANE), jnp.float32)
        for g in range(FOLD):
            at = tile_at(g * span + i)
            first = strips[0][at, :]
            fields = list(coefficients(first, strips[1][at, :], strips[2][at, :], tide, flow_in))
            fields += [strip[at, :] for strip in strips[3:]]
            for f, part in enumerate(fields):
                place = g * FIELDS + f
                total = jnp.where(lane // HALO == place, pltpu.roll(part, lift + place * HALO, 1), total)
            block = g * span + i
            beds = jnp.where(lane == block, pltpu.roll(first, lift_bed + block, 1), beds)
        side[tile_at(i), :] = total
    side[tile_at(span), :] = beds


def pack_side(params, *raw):
    rows, cols = raw[0].shape
    return pl.pallas_call(
        pack_side_kernel,
        name="pack_side",
        out_shape=pltpu.VMEM((rows // FOLD + SUB, LANE), jnp.float32),
        in_specs=[ANY] * 6,
        out_specs=VMEM,
        scratch_shapes=[
            pltpu.VMEM((6, rows, LANE), jnp.float32),
            pltpu.VMEM((2, rows, LANE), jnp.int32),
            pltpu.SMEM(params.shape, jnp.float32),
            pltpu.SemaphoreType.DMA((FIELDS + 1,)),
        ],
        compiler_params=pltpu.CompilerParams(vmem_limit_bytes=4 * MIB),
        cost_estimate=cost(2),
    )(*held(params, *raw, space=pltpu.HBM))


PARTS = 4


def prepare_kernel(
    params_in, bed, mask, kind, stress, hydro, bed_v, root, a, b, pay_a, pay_b,
    mask_v, kind_v, ends, params, load_sems, end_sems, params_sem,
):
    rows, cols = bed.shape
    lanes = cols // LANE
    chunk = rows // PARTS
    loads, copies = [], []
    for c in range(PARTS):
        at = pl.ds(c * chunk, chunk)
        loads.append([
            pltpu.make_async_copy(src.at[at], dst.at[at], load_sems.at[f, c])
            for f, (src, dst) in enumerate(((bed, bed_v), (mask, mask_v), (kind, kind_v)))
        ])
    for f, src in enumerate(moving(stress, hydro)):
        for end, start in enumerate((0, rows - SUB)):
            copies.append(pltpu.make_async_copy(src.at[pl.ds(start, SUB)], ends.at[end, f], end_sems.at[f, end]))
    loads[0].append(pltpu.make_async_copy(params_in, params, params_sem))
    for group in loads + [copies]:
        for copy in group:
            copy.start()
    for copy in loads[0]:
        copy.wait()
    tide, flow_in = level_terms(params)
    for c in range(PARTS):
        for copy in loads[c] if c else ():
            copy.wait()
        for i in range(c * chunk // SUB, (c + 1) * chunk // SUB):
            at = tile_at(i)
            root[at, :], a[at, :], b[at, :] = coefficients(bed_v[at, :], mask_v[at, :], kind_v[at, :], tide, flow_in)
    for copy in copies:
        copy.wait()
    low = rows_of((SUB, cols)) < HALO
    odd = lax.axis_index("ty") % 2 == 1

    def edge_rows(f, end):
        if f < 3:
            return (root, a, b)[f][tile_at(0 if end == 0 else rows // SUB - 1), :]
        return ends[end, f - 3]

    for p in range(FIELDS // 2):
        pairs = []
        for end in range(2):
            both = [edge_rows(f, end) for f in (2 * p, 2 * p + 1)]
            both[1 - end] = pltpu.roll(both[1 - end], HALO, 0)
            pairs.append(jnp.where(low, *both))
        for k in range(lanes):
            at, part = pl.ds(k * GROUP + p * SUB, SUB), slice(k * LANE, (k + 1) * LANE)
            top, bottom = pairs[0][:, part], pairs[1][:, part]
            pay_a[at, :] = jnp.where(odd, top, bottom)
            pay_b[at, :] = jnp.where(odd, bottom, top)
    top = fold_row(bed_v[tile_at(0), :])
    bottom = fold_row(pltpu.roll(bed_v[tile_at(rows // SUB - 1), :], 1, 0))
    at = pl.ds(lanes * GROUP + SUB, SUB)
    pay_a[at, :] = jnp.where(odd, top, bottom)
    pay_b[at, :] = jnp.where(odd, bottom, top)


def fold_row(x):
    row = rows_of((SUB, LANE))
    total = x[:, :LANE]
    for k in range(1, x.shape[1] // LANE):
        total = jnp.where(row == k, pltpu.roll(x[:, k * LANE : (k + 1) * LANE], k, 0), total)
    return total


def prepare(params, *raw):
    rows, cols = raw[0].shape
    tile = pltpu.VMEM((rows, cols), jnp.float32)
    return pl.pallas_call(
        prepare_kernel,
        name="prepare",
        out_shape=[tile] * 4 + [pltpu.VMEM((cols // LANE * GROUP + 2 * SUB, LANE), jnp.float32)] * 2,
        in_specs=[ANY] * 6,
        out_specs=[VMEM] * 6,
        scratch_shapes=[
            pltpu.VMEM((rows, cols), jnp.int32),
            pltpu.VMEM((rows, cols), jnp.int32),
            pltpu.VMEM((2, 5, SUB, cols), jnp.float32),
            pltpu.SMEM(params.shape, jnp.float32),
            pltpu.SemaphoreType.DMA((3, PARTS)),
            pltpu.SemaphoreType.DMA((5, 2)),
            pltpu.SemaphoreType.DMA,
        ],
        compiler_params=pltpu.CompilerParams(vmem_limit_bytes=5 * MIB),
        cost_estimate=cost(2),
    )(*held(params, *raw, space=pltpu.HBM))


def corner_kernel(side, in_a, in_b, pay_a, pay_b):
    at = pl.ds(pay_a.shape[0] - 2 * SUB, SUB)
    odd = lax.axis_index("ty") % 2 == 1
    top = side[pl.ds(0, SUB), :]
    bottom = side[pl.ds(side.shape[0] - 2 * SUB, SUB), :]
    pay_a[at, :] = jnp.where(odd, top, bottom)
    pay_b[at, :] = jnp.where(odd, bottom, top)


def add_corners(side, pay_a, pay_b):
    return pl.pallas_call(
        corner_kernel,
        name="add_corners",
        out_shape=[pltpu.VMEM(pay_a.shape, jnp.float32)] * 2,
        in_specs=[VMEM] * 3,
        out_specs=[VMEM] * 2,
        input_output_aliases={1: 0, 2: 1},
        compiler_params=pltpu.CompilerParams(vmem_limit_bytes=MIB),
        cost_estimate=cost(0.1),
    )(*held(side, pay_a, pay_b))


def side_lanes(at_left):
    drop = jnp.where(at_left, 0, HALO)
    lane = lanes_of((SUB, LANE))
    valid = jnp.where(at_left, lane, LANE - 1 - lane) < HALO

    def unfold(strip, place):
        return pltpu.roll(strip, 2 * LANE - drop - place * HALO, 1)

    return unfold, valid


class Sweep:
    NAMES = (
        ["fc", "fr", "wc", "wr", "e1", "u1"]
        + ["v1", "e2", "u2", "v2", "qc1", "qr1", "qc2", "qr2"]
    )

    def __init__(self, count, wide, get, emit, weights, params, refs, trim):
        self.count, self.wide, self.get, self.emit, self.trim = count, wide, get, emit, trim
        self.__dict__.update(zip(self.NAMES + ["fr_last", "qr_last"], refs))
        cond = lax.axis_index("cond")
        self.slow = 1.0 - 0.2 * params[0, 1]
        total = weights[0]
        for k in range(1, weights.shape[0]):
            total = total + weights[k]
        ones = jnp.ones((SUB, LANE), jnp.float32)
        share = weights[cond].astype(jnp.float32) * ones / (total.astype(jnp.float32) * ones)
        self.scale = jnp.concatenate([-4.0 * params[0, 2] * share] * (wide // LANE), axis=1)

    @classmethod
    def scratch(cls, count, wide):
        block = pltpu.VMEM(((count + 1) * SUB, wide), jnp.float32)
        return [block] * len(cls.NAMES) + [
            pltpu.VMEM((STEPS, SUB, wide), jnp.float32),
            pltpu.VMEM((SUB, wide), jnp.float32),
        ]

    def speed_c(self, i, level, u, wc):
        return (self.slow * u - (east(level) - level) + self.get(3, i)) * wc

    def speed_r(self, i, level, lower, v, wr):
        return (self.slow * v - (south(level, lower) - level) + self.get(4, i)) * wr

    def move(self, n, i, level, lower, u, v, fc, fr, wc, wr):
        u = self.speed_c(i, level, u, wc)
        v = self.speed_r(i, level, lower, v, wr)
        flux_c = fc * u
        flux_r = fr * v
        out = self.get(1, i) * level + self.get(2, i) - (
            flux_c - west(flux_c) + flux_r - north(flux_r, self.fr_last[n])
        )
        self.fr_last[n] = flux_r
        return out, u, v

    def step_one(self, i):
        at = tile_at(i)
        s = self.get(0, i)
        level = 0.3 * self.get(5, i)
        inside = i + 1 < self.count
        face_c = s * east(s)
        face_r = s * south(s, self.get(0, i + 1) if inside else s)
        ratios = []
        for face in (face_c, face_r):
            base = face + 0.1
            inverse = pl.reciprocal(base, approx=True)
            ratios.append(face * (inverse * (2.0 - base * inverse)))
        wc, wr = ratios
        fc = 0.3 * face_c
        fr = 0.3 * face_r
        self.fc[at, :] = fc
        self.fr[at, :] = fr
        self.wc[at, :] = wc
        self.wr[at, :] = wr
        lower = 0.3 * self.get(5, i + 1) if inside else level
        e, u, v = self.move(0, i, level, lower, self.get(6, i), self.get(7, i), fc, fr, wc, wr)
        self.e1[at, :] = e
        self.u1[at, :] = u
        self.v1[at, :] = v
        self.qc1[at, :] = u * jnp.abs(u)
        self.qr1[at, :] = v * jnp.abs(v)

    def step_two(self, i):
        at, after = tile_at(i), tile_at(i + 1)
        e, u, v = self.move(
            1, i, self.e1[at, :], self.e1[after, :], self.u1[at, :], self.v1[at, :],
            self.fc[at, :], self.fr[at, :], self.wc[at, :], self.wr[at, :],
        )
        self.e2[at, :] = e
        if self.trim and i == self.count - 1:
            return
        self.u2[at, :] = u
        self.v2[at, :] = v
        self.qc2[at, :] = self.qc1[at, :] + u * jnp.abs(u)
        self.qr2[at, :] = self.qr1[at, :] + v * jnp.abs(v)

    def step_three(self, i):
        at, after = tile_at(i), tile_at(i + 1)
        if self.trim and i == self.count - 1:
            return
        if self.trim and i == 0:
            wr = self.wr[at, :]
            v = self.speed_r(i, self.e2[at, :], self.e2[after, :], self.v2[at, :], wr)
            self.fr_last[2] = self.fr[at, :] * v
            self.qr_last[...] = wr * (self.qr2[at, :] + v * jnp.abs(v))
            return
        wc, wr = self.wc[at, :], self.wr[at, :]
        e, u, v = self.move(
            2, i, self.e2[at, :], self.e2[after, :], self.u2[at, :], self.v2[at, :],
            self.fc[at, :], self.fr[at, :], wc, wr,
        )
        qc = wc * (self.qc2[at, :] + u * jnp.abs(u))
        qr = wr * (self.qr2[at, :] + v * jnp.abs(v))
        change = (qc - west(qc) + qr - north(qr, self.qr_last[...])) * self.scale
        self.qr_last[...] = qr
        self.emit(i, e * (1.0 / 0.3), u, v, change)

    def run(self):
        self.fr_last[...] = jnp.zeros_like(self.fr_last)
        self.qr_last[...] = jnp.zeros_like(self.qr_last)
        for ref in (self.e1, self.e2):
            ref[tile_at(self.count), :] = jnp.zeros((SUB, self.wide), jnp.float32)
        stages = (self.step_three, self.step_two, self.step_one)
        for t in range(self.count + LAG * (STEPS - 1)):
            for k, stage in enumerate(stages):
                i = t - LAG * (STEPS - 1 - k)
                if 0 <= i < self.count:
                    stage(i)


def reader(root, a, b, stress, hydro, side, unfold, valid):
    rows = root.shape[0]
    span = rows // FOLD // SUB
    fields = [root, a, b] + moving(stress, hydro)

    def read(f, block):
        part = unfold(side[tile_at(block % span), :], (block // span) * FIELDS + f)
        if f == 0:
            part = jnp.where(valid, part, 0.0)
        return jnp.concatenate([fields[f][tile_at(block), :], part], axis=1)

    return read


def quarter_writer(first, quarter, cols, hydro_out, pay):
    lane = lanes_of((SUB, LANE))
    lanes = cols // LANE
    rims = [jnp.zeros((SUB, LANE), jnp.float32)]

    def emit(i, e, u, v, change):
        at = tile_at(first + i)
        for k, value in enumerate((e, u, v)):
            hydro_out[0, k, at, :] = value[:, :cols]
        g = i - 1
        for k in range(lanes):
            pay[tile_at(k * quarter + g), :] = change[:, k * LANE : (k + 1) * LANE]
        rims[0] = jnp.where(lane // 2 == g, pltpu.roll(change[:, cols:], 1 + 2 * g, 1), rims[0])
        if g == quarter - 1:
            pay[tile_at(lanes * quarter), :] = rims[0]

    return emit


def middle_kernel(own, weights, params, root, a, b, stress, hydro, side, *refs):
    hydro_out, pay, *refs = refs[1:] if own else refs
    rows, cols = root.shape
    quarter = rows // SUB // 4
    read = reader(root, a, b, stress, hydro, side, *side_lanes(lax.axis_index("tx") == 0))
    mine = lax.axis_index("cond") % 2
    lower_half = mine == (1 if own else 0)
    first = jnp.where(lower_half, 2 * quarter, quarter) - 1
    emit = quarter_writer(first, quarter, cols, hydro_out, pay)
    Sweep(
        quarter + 2, cols + LANE, lambda f, i: read(f, first + i), emit, weights, params, refs, True
    ).run()


def middle(own, weights, params, fields, side, hydro=None):
    rows, cols = fields[0].shape
    given = (hydro,) if own else ()
    return pl.pallas_call(
        functools.partial(middle_kernel, own),
        name="middle_own" if own else "middle_other",
        out_shape=[
            pltpu.VMEM(fields[4].shape, jnp.float32),
            pltpu.VMEM((cols // LANE * rows // 4 + SUB, LANE), jnp.float32),
        ],
        in_specs=[SMEM, SMEM] + [VMEM] * (6 + own),
        out_specs=[VMEM, VMEM],
        scratch_shapes=Sweep.scratch(rows // SUB // 4 + 2, cols + LANE),
        input_output_aliases={8: 0} if own else {},
        compiler_params=pltpu.CompilerParams(vmem_limit_bytes=10 * MIB),
        cost_estimate=cost(4),
    )(weights, params, *held(*fields, side, *given))


def edge_kernel(
    own, weights, params, root, a, b, stress, hydro, side, far_a, far_b, hydro_in,
    hydro_out, pay, ends, *refs,
):
    rows, cols = root.shape
    blocks = rows // SUB
    quarter = blocks // 4
    lanes = cols // LANE
    unfold, valid = side_lanes(lax.axis_index("tx") == 0)
    read = reader(root, a, b, stress, hydro, side, unfold, valid)
    mine = lax.axis_index("cond") % 2
    top = mine == (0 if own else 1)
    from_a = top == (lax.axis_index("ty") % 2 == 1)
    first = jnp.where(top, -1, blocks - quarter - 1)

    ty = lax.axis_index("ty")
    outside_map = ty == jnp.where(top, 0, lax.axis_size("ty") - 1)
    inner = jnp.where(top, quarter, blocks - quarter - 1)
    corners = pl.ds(lanes * GROUP, SUB)
    for f in range(FIELDS):
        body = read(f, inner)
        parts = []
        for k in range(lanes):
            at = pl.ds(k * GROUP + f // 2 * SUB, SUB)
            part = jnp.where(from_a, far_a[at, :], far_b[at, :])
            moved = pltpu.roll(part, HALO, 0)
            parts.append(jnp.where(top, moved, part) if f % 2 == 0 else jnp.where(top, part, moved))
        corner = jnp.where(from_a, far_a[corners, :], far_b[corners, :])
        corner = jnp.where(top, unfold(corner, (FOLD - 1) * FIELDS + f), unfold(corner, f))
        if f == 0:
            corner = jnp.where(valid, corner, 0.0)
        outer = jnp.concatenate(parts + [corner], axis=1)
        if f == 0:
            outer = jnp.where(outside_map, 0.0, outer)
        ends[0, f] = jnp.where(top, outer, body)
        ends[1, f] = jnp.where(top, body, outer)

    def get(f, i):
        if i == 0 or i == quarter + 1:
            return ends[0 if i == 0 else 1, f]
        return read(f, first + i)

    emit = quarter_writer(first, quarter, cols, hydro_out, pay)
    outside = []

    def finish(i, e, u, v, change):
        if i == 0:
            outside.append(pltpu.roll(change[:, :cols], 1, 0))
        elif i == quarter + 1:
            pay[tile_at(lanes * quarter + 1), :] = fold_row(jnp.where(top, outside[0], change[:, :cols]))
        else:
            emit(i, e, u, v, change)

    Sweep(quarter + 2, cols + LANE, get, finish, weights, params, refs, False).run()


def edge(own, weights, params, fields, side, far_a, far_b, hydro):
    rows, cols = fields[0].shape
    wide = cols + LANE
    return pl.pallas_call(
        functools.partial(edge_kernel, own),
        name="edge_own" if own else "edge_other",
        out_shape=[
            pltpu.VMEM(hydro.shape, jnp.float32),
            pltpu.VMEM((cols // LANE * rows // 4 + 2 * SUB, LANE), jnp.float32),
        ],
        in_specs=[SMEM, SMEM] + [VMEM] * 9,
        out_specs=[VMEM, VMEM],
        scratch_shapes=[pltpu.VMEM((2, FIELDS, SUB, wide), jnp.float32)]
        + Sweep.scratch(rows // SUB // 4 + 2, wide),
        input_output_aliases={10: 0},
        compiler_params=pltpu.CompilerParams(vmem_limit_bytes=12 * MIB),
        cost_estimate=cost(3),
    )(weights, params, *held(*fields, side, far_a, far_b, hydro))


class Update:
    def __init__(self, bed, side, far_a, far_b, own_m, got_m, own_e, got_e, change_v, next_v):
        self.bed, self.side, self.far_a, self.far_b = bed, side, far_a, far_b
        self.parts = {"m": (own_m, got_m), "e": (own_e, got_e)}
        self.change_v, self.next_v = change_v, next_v
        rows, self.cols = bed.shape
        self.blocks = rows // SUB
        self.quarter = self.blocks // 4
        self.lanes = self.cols // LANE
        self.wide = self.cols + LANE
        self.side_bed = side[pl.ds(side.shape[0] - SUB, SUB), :]
        self.drop_bed = jnp.where(lax.axis_index("tx") == 0, 0, 1)
        self.mine = lax.axis_index("cond") % 2
        self.odd = lax.axis_index("ty") % 2 == 1
        col = lanes_of((SUB, self.wide))
        last_c = lax.axis_index("tx") == lax.axis_size("tx") - 1
        first_c = lax.axis_index("tx") == 0
        self.shut_c = (last_c & (col == self.cols - 1)) | (first_c & (col == self.wide - 1))
        self.last_row = rows_of((SUB, self.wide)) == SUB - 1
        self.rims = {}

    def merged(self, q, block):
        own, got = self.parts["e" if q in (0, 3) else "m"]
        at = tile_at(block)
        return jnp.where(self.mine == q // 2, own[at, :], got[at, :])

    def outside(self, q):
        at = pl.ds(self.lanes * GROUP + SUB, SUB)
        a, b = self.far_a[at, :], self.far_b[at, :]
        bed = jnp.where(self.odd, a, b) if q == 0 else jnp.where(self.odd, b, a)
        z = bed + self.merged(q, self.lanes * self.quarter + 1)
        target = SUB - 1 if q == 0 else 0
        parts = [pltpu.roll(z, (SUB + target - k) % SUB, 0) if (target - k) % SUB else z for k in range(self.lanes)]
        return jnp.concatenate(parts + [jnp.zeros((SUB, LANE), jnp.float32)], axis=1)

    def level(self, b, keep):
        if b == -1:
            return self.outside(0)
        if b == self.blocks:
            return self.outside(3)
        q, g = divmod(b, self.quarter)
        change = jnp.concatenate([self.merged(q, k * self.quarter + g) for k in range(self.lanes)], axis=1)
        if keep:
            self.change_v[tile_at(b), :] = change
        if q not in self.rims:
            self.rims[q] = self.merged(q, self.lanes * self.quarter)
        cols_bed = pltpu.roll(self.side_bed, 2 * LANE - self.drop_bed - b, 1)
        cols_change = pltpu.roll(self.rims[q], LANE - 1 - 2 * g, 1)
        return jnp.concatenate([self.bed[tile_at(b), :] + change, cols_bed + cols_change], axis=1)

    def spill(self, slope):
        return 0.25 * (slope - jnp.clip(slope, -1.0, 1.0))

    def south_face(self, z, lower, b):
        out = self.spill(south(z, lower) - z)
        if b == -1:
            return jnp.where((lax.axis_index("ty") == 0) & self.last_row, 0.0, out)
        if b == self.blocks - 1:
            return jnp.where((lax.axis_index("ty") == lax.axis_size("ty") - 1) & self.last_row, 0.0, out)
        return out

    def run(self, first, stop, keep, after=lambda b: None):
        z = self.level(first - 1, keep)
        lower = self.level(first, keep)
        gr = self.south_face(z, lower, first - 1)
        for b in range(first, stop):
            z, lower = lower, self.level(b + 1, keep)
            gr_above, gr = gr, self.south_face(z, lower, b)
            gc = jnp.where(self.shut_c, 0.0, self.spill(east(z) - z))
            out = z + gc - west(gc) + gr - north(gr, gr_above)
            self.next_v[tile_at(b), :] = out[:, : self.cols]
            after(b)


def bed_middle_kernel(
    bed, side, far_a, far_b, own_m, got_m, hydro, bed_next, bed_change, hydro_out, change_v, next_v, sems
):
    rows = bed.shape[0]
    quarter = rows // SUB // 4
    copies = [pltpu.make_async_copy(hydro, hydro_out, sems.at[0])]
    copies[0].start()
    update = Update(bed, side, far_a, far_b, own_m, got_m, None, None, change_v, next_v)
    update.run(quarter + 1, 3 * quarter - 1, True)
    for src, dst, low, high in (
        (change_v, bed_change, quarter, 3 * quarter),
        (next_v, bed_next, quarter + 1, 3 * quarter - 1),
    ):
        at = pl.ds(low * SUB, (high - low) * SUB)
        copies.append(pltpu.make_async_copy(src.at[at], dst.at[at], sems.at[len(copies)]))
        copies[-1].start()
    for copy in copies:
        copy.wait()


def bed_edge_kernel(
    bed, side, far_a, far_b, own_m, got_m, own_e, got_e, next_in, change_in, bed_next, bed_change,
    change_v, next_v, sems,
):
    rows = bed.shape[0]
    blocks = rows // SUB
    quarter = blocks // 4
    update = Update(bed, side, far_a, far_b, own_m, got_m, own_e, got_e, change_v, next_v)
    copies = []

    def send(src, dst, low, high):
        at = pl.ds(low * SUB, (high - low) * SUB)
        copies.append(pltpu.make_async_copy(src.at[at], dst.at[at], sems.at[len(copies)]))
        copies[-1].start()

    update.run(0, quarter + 1, True)
    send(change_v, bed_change, 0, quarter)
    send(next_v, bed_next, 0, quarter + 1)
    update.run(blocks - quarter - 1, blocks, True)
    send(change_v, bed_change, blocks - quarter, blocks)
    send(next_v, bed_next, blocks - quarter - 1, blocks)
    for copy in copies:
        copy.wait()


def bed_scratch(rows, cols):
    return [
        pltpu.VMEM((rows, cols), jnp.float32),
        pltpu.VMEM((rows, cols), jnp.float32),
        pltpu.SemaphoreType.DMA((4,)),
    ]


def bed_middle(bed, side, far_a, far_b, own_m, got_m, hydro):
    return pl.pallas_call(
        bed_middle_kernel,
        name="bed_middle",
        out_shape=[pltpu.HBM(x.shape, jnp.float32) for x in (bed, bed, hydro)],
        in_specs=[VMEM] * 7,
        out_specs=[ANY] * 3,
        scratch_shapes=bed_scratch(*bed.shape),
        compiler_params=pltpu.CompilerParams(vmem_limit_bytes=6 * MIB),
        cost_estimate=cost(4),
    )(*held(bed, side, far_a, far_b, own_m, got_m, hydro))


def bed_edge(bed, side, far_a, far_b, own_m, got_m, own_e, got_e, bed_next, bed_change):
    return pl.pallas_call(
        bed_edge_kernel,
        name="bed_edge",
        out_shape=[pltpu.HBM(bed.shape, jnp.float32)] * 2,
        in_specs=[VMEM] * 8 + [ANY] * 2,
        out_specs=[ANY] * 2,
        scratch_shapes=bed_scratch(*bed.shape),
        input_output_aliases={8: 0, 9: 1},
        compiler_params=pltpu.CompilerParams(vmem_limit_bytes=6 * MIB),
        cost_estimate=cost(2),
    )(
        *held(bed, side, far_a, far_b, own_m, got_m, own_e, got_e),
        *held(bed_next, bed_change, space=pltpu.HBM),
    )


def shards(bed, land_mask, cell_class, weights, cond_params, wave_stress, hydro_state):
    ny = lax.axis_size("ty")
    nc = lax.axis_size("cond")
    raw = (bed, land_mask, cell_class, wave_stress, hydro_state)
    swap = [(i, i ^ 1) for i in range(nc)]

    def pairs(first):
        partner = list(range(ny))
        for i in range(first, ny - 1, 2):
            partner[i], partner[i + 1] = i + 1, i
        return list(enumerate(partner))

    def over_chips(part, beside=()):
        reach = 2
        while reach < nc:
            got = lax.ppermute(part, "cond", [(i, i ^ reach) for i in range(nc)])
            got, beside = lax.optimization_barrier((got, beside))
            part = part + got
            reach = 2 * reach
        return part, beside

    side = lax.ppermute(pack_side(cond_params, *raw), "tx", [(0, 1), (1, 0)])
    bed, *terms, far_a, far_b = prepare(cond_params, *raw)
    fields = (*terms, wave_stress, hydro_state)
    far_a, far_b = add_corners(side, far_a, far_b)
    far_a = lax.ppermute(far_a, "ty", pairs(0))
    hydro, pay = middle(False, weights, cond_params, fields, side)
    hydro, far_a, far_b = lax.optimization_barrier((hydro, far_a, far_b))
    far_b = lax.ppermute(far_b, "ty", pairs(1))
    got = lax.ppermute(pay, "cond", swap)
    hydro, pay = middle(True, weights, cond_params, fields, side, hydro)
    part_m = pay + got
    hydro, part_m = lax.optimization_barrier((hydro, part_m))
    hydro, pay = edge(False, weights, cond_params, fields, side, far_a, far_b, hydro)
    got = lax.ppermute(pay, "cond", swap)
    hydro, pay = edge(True, weights, cond_params, fields, side, far_a, far_b, hydro)
    own_m, hydro = over_chips(part_m, hydro)
    part_e = pay + got
    own_m, _ = lax.optimization_barrier((own_m, part_e))
    got_m = lax.ppermute(own_m, "cond", swap)
    bed_next, bed_change, hydro = bed_middle(bed, side, far_a, far_b, own_m, got_m, hydro)
    own_e, (bed_next, bed_change) = over_chips(part_e, (bed_next, bed_change))
    got_e = lax.ppermute(own_e, "cond", swap)
    bed_next, bed_change = bed_edge(
        bed, side, far_a, far_b, own_m, got_m, own_e, got_e, bed_next, bed_change
    )
    return bed_next, bed_change, hydro


def solution(mesh):
    in_specs = (
        P("ty", "tx"),
        P("ty", "tx"),
        P("ty", "tx"),
        P(),
        P("cond", None),
        P("cond", None, "ty", "tx"),
        P("cond", None, "ty", "tx"),
    )
    out_specs = (P("ty", "tx"), P("ty", "tx"), P("cond", None, "ty", "tx"))
    return jax.shard_map(shards, mesh=mesh, in_specs=in_specs, out_specs=out_specs, check_vma=False)
```

```python
import functools

import jax
import jax.numpy as jnp
from jax import lax
from jax.experimental import pallas as pl
from jax.experimental.pallas import tpu as pltpu
from jax.sharding import PartitionSpec as P

STEPS = 3
HALO = STEPS + 1
SUB = 8
LANE = 128
FIELDS = 8
GROUP = HALO * FIELDS
FOLD = LANE // GROUP
LAG = 2
MIB = 2**20
ANY = pl.BlockSpec(memory_space=pl.ANY)
VMEM = pl.BlockSpec(memory_space=pltpu.VMEM)
SMEM = pl.BlockSpec(memory_space=pltpu.SMEM)


def rows_of(shape):
    return lax.broadcasted_iota(jnp.int32, shape, 0)


def lanes_of(shape):
    return lax.broadcasted_iota(jnp.int32, shape, 1)


def east(x):
    return pltpu.roll(x, x.shape[1] - 1, 1)


def west(x):
    return pltpu.roll(x, 1, 1)


def south(x, below):
    return pltpu.roll(jnp.where(rows_of(x.shape) == 0, below, x), SUB - 1, 0)


def north(x, above):
    return pltpu.roll(jnp.where(rows_of(x.shape) == SUB - 1, above, x), 1, 0)


def tile_at(index):
    if isinstance(index, int):
        return pl.ds(index * SUB, SUB)
    return pl.ds(pl.multiple_of(index * SUB, SUB), SUB)


def held(*arrays, space=pltpu.VMEM):
    return [pltpu.with_memory_space_constraint(x, space) for x in arrays]


def cost(micros):
    return pl.CostEstimate(flops=int(micros * 10**9), bytes_accessed=0, transcendentals=0)


def level_terms(params):
    return params[0, 0] - 1.0, 0.3 * params[0, 3]


def coefficients(bed, mask, kind, tide, flow_in):
    depth = mask.astype(jnp.float32) * (1.0 - 0.5 * jnp.tanh(bed))
    root = depth * lax.rsqrt(jnp.maximum(depth, 1e-12))
    relax = jnp.where(kind == 1, 0.5 * depth, 0.0)
    return root, 1.0 - relax, 0.3 * (relax * tide + jnp.where(kind == 2, flow_in * depth, 0.0))


def moving(stress, hydro):
    return [stress.at[0, k] for k in range(2)] + [hydro.at[0, k] for k in range(3)]


def pack_side_kernel(params_in, bed, mask, kind, stress, hydro, side, reals, ints, params, sems):
    rows, cols = bed.shape
    at_left = lax.axis_index("tx") == 0
    off = pl.multiple_of(jnp.where(at_left, cols - LANE, 0), LANE)
    strips = [reals.at[0], ints.at[0], ints.at[1]] + [reals.at[k] for k in range(1, 6)]
    copies = [
        pltpu.make_async_copy(src.at[:, pl.ds(off, LANE)], strip, sems.at[f])
        for f, (src, strip) in enumerate(zip([bed, mask, kind] + moving(stress, hydro), strips))
    ] + [pltpu.make_async_copy(params_in, params, sems.at[FIELDS])]
    for copy in copies:
        copy.start()
    for copy in copies:
        copy.wait()
    tide, flow_in = level_terms(params)
    lift = jnp.where(at_left, HALO, 0)
    lift_bed = jnp.where(at_left, 1, 0)
    lane = lanes_of((SUB, LANE))
    span = rows // FOLD // SUB
    beds = jnp.zeros((SUB, LANE), jnp.float32)
    for i in range(span):
        total = jnp.zeros((SUB, LANE), jnp.float32)
        for g in range(FOLD):
            at = tile_at(g * span + i)
            first = strips[0][at, :]
            fields = list(coefficients(first, strips[1][at, :], strips[2][at, :], tide, flow_in))
            fields += [strip[at, :] for strip in strips[3:]]
            for f, part in enumerate(fields):
                place = g * FIELDS + f
                total = jnp.where(lane // HALO == place, pltpu.roll(part, lift + place * HALO, 1), total)
            block = g * span + i
            beds = jnp.where(lane == block, pltpu.roll(first, lift_bed + block, 1), beds)
        side[tile_at(i), :] = total
    side[tile_at(span), :] = beds


def pack_side(params, *raw):
    rows, cols = raw[0].shape
    return pl.pallas_call(
        pack_side_kernel,
        name="pack_side",
        out_shape=pltpu.VMEM((rows // FOLD + SUB, LANE), jnp.float32),
        in_specs=[ANY] * 6,
        out_specs=VMEM,
        scratch_shapes=[
            pltpu.VMEM((6, rows, LANE), jnp.float32),
            pltpu.VMEM((2, rows, LANE), jnp.int32),
            pltpu.SMEM(params.shape, jnp.float32),
            pltpu.SemaphoreType.DMA((FIELDS + 1,)),
        ],
        compiler_params=pltpu.CompilerParams(vmem_limit_bytes=4 * MIB),
        cost_estimate=cost(2),
    )(*held(params, *raw, space=pltpu.HBM))


PARTS = 4


def prepare_kernel(
    params_in, bed, mask, kind, stress, hydro, bed_v, root, a, b, pay_a, pay_b,
    mask_v, kind_v, ends, params, load_sems, end_sems, params_sem,
):
    rows, cols = bed.shape
    lanes = cols // LANE
    chunk = rows // PARTS
    loads, copies = [], []
    for c in range(PARTS):
        at = pl.ds(c * chunk, chunk)
        loads.append([
            pltpu.make_async_copy(src.at[at], dst.at[at], load_sems.at[f, c])
            for f, (src, dst) in enumerate(((bed, bed_v), (mask, mask_v), (kind, kind_v)))
        ])
    for f, src in enumerate(moving(stress, hydro)):
        for end, start in enumerate((0, rows - SUB)):
            copies.append(pltpu.make_async_copy(src.at[pl.ds(start, SUB)], ends.at[end, f], end_sems.at[f, end]))
    loads[0].append(pltpu.make_async_copy(params_in, params, params_sem))
    for group in loads + [copies]:
        for copy in group:
            copy.start()
    for copy in loads[0]:
        copy.wait()
    tide, flow_in = level_terms(params)
    for c in range(PARTS):
        for copy in loads[c] if c else ():
            copy.wait()
        for i in range(c * chunk // SUB, (c + 1) * chunk // SUB):
            at = tile_at(i)
            root[at, :], a[at, :], b[at, :] = coefficients(bed_v[at, :], mask_v[at, :], kind_v[at, :], tide, flow_in)
    for copy in copies:
        copy.wait()
    low = rows_of((SUB, cols)) < HALO
    odd = lax.axis_index("ty") % 2 == 1

    def edge_rows(f, end):
        if f < 3:
            return (root, a, b)[f][tile_at(0 if end == 0 else rows // SUB - 1), :]
        return ends[end, f - 3]

    for p in range(FIELDS // 2):
        pairs = []
        for end in range(2):
            both = [edge_rows(f, end) for f in (2 * p, 2 * p + 1)]
            both[1 - end] = pltpu.roll(both[1 - end], HALO, 0)
            pairs.append(jnp.where(low, *both))
        for k in range(lanes):
            at, part = pl.ds(k * GROUP + p * SUB, SUB), slice(k * LANE, (k + 1) * LANE)
            top, bottom = pairs[0][:, part], pairs[1][:, part]
            pay_a[at, :] = jnp.where(odd, top, bottom)
            pay_b[at, :] = jnp.where(odd, bottom, top)
    top = fold_row(bed_v[tile_at(0), :])
    bottom = fold_row(pltpu.roll(bed_v[tile_at(rows // SUB - 1), :], 1, 0))
    at = pl.ds(lanes * GROUP + SUB, SUB)
    pay_a[at, :] = jnp.where(odd, top, bottom)
    pay_b[at, :] = jnp.where(odd, bottom, top)


def fold_row(x):
    row = rows_of((SUB, LANE))
    total = x[:, :LANE]
    for k in range(1, x.shape[1] // LANE):
        total = jnp.where(row == k, pltpu.roll(x[:, k * LANE : (k + 1) * LANE], k, 0), total)
    return total


def prepare(params, *raw):
    rows, cols = raw[0].shape
    tile = pltpu.VMEM((rows, cols), jnp.float32)
    return pl.pallas_call(
        prepare_kernel,
        name="prepare",
        out_shape=[tile] * 4 + [pltpu.VMEM((cols // LANE * GROUP + 2 * SUB, LANE), jnp.float32)] * 2,
        in_specs=[ANY] * 6,
        out_specs=[VMEM] * 6,
        scratch_shapes=[
            pltpu.VMEM((rows, cols), jnp.int32),
            pltpu.VMEM((rows, cols), jnp.int32),
            pltpu.VMEM((2, 5, SUB, cols), jnp.float32),
            pltpu.SMEM(params.shape, jnp.float32),
            pltpu.SemaphoreType.DMA((3, PARTS)),
            pltpu.SemaphoreType.DMA((5, 2)),
            pltpu.SemaphoreType.DMA,
        ],
        compiler_params=pltpu.CompilerParams(vmem_limit_bytes=5 * MIB),
        cost_estimate=cost(2),
    )(*held(params, *raw, space=pltpu.HBM))


def corner_kernel(side, in_a, in_b, pay_a, pay_b):
    at = pl.ds(pay_a.shape[0] - 2 * SUB, SUB)
    odd = lax.axis_index("ty") % 2 == 1
    top = side[pl.ds(0, SUB), :]
    bottom = side[pl.ds(side.shape[0] - 2 * SUB, SUB), :]
    pay_a[at, :] = jnp.where(odd, top, bottom)
    pay_b[at, :] = jnp.where(odd, bottom, top)


def add_corners(side, pay_a, pay_b):
    return pl.pallas_call(
        corner_kernel,
        name="add_corners",
        out_shape=[pltpu.VMEM(pay_a.shape, jnp.float32)] * 2,
        in_specs=[VMEM] * 3,
        out_specs=[VMEM] * 2,
        input_output_aliases={1: 0, 2: 1},
        compiler_params=pltpu.CompilerParams(vmem_limit_bytes=MIB),
        cost_estimate=cost(0.1),
    )(*held(side, pay_a, pay_b))


def side_lanes(at_left):
    drop = jnp.where(at_left, 0, HALO)
    lane = lanes_of((SUB, LANE))
    valid = jnp.where(at_left, lane, LANE - 1 - lane) < HALO

    def unfold(strip, place):
        return pltpu.roll(strip, 2 * LANE - drop - place * HALO, 1)

    return unfold, valid


class Sweep:
    NAMES = (
        ["fc", "fr", "wc", "wr", "e1", "u1"]
        + ["v1", "e2", "u2", "v2", "qc1", "qr1", "qc2", "qr2"]
    )

    def __init__(self, count, wide, get, emit, weights, params, refs, trim):
        self.count, self.wide, self.get, self.emit, self.trim = count, wide, get, emit, trim
        self.__dict__.update(zip(self.NAMES + ["fr_last", "qr_last"], refs))
        cond = lax.axis_index("cond")
        self.slow = 1.0 - 0.2 * params[0, 1]
        total = weights[0]
        for k in range(1, weights.shape[0]):
            total = total + weights[k]
        ones = jnp.ones((SUB, LANE), jnp.float32)
        share = weights[cond].astype(jnp.float32) * ones / (total.astype(jnp.float32) * ones)
        self.scale = jnp.concatenate([-4.0 * params[0, 2] * share] * (wide // LANE), axis=1)

    @classmethod
    def scratch(cls, count, wide):
        block = pltpu.VMEM(((count + 1) * SUB, wide), jnp.float32)
        return [block] * len(cls.NAMES) + [
            pltpu.VMEM((STEPS, SUB, wide), jnp.float32),
            pltpu.VMEM((SUB, wide), jnp.float32),
        ]

    def speed_r(self, i, level, lower, v, wr):
        return (self.slow * v - (south(level, lower) - level) + self.get(4, i)) * wr

    def move(self, n, i, level, lower, u, v, faces, rest):
        right, down = east(level), south(level, lower)
        yield
        fc, fr, wc, wr = faces()
        u = (self.slow * u() - (right - level) + self.get(3, i)) * wc
        v = (self.slow * v() - (down - level) + self.get(4, i)) * wr
        flux_c = fc * u
        flux_r = fr * v
        left, up = west(flux_c), north(flux_r, self.fr_last[n])
        self.fr_last[n] = flux_r
        more = rest(u, v)
        yield
        out = self.get(1, i) * level + self.get(2, i) - (flux_c - left + flux_r - up)
        return out, more

    def step_one(self, i):
        at = tile_at(i)
        s = self.get(0, i)
        inside = i + 1 < self.count
        level = 0.3 * self.get(5, i)
        lower = 0.3 * self.get(5, i + 1) if inside else level
        right, down = east(s), south(s, self.get(0, i + 1) if inside else s)

        def faces():
            ratios = []
            for face in (s * right, s * down):
                base = face + 0.1
                inverse = pl.reciprocal(base, approx=True)
                ratios.append((0.3 * face, face * (inverse * (2.0 - base * inverse))))
            (fc, wc), (fr, wr) = ratios
            for ref, value in ((self.fc, fc), (self.fr, fr), (self.wc, wc), (self.wr, wr)):
                ref[at, :] = value
            return fc, fr, wc, wr

        def rest(u, v):
            self.u1[at, :] = u
            self.v1[at, :] = v
            self.qc1[at, :] = u * jnp.abs(u)
            self.qr1[at, :] = v * jnp.abs(v)

        out, _ = yield from self.move(
            0, i, level, lower, lambda: self.get(6, i), lambda: self.get(7, i), faces, rest
        )
        self.e1[at, :] = out

    def faces_at(self, at):
        return lambda: [ref[at, :] for ref in (self.fc, self.fr, self.wc, self.wr)]

    def step_two(self, i):
        at, after = tile_at(i), tile_at(i + 1)

        def rest(u, v):
            if not (self.trim and i == self.count - 1):
                self.u2[at, :] = u
                self.v2[at, :] = v
                self.qc2[at, :] = self.qc1[at, :] + u * jnp.abs(u)
                self.qr2[at, :] = self.qr1[at, :] + v * jnp.abs(v)

        out, _ = yield from self.move(
            1, i, self.e1[at, :], self.e1[after, :], lambda: self.u1[at, :], lambda: self.v1[at, :],
            self.faces_at(at), rest,
        )
        self.e2[at, :] = out

    def step_three(self, i):
        at, after = tile_at(i), tile_at(i + 1)
        if self.trim and i == self.count - 1:
            return
        if self.trim and i == 0:
            wr = self.wr[at, :]
            v = self.speed_r(i, self.e2[at, :], self.e2[after, :], self.v2[at, :], wr)
            self.fr_last[2] = self.fr[at, :] * v
            self.qr_last[...] = wr * (self.qr2[at, :] + v * jnp.abs(v))
            return

        def rest(u, v):
            qc = self.wc[at, :] * (self.qc2[at, :] + u * jnp.abs(u))
            qr = self.wr[at, :] * (self.qr2[at, :] + v * jnp.abs(v))
            left, up = west(qc), north(qr, self.qr_last[...])
            self.qr_last[...] = qr
            return u, v, qc, qr, left, up

        out, (u, v, qc, qr, left, up) = yield from self.move(
            2, i, self.e2[at, :], self.e2[after, :], lambda: self.u2[at, :], lambda: self.v2[at, :],
            self.faces_at(at), rest,
        )
        self.emit(i, out * (1.0 / 0.3), u, v, (qc - left + qr - up) * self.scale)

    def run(self):
        self.fr_last[...] = jnp.zeros_like(self.fr_last)
        self.qr_last[...] = jnp.zeros_like(self.qr_last)
        for ref in (self.e1, self.e2):
            ref[tile_at(self.count), :] = jnp.zeros((SUB, self.wide), jnp.float32)
        stages = (self.step_three, self.step_two, self.step_one)
        for t in range(self.count + LAG * (STEPS - 1)):
            turns = []
            for k, stage in enumerate(stages):
                i = t - LAG * (STEPS - 1 - k)
                if 0 <= i < self.count:
                    turns.append(stage(i))
            while turns:
                turns = [turn for turn in turns if next(turn, True) is None]


def reader(root, a, b, stress, hydro, side, unfold, valid):
    rows = root.shape[0]
    span = rows // FOLD // SUB
    fields = [root, a, b] + moving(stress, hydro)

    def read(f, block):
        part = unfold(side[tile_at(block % span), :], (block // span) * FIELDS + f)
        if f == 0:
            part = jnp.where(valid, part, 0.0)
        return jnp.concatenate([fields[f][tile_at(block), :], part], axis=1)

    return read


def quarter_writer(first, quarter, cols, hydro_out, pay):
    lane = lanes_of((SUB, LANE))
    lanes = cols // LANE
    rims = [jnp.zeros((SUB, LANE), jnp.float32)]

    def emit(i, e, u, v, change):
        at = tile_at(first + i)
        for k, value in enumerate((e, u, v)):
            hydro_out[0, k, at, :] = value[:, :cols]
        g = i - 1
        for k in range(lanes):
            pay[tile_at(k * quarter + g), :] = change[:, k * LANE : (k + 1) * LANE]
        rims[0] = jnp.where(lane // 2 == g, pltpu.roll(change[:, cols:], 1 + 2 * g, 1), rims[0])
        if g == quarter - 1:
            pay[tile_at(lanes * quarter), :] = rims[0]

    return emit


def middle_kernel(own, weights, params, root, a, b, stress, hydro, side, *refs):
    hydro_out, pay, *refs = refs[1:] if own else refs
    rows, cols = root.shape
    quarter = rows // SUB // 4
    read = reader(root, a, b, stress, hydro, side, *side_lanes(lax.axis_index("tx") == 0))
    mine = lax.axis_index("cond") % 2
    lower_half = mine == (1 if own else 0)
    first = jnp.where(lower_half, 2 * quarter, quarter) - 1
    emit = quarter_writer(first, quarter, cols, hydro_out, pay)
    Sweep(
        quarter + 2, cols + LANE, lambda f, i: read(f, first + i), emit, weights, params, refs, True
    ).run()


def middle(own, weights, params, fields, side, hydro=None):
    rows, cols = fields[0].shape
    given = (hydro,) if own else ()
    return pl.pallas_call(
        functools.partial(middle_kernel, own),
        name="middle_own" if own else "middle_other",
        out_shape=[
            pltpu.VMEM(fields[4].shape, jnp.float32),
            pltpu.VMEM((cols // LANE * rows // 4 + SUB, LANE), jnp.float32),
        ],
        in_specs=[SMEM, SMEM] + [VMEM] * (6 + own),
        out_specs=[VMEM, VMEM],
        scratch_shapes=Sweep.scratch(rows // SUB // 4 + 2, cols + LANE),
        input_output_aliases={8: 0} if own else {},
        compiler_params=pltpu.CompilerParams(vmem_limit_bytes=10 * MIB),
        cost_estimate=cost(4),
    )(weights, params, *held(*fields, side, *given))


def edge_kernel(
    own, weights, params, root, a, b, stress, hydro, side, far_a, far_b, hydro_in,
    hydro_out, pay, ends, *refs,
):
    rows, cols = root.shape
    blocks = rows // SUB
    quarter = blocks // 4
    lanes = cols // LANE
    unfold, valid = side_lanes(lax.axis_index("tx") == 0)
    read = reader(root, a, b, stress, hydro, side, unfold, valid)
    mine = lax.axis_index("cond") % 2
    top = mine == (0 if own else 1)
    from_a = top == (lax.axis_index("ty") % 2 == 1)
    first = jnp.where(top, -1, blocks - quarter - 1)

    ty = lax.axis_index("ty")
    outside_map = ty == jnp.where(top, 0, lax.axis_size("ty") - 1)
    inner = jnp.where(top, quarter, blocks - quarter - 1)
    corners = pl.ds(lanes * GROUP, SUB)
    for f in range(FIELDS):
        body = read(f, inner)
        parts = []
        for k in range(lanes):
            at = pl.ds(k * GROUP + f // 2 * SUB, SUB)
            part = jnp.where(from_a, far_a[at, :], far_b[at, :])
            moved = pltpu.roll(part, HALO, 0)
            parts.append(jnp.where(top, moved, part) if f % 2 == 0 else jnp.where(top, part, moved))
        corner = jnp.where(from_a, far_a[corners, :], far_b[corners, :])
        corner = jnp.where(top, unfold(corner, (FOLD - 1) * FIELDS + f), unfold(corner, f))
        if f == 0:
            corner = jnp.where(valid, corner, 0.0)
        outer = jnp.concatenate(parts + [corner], axis=1)
        if f == 0:
            outer = jnp.where(outside_map, 0.0, outer)
        ends[0, f] = jnp.where(top, outer, body)
        ends[1, f] = jnp.where(top, body, outer)

    def get(f, i):
        if i == 0 or i == quarter + 1:
            return ends[0 if i == 0 else 1, f]
        return read(f, first + i)

    emit = quarter_writer(first, quarter, cols, hydro_out, pay)
    outside = []

    def finish(i, e, u, v, change):
        if i == 0:
            outside.append(pltpu.roll(change[:, :cols], 1, 0))
        elif i == quarter + 1:
            pay[tile_at(lanes * quarter + 1), :] = fold_row(jnp.where(top, outside[0], change[:, :cols]))
        else:
            emit(i, e, u, v, change)

    Sweep(quarter + 2, cols + LANE, get, finish, weights, params, refs, False).run()


def edge(own, weights, params, fields, side, far_a, far_b, hydro):
    rows, cols = fields[0].shape
    wide = cols + LANE
    return pl.pallas_call(
        functools.partial(edge_kernel, own),
        name="edge_own" if own else "edge_other",
        out_shape=[
            pltpu.VMEM(hydro.shape, jnp.float32),
            pltpu.VMEM((cols // LANE * rows // 4 + 2 * SUB, LANE), jnp.float32),
        ],
        in_specs=[SMEM, SMEM] + [VMEM] * 9,
        out_specs=[VMEM, VMEM],
        scratch_shapes=[pltpu.VMEM((2, FIELDS, SUB, wide), jnp.float32)]
        + Sweep.scratch(rows // SUB // 4 + 2, wide),
        input_output_aliases={10: 0},
        compiler_params=pltpu.CompilerParams(vmem_limit_bytes=12 * MIB),
        cost_estimate=cost(3),
    )(weights, params, *held(*fields, side, far_a, far_b, hydro))


class Update:
    def __init__(self, bed, side, far_a, far_b, own_m, got_m, own_e, got_e, change_v, next_v):
        self.bed, self.side, self.far_a, self.far_b = bed, side, far_a, far_b
        self.parts = {"m": (own_m, got_m), "e": (own_e, got_e)}
        self.change_v, self.next_v = change_v, next_v
        rows, self.cols = bed.shape
        self.blocks = rows // SUB
        self.quarter = self.blocks // 4
        self.lanes = self.cols // LANE
        self.wide = self.cols + LANE
        self.side_bed = side[pl.ds(side.shape[0] - SUB, SUB), :]
        self.drop_bed = jnp.where(lax.axis_index("tx") == 0, 0, 1)
        self.mine = lax.axis_index("cond") % 2
        self.odd = lax.axis_index("ty") % 2 == 1
        col = lanes_of((SUB, self.wide))
        last_c = lax.axis_index("tx") == lax.axis_size("tx") - 1
        first_c = lax.axis_index("tx") == 0
        self.shut_c = (last_c & (col == self.cols - 1)) | (first_c & (col == self.wide - 1))
        self.last_row = rows_of((SUB, self.wide)) == SUB - 1
        self.rims = {}

    def merged(self, q, block):
        own, got = self.parts["e" if q in (0, 3) else "m"]
        at = tile_at(block)
        return jnp.where(self.mine == q // 2, own[at, :], got[at, :])

    def outside(self, q):
        at = pl.ds(self.lanes * GROUP + SUB, SUB)
        a, b = self.far_a[at, :], self.far_b[at, :]
        bed = jnp.where(self.odd, a, b) if q == 0 else jnp.where(self.odd, b, a)
        z = bed + self.merged(q, self.lanes * self.quarter + 1)
        target = SUB - 1 if q == 0 else 0
        parts = [pltpu.roll(z, (SUB + target - k) % SUB, 0) if (target - k) % SUB else z for k in range(self.lanes)]
        return jnp.concatenate(parts + [jnp.zeros((SUB, LANE), jnp.float32)], axis=1)

    def level(self, b, keep):
        if b == -1:
            return self.outside(0)
        if b == self.blocks:
            return self.outside(3)
        q, g = divmod(b, self.quarter)
        change = jnp.concatenate([self.merged(q, k * self.quarter + g) for k in range(self.lanes)], axis=1)
        if keep:
            self.change_v[tile_at(b), :] = change
        if q not in self.rims:
            self.rims[q] = self.merged(q, self.lanes * self.quarter)
        cols_bed = pltpu.roll(self.side_bed, 2 * LANE - self.drop_bed - b, 1)
        cols_change = pltpu.roll(self.rims[q], LANE - 1 - 2 * g, 1)
        return jnp.concatenate([self.bed[tile_at(b), :] + change, cols_bed + cols_change], axis=1)

    def spill(self, slope):
        return 0.25 * (slope - jnp.clip(slope, -1.0, 1.0))

    def south_face(self, z, lower, b):
        out = self.spill(south(z, lower) - z)
        if b == -1:
            return jnp.where((lax.axis_index("ty") == 0) & self.last_row, 0.0, out)
        if b == self.blocks - 1:
            return jnp.where((lax.axis_index("ty") == lax.axis_size("ty") - 1) & self.last_row, 0.0, out)
        return out

    def run(self, first, stop, keep, after=lambda b: None):
        z = self.level(first - 1, keep)
        lower = self.level(first, keep)
        gr = self.south_face(z, lower, first - 1)
        for b in range(first, stop):
            z, lower = lower, self.level(b + 1, keep)
            gr_above, gr = gr, self.south_face(z, lower, b)
            gc = jnp.where(self.shut_c, 0.0, self.spill(east(z) - z))
            out = z + gc - west(gc) + gr - north(gr, gr_above)
            self.next_v[tile_at(b), :] = out[:, : self.cols]
            after(b)


def bed_middle_kernel(
    bed, side, far_a, far_b, own_m, got_m, hydro, bed_next, bed_change, hydro_out, change_v, next_v, sems
):
    rows = bed.shape[0]
    quarter = rows // SUB // 4
    copies = [pltpu.make_async_copy(hydro, hydro_out, sems.at[0])]
    copies[0].start()
    update = Update(bed, side, far_a, far_b, own_m, got_m, None, None, change_v, next_v)
    update.run(quarter + 1, 3 * quarter - 1, True)
    for src, dst, low, high in (
        (change_v, bed_change, quarter, 3 * quarter),
        (next_v, bed_next, quarter + 1, 3 * quarter - 1),
    ):
        at = pl.ds(low * SUB, (high - low) * SUB)
        copies.append(pltpu.make_async_copy(src.at[at], dst.at[at], sems.at[len(copies)]))
        copies[-1].start()
    for copy in copies:
        copy.wait()


def bed_edge_kernel(
    bed, side, far_a, far_b, own_m, got_m, own_e, got_e, next_in, change_in, bed_next, bed_change,
    change_v, next_v, sems,
):
    rows = bed.shape[0]
    blocks = rows // SUB
    quarter = blocks // 4
    update = Update(bed, side, far_a, far_b, own_m, got_m, own_e, got_e, change_v, next_v)
    copies = []

    def send(src, dst, low, high):
        at = pl.ds(low * SUB, (high - low) * SUB)
        copies.append(pltpu.make_async_copy(src.at[at], dst.at[at], sems.at[len(copies)]))
        copies[-1].start()

    update.run(0, quarter + 1, True)
    send(change_v, bed_change, 0, quarter)
    send(next_v, bed_next, 0, quarter + 1)
    update.run(blocks - quarter - 1, blocks, True)
    send(change_v, bed_change, blocks - quarter, blocks)
    send(next_v, bed_next, blocks - quarter - 1, blocks)
    for copy in copies:
        copy.wait()


def bed_scratch(rows, cols):
    return [
        pltpu.VMEM((rows, cols), jnp.float32),
        pltpu.VMEM((rows, cols), jnp.float32),
        pltpu.SemaphoreType.DMA((4,)),
    ]


def bed_middle(bed, side, far_a, far_b, own_m, got_m, hydro):
    return pl.pallas_call(
        bed_middle_kernel,
        name="bed_middle",
        out_shape=[pltpu.HBM(x.shape, jnp.float32) for x in (bed, bed, hydro)],
        in_specs=[VMEM] * 7,
        out_specs=[ANY] * 3,
        scratch_shapes=bed_scratch(*bed.shape),
        compiler_params=pltpu.CompilerParams(vmem_limit_bytes=6 * MIB),
        cost_estimate=cost(4),
    )(*held(bed, side, far_a, far_b, own_m, got_m, hydro))


def bed_edge(bed, side, far_a, far_b, own_m, got_m, own_e, got_e, bed_next, bed_change):
    return pl.pallas_call(
        bed_edge_kernel,
        name="bed_edge",
        out_shape=[pltpu.HBM(bed.shape, jnp.float32)] * 2,
        in_specs=[VMEM] * 8 + [ANY] * 2,
        out_specs=[ANY] * 2,
        scratch_shapes=bed_scratch(*bed.shape),
        input_output_aliases={8: 0, 9: 1},
        compiler_params=pltpu.CompilerParams(vmem_limit_bytes=6 * MIB),
        cost_estimate=cost(2),
    )(
        *held(bed, side, far_a, far_b, own_m, got_m, own_e, got_e),
        *held(bed_next, bed_change, space=pltpu.HBM),
    )


def shards(bed, land_mask, cell_class, weights, cond_params, wave_stress, hydro_state):
    ny = lax.axis_size("ty")
    nc = lax.axis_size("cond")
    raw = (bed, land_mask, cell_class, wave_stress, hydro_state)
    swap = [(i, i ^ 1) for i in range(nc)]

    def pairs(first):
        partner = list(range(ny))
        for i in range(first, ny - 1, 2):
            partner[i], partner[i + 1] = i + 1, i
        return list(enumerate(partner))

    def over_chips(part, beside=()):
        reach = 2
        while reach < nc:
            got = lax.ppermute(part, "cond", [(i, i ^ reach) for i in range(nc)])
            got, beside = lax.optimization_barrier((got, beside))
            part = part + got
            reach = 2 * reach
        return part, beside

    side = lax.ppermute(pack_side(cond_params, *raw), "tx", [(0, 1), (1, 0)])
    bed, *terms, far_a, far_b = prepare(cond_params, *raw)
    fields = (*terms, wave_stress, hydro_state)
    far_a, far_b = add_corners(side, far_a, far_b)
    far_a = lax.ppermute(far_a, "ty", pairs(0))
    hydro, pay = middle(False, weights, cond_params, fields, side)
    hydro, far_a, far_b = lax.optimization_barrier((hydro, far_a, far_b))
    far_b = lax.ppermute(far_b, "ty", pairs(1))
    got = lax.ppermute(pay, "cond", swap)
    hydro, pay = middle(True, weights, cond_params, fields, side, hydro)
    part_m = pay + got
    hydro, part_m = lax.optimization_barrier((hydro, part_m))
    hydro, pay = edge(False, weights, cond_params, fields, side, far_a, far_b, hydro)
    got = lax.ppermute(pay, "cond", swap)
    hydro, pay = edge(True, weights, cond_params, fields, side, far_a, far_b, hydro)
    own_m, hydro = over_chips(part_m, hydro)
    part_e = pay + got
    own_m, _ = lax.optimization_barrier((own_m, part_e))
    got_m = lax.ppermute(own_m, "cond", swap)
    bed_next, bed_change, hydro = bed_middle(bed, side, far_a, far_b, own_m, got_m, hydro)
    own_e, (bed_next, bed_change) = over_chips(part_e, (bed_next, bed_change))
    got_e = lax.ppermute(own_e, "cond", swap)
    bed_next, bed_change = bed_edge(
        bed, side, far_a, far_b, own_m, got_m, own_e, got_e, bed_next, bed_change
    )
    return bed_next, bed_change, hydro


def solution(mesh):
    in_specs = (
        P("ty", "tx"),
        P("ty", "tx"),
        P("ty", "tx"),
        P(),
        P("cond", None),
        P("cond", None, "ty", "tx"),
        P("cond", None, "ty", "tx"),
    )
    out_specs = (P("ty", "tx"), P("ty", "tx"), P("cond", None, "ty", "tx"))
    return jax.shard_map(shards, mesh=mesh, in_specs=in_specs, out_specs=out_specs, check_vma=False)
```

```python
import functools

import jax
import jax.numpy as jnp
from jax import lax
from jax.experimental import pallas as pl
from jax.experimental.pallas import tpu as pltpu
from jax.sharding import PartitionSpec as P

STEPS = 3
HALO = STEPS + 1
SUB = 8
LANE = 128
FIELDS = 8
GROUP = HALO * FIELDS
FOLD = LANE // GROUP
LAG = 2
MIB = 2**20
ANY = pl.BlockSpec(memory_space=pl.ANY)
VMEM = pl.BlockSpec(memory_space=pltpu.VMEM)
SMEM = pl.BlockSpec(memory_space=pltpu.SMEM)


def rows_of(shape):
    return lax.broadcasted_iota(jnp.int32, shape, 0)


def lanes_of(shape):
    return lax.broadcasted_iota(jnp.int32, shape, 1)


def east(x):
    return pltpu.roll(x, x.shape[1] - 1, 1)


def west(x):
    return pltpu.roll(x, 1, 1)


def south(x, below):
    return pltpu.roll(jnp.where(rows_of(x.shape) == 0, below, x), SUB - 1, 0)


def north(x, above):
    return pltpu.roll(jnp.where(rows_of(x.shape) == SUB - 1, above, x), 1, 0)


def tile_at(index):
    if isinstance(index, int):
        return pl.ds(index * SUB, SUB)
    return pl.ds(pl.multiple_of(index * SUB, SUB), SUB)


def held(*arrays, space=pltpu.VMEM):
    return [pltpu.with_memory_space_constraint(x, space) for x in arrays]


def cost(micros):
    return pl.CostEstimate(flops=int(micros * 10**9), bytes_accessed=0, transcendentals=0)


def level_terms(params):
    return params[0, 0] - 1.0, 0.3 * params[0, 3]


def coefficients(bed, mask, kind, tide, flow_in):
    depth = mask.astype(jnp.float32) * (1.0 - 0.5 * jnp.tanh(bed))
    root = depth * lax.rsqrt(jnp.maximum(depth, 1e-12))
    relax = jnp.where(kind == 1, 0.5 * depth, 0.0)
    return root, 1.0 - relax, 0.3 * (relax * tide + jnp.where(kind == 2, flow_in * depth, 0.0))


def moving(stress, hydro):
    return [stress.at[0, k] for k in range(2)] + [hydro.at[0, k] for k in range(3)]


def pack_side_kernel(params_in, bed, mask, kind, stress, hydro, side, reals, ints, params, sems):
    rows, cols = bed.shape
    at_left = lax.axis_index("tx") == 0
    off = pl.multiple_of(jnp.where(at_left, cols - LANE, 0), LANE)
    strips = [reals.at[0], ints.at[0], ints.at[1]] + [reals.at[k] for k in range(1, 6)]
    copies = [
        pltpu.make_async_copy(src.at[:, pl.ds(off, LANE)], strip, sems.at[f])
        for f, (src, strip) in enumerate(zip([bed, mask, kind] + moving(stress, hydro), strips))
    ] + [pltpu.make_async_copy(params_in, params, sems.at[FIELDS])]
    for copy in copies:
        copy.start()
    for copy in copies:
        copy.wait()
    tide, flow_in = level_terms(params)
    lift = jnp.where(at_left, HALO, 0)
    lift_bed = jnp.where(at_left, 1, 0)
    lane = lanes_of((SUB, LANE))
    span = rows // FOLD // SUB
    beds = jnp.zeros((SUB, LANE), jnp.float32)
    for i in range(span):
        total = jnp.zeros((SUB, LANE), jnp.float32)
        for g in range(FOLD):
            at = tile_at(g * span + i)
            first = strips[0][at, :]
            fields = list(coefficients(first, strips[1][at, :], strips[2][at, :], tide, flow_in))
            fields += [strip[at, :] for strip in strips[3:]]
            for f, part in enumerate(fields):
                place = g * FIELDS + f
                total = jnp.where(lane // HALO == place, pltpu.roll(part, lift + place * HALO, 1), total)
            block = g * span + i
            beds = jnp.where(lane == block, pltpu.roll(first, lift_bed + block, 1), beds)
        side[tile_at(i), :] = total
    side[tile_at(span), :] = beds


def pack_side(params, *raw):
    rows, cols = raw[0].shape
    return pl.pallas_call(
        pack_side_kernel,
        name="pack_side",
        out_shape=pltpu.VMEM((rows // FOLD + SUB, LANE), jnp.float32),
        in_specs=[ANY] * 6,
        out_specs=VMEM,
        scratch_shapes=[
            pltpu.VMEM((6, rows, LANE), jnp.float32),
            pltpu.VMEM((2, rows, LANE), jnp.int32),
            pltpu.SMEM(params.shape, jnp.float32),
            pltpu.SemaphoreType.DMA((FIELDS + 1,)),
        ],
        compiler_params=pltpu.CompilerParams(vmem_limit_bytes=4 * MIB),
        cost_estimate=cost(2),
    )(*held(params, *raw, space=pltpu.HBM))


PARTS = 4


def prepare_kernel(
    params_in, bed, mask, kind, stress, hydro, bed_v, root, a, b, pay_a, pay_b,
    mask_v, kind_v, ends, params, load_sems, end_sems, params_sem,
):
    rows, cols = bed.shape
    lanes = cols // LANE
    chunk = rows // PARTS
    loads, copies = [], []
    for c in range(PARTS):
        at = pl.ds(c * chunk, chunk)
        loads.append([
            pltpu.make_async_copy(src.at[at], dst.at[at], load_sems.at[f, c])
            for f, (src, dst) in enumerate(((bed, bed_v), (mask, mask_v), (kind, kind_v)))
        ])
    for f, src in enumerate(moving(stress, hydro)):
        for end, start in enumerate((0, rows - SUB)):
            copies.append(pltpu.make_async_copy(src.at[pl.ds(start, SUB)], ends.at[end, f], end_sems.at[f, end]))
    loads[0].append(pltpu.make_async_copy(params_in, params, params_sem))
    for group in loads + [copies]:
        for copy in group:
            copy.start()
    for copy in loads[0]:
        copy.wait()
    tide, flow_in = level_terms(params)
    for c in range(PARTS):
        for copy in loads[c] if c else ():
            copy.wait()
        for i in range(c * chunk // SUB, (c + 1) * chunk // SUB):
            at = tile_at(i)
            root[at, :], a[at, :], b[at, :] = coefficients(bed_v[at, :], mask_v[at, :], kind_v[at, :], tide, flow_in)
    for copy in copies:
        copy.wait()
    low = rows_of((SUB, cols)) < HALO
    odd = lax.axis_index("ty") % 2 == 1

    def edge_rows(f, end):
        if f < 3:
            return (root, a, b)[f][tile_at(0 if end == 0 else rows // SUB - 1), :]
        return ends[end, f - 3]

    for p in range(FIELDS // 2):
        pairs = []
        for end in range(2):
            both = [edge_rows(f, end) for f in (2 * p, 2 * p + 1)]
            both[1 - end] = pltpu.roll(both[1 - end], HALO, 0)
            pairs.append(jnp.where(low, *both))
        for k in range(lanes):
            at, part = pl.ds(k * GROUP + p * SUB, SUB), slice(k * LANE, (k + 1) * LANE)
            top, bottom = pairs[0][:, part], pairs[1][:, part]
            pay_a[at, :] = jnp.where(odd, top, bottom)
            pay_b[at, :] = jnp.where(odd, bottom, top)
    top = fold_row(bed_v[tile_at(0), :])
    bottom = fold_row(pltpu.roll(bed_v[tile_at(rows // SUB - 1), :], 1, 0))
    at = pl.ds(lanes * GROUP + SUB, SUB)
    pay_a[at, :] = jnp.where(odd, top, bottom)
    pay_b[at, :] = jnp.where(odd, bottom, top)


def fold_row(x):
    row = rows_of((SUB, LANE))
    total = x[:, :LANE]
    for k in range(1, x.shape[1] // LANE):
        total = jnp.where(row == k, pltpu.roll(x[:, k * LANE : (k + 1) * LANE], k, 0), total)
    return total


def prepare(params, *raw):
    rows, cols = raw[0].shape
    tile = pltpu.VMEM((rows, cols), jnp.float32)
    return pl.pallas_call(
        prepare_kernel,
        name="prepare",
        out_shape=[tile] * 4 + [pltpu.VMEM((cols // LANE * GROUP + 2 * SUB, LANE), jnp.float32)] * 2,
        in_specs=[ANY] * 6,
        out_specs=[VMEM] * 6,
        scratch_shapes=[
            pltpu.VMEM((rows, cols), jnp.int32),
            pltpu.VMEM((rows, cols), jnp.int32),
            pltpu.VMEM((2, 5, SUB, cols), jnp.float32),
            pltpu.SMEM(params.shape, jnp.float32),
            pltpu.SemaphoreType.DMA((3, PARTS)),
            pltpu.SemaphoreType.DMA((5, 2)),
            pltpu.SemaphoreType.DMA,
        ],
        compiler_params=pltpu.CompilerParams(vmem_limit_bytes=5 * MIB),
        cost_estimate=cost(2),
    )(*held(params, *raw, space=pltpu.HBM))


def corner_kernel(side, in_a, in_b, pay_a, pay_b):
    at = pl.ds(pay_a.shape[0] - 2 * SUB, SUB)
    odd = lax.axis_index("ty") % 2 == 1
    top = side[pl.ds(0, SUB), :]
    bottom = side[pl.ds(side.shape[0] - 2 * SUB, SUB), :]
    pay_a[at, :] = jnp.where(odd, top, bottom)
    pay_b[at, :] = jnp.where(odd, bottom, top)


def add_corners(side, pay_a, pay_b):
    return pl.pallas_call(
        corner_kernel,
        name="add_corners",
        out_shape=[pltpu.VMEM(pay_a.shape, jnp.float32)] * 2,
        in_specs=[VMEM] * 3,
        out_specs=[VMEM] * 2,
        input_output_aliases={1: 0, 2: 1},
        compiler_params=pltpu.CompilerParams(vmem_limit_bytes=MIB),
        cost_estimate=cost(0.1),
    )(*held(side, pay_a, pay_b))


def side_lanes(at_left):
    drop = jnp.where(at_left, 0, HALO)
    lane = lanes_of((SUB, LANE))
    valid = jnp.where(at_left, lane, LANE - 1 - lane) < HALO

    def unfold(strip, place):
        return pltpu.roll(strip, 2 * LANE - drop - place * HALO, 1)

    return unfold, valid


class Sweep:
    NAMES = (
        ["fc", "fr", "wc", "wr", "e1", "u1"]
        + ["v1", "e2", "u2", "v2", "qc1", "qr1", "qc2", "qr2"]
    )

    def __init__(self, count, wide, get, emit, weights, params, refs, trim):
        self.count, self.wide, self.get, self.emit, self.trim = count, wide, get, emit, trim
        self.__dict__.update(zip(self.NAMES + ["fr_last", "qr_last"], refs))
        cond = lax.axis_index("cond")
        self.slow = 1.0 - 0.2 * params[0, 1]
        total = weights[0]
        for k in range(1, weights.shape[0]):
            total = total + weights[k]
        ones = jnp.ones((SUB, LANE), jnp.float32)
        share = weights[cond].astype(jnp.float32) * ones / (total.astype(jnp.float32) * ones)
        self.scale = jnp.concatenate([-4.0 * params[0, 2] * share] * (wide // LANE), axis=1)

    @classmethod
    def scratch(cls, count, wide):
        block = pltpu.VMEM(((count + 1) * SUB, wide), jnp.float32)
        return [block] * len(cls.NAMES) + [
            pltpu.VMEM((STEPS, SUB, wide), jnp.float32),
            pltpu.VMEM((SUB, wide), jnp.float32),
        ]

    def speed_r(self, i, level, lower, v, wr):
        return (self.slow * v - (south(level, lower) - level) + self.get(4, i)) * wr

    def move(self, n, i, level, lower, u, v, faces, rest):
        right, down = east(level), south(level, lower)
        yield
        fc, fr, wc, wr = faces()
        u = (self.slow * u() - (right - level) + self.get(3, i)) * wc
        v = (self.slow * v() - (down - level) + self.get(4, i)) * wr
        flux_c = fc * u
        flux_r = fr * v
        left, up = west(flux_c), north(flux_r, self.fr_last[n])
        self.fr_last[n] = flux_r
        more = rest(u, v)
        yield
        out = self.get(1, i) * level + self.get(2, i) - (flux_c - left + flux_r - up)
        return out, more

    def step_one(self, i):
        at = tile_at(i)
        s = self.get(0, i)
        inside = i + 1 < self.count
        level = 0.3 * self.get(5, i)
        lower = 0.3 * self.get(5, i + 1) if inside else level
        right, down = east(s), south(s, self.get(0, i + 1) if inside else s)

        def faces():
            ratios = []
            for face in (s * right, s * down):
                base = face + 0.1
                inverse = pl.reciprocal(base, approx=True)
                ratios.append((0.3 * face, face * (inverse * (2.0 - base * inverse))))
            (fc, wc), (fr, wr) = ratios
            for ref, value in ((self.fc, fc), (self.fr, fr), (self.wc, wc), (self.wr, wr)):
                ref[at, :] = value
            return fc, fr, wc, wr

        def rest(u, v):
            self.u1[at, :] = u
            self.v1[at, :] = v
            self.qc1[at, :] = u * jnp.abs(u)
            self.qr1[at, :] = v * jnp.abs(v)

        out, _ = yield from self.move(
            0, i, level, lower, lambda: self.get(6, i), lambda: self.get(7, i), faces, rest
        )
        self.e1[at, :] = out

    def faces_at(self, at):
        return lambda: [ref[at, :] for ref in (self.fc, self.fr, self.wc, self.wr)]

    def step_two(self, i):
        at, after = tile_at(i), tile_at(i + 1)

        def rest(u, v):
            if not (self.trim and i == self.count - 1):
                self.u2[at, :] = u
                self.v2[at, :] = v
                self.qc2[at, :] = self.qc1[at, :] + u * jnp.abs(u)
                self.qr2[at, :] = self.qr1[at, :] + v * jnp.abs(v)

        out, _ = yield from self.move(
            1, i, self.e1[at, :], self.e1[after, :], lambda: self.u1[at, :], lambda: self.v1[at, :],
            self.faces_at(at), rest,
        )
        self.e2[at, :] = out

    def step_three(self, i):
        at, after = tile_at(i), tile_at(i + 1)
        if self.trim and i == self.count - 1:
            return
        if self.trim and i == 0:
            wr = self.wr[at, :]
            v = self.speed_r(i, self.e2[at, :], self.e2[after, :], self.v2[at, :], wr)
            self.fr_last[2] = self.fr[at, :] * v
            self.qr_last[...] = wr * (self.qr2[at, :] + v * jnp.abs(v))
            return

        def rest(u, v):
            qc = self.wc[at, :] * (self.qc2[at, :] + u * jnp.abs(u))
            qr = self.wr[at, :] * (self.qr2[at, :] + v * jnp.abs(v))
            left, up = west(qc), north(qr, self.qr_last[...])
            self.qr_last[...] = qr
            return u, v, qc, qr, left, up

        out, (u, v, qc, qr, left, up) = yield from self.move(
            2, i, self.e2[at, :], self.e2[after, :], lambda: self.u2[at, :], lambda: self.v2[at, :],
            self.faces_at(at), rest,
        )
        self.emit(i, out * (1.0 / 0.3), u, v, (qc - left + qr - up) * self.scale)

    def run(self):
        self.fr_last[...] = jnp.zeros_like(self.fr_last)
        self.qr_last[...] = jnp.zeros_like(self.qr_last)
        for ref in (self.e1, self.e2):
            ref[tile_at(self.count), :] = jnp.zeros((SUB, self.wide), jnp.float32)
        turns = []
        for t in range(self.count + LAG * (STEPS - 1)):
            for k, stage in enumerate((self.step_one, self.step_two, self.step_three)):
                if 0 <= t - LAG * k < self.count:
                    turns.append(stage(t - LAG * k))
        pipeline(turns)


def pipeline(turns):
    active = []
    for turn in turns:
        active = [one for one in active if next(one, True) is None]
        if next(turn, True) is None:
            active.append(turn)
    while active:
        active = [one for one in active if next(one, True) is None]


def reader(root, a, b, stress, hydro, side, unfold, valid):
    rows = root.shape[0]
    span = rows // FOLD // SUB
    fields = [root, a, b] + moving(stress, hydro)

    def read(f, block):
        part = unfold(side[tile_at(block % span), :], (block // span) * FIELDS + f)
        if f == 0:
            part = jnp.where(valid, part, 0.0)
        return jnp.concatenate([fields[f][tile_at(block), :], part], axis=1)

    return read


def quarter_writer(first, quarter, cols, hydro_out, pay):
    lane = lanes_of((SUB, LANE))
    lanes = cols // LANE
    rims = [jnp.zeros((SUB, LANE), jnp.float32)]

    def emit(i, e, u, v, change):
        at = tile_at(first + i)
        for k, value in enumerate((e, u, v)):
            hydro_out[0, k, at, :] = value[:, :cols]
        g = i - 1
        for k in range(lanes):
            pay[tile_at(k * quarter + g), :] = change[:, k * LANE : (k + 1) * LANE]
        rims[0] = jnp.where(lane // 2 == g, pltpu.roll(change[:, cols:], 1 + 2 * g, 1), rims[0])
        if g == quarter - 1:
            pay[tile_at(lanes * quarter), :] = rims[0]

    return emit


def middle_kernel(own, weights, params, root, a, b, stress, hydro, side, *refs):
    hydro_out, pay, *refs = refs[1:] if own else refs
    rows, cols = root.shape
    quarter = rows // SUB // 4
    read = reader(root, a, b, stress, hydro, side, *side_lanes(lax.axis_index("tx") == 0))
    mine = lax.axis_index("cond") % 2
    lower_half = mine == (1 if own else 0)
    first = jnp.where(lower_half, 2 * quarter, quarter) - 1
    emit = quarter_writer(first, quarter, cols, hydro_out, pay)
    Sweep(
        quarter + 2, cols + LANE, lambda f, i: read(f, first + i), emit, weights, params, refs, True
    ).run()


def middle(own, weights, params, fields, side, hydro=None):
    rows, cols = fields[0].shape
    given = (hydro,) if own else ()
    return pl.pallas_call(
        functools.partial(middle_kernel, own),
        name="middle_own" if own else "middle_other",
        out_shape=[
            pltpu.VMEM(fields[4].shape, jnp.float32),
            pltpu.VMEM((cols // LANE * rows // 4 + SUB, LANE), jnp.float32),
        ],
        in_specs=[SMEM, SMEM] + [VMEM] * (6 + own),
        out_specs=[VMEM, VMEM],
        scratch_shapes=Sweep.scratch(rows // SUB // 4 + 2, cols + LANE),
        input_output_aliases={8: 0} if own else {},
        compiler_params=pltpu.CompilerParams(vmem_limit_bytes=10 * MIB),
        cost_estimate=cost(4),
    )(weights, params, *held(*fields, side, *given))


def edge_kernel(
    own, weights, params, root, a, b, stress, hydro, side, far_a, far_b, hydro_in,
    hydro_out, pay, ends, *refs,
):
    rows, cols = root.shape
    blocks = rows // SUB
    quarter = blocks // 4
    lanes = cols // LANE
    unfold, valid = side_lanes(lax.axis_index("tx") == 0)
    read = reader(root, a, b, stress, hydro, side, unfold, valid)
    mine = lax.axis_index("cond") % 2
    top = mine == (0 if own else 1)
    from_a = top == (lax.axis_index("ty") % 2 == 1)
    first = jnp.where(top, -1, blocks - quarter - 1)

    ty = lax.axis_index("ty")
    outside_map = ty == jnp.where(top, 0, lax.axis_size("ty") - 1)
    inner = jnp.where(top, quarter, blocks - quarter - 1)
    corners = pl.ds(lanes * GROUP, SUB)
    for f in range(FIELDS):
        body = read(f, inner)
        parts = []
        for k in range(lanes):
            at = pl.ds(k * GROUP + f // 2 * SUB, SUB)
            part = jnp.where(from_a, far_a[at, :], far_b[at, :])
            moved = pltpu.roll(part, HALO, 0)
            parts.append(jnp.where(top, moved, part) if f % 2 == 0 else jnp.where(top, part, moved))
        corner = jnp.where(from_a, far_a[corners, :], far_b[corners, :])
        corner = jnp.where(top, unfold(corner, (FOLD - 1) * FIELDS + f), unfold(corner, f))
        if f == 0:
            corner = jnp.where(valid, corner, 0.0)
        outer = jnp.concatenate(parts + [corner], axis=1)
        if f == 0:
            outer = jnp.where(outside_map, 0.0, outer)
        ends[0, f] = jnp.where(top, outer, body)
        ends[1, f] = jnp.where(top, body, outer)

    def get(f, i):
        if i == 0 or i == quarter + 1:
            return ends[0 if i == 0 else 1, f]
        return read(f, first + i)

    emit = quarter_writer(first, quarter, cols, hydro_out, pay)
    outside = []

    def finish(i, e, u, v, change):
        if i == 0:
            outside.append(pltpu.roll(change[:, :cols], 1, 0))
        elif i == quarter + 1:
            pay[tile_at(lanes * quarter + 1), :] = fold_row(jnp.where(top, outside[0], change[:, :cols]))
        else:
            emit(i, e, u, v, change)

    Sweep(quarter + 2, cols + LANE, get, finish, weights, params, refs, False).run()


def edge(own, weights, params, fields, side, far_a, far_b, hydro):
    rows, cols = fields[0].shape
    wide = cols + LANE
    return pl.pallas_call(
        functools.partial(edge_kernel, own),
        name="edge_own" if own else "edge_other",
        out_shape=[
            pltpu.VMEM(hydro.shape, jnp.float32),
            pltpu.VMEM((cols // LANE * rows // 4 + 2 * SUB, LANE), jnp.float32),
        ],
        in_specs=[SMEM, SMEM] + [VMEM] * 9,
        out_specs=[VMEM, VMEM],
        scratch_shapes=[pltpu.VMEM((2, FIELDS, SUB, wide), jnp.float32)]
        + Sweep.scratch(rows // SUB // 4 + 2, wide),
        input_output_aliases={10: 0},
        compiler_params=pltpu.CompilerParams(vmem_limit_bytes=12 * MIB),
        cost_estimate=cost(3),
    )(weights, params, *held(*fields, side, far_a, far_b, hydro))


class Update:
    def __init__(self, bed, side, far_a, far_b, own_m, got_m, own_e, got_e, change_v, next_v):
        self.bed, self.side, self.far_a, self.far_b = bed, side, far_a, far_b
        self.parts = {"m": (own_m, got_m), "e": (own_e, got_e)}
        self.change_v, self.next_v = change_v, next_v
        rows, self.cols = bed.shape
        self.blocks = rows // SUB
        self.quarter = self.blocks // 4
        self.lanes = self.cols // LANE
        self.wide = self.cols + LANE
        self.side_bed = side[pl.ds(side.shape[0] - SUB, SUB), :]
        self.drop_bed = jnp.where(lax.axis_index("tx") == 0, 0, 1)
        self.mine = lax.axis_index("cond") % 2
        self.odd = lax.axis_index("ty") % 2 == 1
        col = lanes_of((SUB, self.wide))
        last_c = lax.axis_index("tx") == lax.axis_size("tx") - 1
        first_c = lax.axis_index("tx") == 0
        self.shut_c = (last_c & (col == self.cols - 1)) | (first_c & (col == self.wide - 1))
        self.last_row = rows_of((SUB, self.wide)) == SUB - 1
        self.rims = {}

    def merged(self, q, block):
        own, got = self.parts["e" if q in (0, 3) else "m"]
        at = tile_at(block)
        return jnp.where(self.mine == q // 2, own[at, :], got[at, :])

    def outside(self, q):
        at = pl.ds(self.lanes * GROUP + SUB, SUB)
        a, b = self.far_a[at, :], self.far_b[at, :]
        bed = jnp.where(self.odd, a, b) if q == 0 else jnp.where(self.odd, b, a)
        z = bed + self.merged(q, self.lanes * self.quarter + 1)
        target = SUB - 1 if q == 0 else 0
        parts = [pltpu.roll(z, (SUB + target - k) % SUB, 0) if (target - k) % SUB else z for k in range(self.lanes)]
        return jnp.concatenate(parts + [jnp.zeros((SUB, LANE), jnp.float32)], axis=1)

    def level(self, b, keep):
        if b == -1:
            return self.outside(0)
        if b == self.blocks:
            return self.outside(3)
        q, g = divmod(b, self.quarter)
        change = jnp.concatenate([self.merged(q, k * self.quarter + g) for k in range(self.lanes)], axis=1)
        if keep:
            self.change_v[tile_at(b), :] = change
        if q not in self.rims:
            self.rims[q] = self.merged(q, self.lanes * self.quarter)
        cols_bed = pltpu.roll(self.side_bed, 2 * LANE - self.drop_bed - b, 1)
        cols_change = pltpu.roll(self.rims[q], LANE - 1 - 2 * g, 1)
        return jnp.concatenate([self.bed[tile_at(b), :] + change, cols_bed + cols_change], axis=1)

    def spill(self, slope):
        return 0.25 * (slope - jnp.clip(slope, -1.0, 1.0))

    def south_face(self, slope, b):
        out = self.spill(slope)
        if b == -1:
            return jnp.where((lax.axis_index("ty") == 0) & self.last_row, 0.0, out)
        if b == self.blocks - 1:
            return jnp.where((lax.axis_index("ty") == lax.axis_size("ty") - 1) & self.last_row, 0.0, out)
        return out

    def block(self, b, keep):
        z, lower = self.ahead, self.level(b + 1, keep)
        self.ahead = lower
        right, down = east(z), south(z, lower)
        yield
        gc = jnp.where(self.shut_c, 0.0, self.spill(right - z))
        gr = self.south_face(down - z, b)
        left, up = west(gc), north(gr, self.gr_above)
        self.gr_above = gr
        yield
        out = z + gc - left + gr - up
        self.next_v[tile_at(b), :] = out[:, : self.cols]

    def run(self, first, stop, keep):
        z = self.level(first - 1, keep)
        self.ahead = self.level(first, keep)
        self.gr_above = self.south_face(south(z, self.ahead) - z, first - 1)
        pipeline([self.block(b, keep) for b in range(first, stop)])


def bed_middle_kernel(
    bed, side, far_a, far_b, own_m, got_m, hydro, bed_next, bed_change, hydro_out, change_v, next_v, sems
):
    rows = bed.shape[0]
    quarter = rows // SUB // 4
    copies = [pltpu.make_async_copy(hydro, hydro_out, sems.at[0])]
    copies[0].start()
    update = Update(bed, side, far_a, far_b, own_m, got_m, None, None, change_v, next_v)
    update.run(quarter + 1, 3 * quarter - 1, True)
    for src, dst, low, high in (
        (change_v, bed_change, quarter, 3 * quarter),
        (next_v, bed_next, quarter + 1, 3 * quarter - 1),
    ):
        at = pl.ds(low * SUB, (high - low) * SUB)
        copies.append(pltpu.make_async_copy(src.at[at], dst.at[at], sems.at[len(copies)]))
        copies[-1].start()
    for copy in copies:
        copy.wait()


def bed_edge_kernel(
    bed, side, far_a, far_b, own_m, got_m, own_e, got_e, next_in, change_in, bed_next, bed_change,
    change_v, next_v, sems,
):
    rows = bed.shape[0]
    blocks = rows // SUB
    quarter = blocks // 4
    update = Update(bed, side, far_a, far_b, own_m, got_m, own_e, got_e, change_v, next_v)
    copies = []

    def send(src, dst, low, high):
        at = pl.ds(low * SUB, (high - low) * SUB)
        copies.append(pltpu.make_async_copy(src.at[at], dst.at[at], sems.at[len(copies)]))
        copies[-1].start()

    update.run(0, quarter + 1, True)
    send(change_v, bed_change, 0, quarter)
    send(next_v, bed_next, 0, quarter + 1)
    update.run(blocks - quarter - 1, blocks, True)
    send(change_v, bed_change, blocks - quarter, blocks)
    send(next_v, bed_next, blocks - quarter - 1, blocks)
    for copy in copies:
        copy.wait()


def bed_scratch(rows, cols):
    return [
        pltpu.VMEM((rows, cols), jnp.float32),
        pltpu.VMEM((rows, cols), jnp.float32),
        pltpu.SemaphoreType.DMA((4,)),
    ]


def bed_middle(bed, side, far_a, far_b, own_m, got_m, hydro):
    return pl.pallas_call(
        bed_middle_kernel,
        name="bed_middle",
        out_shape=[pltpu.HBM(x.shape, jnp.float32) for x in (bed, bed, hydro)],
        in_specs=[VMEM] * 7,
        out_specs=[ANY] * 3,
        scratch_shapes=bed_scratch(*bed.shape),
        compiler_params=pltpu.CompilerParams(vmem_limit_bytes=6 * MIB),
        cost_estimate=cost(4),
    )(*held(bed, side, far_a, far_b, own_m, got_m, hydro))


def bed_edge(bed, side, far_a, far_b, own_m, got_m, own_e, got_e, bed_next, bed_change):
    return pl.pallas_call(
        bed_edge_kernel,
        name="bed_edge",
        out_shape=[pltpu.HBM(bed.shape, jnp.float32)] * 2,
        in_specs=[VMEM] * 8 + [ANY] * 2,
        out_specs=[ANY] * 2,
        scratch_shapes=bed_scratch(*bed.shape),
        input_output_aliases={8: 0, 9: 1},
        compiler_params=pltpu.CompilerParams(vmem_limit_bytes=6 * MIB),
        cost_estimate=cost(2),
    )(
        *held(bed, side, far_a, far_b, own_m, got_m, own_e, got_e),
        *held(bed_next, bed_change, space=pltpu.HBM),
    )


def shards(bed, land_mask, cell_class, weights, cond_params, wave_stress, hydro_state):
    ny = lax.axis_size("ty")
    nc = lax.axis_size("cond")
    raw = (bed, land_mask, cell_class, wave_stress, hydro_state)
    swap = [(i, i ^ 1) for i in range(nc)]

    def pairs(first):
        partner = list(range(ny))
        for i in range(first, ny - 1, 2):
            partner[i], partner[i + 1] = i + 1, i
        return list(enumerate(partner))

    def over_chips(part, beside=()):
        reach = 2
        while reach < nc:
            got = lax.ppermute(part, "cond", [(i, i ^ reach) for i in range(nc)])
            got, beside = lax.optimization_barrier((got, beside))
            part = part + got
            reach = 2 * reach
        return part, beside

    side = lax.ppermute(pack_side(cond_params, *raw), "tx", [(0, 1), (1, 0)])
    bed, *terms, far_a, far_b = prepare(cond_params, *raw)
    fields = (*terms, wave_stress, hydro_state)
    far_a, far_b = add_corners(side, far_a, far_b)
    far_a = lax.ppermute(far_a, "ty", pairs(0))
    hydro, pay = middle(False, weights, cond_params, fields, side)
    hydro, far_a, far_b = lax.optimization_barrier((hydro, far_a, far_b))
    far_b = lax.ppermute(far_b, "ty", pairs(1))
    got = lax.ppermute(pay, "cond", swap)
    hydro, pay = middle(True, weights, cond_params, fields, side, hydro)
    part_m = pay + got
    hydro, part_m = lax.optimization_barrier((hydro, part_m))
    hydro, pay = edge(False, weights, cond_params, fields, side, far_a, far_b, hydro)
    got = lax.ppermute(pay, "cond", swap)
    hydro, pay = edge(True, weights, cond_params, fields, side, far_a, far_b, hydro)
    own_m, hydro = over_chips(part_m, hydro)
    part_e = pay + got
    own_m, _ = lax.optimization_barrier((own_m, part_e))
    got_m = lax.ppermute(own_m, "cond", swap)
    bed_next, bed_change, hydro = bed_middle(bed, side, far_a, far_b, own_m, got_m, hydro)
    own_e, (bed_next, bed_change) = over_chips(part_e, (bed_next, bed_change))
    got_e = lax.ppermute(own_e, "cond", swap)
    bed_next, bed_change = bed_edge(
        bed, side, far_a, far_b, own_m, got_m, own_e, got_e, bed_next, bed_change
    )
    return bed_next, bed_change, hydro


def solution(mesh):
    in_specs = (
        P("ty", "tx"),
        P("ty", "tx"),
        P("ty", "tx"),
        P(),
        P("cond", None),
        P("cond", None, "ty", "tx"),
        P("cond", None, "ty", "tx"),
    )
    out_specs = (P("ty", "tx"), P("ty", "tx"), P("cond", None, "ty", "tx"))
    return jax.shard_map(shards, mesh=mesh, in_specs=in_specs, out_specs=out_specs, check_vma=False)
```

```python
import functools

import jax
import jax.numpy as jnp
from jax import lax
from jax.experimental import pallas as pl
from jax.experimental.pallas import tpu as pltpu
from jax.sharding import PartitionSpec as P

STEPS = 3
HALO = STEPS + 1
SUB = 8
LANE = 128
FIELDS = 8
GROUP = HALO * FIELDS
FOLD = LANE // GROUP
LAG = 2
GROUP_TILES = 4
MIB = 2**20
ANY = pl.BlockSpec(memory_space=pl.ANY)
VMEM = pl.BlockSpec(memory_space=pltpu.VMEM)
SMEM = pl.BlockSpec(memory_space=pltpu.SMEM)


def rows_of(shape):
    return lax.broadcasted_iota(jnp.int32, shape, 0)


def lanes_of(shape):
    return lax.broadcasted_iota(jnp.int32, shape, 1)


def east(x):
    return pltpu.roll(x, x.shape[1] - 1, 1)


def west(x):
    return pltpu.roll(x, 1, 1)


def south(x, below):
    return pltpu.roll(jnp.where(rows_of(x.shape) == 0, below, x), SUB - 1, 0)


def north(x, above):
    return pltpu.roll(jnp.where(rows_of(x.shape) == SUB - 1, above, x), 1, 0)


def tile_at(index):
    if isinstance(index, int):
        return pl.ds(index * SUB, SUB)
    return pl.ds(pl.multiple_of(index * SUB, SUB), SUB)


def held(*arrays, space=pltpu.VMEM):
    return [pltpu.with_memory_space_constraint(x, space) for x in arrays]


def cost(micros):
    return pl.CostEstimate(flops=int(micros * 10**9), bytes_accessed=0, transcendentals=0)


def level_terms(params):
    return params[0, 0] - 1.0, 0.3 * params[0, 3]


def coefficients(bed, mask, kind, tide, flow_in):
    depth = mask.astype(jnp.float32) * (1.0 - 0.5 * jnp.tanh(bed))
    root = depth * lax.rsqrt(jnp.maximum(depth, 1e-12))
    relax = jnp.where(kind == 1, 0.5 * depth, 0.0)
    return root, 1.0 - relax, 0.3 * (relax * tide + jnp.where(kind == 2, flow_in * depth, 0.0))


def moving(stress, hydro):
    return [stress.at[0, k] for k in range(2)] + [hydro.at[0, k] for k in range(3)]


def pack_side_kernel(params_in, bed, mask, kind, stress, hydro, side, reals, ints, params, sems):
    rows, cols = bed.shape
    at_left = lax.axis_index("tx") == 0
    off = pl.multiple_of(jnp.where(at_left, cols - LANE, 0), LANE)
    strips = [reals.at[0], ints.at[0], ints.at[1]] + [reals.at[k] for k in range(1, 6)]
    copies = [
        pltpu.make_async_copy(src.at[:, pl.ds(off, LANE)], strip, sems.at[f])
        for f, (src, strip) in enumerate(zip([bed, mask, kind] + moving(stress, hydro), strips))
    ] + [pltpu.make_async_copy(params_in, params, sems.at[FIELDS])]
    for copy in copies:
        copy.start()
    for copy in copies:
        copy.wait()
    tide, flow_in = level_terms(params)
    lift = jnp.where(at_left, HALO, 0)
    lift_bed = jnp.where(at_left, 1, 0)
    lane = lanes_of((SUB, LANE))
    span = rows // FOLD // SUB
    beds = jnp.zeros((SUB, LANE), jnp.float32)
    for i in range(span):
        total = jnp.zeros((SUB, LANE), jnp.float32)
        for g in range(FOLD):
            at = tile_at(g * span + i)
            first = strips[0][at, :]
            fields = list(coefficients(first, strips[1][at, :], strips[2][at, :], tide, flow_in))
            fields += [strip[at, :] for strip in strips[3:]]
            for f, part in enumerate(fields):
                place = g * FIELDS + f
                total = jnp.where(lane // HALO == place, pltpu.roll(part, lift + place * HALO, 1), total)
            block = g * span + i
            beds = jnp.where(lane == block, pltpu.roll(first, lift_bed + block, 1), beds)
        side[tile_at(i), :] = total
    side[tile_at(span), :] = beds


def pack_side(params, *raw):
    rows, cols = raw[0].shape
    return pl.pallas_call(
        pack_side_kernel,
        name="pack_side",
        out_shape=pltpu.VMEM((rows // FOLD + SUB, LANE), jnp.float32),
        in_specs=[ANY] * 6,
        out_specs=VMEM,
        scratch_shapes=[
            pltpu.VMEM((6, rows, LANE), jnp.float32),
            pltpu.VMEM((2, rows, LANE), jnp.int32),
            pltpu.SMEM(params.shape, jnp.float32),
            pltpu.SemaphoreType.DMA((FIELDS + 1,)),
        ],
        compiler_params=pltpu.CompilerParams(vmem_limit_bytes=4 * MIB),
        cost_estimate=cost(2),
    )(*held(params, *raw, space=pltpu.HBM))


PARTS = 4


def prepare_kernel(
    params_in, bed, mask, kind, stress, hydro, bed_v, root, a, b, pay_a, pay_b,
    mask_v, kind_v, ends, params, load_sems, end_sems, params_sem,
):
    rows, cols = bed.shape
    lanes = cols // LANE
    chunk = rows // PARTS
    loads, copies = [], []
    for c in range(PARTS):
        at = pl.ds(c * chunk, chunk)
        loads.append([
            pltpu.make_async_copy(src.at[at], dst.at[at], load_sems.at[f, c])
            for f, (src, dst) in enumerate(((bed, bed_v), (mask, mask_v), (kind, kind_v)))
        ])
    for f, src in enumerate(moving(stress, hydro)):
        for end, start in enumerate((0, rows - SUB)):
            copies.append(pltpu.make_async_copy(src.at[pl.ds(start, SUB)], ends.at[end, f], end_sems.at[f, end]))
    loads[0].append(pltpu.make_async_copy(params_in, params, params_sem))
    for group in loads + [copies]:
        for copy in group:
            copy.start()
    for copy in loads[0]:
        copy.wait()
    tide, flow_in = level_terms(params)
    for c in range(PARTS):
        for copy in loads[c] if c else ():
            copy.wait()
        for i in range(c * chunk // SUB, (c + 1) * chunk // SUB):
            at = tile_at(i)
            root[at, :], a[at, :], b[at, :] = coefficients(bed_v[at, :], mask_v[at, :], kind_v[at, :], tide, flow_in)
    for copy in copies:
        copy.wait()
    low = rows_of((SUB, cols)) < HALO
    odd = lax.axis_index("ty") % 2 == 1

    def edge_rows(f, end):
        if f < 3:
            return (root, a, b)[f][tile_at(0 if end == 0 else rows // SUB - 1), :]
        return ends[end, f - 3]

    for p in range(FIELDS // 2):
        pairs = []
        for end in range(2):
            both = [edge_rows(f, end) for f in (2 * p, 2 * p + 1)]
            both[1 - end] = pltpu.roll(both[1 - end], HALO, 0)
            pairs.append(jnp.where(low, *both))
        for k in range(lanes):
            at, part = pl.ds(k * GROUP + p * SUB, SUB), slice(k * LANE, (k + 1) * LANE)
            top, bottom = pairs[0][:, part], pairs[1][:, part]
            pay_a[at, :] = jnp.where(odd, top, bottom)
            pay_b[at, :] = jnp.where(odd, bottom, top)
    top = fold_row([bed_v[tile_at(0), lanes_at(k)] for k in range(lanes)])
    bottom = fold_row([pltpu.roll(bed_v[tile_at(rows // SUB - 1), lanes_at(k)], 1, 0) for k in range(lanes)])
    at = pl.ds(lanes * GROUP + SUB, SUB)
    pay_a[at, :] = jnp.where(odd, top, bottom)
    pay_b[at, :] = jnp.where(odd, bottom, top)


def fold_row(x):
    row = rows_of((SUB, LANE))
    total = x[0]
    for k in range(1, len(x)):
        total = jnp.where(row == k, pltpu.roll(x[k], k, 0), total)
    return total


def prepare(params, *raw):
    rows, cols = raw[0].shape
    tile = pltpu.VMEM((rows, cols), jnp.float32)
    return pl.pallas_call(
        prepare_kernel,
        name="prepare",
        out_shape=[tile] * 4 + [pltpu.VMEM((cols // LANE * GROUP + 2 * SUB, LANE), jnp.float32)] * 2,
        in_specs=[ANY] * 6,
        out_specs=[VMEM] * 6,
        scratch_shapes=[
            pltpu.VMEM((rows, cols), jnp.int32),
            pltpu.VMEM((rows, cols), jnp.int32),
            pltpu.VMEM((2, 5, SUB, cols), jnp.float32),
            pltpu.SMEM(params.shape, jnp.float32),
            pltpu.SemaphoreType.DMA((3, PARTS)),
            pltpu.SemaphoreType.DMA((5, 2)),
            pltpu.SemaphoreType.DMA,
        ],
        compiler_params=pltpu.CompilerParams(vmem_limit_bytes=5 * MIB),
        cost_estimate=cost(2),
    )(*held(params, *raw, space=pltpu.HBM))


def corner_kernel(side, in_a, in_b, pay_a, pay_b):
    at = pl.ds(pay_a.shape[0] - 2 * SUB, SUB)
    odd = lax.axis_index("ty") % 2 == 1
    top = side[pl.ds(0, SUB), :]
    bottom = side[pl.ds(side.shape[0] - 2 * SUB, SUB), :]
    pay_a[at, :] = jnp.where(odd, top, bottom)
    pay_b[at, :] = jnp.where(odd, bottom, top)


def add_corners(side, pay_a, pay_b):
    return pl.pallas_call(
        corner_kernel,
        name="add_corners",
        out_shape=[pltpu.VMEM(pay_a.shape, jnp.float32)] * 2,
        in_specs=[VMEM] * 3,
        out_specs=[VMEM] * 2,
        input_output_aliases={1: 0, 2: 1},
        compiler_params=pltpu.CompilerParams(vmem_limit_bytes=MIB),
        cost_estimate=cost(0.1),
    )(*held(side, pay_a, pay_b))


def side_lanes(at_left):
    drop = jnp.where(at_left, 0, HALO)
    lane = lanes_of((SUB, LANE))
    valid = jnp.where(at_left, lane, LANE - 1 - lane) < HALO

    def unfold(strip, place):
        return pltpu.roll(strip, 2 * LANE - drop - place * HALO, 1)

    return unfold, valid


class Sweep:
    NAMES = ["fc", "fr", "wc", "wr", "e1", "u1"] + ["v1", "e2", "u2", "v2"] + ["qc1", "qr1", "qc2", "qr2"]

    def __init__(self, count, tiles, get, emit, weights, params, refs, trim):
        self.count, self.tiles, self.get, self.emit, self.trim = count, tiles, get, emit, trim
        self.__dict__.update(zip(self.NAMES + ["fr_last", "qr_last"], refs))
        cond = lax.axis_index("cond")
        self.slow = 1.0 - 0.2 * params[0, 1]
        total = weights[0]
        for k in range(1, weights.shape[0]):
            total = total + weights[k]
        ones = jnp.ones((SUB, LANE), jnp.float32)
        share = weights[cond].astype(jnp.float32) * ones / (total.astype(jnp.float32) * ones)
        self.scale = -4.0 * params[0, 2] * share
        lane, row = lanes_of((SUB, LANE)), rows_of((SUB, LANE))
        self.last_lane, self.first_lane = lane == LANE - 1, lane == 0
        self.last_row, self.first_row = row == SUB - 1, row == 0
        own = list(range(tiles - 1))
        self.groups = [[tiles - 1]] + [own[k : k + GROUP_TILES] for k in range(0, tiles - 1, GROUP_TILES)]

    @classmethod
    def scratch(cls, count, tiles):
        block = pltpu.VMEM((tiles, (count + 1) * SUB, LANE), jnp.float32)
        return [block] * len(cls.NAMES) + [
            pltpu.VMEM((STEPS, tiles, SUB, LANE), jnp.float32),
            pltpu.VMEM((tiles, SUB, LANE), jnp.float32),
        ]

    def south(self, x, below):
        return pltpu.roll(jnp.where(self.first_row, below, x), SUB - 1, 0)

    def north(self, x, above):
        return pltpu.roll(jnp.where(self.last_row, above, x), 1, 0)

    def eastward(self, values):
        kept = {}

        def one(k):
            if k not in kept:
                value = values(k)
                kept[k] = value, pltpu.roll(value, LANE - 1, 1)
            return kept[k]

        def both(k):
            value, rolled = one(k)
            return value, jnp.where(self.last_lane, one((k + 1) % self.tiles)[1], rolled)

        return both

    def west(self, rolled, k):
        return jnp.where(self.first_lane, rolled[(k - 1) % self.tiles], rolled[k])

    def move(self, n, i, level, lower, speeds, start, faces, keep, done):
        levels = self.eastward(level)
        flux, rolled, base, ups = {}, {}, {}, {}

        def close(k):
            done(k, base[k] + ups[k] - flux[k] + self.west(rolled, k))

        for group in self.groups:
            opened = []
            for k in group:
                here, right = levels(k)
                opened.append((k, here, right, self.south(here, lower(k)), start(k)))
            yield
            for k, here, right, down, begun in opened:
                fc, fr, wc, wr = faces(k, begun)
                u, v = speeds(k)
                u = (self.slow * u - (right - here) + self.get(3, i, k)) * wc
                v = (self.slow * v - (down - here) + self.get(4, i, k)) * wr
                flux[k] = fc * u
                rolled[k] = pltpu.roll(flux[k], 1, 1)
                flux_r = fr * v
                ups[k] = self.north(flux_r, self.fr_last[n, k])
                self.fr_last[n, k] = flux_r
                base[k] = self.get(1, i, k) * here + self.get(2, i, k) - flux_r
                keep(k, u, v)
            yield
            for k in group:
                if k < self.tiles - 1:
                    close(k)
        close(self.tiles - 1)

    def step_one(self, i):
        at = tile_at(i)
        inside = i + 1 < self.count
        roots = self.eastward(lambda k: self.get(0, i, k))

        def start(k):
            s, right = roots(k)
            return s, right, self.south(s, self.get(0, i + 1, k) if inside else s)

        def faces(k, begun):
            s, right, down = begun
            out = []
            for other, face_ref, wet_ref in ((right, self.fc, self.wc), (down, self.fr, self.wr)):
                face = s * other
                base = face + 0.1
                inverse = pl.reciprocal(base, approx=True)
                out.append((0.3 * face, face * (inverse * (2.0 - base * inverse))))
                face_ref[k, at, :], wet_ref[k, at, :] = out[-1]
            (fc, wc), (fr, wr) = out
            return fc, fr, wc, wr

        def keep(k, u, v):
            self.u1[k, at, :] = u
            self.v1[k, at, :] = v
            self.qc1[k, at, :] = u * jnp.abs(u)
            self.qr1[k, at, :] = v * jnp.abs(v)

        def done(k, e):
            self.e1[k, at, :] = e

        level = lambda k: 0.3 * self.get(5, i, k)
        lower = lambda k: 0.3 * self.get(5, i + 1 if inside else i, k)
        speeds = lambda k: (self.get(6, i, k), self.get(7, i, k))
        return self.move(0, i, level, lower, speeds, start, faces, keep, done)

    def later(self, n, i, e, u, v, keep, done):
        at, after = tile_at(i), tile_at(i + 1)
        faces = lambda k, _: [ref[k, at, :] for ref in (self.fc, self.fr, self.wc, self.wr)]
        speeds = lambda k: (u[k, at, :], v[k, at, :])
        return self.move(
            n, i, lambda k: e[k, at, :], lambda k: e[k, after, :], speeds, lambda k: None, faces, keep, done
        )

    def step_two(self, i):
        at = tile_at(i)

        def keep(k, u, v):
            if not (self.trim and i == self.count - 1):
                self.u2[k, at, :] = u
                self.v2[k, at, :] = v
                self.qc2[k, at, :] = self.qc1[k, at, :] + u * jnp.abs(u)
                self.qr2[k, at, :] = self.qr1[k, at, :] + v * jnp.abs(v)

        def done(k, e):
            self.e2[k, at, :] = e

        return self.later(1, i, self.e1, self.u1, self.v1, keep, done)

    def step_three(self, i):
        at, after = tile_at(i), tile_at(i + 1)
        if self.trim and i == self.count - 1:
            return iter(())
        if self.trim and i == 0:
            for k in range(self.tiles):
                here, wr = self.e2[k, at, :], self.wr[k, at, :]
                lower = self.e2[k, after, :]
                v = (self.slow * self.v2[k, at, :] - (self.south(here, lower) - here) + self.get(4, i, k)) * wr
                self.fr_last[2, k] = self.fr[k, at, :] * v
                self.qr_last[k] = wr * (self.qr2[k, at, :] + v * jnp.abs(v))
            return iter(())
        rolled, parts = {}, {}

        def keep(k, u, v):
            self.emit(i, 1, k, u)
            self.emit(i, 2, k, v)
            qc = self.wc[k, at, :] * (self.qc2[k, at, :] + u * jnp.abs(u))
            qr = self.wr[k, at, :] * (self.qr2[k, at, :] + v * jnp.abs(v))
            rolled[k] = pltpu.roll(qc, 1, 1)
            parts[k] = qc + qr, self.north(qr, self.qr_last[k])
            self.qr_last[k] = qr

        def done(k, e):
            self.emit(i, 0, k, e * (1.0 / 0.3))
            part, up = parts[k]
            self.emit(i, 3, k, (part - up - self.west(rolled, k)) * self.scale)

        return self.later(2, i, self.e2, self.u2, self.v2, keep, done)

    def run(self):
        self.fr_last[...] = jnp.zeros_like(self.fr_last)
        self.qr_last[...] = jnp.zeros_like(self.qr_last)
        for ref in (self.e1, self.e2):
            ref[:, tile_at(self.count), :] = jnp.zeros((self.tiles, SUB, LANE), jnp.float32)
        stages = (self.step_three, self.step_two, self.step_one)
        for t in range(self.count + LAG * (STEPS - 1)):
            turns = []
            for k, stage in enumerate(stages):
                i = t - LAG * (STEPS - 1 - k)
                if 0 <= i < self.count:
                    turns.append(stage(i))
            while turns:
                turns = [turn for turn in turns if next(turn, True) is None]


def lanes_at(k):
    return slice(k * LANE, (k + 1) * LANE)


def reader(root, a, b, stress, hydro, side, unfold, valid):
    rows, cols = root.shape
    span = rows // FOLD // SUB
    tiles = cols // LANE
    fields = [root, a, b] + moving(stress, hydro)

    def read(f, block, k):
        if k < tiles:
            return fields[f][tile_at(block), lanes_at(k)]
        part = unfold(side[tile_at(block % span), :], (block // span) * FIELDS + f)
        return jnp.where(valid, part, 0.0) if f == 0 else part

    return read


def quarter_writer(first, quarter, cols, hydro_out, pay):
    lane = lanes_of((SUB, LANE))
    tiles = cols // LANE
    rims = [jnp.zeros((SUB, LANE), jnp.float32)]

    def emit(i, what, k, value):
        g = i - 1
        if what < 3:
            if k < tiles:
                hydro_out[0, what, tile_at(first + i), lanes_at(k)] = value
        elif k < tiles:
            pay[tile_at(k * quarter + g), :] = value
        else:
            rims[0] = jnp.where(lane // 2 == g, pltpu.roll(value, 1 + 2 * g, 1), rims[0])
            if g == quarter - 1:
                pay[tile_at(tiles * quarter), :] = rims[0]

    return emit


def middle_kernel(own, weights, params, root, a, b, stress, hydro, side, *refs):
    hydro_out, pay, *refs = refs[1:] if own else refs
    rows, cols = root.shape
    quarter = rows // SUB // 4
    read = reader(root, a, b, stress, hydro, side, *side_lanes(lax.axis_index("tx") == 0))
    mine = lax.axis_index("cond") % 2
    lower_half = mine == (1 if own else 0)
    first = jnp.where(lower_half, 2 * quarter, quarter) - 1
    emit = quarter_writer(first, quarter, cols, hydro_out, pay)
    Sweep(
        quarter + 2, cols // LANE + 1, lambda f, i, k: read(f, first + i, k), emit, weights, params, refs, True
    ).run()


def middle(own, weights, params, fields, side, hydro=None):
    rows, cols = fields[0].shape
    given = (hydro,) if own else ()
    return pl.pallas_call(
        functools.partial(middle_kernel, own),
        name="middle_own" if own else "middle_other",
        out_shape=[
            pltpu.VMEM(fields[4].shape, jnp.float32),
            pltpu.VMEM((cols // LANE * rows // 4 + SUB, LANE), jnp.float32),
        ],
        in_specs=[SMEM, SMEM] + [VMEM] * (6 + own),
        out_specs=[VMEM, VMEM],
        scratch_shapes=Sweep.scratch(rows // SUB // 4 + 2, cols // LANE + 1),
        input_output_aliases={8: 0} if own else {},
        compiler_params=pltpu.CompilerParams(vmem_limit_bytes=10 * MIB),
        cost_estimate=cost(4),
    )(weights, params, *held(*fields, side, *given))


def edge_kernel(
    own, weights, params, root, a, b, stress, hydro, side, far_a, far_b, hydro_in,
    hydro_out, pay, ends, *refs,
):
    rows, cols = root.shape
    blocks = rows // SUB
    quarter = blocks // 4
    lanes = cols // LANE
    unfold, valid = side_lanes(lax.axis_index("tx") == 0)
    read = reader(root, a, b, stress, hydro, side, unfold, valid)
    mine = lax.axis_index("cond") % 2
    top = mine == (0 if own else 1)
    from_a = top == (lax.axis_index("ty") % 2 == 1)
    first = jnp.where(top, -1, blocks - quarter - 1)

    ty = lax.axis_index("ty")
    outside_map = ty == jnp.where(top, 0, lax.axis_size("ty") - 1)
    inner = jnp.where(top, quarter, blocks - quarter - 1)
    corners = pl.ds(lanes * GROUP, SUB)
    for f in range(FIELDS):
        for k in range(lanes + 1):
            body = read(f, inner, k)
            if k < lanes:
                at = pl.ds(k * GROUP + f // 2 * SUB, SUB)
                part = jnp.where(from_a, far_a[at, :], far_b[at, :])
                moved = pltpu.roll(part, HALO, 0)
                outer = jnp.where(top, moved, part) if f % 2 == 0 else jnp.where(top, part, moved)
            else:
                corner = jnp.where(from_a, far_a[corners, :], far_b[corners, :])
                outer = jnp.where(top, unfold(corner, (FOLD - 1) * FIELDS + f), unfold(corner, f))
                if f == 0:
                    outer = jnp.where(valid, outer, 0.0)
            if f == 0:
                outer = jnp.where(outside_map, 0.0, outer)
            ends[0, f, k] = jnp.where(top, outer, body)
            ends[1, f, k] = jnp.where(top, body, outer)

    def get(f, i, k):
        if i == 0 or i == quarter + 1:
            return ends[0 if i == 0 else 1, f, k]
        return read(f, first + i, k)

    emit = quarter_writer(first, quarter, cols, hydro_out, pay)
    outside = {0: [], quarter + 1: []}

    def finish(i, what, k, value):
        if i not in outside:
            emit(i, what, k, value)
        elif what == 3 and k < lanes:
            outside[i].append(value)
            if i and k == lanes - 1:
                rim = [jnp.where(top, pltpu.roll(x, 1, 0), y) for x, y in zip(outside[0], outside[i])]
                pay[tile_at(lanes * quarter + 1), :] = fold_row(rim)

    Sweep(quarter + 2, lanes + 1, get, finish, weights, params, refs, False).run()


def edge(own, weights, params, fields, side, far_a, far_b, hydro):
    rows, cols = fields[0].shape
    return pl.pallas_call(
        functools.partial(edge_kernel, own),
        name="edge_own" if own else "edge_other",
        out_shape=[
            pltpu.VMEM(hydro.shape, jnp.float32),
            pltpu.VMEM((cols // LANE * rows // 4 + 2 * SUB, LANE), jnp.float32),
        ],
        in_specs=[SMEM, SMEM] + [VMEM] * 9,
        out_specs=[VMEM, VMEM],
        scratch_shapes=[pltpu.VMEM((2, FIELDS, cols // LANE + 1, SUB, LANE), jnp.float32)]
        + Sweep.scratch(rows // SUB // 4 + 2, cols // LANE + 1),
        input_output_aliases={10: 0},
        compiler_params=pltpu.CompilerParams(vmem_limit_bytes=12 * MIB),
        cost_estimate=cost(3),
    )(weights, params, *held(*fields, side, far_a, far_b, hydro))


class Update:
    def __init__(self, bed, side, far_a, far_b, own_m, got_m, own_e, got_e, change_v, next_v):
        self.bed, self.side, self.far_a, self.far_b = bed, side, far_a, far_b
        self.parts = {"m": (own_m, got_m), "e": (own_e, got_e)}
        self.change_v, self.next_v = change_v, next_v
        rows, self.cols = bed.shape
        self.blocks = rows // SUB
        self.quarter = self.blocks // 4
        self.lanes = self.cols // LANE
        self.wide = self.cols + LANE
        self.side_bed = side[pl.ds(side.shape[0] - SUB, SUB), :]
        self.drop_bed = jnp.where(lax.axis_index("tx") == 0, 0, 1)
        self.mine = lax.axis_index("cond") % 2
        self.odd = lax.axis_index("ty") % 2 == 1
        col = lanes_of((SUB, self.wide))
        last_c = lax.axis_index("tx") == lax.axis_size("tx") - 1
        first_c = lax.axis_index("tx") == 0
        self.shut_c = (last_c & (col == self.cols - 1)) | (first_c & (col == self.wide - 1))
        self.last_row = rows_of((SUB, self.wide)) == SUB - 1
        self.rims = {}

    def merged(self, q, block):
        own, got = self.parts["e" if q in (0, 3) else "m"]
        at = tile_at(block)
        return jnp.where(self.mine == q // 2, own[at, :], got[at, :])

    def outside(self, q):
        at = pl.ds(self.lanes * GROUP + SUB, SUB)
        a, b = self.far_a[at, :], self.far_b[at, :]
        bed = jnp.where(self.odd, a, b) if q == 0 else jnp.where(self.odd, b, a)
        z = bed + self.merged(q, self.lanes * self.quarter + 1)
        target = SUB - 1 if q == 0 else 0
        parts = [pltpu.roll(z, (SUB + target - k) % SUB, 0) if (target - k) % SUB else z for k in range(self.lanes)]
        return jnp.concatenate(parts + [jnp.zeros((SUB, LANE), jnp.float32)], axis=1)

    def level(self, b, keep):
        if b == -1:
            return self.outside(0)
        if b == self.blocks:
            return self.outside(3)
        q, g = divmod(b, self.quarter)
        change = jnp.concatenate([self.merged(q, k * self.quarter + g) for k in range(self.lanes)], axis=1)
        if keep:
            self.change_v[tile_at(b), :] = change
        if q not in self.rims:
            self.rims[q] = self.merged(q, self.lanes * self.quarter)
        cols_bed = pltpu.roll(self.side_bed, 2 * LANE - self.drop_bed - b, 1)
        cols_change = pltpu.roll(self.rims[q], LANE - 1 - 2 * g, 1)
        return jnp.concatenate([self.bed[tile_at(b), :] + change, cols_bed + cols_change], axis=1)

    def spill(self, slope):
        return 0.25 * (slope - jnp.clip(slope, -1.0, 1.0))

    def south_face(self, z, lower, b):
        out = self.spill(south(z, lower) - z)
        if b == -1:
            return jnp.where((lax.axis_index("ty") == 0) & self.last_row, 0.0, out)
        if b == self.blocks - 1:
            return jnp.where((lax.axis_index("ty") == lax.axis_size("ty") - 1) & self.last_row, 0.0, out)
        return out

    def run(self, first, stop, keep, after=lambda b: None):
        z = self.level(first - 1, keep)
        lower = self.level(first, keep)
        gr = self.south_face(z, lower, first - 1)
        for b in range(first, stop):
            z, lower = lower, self.level(b + 1, keep)
            gr_above, gr = gr, self.south_face(z, lower, b)
            gc = jnp.where(self.shut_c, 0.0, self.spill(east(z) - z))
            out = z + gc - west(gc) + gr - north(gr, gr_above)
            self.next_v[tile_at(b), :] = out[:, : self.cols]
            after(b)


def bed_middle_kernel(
    bed, side, far_a, far_b, own_m, got_m, hydro, bed_next, bed_change, hydro_out, change_v, next_v, sems
):
    rows = bed.shape[0]
    quarter = rows // SUB // 4
    copies = [pltpu.make_async_copy(hydro, hydro_out, sems.at[0])]
    copies[0].start()
    update = Update(bed, side, far_a, far_b, own_m, got_m, None, None, change_v, next_v)
    update.run(quarter + 1, 3 * quarter - 1, True)
    for src, dst, low, high in (
        (change_v, bed_change, quarter, 3 * quarter),
        (next_v, bed_next, quarter + 1, 3 * quarter - 1),
    ):
        at = pl.ds(low * SUB, (high - low) * SUB)
        copies.append(pltpu.make_async_copy(src.at[at], dst.at[at], sems.at[len(copies)]))
        copies[-1].start()
    for copy in copies:
        copy.wait()


def bed_edge_kernel(
    bed, side, far_a, far_b, own_m, got_m, own_e, got_e, next_in, change_in, bed_next, bed_change,
    change_v, next_v, sems,
):
    rows = bed.shape[0]
    blocks = rows // SUB
    quarter = blocks // 4
    update = Update(bed, side, far_a, far_b, own_m, got_m, own_e, got_e, change_v, next_v)
    copies = []

    def send(src, dst, low, high):
        at = pl.ds(low * SUB, (high - low) * SUB)
        copies.append(pltpu.make_async_copy(src.at[at], dst.at[at], sems.at[len(copies)]))
        copies[-1].start()

    update.run(0, quarter + 1, True)
    send(change_v, bed_change, 0, quarter)
    send(next_v, bed_next, 0, quarter + 1)
    update.run(blocks - quarter - 1, blocks, True)
    send(change_v, bed_change, blocks - quarter, blocks)
    send(next_v, bed_next, blocks - quarter - 1, blocks)
    for copy in copies:
        copy.wait()


def bed_scratch(rows, cols):
    return [
        pltpu.VMEM((rows, cols), jnp.float32),
        pltpu.VMEM((rows, cols), jnp.float32),
        pltpu.SemaphoreType.DMA((4,)),
    ]


def bed_middle(bed, side, far_a, far_b, own_m, got_m, hydro):
    return pl.pallas_call(
        bed_middle_kernel,
        name="bed_middle",
        out_shape=[pltpu.HBM(x.shape, jnp.float32) for x in (bed, bed, hydro)],
        in_specs=[VMEM] * 7,
        out_specs=[ANY] * 3,
        scratch_shapes=bed_scratch(*bed.shape),
        compiler_params=pltpu.CompilerParams(vmem_limit_bytes=6 * MIB),
        cost_estimate=cost(4),
    )(*held(bed, side, far_a, far_b, own_m, got_m, hydro))


def bed_edge(bed, side, far_a, far_b, own_m, got_m, own_e, got_e, bed_next, bed_change):
    return pl.pallas_call(
        bed_edge_kernel,
        name="bed_edge",
        out_shape=[pltpu.HBM(bed.shape, jnp.float32)] * 2,
        in_specs=[VMEM] * 8 + [ANY] * 2,
        out_specs=[ANY] * 2,
        scratch_shapes=bed_scratch(*bed.shape),
        input_output_aliases={8: 0, 9: 1},
        compiler_params=pltpu.CompilerParams(vmem_limit_bytes=6 * MIB),
        cost_estimate=cost(2),
    )(
        *held(bed, side, far_a, far_b, own_m, got_m, own_e, got_e),
        *held(bed_next, bed_change, space=pltpu.HBM),
    )


def shards(bed, land_mask, cell_class, weights, cond_params, wave_stress, hydro_state):
    ny = lax.axis_size("ty")
    nc = lax.axis_size("cond")
    raw = (bed, land_mask, cell_class, wave_stress, hydro_state)
    swap = [(i, i ^ 1) for i in range(nc)]

    def pairs(first):
        partner = list(range(ny))
        for i in range(first, ny - 1, 2):
            partner[i], partner[i + 1] = i + 1, i
        return list(enumerate(partner))

    def over_chips(part, beside=()):
        reach = 2
        while reach < nc:
            got = lax.ppermute(part, "cond", [(i, i ^ reach) for i in range(nc)])
            got, beside = lax.optimization_barrier((got, beside))
            part = part + got
            reach = 2 * reach
        return part, beside

    side = lax.ppermute(pack_side(cond_params, *raw), "tx", [(0, 1), (1, 0)])
    bed, *terms, far_a, far_b = prepare(cond_params, *raw)
    fields = (*terms, wave_stress, hydro_state)
    far_a, far_b = add_corners(side, far_a, far_b)
    far_a = lax.ppermute(far_a, "ty", pairs(0))
    hydro, pay = middle(False, weights, cond_params, fields, side)
    hydro, far_a, far_b = lax.optimization_barrier((hydro, far_a, far_b))
    far_b = lax.ppermute(far_b, "ty", pairs(1))
    got = lax.ppermute(pay, "cond", swap)
    hydro, pay = middle(True, weights, cond_params, fields, side, hydro)
    part_m = pay + got
    hydro, part_m = lax.optimization_barrier((hydro, part_m))
    hydro, pay = edge(False, weights, cond_params, fields, side, far_a, far_b, hydro)
    got = lax.ppermute(pay, "cond", swap)
    hydro, pay = edge(True, weights, cond_params, fields, side, far_a, far_b, hydro)
    own_m, hydro = over_chips(part_m, hydro)
    part_e = pay + got
    own_m, _ = lax.optimization_barrier((own_m, part_e))
    got_m = lax.ppermute(own_m, "cond", swap)
    bed_next, bed_change, hydro = bed_middle(bed, side, far_a, far_b, own_m, got_m, hydro)
    own_e, (bed_next, bed_change) = over_chips(part_e, (bed_next, bed_change))
    got_e = lax.ppermute(own_e, "cond", swap)
    bed_next, bed_change = bed_edge(
        bed, side, far_a, far_b, own_m, got_m, own_e, got_e, bed_next, bed_change
    )
    return bed_next, bed_change, hydro


def solution(mesh):
    in_specs = (
        P("ty", "tx"),
        P("ty", "tx"),
        P("ty", "tx"),
        P(),
        P("cond", None),
        P("cond", None, "ty", "tx"),
        P("cond", None, "ty", "tx"),
    )
    out_specs = (P("ty", "tx"), P("ty", "tx"), P("cond", None, "ty", "tx"))
    return jax.shard_map(shards, mesh=mesh, in_specs=in_specs, out_specs=out_specs, check_vma=False)
```

```python
import functools

import jax
import jax.numpy as jnp
from jax import lax
from jax.experimental import pallas as pl
from jax.experimental.pallas import tpu as pltpu
from jax.sharding import PartitionSpec as P

STEPS = 3
HALO = STEPS + 1
SUB = 8
LANE = 128
FIELDS = 8
GROUP = HALO * FIELDS
FOLD = LANE // GROUP
LAG = 2
MIB = 2**20
ANY = pl.BlockSpec(memory_space=pl.ANY)
VMEM = pl.BlockSpec(memory_space=pltpu.VMEM)
SMEM = pl.BlockSpec(memory_space=pltpu.SMEM)


def rows_of(shape):
    return lax.broadcasted_iota(jnp.int32, shape, 0)


def lanes_of(shape):
    return lax.broadcasted_iota(jnp.int32, shape, 1)


def east(x):
    return pltpu.roll(x, x.shape[1] - 1, 1)


def west(x):
    return pltpu.roll(x, 1, 1)


def south(x, below):
    return pltpu.roll(jnp.where(rows_of(x.shape) == 0, below, x), SUB - 1, 0)


def north(x, above):
    return pltpu.roll(jnp.where(rows_of(x.shape) == SUB - 1, above, x), 1, 0)


def tile_at(index):
    if isinstance(index, int):
        return pl.ds(index * SUB, SUB)
    return pl.ds(pl.multiple_of(index * SUB, SUB), SUB)


def held(*arrays, space=pltpu.VMEM):
    return [pltpu.with_memory_space_constraint(x, space) for x in arrays]


def cost(micros):
    return pl.CostEstimate(flops=int(micros * 10**9), bytes_accessed=0, transcendentals=0)


def level_terms(params):
    return params[0, 0] - 1.0, 0.3 * params[0, 3]


def coefficients(bed, mask, kind, tide, flow_in):
    depth = mask.astype(jnp.float32) * (1.0 - 0.5 * jnp.tanh(bed))
    root = depth * lax.rsqrt(jnp.maximum(depth, 1e-12))
    relax = jnp.where(kind == 1, 0.5 * depth, 0.0)
    return root, 1.0 - relax, 0.3 * (relax * tide + jnp.where(kind == 2, flow_in * depth, 0.0))


def moving(stress, hydro):
    return [stress.at[0, k] for k in range(2)] + [hydro.at[0, k] for k in range(3)]


def pack_side_kernel(params_in, bed, mask, kind, stress, hydro, side, reals, ints, params, sems):
    rows, cols = bed.shape
    at_left = lax.axis_index("tx") == 0
    off = pl.multiple_of(jnp.where(at_left, cols - LANE, 0), LANE)
    strips = [reals.at[0], ints.at[0], ints.at[1]] + [reals.at[k] for k in range(1, 6)]
    copies = [
        pltpu.make_async_copy(src.at[:, pl.ds(off, LANE)], strip, sems.at[f])
        for f, (src, strip) in enumerate(zip([bed, mask, kind] + moving(stress, hydro), strips))
    ] + [pltpu.make_async_copy(params_in, params, sems.at[FIELDS])]
    for copy in copies:
        copy.start()
    for copy in copies:
        copy.wait()
    tide, flow_in = level_terms(params)
    lift = jnp.where(at_left, HALO, 0)
    lift_bed = jnp.where(at_left, 1, 0)
    lane = lanes_of((SUB, LANE))
    span = rows // FOLD // SUB
    beds = jnp.zeros((SUB, LANE), jnp.float32)
    for i in range(span):
        total = jnp.zeros((SUB, LANE), jnp.float32)
        for g in range(FOLD):
            at = tile_at(g * span + i)
            first = strips[0][at, :]
            fields = list(coefficients(first, strips[1][at, :], strips[2][at, :], tide, flow_in))
            fields += [strip[at, :] for strip in strips[3:]]
            for f, part in enumerate(fields):
                place = g * FIELDS + f
                total = jnp.where(lane // HALO == place, pltpu.roll(part, lift + place * HALO, 1), total)
            block = g * span + i
            beds = jnp.where(lane == block, pltpu.roll(first, lift_bed + block, 1), beds)
        side[tile_at(i), :] = total
    side[tile_at(span), :] = beds


def pack_side(params, *raw):
    rows, cols = raw[0].shape
    return pl.pallas_call(
        pack_side_kernel,
        name="pack_side",
        out_shape=pltpu.VMEM((rows // FOLD + SUB, LANE), jnp.float32),
        in_specs=[ANY] * 6,
        out_specs=VMEM,
        scratch_shapes=[
            pltpu.VMEM((6, rows, LANE), jnp.float32),
            pltpu.VMEM((2, rows, LANE), jnp.int32),
            pltpu.SMEM(params.shape, jnp.float32),
            pltpu.SemaphoreType.DMA((FIELDS + 1,)),
        ],
        compiler_params=pltpu.CompilerParams(vmem_limit_bytes=4 * MIB),
        cost_estimate=cost(2),
    )(*held(params, *raw, space=pltpu.HBM))


PARTS = 4


def prepare_kernel(
    params_in, bed, mask, kind, stress, hydro, bed_v, root, a, b, pay_a, pay_b,
    mask_v, kind_v, ends, params, load_sems, end_sems, params_sem,
):
    rows, cols = bed.shape
    lanes = cols // LANE
    chunk = rows // PARTS
    loads, copies = [], []
    for c in range(PARTS):
        at = pl.ds(c * chunk, chunk)
        loads.append([
            pltpu.make_async_copy(src.at[at], dst.at[at], load_sems.at[f, c])
            for f, (src, dst) in enumerate(((bed, bed_v), (mask, mask_v), (kind, kind_v)))
        ])
    for f, src in enumerate(moving(stress, hydro)):
        for end, start in enumerate((0, rows - SUB)):
            copies.append(pltpu.make_async_copy(src.at[pl.ds(start, SUB)], ends.at[end, f], end_sems.at[f, end]))
    loads[0].append(pltpu.make_async_copy(params_in, params, params_sem))
    for group in loads + [copies]:
        for copy in group:
            copy.start()
    for copy in loads[0]:
        copy.wait()
    tide, flow_in = level_terms(params)
    for c in range(PARTS):
        for copy in loads[c] if c else ():
            copy.wait()
        for i in range(c * chunk // SUB, (c + 1) * chunk // SUB):
            at = tile_at(i)
            root[at, :], a[at, :], b[at, :] = coefficients(bed_v[at, :], mask_v[at, :], kind_v[at, :], tide, flow_in)
    for copy in copies:
        copy.wait()
    low = rows_of((SUB, cols)) < HALO
    odd = lax.axis_index("ty") % 2 == 1

    def edge_rows(f, end):
        if f < 3:
            return (root, a, b)[f][tile_at(0 if end == 0 else rows // SUB - 1), :]
        return ends[end, f - 3]

    for p in range(FIELDS // 2):
        pairs = []
        for end in range(2):
            both = [edge_rows(f, end) for f in (2 * p, 2 * p + 1)]
            both[1 - end] = pltpu.roll(both[1 - end], HALO, 0)
            pairs.append(jnp.where(low, *both))
        for k in range(lanes):
            at, part = pl.ds(k * GROUP + p * SUB, SUB), slice(k * LANE, (k + 1) * LANE)
            top, bottom = pairs[0][:, part], pairs[1][:, part]
            pay_a[at, :] = jnp.where(odd, top, bottom)
            pay_b[at, :] = jnp.where(odd, bottom, top)
    top = fold_row(bed_v[tile_at(0), :])
    bottom = fold_row(pltpu.roll(bed_v[tile_at(rows // SUB - 1), :], 1, 0))
    at = pl.ds(lanes * GROUP + SUB, SUB)
    pay_a[at, :] = jnp.where(odd, top, bottom)
    pay_b[at, :] = jnp.where(odd, bottom, top)


def fold_row(x):
    row = rows_of((SUB, LANE))
    total = x[:, :LANE]
    for k in range(1, x.shape[1] // LANE):
        total = jnp.where(row == k, pltpu.roll(x[:, k * LANE : (k + 1) * LANE], k, 0), total)
    return total


def prepare(params, *raw):
    rows, cols = raw[0].shape
    tile = pltpu.VMEM((rows, cols), jnp.float32)
    return pl.pallas_call(
        prepare_kernel,
        name="prepare",
        out_shape=[tile] * 4 + [pltpu.VMEM((cols // LANE * GROUP + 2 * SUB, LANE), jnp.float32)] * 2,
        in_specs=[ANY] * 6,
        out_specs=[VMEM] * 6,
        scratch_shapes=[
            pltpu.VMEM((rows, cols), jnp.int32),
            pltpu.VMEM((rows, cols), jnp.int32),
            pltpu.VMEM((2, 5, SUB, cols), jnp.float32),
            pltpu.SMEM(params.shape, jnp.float32),
            pltpu.SemaphoreType.DMA((3, PARTS)),
            pltpu.SemaphoreType.DMA((5, 2)),
            pltpu.SemaphoreType.DMA,
        ],
        compiler_params=pltpu.CompilerParams(vmem_limit_bytes=5 * MIB),
        cost_estimate=cost(2),
    )(*held(params, *raw, space=pltpu.HBM))


def corner_kernel(side, in_a, in_b, pay_a, pay_b):
    at = pl.ds(pay_a.shape[0] - 2 * SUB, SUB)
    odd = lax.axis_index("ty") % 2 == 1
    top = side[pl.ds(0, SUB), :]
    bottom = side[pl.ds(side.shape[0] - 2 * SUB, SUB), :]
    pay_a[at, :] = jnp.where(odd, top, bottom)
    pay_b[at, :] = jnp.where(odd, bottom, top)


def add_corners(side, pay_a, pay_b):
    return pl.pallas_call(
        corner_kernel,
        name="add_corners",
        out_shape=[pltpu.VMEM(pay_a.shape, jnp.float32)] * 2,
        in_specs=[VMEM] * 3,
        out_specs=[VMEM] * 2,
        input_output_aliases={1: 0, 2: 1},
        compiler_params=pltpu.CompilerParams(vmem_limit_bytes=MIB),
        cost_estimate=cost(0.1),
    )(*held(side, pay_a, pay_b))


def side_lanes():
    at_left = lax.axis_index("tx") == 0
    drop = jnp.where(at_left, 0, HALO)
    lane = lanes_of((SUB, LANE))
    valid = jnp.where(at_left, lane, LANE - 1 - lane) < HALO
    return lambda strip: pltpu.roll(strip, LANE - drop, 1), valid


def unfold(strip, place):
    return pltpu.roll(strip, (LANE - place * HALO) % LANE, 1) if place else strip


def by_flag(flag, run):
    pl.when(flag)(lambda: run(True))
    pl.when(jnp.logical_not(flag))(lambda: run(False))


class Sweep:
    NAMES = (
        ["fc", "fr", "wc", "wr", "e1", "u1"]
        + ["v1", "e2", "u2", "v2", "qc1", "qr1", "qc2", "qr2"]
    )

    def __init__(self, count, wide, get, emit, weights, params, refs, trim):
        self.count, self.wide, self.get, self.emit, self.trim = count, wide, get, emit, trim
        self.__dict__.update(zip(self.NAMES + ["fr_last", "qr_last"], refs))
        cond = lax.axis_index("cond")
        self.slow = 1.0 - 0.2 * params[0, 1]
        total = weights[0]
        for k in range(1, weights.shape[0]):
            total = total + weights[k]
        ones = jnp.ones((SUB, LANE), jnp.float32)
        share = weights[cond].astype(jnp.float32) * ones / (total.astype(jnp.float32) * ones)
        self.scale = jnp.concatenate([-4.0 * params[0, 2] * share] * (wide // LANE), axis=1)

    @classmethod
    def scratch(cls, count, wide):
        block = pltpu.VMEM(((count + 1) * SUB, wide), jnp.float32)
        return [block] * len(cls.NAMES) + [
            pltpu.VMEM((STEPS, SUB, wide), jnp.float32),
            pltpu.VMEM((SUB, wide), jnp.float32),
        ]

    def speed_r(self, i, level, lower, v, wr):
        return (self.slow * v - (south(level, lower) - level) + self.get(4, i)) * wr

    def move(self, n, i, level, lower, u, v, faces, rest):
        right, down = east(level), south(level, lower)
        yield
        fc, fr, wc, wr = faces()
        u = (self.slow * u() - (right - level) + self.get(3, i)) * wc
        v = (self.slow * v() - (down - level) + self.get(4, i)) * wr
        flux_c = fc * u
        flux_r = fr * v
        left, up = west(flux_c), north(flux_r, self.fr_last[n])
        self.fr_last[n] = flux_r
        more = rest(u, v)
        yield
        out = self.get(1, i) * level + self.get(2, i) - (flux_c - left + flux_r - up)
        return out, more

    def step_one(self, i):
        at = tile_at(i)
        s = self.get(0, i)
        inside = i + 1 < self.count
        level = 0.3 * self.get(5, i)
        lower = 0.3 * self.get(5, i + 1) if inside else level
        right, down = east(s), south(s, self.get(0, i + 1) if inside else s)

        def faces():
            ratios = []
            for face in (s * right, s * down):
                base = face + 0.1
                inverse = pl.reciprocal(base, approx=True)
                ratios.append((0.3 * face, face * (inverse * (2.0 - base * inverse))))
            (fc, wc), (fr, wr) = ratios
            for ref, value in ((self.fc, fc), (self.fr, fr), (self.wc, wc), (self.wr, wr)):
                ref[at, :] = value
            return fc, fr, wc, wr

        def rest(u, v):
            self.u1[at, :] = u
            self.v1[at, :] = v
            self.qc1[at, :] = u * jnp.abs(u)
            self.qr1[at, :] = v * jnp.abs(v)

        out, _ = yield from self.move(
            0, i, level, lower, lambda: self.get(6, i), lambda: self.get(7, i), faces, rest
        )
        self.e1[at, :] = out

    def faces_at(self, at):
        return lambda: [ref[at, :] for ref in (self.fc, self.fr, self.wc, self.wr)]

    def step_two(self, i):
        at, after = tile_at(i), tile_at(i + 1)

        def rest(u, v):
            if not (self.trim and i == self.count - 1):
                self.u2[at, :] = u
                self.v2[at, :] = v
                self.qc2[at, :] = self.qc1[at, :] + u * jnp.abs(u)
                self.qr2[at, :] = self.qr1[at, :] + v * jnp.abs(v)

        out, _ = yield from self.move(
            1, i, self.e1[at, :], self.e1[after, :], lambda: self.u1[at, :], lambda: self.v1[at, :],
            self.faces_at(at), rest,
        )
        self.e2[at, :] = out

    def step_three(self, i):
        at, after = tile_at(i), tile_at(i + 1)
        if self.trim and i == self.count - 1:
            return
        if self.trim and i == 0:
            wr = self.wr[at, :]
            v = self.speed_r(i, self.e2[at, :], self.e2[after, :], self.v2[at, :], wr)
            self.fr_last[2] = self.fr[at, :] * v
            self.qr_last[...] = wr * (self.qr2[at, :] + v * jnp.abs(v))
            return

        def rest(u, v):
            qc = self.wc[at, :] * (self.qc2[at, :] + u * jnp.abs(u))
            qr = self.wr[at, :] * (self.qr2[at, :] + v * jnp.abs(v))
            left, up = west(qc), north(qr, self.qr_last[...])
            self.qr_last[...] = qr
            return u, v, qc, qr, left, up

        out, (u, v, qc, qr, left, up) = yield from self.move(
            2, i, self.e2[at, :], self.e2[after, :], lambda: self.u2[at, :], lambda: self.v2[at, :],
            self.faces_at(at), rest,
        )
        self.emit(i, out * (1.0 / 0.3), u, v, (qc - left + qr - up) * self.scale)

    def run(self):
        self.fr_last[...] = jnp.zeros_like(self.fr_last)
        self.qr_last[...] = jnp.zeros_like(self.qr_last)
        for ref in (self.e1, self.e2):
            ref[tile_at(self.count), :] = jnp.zeros((SUB, self.wide), jnp.float32)
        stages = (self.step_three, self.step_two, self.step_one)
        for t in range(self.count + LAG * (STEPS - 1)):
            turns = []
            for k, stage in enumerate(stages):
                i = t - LAG * (STEPS - 1 - k)
                if 0 <= i < self.count:
                    turns.append(stage(i))
            while turns:
                turns = [turn for turn in turns if next(turn, True) is None]


def reader(root, a, b, stress, hydro, side, side_x):
    rows = root.shape[0]
    span = rows // FOLD // SUB
    fields = [root, a, b] + moving(stress, hydro)
    turn, valid = side_lanes()
    for g in range(span):
        side_x[tile_at(g), :] = turn(side[tile_at(g), :])

    def read(f, block):
        part = unfold(side_x[tile_at(block % span), :], (block // span) * FIELDS + f)
        if f == 0:
            part = jnp.where(valid, part, 0.0)
        return jnp.concatenate([fields[f][tile_at(block), :], part], axis=1)

    return read


def quarter_writer(first, quarter, cols, hydro_out, pay):
    lane = lanes_of((SUB, LANE))
    lanes = cols // LANE
    rims = [jnp.zeros((SUB, LANE), jnp.float32)]

    def emit(i, e, u, v, change):
        at = tile_at(first + i)
        for k, value in enumerate((e, u, v)):
            hydro_out[0, k, at, :] = value[:, :cols]
        g = i - 1
        for k in range(lanes):
            pay[tile_at(k * quarter + g), :] = change[:, k * LANE : (k + 1) * LANE]
        rims[0] = jnp.where(lane // 2 == g, pltpu.roll(change[:, cols:], 1 + 2 * g, 1), rims[0])
        if g == quarter - 1:
            pay[tile_at(lanes * quarter), :] = rims[0]

    return emit


def middle_kernel(own, weights, params, root, a, b, stress, hydro, side, *refs):
    hydro_out, pay, side_x, *refs = refs[1:] if own else refs
    rows, cols = root.shape
    quarter = rows // SUB // 4
    read = reader(root, a, b, stress, hydro, side, side_x)

    def run(lower_half):
        first = (2 * quarter if lower_half else quarter) - 1
        emit = quarter_writer(first, quarter, cols, hydro_out, pay)
        get = lambda f, i: read(f, first + i)
        Sweep(quarter + 2, cols + LANE, get, emit, weights, params, refs, True).run()

    by_flag(lax.axis_index("cond") % 2 == (1 if own else 0), run)


def middle(own, weights, params, fields, side, hydro=None):
    rows, cols = fields[0].shape
    given = (hydro,) if own else ()
    return pl.pallas_call(
        functools.partial(middle_kernel, own),
        name="middle_own" if own else "middle_other",
        out_shape=[
            pltpu.VMEM(fields[4].shape, jnp.float32),
            pltpu.VMEM((cols // LANE * rows // 4 + SUB, LANE), jnp.float32),
        ],
        in_specs=[SMEM, SMEM] + [VMEM] * (6 + own),
        out_specs=[VMEM, VMEM],
        scratch_shapes=[pltpu.VMEM(side.shape, jnp.float32)] + Sweep.scratch(rows // SUB // 4 + 2, cols + LANE),
        input_output_aliases={8: 0} if own else {},
        compiler_params=pltpu.CompilerParams(vmem_limit_bytes=10 * MIB),
        cost_estimate=cost(4),
    )(weights, params, *held(*fields, side, *given))


def edge_kernel(
    own, weights, params, root, a, b, stress, hydro, side, far_a, far_b, hydro_in,
    hydro_out, pay, ends, side_x, *refs,
):
    rows, cols = root.shape
    blocks = rows // SUB
    quarter = blocks // 4
    lanes = cols // LANE
    read = reader(root, a, b, stress, hydro, side, side_x)
    turn, valid = side_lanes()
    ty = lax.axis_index("ty")
    corners = pl.ds(lanes * GROUP, SUB)

    def run(top):
        from_a = ty % 2 == (1 if top else 0)
        first = -1 if top else blocks - quarter - 1
        outside_map = ty == (0 if top else lax.axis_size("ty") - 1)
        inner = quarter if top else blocks - quarter - 1
        corner = turn(jnp.where(from_a, far_a[corners, :], far_b[corners, :]))
        for f in range(FIELDS):
            body = read(f, inner)
            parts = []
            for k in range(lanes):
                at = pl.ds(k * GROUP + f // 2 * SUB, SUB)
                part = jnp.where(from_a, far_a[at, :], far_b[at, :])
                parts.append(pltpu.roll(part, HALO, 0) if top == (f % 2 == 0) else part)
            end = unfold(corner, ((FOLD - 1) * FIELDS if top else 0) + f)
            if f == 0:
                end = jnp.where(valid, end, 0.0)
            outer = jnp.concatenate(parts + [end], axis=1)
            if f == 0:
                outer = jnp.where(outside_map, 0.0, outer)
            ends[0, f], ends[1, f] = (outer, body) if top else (body, outer)

        def get(f, i):
            if i == 0 or i == quarter + 1:
                return ends[0 if i == 0 else 1, f]
            return read(f, first + i)

        emit = quarter_writer(first, quarter, cols, hydro_out, pay)

        def finish(i, e, u, v, change):
            if 1 <= i <= quarter:
                emit(i, e, u, v, change)
            elif i == (0 if top else quarter + 1):
                rim = change[:, :cols]
                pay[tile_at(lanes * quarter + 1), :] = fold_row(pltpu.roll(rim, 1, 0) if top else rim)

        Sweep(quarter + 2, cols + LANE, get, finish, weights, params, refs, False).run()

    by_flag(lax.axis_index("cond") % 2 == (0 if own else 1), run)


def edge(own, weights, params, fields, side, far_a, far_b, hydro):
    rows, cols = fields[0].shape
    wide = cols + LANE
    return pl.pallas_call(
        functools.partial(edge_kernel, own),
        name="edge_own" if own else "edge_other",
        out_shape=[
            pltpu.VMEM(hydro.shape, jnp.float32),
            pltpu.VMEM((cols // LANE * rows // 4 + 2 * SUB, LANE), jnp.float32),
        ],
        in_specs=[SMEM, SMEM] + [VMEM] * 9,
        out_specs=[VMEM, VMEM],
        scratch_shapes=[pltpu.VMEM((2, FIELDS, SUB, wide), jnp.float32), pltpu.VMEM(side.shape, jnp.float32)]
        + Sweep.scratch(rows // SUB // 4 + 2, wide),
        input_output_aliases={10: 0},
        compiler_params=pltpu.CompilerParams(vmem_limit_bytes=12 * MIB),
        cost_estimate=cost(3),
    )(weights, params, *held(*fields, side, far_a, far_b, hydro))


class Update:
    def __init__(self, bed, side, far_a, far_b, own_m, got_m, own_e, got_e, change_v, next_v):
        self.bed, self.side, self.far_a, self.far_b = bed, side, far_a, far_b
        self.parts = {"m": (own_m, got_m), "e": (own_e, got_e)}
        self.change_v, self.next_v = change_v, next_v
        rows, self.cols = bed.shape
        self.blocks = rows // SUB
        self.quarter = self.blocks // 4
        self.lanes = self.cols // LANE
        self.wide = self.cols + LANE
        self.side_bed = side[pl.ds(side.shape[0] - SUB, SUB), :]
        self.drop_bed = jnp.where(lax.axis_index("tx") == 0, 0, 1)
        self.mine = lax.axis_index("cond") % 2
        self.odd = lax.axis_index("ty") % 2 == 1
        col = lanes_of((SUB, self.wide))
        last_c = lax.axis_index("tx") == lax.axis_size("tx") - 1
        first_c = lax.axis_index("tx") == 0
        self.shut_c = (last_c & (col == self.cols - 1)) | (first_c & (col == self.wide - 1))
        self.last_row = rows_of((SUB, self.wide)) == SUB - 1
        self.rims = {}

    def merged(self, q, block):
        own, got = self.parts["e" if q in (0, 3) else "m"]
        at = tile_at(block)
        return jnp.where(self.mine == q // 2, own[at, :], got[at, :])

    def outside(self, q):
        at = pl.ds(self.lanes * GROUP + SUB, SUB)
        a, b = self.far_a[at, :], self.far_b[at, :]
        bed = jnp.where(self.odd, a, b) if q == 0 else jnp.where(self.odd, b, a)
        z = bed + self.merged(q, self.lanes * self.quarter + 1)
        target = SUB - 1 if q == 0 else 0
        parts = [pltpu.roll(z, (SUB + target - k) % SUB, 0) if (target - k) % SUB else z for k in range(self.lanes)]
        return jnp.concatenate(parts + [jnp.zeros((SUB, LANE), jnp.float32)], axis=1)

    def level(self, b, keep):
        if b == -1:
            return self.outside(0)
        if b == self.blocks:
            return self.outside(3)
        q, g = divmod(b, self.quarter)
        change = jnp.concatenate([self.merged(q, k * self.quarter + g) for k in range(self.lanes)], axis=1)
        if keep:
            self.change_v[tile_at(b), :] = change
        if q not in self.rims:
            self.rims[q] = self.merged(q, self.lanes * self.quarter)
        cols_bed = pltpu.roll(self.side_bed, 2 * LANE - self.drop_bed - b, 1)
        cols_change = pltpu.roll(self.rims[q], LANE - 1 - 2 * g, 1)
        return jnp.concatenate([self.bed[tile_at(b), :] + change, cols_bed + cols_change], axis=1)

    def spill(self, slope):
        return 0.25 * (slope - jnp.clip(slope, -1.0, 1.0))

    def south_face(self, z, lower, b):
        out = self.spill(south(z, lower) - z)
        if b == -1:
            return jnp.where((lax.axis_index("ty") == 0) & self.last_row, 0.0, out)
        if b == self.blocks - 1:
            return jnp.where((lax.axis_index("ty") == lax.axis_size("ty") - 1) & self.last_row, 0.0, out)
        return out

    def run(self, first, stop, keep, after=lambda b: None):
        z = self.level(first - 1, keep)
        lower = self.level(first, keep)
        gr = self.south_face(z, lower, first - 1)
        for b in range(first, stop):
            z, lower = lower, self.level(b + 1, keep)
            gr_above, gr = gr, self.south_face(z, lower, b)
            gc = jnp.where(self.shut_c, 0.0, self.spill(east(z) - z))
            out = z + gc - west(gc) + gr - north(gr, gr_above)
            self.next_v[tile_at(b), :] = out[:, : self.cols]
            after(b)


def bed_middle_kernel(
    bed, side, far_a, far_b, own_m, got_m, hydro, bed_next, bed_change, hydro_out, change_v, next_v, sems
):
    rows = bed.shape[0]
    quarter = rows // SUB // 4
    copies = [pltpu.make_async_copy(hydro, hydro_out, sems.at[0])]
    copies[0].start()
    update = Update(bed, side, far_a, far_b, own_m, got_m, None, None, change_v, next_v)
    update.run(quarter + 1, 3 * quarter - 1, True)
    for src, dst, low, high in (
        (change_v, bed_change, quarter, 3 * quarter),
        (next_v, bed_next, quarter + 1, 3 * quarter - 1),
    ):
        at = pl.ds(low * SUB, (high - low) * SUB)
        copies.append(pltpu.make_async_copy(src.at[at], dst.at[at], sems.at[len(copies)]))
        copies[-1].start()
    for copy in copies:
        copy.wait()


def bed_edge_kernel(
    bed, side, far_a, far_b, own_m, got_m, own_e, got_e, next_in, change_in, bed_next, bed_change,
    change_v, next_v, sems,
):
    rows = bed.shape[0]
    blocks = rows // SUB
    quarter = blocks // 4
    update = Update(bed, side, far_a, far_b, own_m, got_m, own_e, got_e, change_v, next_v)
    copies = []

    def send(src, dst, low, high):
        at = pl.ds(low * SUB, (high - low) * SUB)
        copies.append(pltpu.make_async_copy(src.at[at], dst.at[at], sems.at[len(copies)]))
        copies[-1].start()

    update.run(0, quarter + 1, True)
    send(change_v, bed_change, 0, quarter)
    send(next_v, bed_next, 0, quarter + 1)
    update.run(blocks - quarter - 1, blocks, True)
    send(change_v, bed_change, blocks - quarter, blocks)
    send(next_v, bed_next, blocks - quarter - 1, blocks)
    for copy in copies:
        copy.wait()


def bed_scratch(rows, cols):
    return [
        pltpu.VMEM((rows, cols), jnp.float32),
        pltpu.VMEM((rows, cols), jnp.float32),
        pltpu.SemaphoreType.DMA((4,)),
    ]


def bed_middle(bed, side, far_a, far_b, own_m, got_m, hydro):
    return pl.pallas_call(
        bed_middle_kernel,
        name="bed_middle",
        out_shape=[pltpu.HBM(x.shape, jnp.float32) for x in (bed, bed, hydro)],
        in_specs=[VMEM] * 7,
        out_specs=[ANY] * 3,
        scratch_shapes=bed_scratch(*bed.shape),
        compiler_params=pltpu.CompilerParams(vmem_limit_bytes=6 * MIB),
        cost_estimate=cost(4),
    )(*held(bed, side, far_a, far_b, own_m, got_m, hydro))


def bed_edge(bed, side, far_a, far_b, own_m, got_m, own_e, got_e, bed_next, bed_change):
    return pl.pallas_call(
        bed_edge_kernel,
        name="bed_edge",
        out_shape=[pltpu.HBM(bed.shape, jnp.float32)] * 2,
        in_specs=[VMEM] * 8 + [ANY] * 2,
        out_specs=[ANY] * 2,
        scratch_shapes=bed_scratch(*bed.shape),
        input_output_aliases={8: 0, 9: 1},
        compiler_params=pltpu.CompilerParams(vmem_limit_bytes=6 * MIB),
        cost_estimate=cost(2),
    )(
        *held(bed, side, far_a, far_b, own_m, got_m, own_e, got_e),
        *held(bed_next, bed_change, space=pltpu.HBM),
    )


def shards(bed, land_mask, cell_class, weights, cond_params, wave_stress, hydro_state):
    ny = lax.axis_size("ty")
    nc = lax.axis_size("cond")
    raw = (bed, land_mask, cell_class, wave_stress, hydro_state)
    swap = [(i, i ^ 1) for i in range(nc)]

    def pairs(first):
        partner = list(range(ny))
        for i in range(first, ny - 1, 2):
            partner[i], partner[i + 1] = i + 1, i
        return list(enumerate(partner))

    def over_chips(part, beside=()):
        reach = 2
        while reach < nc:
            got = lax.ppermute(part, "cond", [(i, i ^ reach) for i in range(nc)])
            got, beside = lax.optimization_barrier((got, beside))
            part = part + got
            reach = 2 * reach
        return part, beside

    side = lax.ppermute(pack_side(cond_params, *raw), "tx", [(0, 1), (1, 0)])
    bed, *terms, far_a, far_b = prepare(cond_params, *raw)
    fields = (*terms, wave_stress, hydro_state)
    far_a, far_b = add_corners(side, far_a, far_b)
    far_a = lax.ppermute(far_a, "ty", pairs(0))
    hydro, pay = middle(False, weights, cond_params, fields, side)
    hydro, far_a, far_b = lax.optimization_barrier((hydro, far_a, far_b))
    far_b = lax.ppermute(far_b, "ty", pairs(1))
    got = lax.ppermute(pay, "cond", swap)
    hydro, pay = middle(True, weights, cond_params, fields, side, hydro)
    part_m = pay + got
    hydro, part_m = lax.optimization_barrier((hydro, part_m))
    hydro, pay = edge(False, weights, cond_params, fields, side, far_a, far_b, hydro)
    got = lax.ppermute(pay, "cond", swap)
    hydro, pay = edge(True, weights, cond_params, fields, side, far_a, far_b, hydro)
    own_m, hydro = over_chips(part_m, hydro)
    part_e = pay + got
    own_m, _ = lax.optimization_barrier((own_m, part_e))
    got_m = lax.ppermute(own_m, "cond", swap)
    bed_next, bed_change, hydro = bed_middle(bed, side, far_a, far_b, own_m, got_m, hydro)
    own_e, (bed_next, bed_change) = over_chips(part_e, (bed_next, bed_change))
    got_e = lax.ppermute(own_e, "cond", swap)
    bed_next, bed_change = bed_edge(
        bed, side, far_a, far_b, own_m, got_m, own_e, got_e, bed_next, bed_change
    )
    return bed_next, bed_change, hydro


def solution(mesh):
    in_specs = (
        P("ty", "tx"),
        P("ty", "tx"),
        P("ty", "tx"),
        P(),
        P("cond", None),
        P("cond", None, "ty", "tx"),
        P("cond", None, "ty", "tx"),
    )
    out_specs = (P("ty", "tx"), P("ty", "tx"), P("cond", None, "ty", "tx"))
    return jax.shard_map(shards, mesh=mesh, in_specs=in_specs, out_specs=out_specs, check_vma=False)
```

```python
import functools

import jax
import jax.numpy as jnp
from jax import lax
from jax.experimental import pallas as pl
from jax.experimental.pallas import tpu as pltpu
from jax.sharding import PartitionSpec as P

STEPS = 3
HALO = STEPS + 1
SUB = 8
LANE = 128
FIELDS = 8
GROUP = HALO * FIELDS
FOLD = LANE // GROUP
LAG = 2
MIB = 2**20
ANY = pl.BlockSpec(memory_space=pl.ANY)
VMEM = pl.BlockSpec(memory_space=pltpu.VMEM)
SMEM = pl.BlockSpec(memory_space=pltpu.SMEM)


def rows_of(shape):
    return lax.broadcasted_iota(jnp.int32, shape, 0)


def lanes_of(shape):
    return lax.broadcasted_iota(jnp.int32, shape, 1)


def east(x):
    return pltpu.roll(x, x.shape[1] - 1, 1)


def west(x):
    return pltpu.roll(x, 1, 1)


def south(x, below):
    return pltpu.roll(jnp.where(rows_of(x.shape) == 0, below, x), SUB - 1, 0)


def north(x, above):
    return pltpu.roll(jnp.where(rows_of(x.shape) == SUB - 1, above, x), 1, 0)


def tile_at(index):
    if isinstance(index, int):
        return pl.ds(index * SUB, SUB)
    return pl.ds(pl.multiple_of(index * SUB, SUB), SUB)


def held(*arrays, space=pltpu.VMEM):
    return [pltpu.with_memory_space_constraint(x, space) for x in arrays]


def cost(micros):
    return pl.CostEstimate(flops=int(micros * 10**9), bytes_accessed=0, transcendentals=0)


def level_terms(params):
    return params[0, 0] - 1.0, 0.3 * params[0, 3]


def coefficients(bed, mask, kind, tide, flow_in):
    depth = mask.astype(jnp.float32) * (1.0 - 0.5 * jnp.tanh(bed))
    root = depth * lax.rsqrt(jnp.maximum(depth, 1e-12))
    relax = jnp.where(kind == 1, 0.5 * depth, 0.0)
    return root, 1.0 - relax, 0.3 * (relax * tide + jnp.where(kind == 2, flow_in * depth, 0.0))


def moving(stress, hydro):
    return [stress.at[0, k] for k in range(2)] + [hydro.at[0, k] for k in range(3)]


def pack_side_kernel(params_in, bed, mask, kind, stress, hydro, side, reals, ints, params, sems):
    rows, cols = bed.shape
    at_left = lax.axis_index("tx") == 0
    off = pl.multiple_of(jnp.where(at_left, cols - LANE, 0), LANE)
    strips = [reals.at[0], ints.at[0], ints.at[1]] + [reals.at[k] for k in range(1, 6)]
    copies = [
        pltpu.make_async_copy(src.at[:, pl.ds(off, LANE)], strip, sems.at[f])
        for f, (src, strip) in enumerate(zip([bed, mask, kind] + moving(stress, hydro), strips))
    ] + [pltpu.make_async_copy(params_in, params, sems.at[FIELDS])]
    for copy in copies:
        copy.start()
    for copy in copies:
        copy.wait()
    tide, flow_in = level_terms(params)
    lift = jnp.where(at_left, HALO, 0)
    lift_bed = jnp.where(at_left, 1, 0)
    lane = lanes_of((SUB, LANE))
    span = rows // FOLD // SUB
    beds = jnp.zeros((SUB, LANE), jnp.float32)
    for i in range(span):
        total = jnp.zeros((SUB, LANE), jnp.float32)
        for g in range(FOLD):
            at = tile_at(g * span + i)
            first = strips[0][at, :]
            fields = list(coefficients(first, strips[1][at, :], strips[2][at, :], tide, flow_in))
            fields += [strip[at, :] for strip in strips[3:]]
            for f, part in enumerate(fields):
                place = g * FIELDS + f
                total = jnp.where(lane // HALO == place, pltpu.roll(part, lift + place * HALO, 1), total)
            block = g * span + i
            beds = jnp.where(lane == block, pltpu.roll(first, lift_bed + block, 1), beds)
        side[tile_at(i), :] = total
    side[tile_at(span), :] = beds


def pack_side(params, *raw):
    rows, cols = raw[0].shape
    return pl.pallas_call(
        pack_side_kernel,
        name="pack_side",
        out_shape=pltpu.VMEM((rows // FOLD + SUB, LANE), jnp.float32),
        in_specs=[ANY] * 6,
        out_specs=VMEM,
        scratch_shapes=[
            pltpu.VMEM((6, rows, LANE), jnp.float32),
            pltpu.VMEM((2, rows, LANE), jnp.int32),
            pltpu.SMEM(params.shape, jnp.float32),
            pltpu.SemaphoreType.DMA((FIELDS + 1,)),
        ],
        compiler_params=pltpu.CompilerParams(vmem_limit_bytes=4 * MIB),
        cost_estimate=cost(2),
    )(*held(params, *raw, space=pltpu.HBM))


PARTS = 4


def prepare_kernel(
    params_in, bed, mask, kind, stress, hydro, bed_v, root, a, b, pay_a, pay_b,
    mask_v, kind_v, ends, params, load_sems, end_sems, params_sem,
):
    rows, cols = bed.shape
    lanes = cols // LANE
    chunk = rows // PARTS
    loads, copies = [], []
    for c in range(PARTS):
        at = pl.ds(c * chunk, chunk)
        loads.append([
            pltpu.make_async_copy(src.at[at], dst.at[at], load_sems.at[f, c])
            for f, (src, dst) in enumerate(((bed, bed_v), (mask, mask_v), (kind, kind_v)))
        ])
    for f, src in enumerate(moving(stress, hydro)):
        for end, start in enumerate((0, rows - SUB)):
            copies.append(pltpu.make_async_copy(src.at[pl.ds(start, SUB)], ends.at[end, f], end_sems.at[f, end]))
    loads[0].append(pltpu.make_async_copy(params_in, params, params_sem))
    for group in loads + [copies]:
        for copy in group:
            copy.start()
    for copy in loads[0]:
        copy.wait()
    tide, flow_in = level_terms(params)
    for c in range(PARTS):
        for copy in loads[c] if c else ():
            copy.wait()
        for i in range(c * chunk // SUB, (c + 1) * chunk // SUB):
            at = tile_at(i)
            root[at, :], a[at, :], b[at, :] = coefficients(bed_v[at, :], mask_v[at, :], kind_v[at, :], tide, flow_in)
    for copy in copies:
        copy.wait()
    low = rows_of((SUB, cols)) < HALO
    odd = lax.axis_index("ty") % 2 == 1

    def edge_rows(f, end):
        if f < 3:
            return (root, a, b)[f][tile_at(0 if end == 0 else rows // SUB - 1), :]
        return ends[end, f - 3]

    for p in range(FIELDS // 2):
        pairs = []
        for end in range(2):
            both = [edge_rows(f, end) for f in (2 * p, 2 * p + 1)]
            both[1 - end] = pltpu.roll(both[1 - end], HALO, 0)
            pairs.append(jnp.where(low, *both))
        for k in range(lanes):
            at, part = pl.ds(k * GROUP + p * SUB, SUB), slice(k * LANE, (k + 1) * LANE)
            top, bottom = pairs[0][:, part], pairs[1][:, part]
            pay_a[at, :] = jnp.where(odd, top, bottom)
            pay_b[at, :] = jnp.where(odd, bottom, top)
    top = fold_row(bed_v[tile_at(0), :])
    bottom = fold_row(pltpu.roll(bed_v[tile_at(rows // SUB - 1), :], 1, 0))
    at = pl.ds(lanes * GROUP + SUB, SUB)
    pay_a[at, :] = jnp.where(odd, top, bottom)
    pay_b[at, :] = jnp.where(odd, bottom, top)


def fold_row(x):
    row = rows_of((SUB, LANE))
    total = x[:, :LANE]
    for k in range(1, x.shape[1] // LANE):
        total = jnp.where(row == k, pltpu.roll(x[:, k * LANE : (k + 1) * LANE], k, 0), total)
    return total


def prepare(params, *raw):
    rows, cols = raw[0].shape
    tile = pltpu.VMEM((rows, cols), jnp.float32)
    return pl.pallas_call(
        prepare_kernel,
        name="prepare",
        out_shape=[tile] * 4 + [pltpu.VMEM((cols // LANE * GROUP + 2 * SUB, LANE), jnp.float32)] * 2,
        in_specs=[ANY] * 6,
        out_specs=[VMEM] * 6,
        scratch_shapes=[
            pltpu.VMEM((rows, cols), jnp.int32),
            pltpu.VMEM((rows, cols), jnp.int32),
            pltpu.VMEM((2, 5, SUB, cols), jnp.float32),
            pltpu.SMEM(params.shape, jnp.float32),
            pltpu.SemaphoreType.DMA((3, PARTS)),
            pltpu.SemaphoreType.DMA((5, 2)),
            pltpu.SemaphoreType.DMA,
        ],
        compiler_params=pltpu.CompilerParams(vmem_limit_bytes=5 * MIB),
        cost_estimate=cost(2),
    )(*held(params, *raw, space=pltpu.HBM))


def corner_kernel(side, in_a, in_b, pay_a, pay_b):
    at = pl.ds(pay_a.shape[0] - 2 * SUB, SUB)
    odd = lax.axis_index("ty") % 2 == 1
    top = side[pl.ds(0, SUB), :]
    bottom = side[pl.ds(side.shape[0] - 2 * SUB, SUB), :]
    pay_a[at, :] = jnp.where(odd, top, bottom)
    pay_b[at, :] = jnp.where(odd, bottom, top)


def add_corners(side, pay_a, pay_b):
    return pl.pallas_call(
        corner_kernel,
        name="add_corners",
        out_shape=[pltpu.VMEM(pay_a.shape, jnp.float32)] * 2,
        in_specs=[VMEM] * 3,
        out_specs=[VMEM] * 2,
        input_output_aliases={1: 0, 2: 1},
        compiler_params=pltpu.CompilerParams(vmem_limit_bytes=MIB),
        cost_estimate=cost(0.1),
    )(*held(side, pay_a, pay_b))


def side_lanes():
    at_left = lax.axis_index("tx") == 0
    drop = jnp.where(at_left, 0, HALO)
    lane = lanes_of((SUB, LANE))
    valid = jnp.where(at_left, lane, LANE - 1 - lane) < HALO
    return lambda strip: pltpu.roll(strip, LANE - drop, 1), valid


def unfold(strip, place):
    return pltpu.roll(strip, (LANE - place * HALO) % LANE, 1) if place else strip


def by_flag(flag, run):
    pl.when(flag)(lambda: run(True))
    pl.when(jnp.logical_not(flag))(lambda: run(False))


class Sweep:
    NAMES = (
        ["fc", "fr", "wc", "wr", "e1", "u1"]
        + ["v1", "e2", "u2", "v2", "qc1", "qr1", "qc2", "qr2"]
    )

    def __init__(self, count, wide, get, emit, weights, params, refs, trim):
        self.count, self.wide, self.get, self.emit, self.trim = count, wide, get, emit, trim
        self.__dict__.update(zip(self.NAMES + ["fr_last", "qr_last"], refs))
        cond = lax.axis_index("cond")
        self.slow = 1.0 - 0.2 * params[0, 1]
        total = weights[0]
        for k in range(1, weights.shape[0]):
            total = total + weights[k]
        ones = jnp.ones((SUB, LANE), jnp.float32)
        share = weights[cond].astype(jnp.float32) * ones / (total.astype(jnp.float32) * ones)
        self.scale = jnp.concatenate([-4.0 * params[0, 2] * share] * (wide // LANE), axis=1)

    @classmethod
    def scratch(cls, count, wide):
        block = pltpu.VMEM(((count + 1) * SUB, wide), jnp.float32)
        return [block] * len(cls.NAMES) + [
            pltpu.VMEM((STEPS, SUB, wide), jnp.float32),
            pltpu.VMEM((SUB, wide), jnp.float32),
        ]

    def speed_r(self, i, level, lower, v, wr):
        return (self.slow * v - (south(level, lower) - level) + self.get(4, i)) * wr

    def move(self, n, i, level, lower, u, v, faces, rest):
        right, down = east(level), south(level, lower)
        yield
        fc, fr, wc, wr = faces()
        u = (self.slow * u() - (right - level) + self.get(3, i)) * wc
        v = (self.slow * v() - (down - level) + self.get(4, i)) * wr
        flux_c = fc * u
        flux_r = fr * v
        left, up = west(flux_c), north(flux_r, self.fr_last[n])
        self.fr_last[n] = flux_r
        more = rest(u, v)
        yield
        out = self.get(1, i) * level + self.get(2, i) - (flux_c - left + flux_r - up)
        return out, more

    def step_one(self, i):
        at = tile_at(i)
        s = self.get(0, i)
        inside = i + 1 < self.count
        level = 0.3 * self.get(5, i)
        lower = 0.3 * self.get(5, i + 1) if inside else level
        right, down = east(s), south(s, self.get(0, i + 1) if inside else s)

        def faces():
            ratios = []
            for face in (s * right, s * down):
                base = face + 0.1
                inverse = pl.reciprocal(base, approx=True)
                ratios.append((0.3 * face, face * (inverse * (2.0 - base * inverse))))
            (fc, wc), (fr, wr) = ratios
            for ref, value in ((self.fc, fc), (self.fr, fr), (self.wc, wc), (self.wr, wr)):
                ref[at, :] = value
            return fc, fr, wc, wr

        def rest(u, v):
            self.u1[at, :] = u
            self.v1[at, :] = v
            self.qc1[at, :] = u * jnp.abs(u)
            self.qr1[at, :] = v * jnp.abs(v)

        out, _ = yield from self.move(
            0, i, level, lower, lambda: self.get(6, i), lambda: self.get(7, i), faces, rest
        )
        self.e1[at, :] = out

    def faces_at(self, at):
        return lambda: [ref[at, :] for ref in (self.fc, self.fr, self.wc, self.wr)]

    def step_two(self, i):
        at, after = tile_at(i), tile_at(i + 1)

        def rest(u, v):
            if not (self.trim and i == self.count - 1):
                self.u2[at, :] = u
                self.v2[at, :] = v
                self.qc2[at, :] = self.qc1[at, :] + u * jnp.abs(u)
                self.qr2[at, :] = self.qr1[at, :] + v * jnp.abs(v)

        out, _ = yield from self.move(
            1, i, self.e1[at, :], self.e1[after, :], lambda: self.u1[at, :], lambda: self.v1[at, :],
            self.faces_at(at), rest,
        )
        self.e2[at, :] = out

    def step_three(self, i):
        at, after = tile_at(i), tile_at(i + 1)
        if self.trim and i == self.count - 1:
            return
        if self.trim and i == 0:
            wr = self.wr[at, :]
            v = self.speed_r(i, self.e2[at, :], self.e2[after, :], self.v2[at, :], wr)
            self.fr_last[2] = self.fr[at, :] * v
            self.qr_last[...] = wr * (self.qr2[at, :] + v * jnp.abs(v))
            return

        def rest(u, v):
            qc = self.wc[at, :] * (self.qc2[at, :] + u * jnp.abs(u))
            qr = self.wr[at, :] * (self.qr2[at, :] + v * jnp.abs(v))
            left, up = west(qc), north(qr, self.qr_last[...])
            self.qr_last[...] = qr
            return u, v, qc, qr, left, up

        out, (u, v, qc, qr, left, up) = yield from self.move(
            2, i, self.e2[at, :], self.e2[after, :], lambda: self.u2[at, :], lambda: self.v2[at, :],
            self.faces_at(at), rest,
        )
        self.emit(i, out * (1.0 / 0.3), u, v, (qc - left + qr - up) * self.scale)

    def run(self):
        self.fr_last[...] = jnp.zeros_like(self.fr_last)
        self.qr_last[...] = jnp.zeros_like(self.qr_last)
        for ref in (self.e1, self.e2):
            ref[tile_at(self.count), :] = jnp.zeros((SUB, self.wide), jnp.float32)
        stages = (self.step_three, self.step_two, self.step_one)
        for t in range(self.count + LAG * (STEPS - 1)):
            turns = []
            for k, stage in enumerate(stages):
                i = t - LAG * (STEPS - 1 - k)
                if 0 <= i < self.count:
                    turns.append(stage(i))
            while turns:
                turns = [turn for turn in turns if next(turn, True) is None]


def reader(root, a, b, stress, hydro, side, side_x):
    rows = root.shape[0]
    span = rows // FOLD // SUB
    fields = [root, a, b] + moving(stress, hydro)
    turn, valid = side_lanes()
    for g in range(span):
        side_x[tile_at(g), :] = turn(side[tile_at(g), :])

    def read(f, block):
        part = unfold(side_x[tile_at(block % span), :], (block // span) * FIELDS + f)
        if f == 0:
            part = jnp.where(valid, part, 0.0)
        return jnp.concatenate([fields[f][tile_at(block), :], part], axis=1)

    return read


def quarter_writer(first, quarter, cols, hydro_out, pay):
    lane = lanes_of((SUB, LANE))
    lanes = cols // LANE
    rims = [jnp.zeros((SUB, LANE), jnp.float32)]

    def emit(i, e, u, v, change):
        at = tile_at(first + i)
        for k, value in enumerate((e, u, v)):
            hydro_out[0, k, at, :] = value[:, :cols]
        g = i - 1
        for k in range(lanes):
            pay[tile_at(k * quarter + g), :] = change[:, k * LANE : (k + 1) * LANE]
        rims[0] = jnp.where(lane // 2 == g, pltpu.roll(change[:, cols:], 1 + 2 * g, 1), rims[0])
        if g == quarter - 1:
            pay[tile_at(lanes * quarter), :] = rims[0]

    return emit


def middle_kernel(own, weights, params, root, a, b, stress, hydro, side, *refs):
    hydro_out, pay, side_x, *refs = refs[1:] if own else refs
    rows, cols = root.shape
    quarter = rows // SUB // 4
    read = reader(root, a, b, stress, hydro, side, side_x)

    def run(lower_half):
        first = (2 * quarter if lower_half else quarter) - 1
        emit = quarter_writer(first, quarter, cols, hydro_out, pay)
        get = lambda f, i: read(f, first + i)
        Sweep(quarter + 2, cols + LANE, get, emit, weights, params, refs, True).run()

    by_flag(lax.axis_index("cond") % 2 == (1 if own else 0), run)


def middle(own, weights, params, fields, side, hydro=None):
    rows, cols = fields[0].shape
    given = (hydro,) if own else ()
    return pl.pallas_call(
        functools.partial(middle_kernel, own),
        name="middle_own" if own else "middle_other",
        out_shape=[
            pltpu.VMEM(fields[4].shape, jnp.float32),
            pltpu.VMEM((cols // LANE * rows // 4 + SUB, LANE), jnp.float32),
        ],
        in_specs=[SMEM, SMEM] + [VMEM] * (6 + own),
        out_specs=[VMEM, VMEM],
        scratch_shapes=[pltpu.VMEM(side.shape, jnp.float32)] + Sweep.scratch(rows // SUB // 4 + 2, cols + LANE),
        input_output_aliases={8: 0} if own else {},
        compiler_params=pltpu.CompilerParams(vmem_limit_bytes=10 * MIB),
        cost_estimate=cost(4),
    )(weights, params, *held(*fields, side, *given))


def edge_kernel(
    own, weights, params, root, a, b, stress, hydro, side, far_a, far_b, hydro_in,
    hydro_out, pay, ends, side_x, *refs,
):
    rows, cols = root.shape
    blocks = rows // SUB
    quarter = blocks // 4
    lanes = cols // LANE
    read = reader(root, a, b, stress, hydro, side, side_x)
    turn, valid = side_lanes()
    ty = lax.axis_index("ty")
    corners = pl.ds(lanes * GROUP, SUB)

    def run(top):
        from_a = ty % 2 == (1 if top else 0)
        first = -1 if top else blocks - quarter - 1
        outside_map = ty == (0 if top else lax.axis_size("ty") - 1)
        inner = quarter if top else blocks - quarter - 1
        corner = turn(jnp.where(from_a, far_a[corners, :], far_b[corners, :]))
        for f in range(FIELDS):
            body = read(f, inner)
            parts = []
            for k in range(lanes):
                at = pl.ds(k * GROUP + f // 2 * SUB, SUB)
                part = jnp.where(from_a, far_a[at, :], far_b[at, :])
                parts.append(pltpu.roll(part, HALO, 0) if top == (f % 2 == 0) else part)
            end = unfold(corner, ((FOLD - 1) * FIELDS if top else 0) + f)
            if f == 0:
                end = jnp.where(valid, end, 0.0)
            outer = jnp.concatenate(parts + [end], axis=1)
            if f == 0:
                outer = jnp.where(outside_map, 0.0, outer)
            ends[0, f], ends[1, f] = (outer, body) if top else (body, outer)

        def get(f, i):
            if i == 0 or i == quarter + 1:
                return ends[0 if i == 0 else 1, f]
            return read(f, first + i)

        emit = quarter_writer(first, quarter, cols, hydro_out, pay)

        def finish(i, e, u, v, change):
            if 1 <= i <= quarter:
                emit(i, e, u, v, change)
            elif i == (0 if top else quarter + 1):
                rim = change[:, :cols]
                pay[tile_at(lanes * quarter + 1), :] = fold_row(pltpu.roll(rim, 1, 0) if top else rim)

        Sweep(quarter + 2, cols + LANE, get, finish, weights, params, refs, False).run()

    by_flag(lax.axis_index("cond") % 2 == (0 if own else 1), run)


def edge(own, weights, params, fields, side, far_a, far_b, hydro):
    rows, cols = fields[0].shape
    wide = cols + LANE
    return pl.pallas_call(
        functools.partial(edge_kernel, own),
        name="edge_own" if own else "edge_other",
        out_shape=[
            pltpu.VMEM(hydro.shape, jnp.float32),
            pltpu.VMEM((cols // LANE * rows // 4 + 2 * SUB, LANE), jnp.float32),
        ],
        in_specs=[SMEM, SMEM] + [VMEM] * 9,
        out_specs=[VMEM, VMEM],
        scratch_shapes=[pltpu.VMEM((2, FIELDS, SUB, wide), jnp.float32), pltpu.VMEM(side.shape, jnp.float32)]
        + Sweep.scratch(rows // SUB // 4 + 2, wide),
        input_output_aliases={10: 0},
        compiler_params=pltpu.CompilerParams(vmem_limit_bytes=12 * MIB),
        cost_estimate=cost(3),
    )(weights, params, *held(*fields, side, far_a, far_b, hydro))


class Update:
    def __init__(self, bed, side, far_a, far_b, own_m, got_m, own_e, got_e, change_v, next_v):
        self.bed, self.side, self.far_a, self.far_b = bed, side, far_a, far_b
        self.parts = {"m": (own_m, got_m), "e": (own_e, got_e)}
        self.change_v, self.next_v = change_v, next_v
        rows, self.cols = bed.shape
        self.blocks = rows // SUB
        self.quarter = self.blocks // 4
        self.lanes = self.cols // LANE
        self.wide = self.cols + LANE
        self.side_bed = side[pl.ds(side.shape[0] - SUB, SUB), :]
        self.drop_bed = jnp.where(lax.axis_index("tx") == 0, 0, 1)
        self.mine = lax.axis_index("cond") % 2
        self.odd = lax.axis_index("ty") % 2 == 1
        col = lanes_of((SUB, self.wide))
        last_c = lax.axis_index("tx") == lax.axis_size("tx") - 1
        first_c = lax.axis_index("tx") == 0
        self.shut_c = (last_c & (col == self.cols - 1)) | (first_c & (col == self.wide - 1))
        self.last_row = rows_of((SUB, self.wide)) == SUB - 1
        self.rims = {}

    def merged(self, q, block):
        own, got = self.parts["e" if q in (0, 3) else "m"]
        at = tile_at(block)
        return jnp.where(self.mine == q // 2, own[at, :], got[at, :])

    def outside(self, q):
        at = pl.ds(self.lanes * GROUP + SUB, SUB)
        a, b = self.far_a[at, :], self.far_b[at, :]
        bed = jnp.where(self.odd, a, b) if q == 0 else jnp.where(self.odd, b, a)
        z = bed + self.merged(q, self.lanes * self.quarter + 1)
        target = SUB - 1 if q == 0 else 0
        parts = [pltpu.roll(z, (SUB + target - k) % SUB, 0) if (target - k) % SUB else z for k in range(self.lanes)]
        return jnp.concatenate(parts + [jnp.zeros((SUB, LANE), jnp.float32)], axis=1)

    def level(self, b, keep):
        if b == -1:
            return self.outside(0)
        if b == self.blocks:
            return self.outside(3)
        q, g = divmod(b, self.quarter)
        change = jnp.concatenate([self.merged(q, k * self.quarter + g) for k in range(self.lanes)], axis=1)
        if keep:
            self.change_v[tile_at(b), :] = change
        if q not in self.rims:
            self.rims[q] = self.merged(q, self.lanes * self.quarter)
        cols_bed = pltpu.roll(self.side_bed, 2 * LANE - self.drop_bed - b, 1)
        cols_change = pltpu.roll(self.rims[q], LANE - 1 - 2 * g, 1)
        return jnp.concatenate([self.bed[tile_at(b), :] + change, cols_bed + cols_change], axis=1)

    def spill(self, slope):
        return 0.25 * (slope - jnp.clip(slope, -1.0, 1.0))

    def south_face(self, z, lower, b):
        out = self.spill(south(z, lower) - z)
        if b == -1:
            return jnp.where((lax.axis_index("ty") == 0) & self.last_row, 0.0, out)
        if b == self.blocks - 1:
            return jnp.where((lax.axis_index("ty") == lax.axis_size("ty") - 1) & self.last_row, 0.0, out)
        return out

    def run(self, first, stop, keep, after=lambda b: None):
        z = self.level(first - 1, keep)
        lower = self.level(first, keep)
        gr = self.south_face(z, lower, first - 1)
        for b in range(first, stop):
            z, lower = lower, self.level(b + 1, keep)
            gr_above, gr = gr, self.south_face(z, lower, b)
            gc = jnp.where(self.shut_c, 0.0, self.spill(east(z) - z))
            out = z + gc - west(gc) + gr - north(gr, gr_above)
            self.next_v[tile_at(b), :] = out[:, : self.cols]
            after(b)


def bed_middle_kernel(
    bed, side, far_a, far_b, own_m, got_m, hydro, bed_next, bed_change, hydro_out, change_v, next_v, sems
):
    rows = bed.shape[0]
    quarter = rows // SUB // 4
    copies = [pltpu.make_async_copy(hydro, hydro_out, sems.at[0])]
    copies[0].start()
    update = Update(bed, side, far_a, far_b, own_m, got_m, None, None, change_v, next_v)
    update.run(quarter + 1, 3 * quarter - 1, True)
    for src, dst, low, high in (
        (change_v, bed_change, quarter, 3 * quarter),
        (next_v, bed_next, quarter + 1, 3 * quarter - 1),
    ):
        at = pl.ds(low * SUB, (high - low) * SUB)
        copies.append(pltpu.make_async_copy(src.at[at], dst.at[at], sems.at[len(copies)]))
        copies[-1].start()
    for copy in copies:
        copy.wait()


def bed_edge_kernel(
    own, bed, side, far_a, far_b, own_m, got_m, part_e, next_in, change_in, bed_next, bed_change,
    change_v, next_v, sems,
):
    blocks = bed.shape[0] // SUB
    quarter = blocks // 4
    update = Update(bed, side, far_a, far_b, own_m, got_m, part_e, part_e, change_v, next_v)

    def run(top):
        rows = (0, quarter + 1) if top else (blocks - quarter - 1, blocks)
        changes = (0, quarter) if top else (blocks - quarter, blocks)
        update.run(*rows, True)
        copies = []
        for n, (src, dst, (low, high)) in enumerate(((change_v, bed_change, changes), (next_v, bed_next, rows))):
            at = pl.ds(low * SUB, (high - low) * SUB)
            copies.append(pltpu.make_async_copy(src.at[at], dst.at[at], sems.at[n]))
            copies[-1].start()
        for copy in copies:
            copy.wait()

    by_flag(lax.axis_index("cond") % 2 == (0 if own else 1), run)


def bed_scratch(rows, cols):
    return [
        pltpu.VMEM((rows, cols), jnp.float32),
        pltpu.VMEM((rows, cols), jnp.float32),
        pltpu.SemaphoreType.DMA((4,)),
    ]


def bed_middle(bed, side, far_a, far_b, own_m, got_m, hydro):
    return pl.pallas_call(
        bed_middle_kernel,
        name="bed_middle",
        out_shape=[pltpu.HBM(x.shape, jnp.float32) for x in (bed, bed, hydro)],
        in_specs=[VMEM] * 7,
        out_specs=[ANY] * 3,
        scratch_shapes=bed_scratch(*bed.shape),
        compiler_params=pltpu.CompilerParams(vmem_limit_bytes=6 * MIB),
        cost_estimate=cost(4),
    )(*held(bed, side, far_a, far_b, own_m, got_m, hydro))


def bed_edge(own, bed, side, far_a, far_b, own_m, got_m, part_e, bed_next, bed_change):
    return pl.pallas_call(
        functools.partial(bed_edge_kernel, own),
        name="bed_own" if own else "bed_other",
        out_shape=[pltpu.HBM(bed.shape, jnp.float32)] * 2,
        in_specs=[VMEM] * 7 + [ANY] * 2,
        out_specs=[ANY] * 2,
        scratch_shapes=bed_scratch(*bed.shape),
        input_output_aliases={7: 0, 8: 1},
        compiler_params=pltpu.CompilerParams(vmem_limit_bytes=6 * MIB),
        cost_estimate=cost(3),
    )(
        *held(bed, side, far_a, far_b, own_m, got_m, part_e),
        *held(bed_next, bed_change, space=pltpu.HBM),
    )


def shards(bed, land_mask, cell_class, weights, cond_params, wave_stress, hydro_state):
    ny = lax.axis_size("ty")
    nc = lax.axis_size("cond")
    raw = (bed, land_mask, cell_class, wave_stress, hydro_state)
    swap = [(i, i ^ 1) for i in range(nc)]

    def pairs(first):
        partner = list(range(ny))
        for i in range(first, ny - 1, 2):
            partner[i], partner[i + 1] = i + 1, i
        return list(enumerate(partner))

    def over_chips(part, beside=()):
        reach = 2
        while reach < nc:
            got = lax.ppermute(part, "cond", [(i, i ^ reach) for i in range(nc)])
            got, beside = lax.optimization_barrier((got, beside))
            part = part + got
            reach = 2 * reach
        return part, beside

    side = lax.ppermute(pack_side(cond_params, *raw), "tx", [(0, 1), (1, 0)])
    bed, *terms, far_a, far_b = prepare(cond_params, *raw)
    fields = (*terms, wave_stress, hydro_state)
    far_a, far_b = add_corners(side, far_a, far_b)
    far_a = lax.ppermute(far_a, "ty", pairs(0))
    hydro, pay = middle(False, weights, cond_params, fields, side)
    hydro, far_a, far_b = lax.optimization_barrier((hydro, far_a, far_b))
    far_b = lax.ppermute(far_b, "ty", pairs(1))
    got = lax.ppermute(pay, "cond", swap)
    hydro, pay = middle(True, weights, cond_params, fields, side, hydro)
    part_m = pay + got
    hydro, part_m = lax.optimization_barrier((hydro, part_m))
    hydro, pay = edge(False, weights, cond_params, fields, side, far_a, far_b, hydro)
    got = lax.ppermute(pay, "cond", swap)
    hydro, pay = edge(True, weights, cond_params, fields, side, far_a, far_b, hydro)
    own_m, hydro = over_chips(part_m, hydro)
    part_e = pay + got
    own_m, _ = lax.optimization_barrier((own_m, part_e))
    got_m = lax.ppermute(own_m, "cond", swap)
    bed_next, bed_change, hydro = bed_middle(bed, side, far_a, far_b, own_m, got_m, hydro)
    own_e, (bed_next, bed_change) = over_chips(part_e, (bed_next, bed_change))
    got_e = lax.ppermute(own_e, "cond", swap)
    given = (bed, side, far_a, far_b, own_m, got_m)
    bed_next, bed_change = bed_edge(True, *given, own_e, bed_next, bed_change)
    bed_next, bed_change = bed_edge(False, *given, got_e, bed_next, bed_change)
    return bed_next, bed_change, hydro


def solution(mesh):
    in_specs = (
        P("ty", "tx"),
        P("ty", "tx"),
        P("ty", "tx"),
        P(),
        P("cond", None),
        P("cond", None, "ty", "tx"),
        P("cond", None, "ty", "tx"),
    )
    out_specs = (P("ty", "tx"), P("ty", "tx"), P("cond", None, "ty", "tx"))
    return jax.shard_map(shards, mesh=mesh, in_specs=in_specs, out_specs=out_specs, check_vma=False)
```

```python
import functools

import jax
import jax.numpy as jnp
from jax import lax
from jax.experimental import pallas as pl
from jax.experimental.pallas import tpu as pltpu
from jax.sharding import PartitionSpec as P

STEPS = 3
HALO = STEPS + 1
SUB = 8
LANE = 128
FIELDS = 8
GROUP = HALO * FIELDS
FOLD = LANE // GROUP
LAG = 2
MIB = 2**20
ANY = pl.BlockSpec(memory_space=pl.ANY)
VMEM = pl.BlockSpec(memory_space=pltpu.VMEM)
SMEM = pl.BlockSpec(memory_space=pltpu.SMEM)


def rows_of(shape):
    return lax.broadcasted_iota(jnp.int32, shape, 0)


def lanes_of(shape):
    return lax.broadcasted_iota(jnp.int32, shape, 1)


def east(x):
    return pltpu.roll(x, x.shape[1] - 1, 1)


def west(x):
    return pltpu.roll(x, 1, 1)


def south(x, below):
    return pltpu.roll(jnp.where(rows_of(x.shape) == 0, below, x), SUB - 1, 0)


def north(x, above):
    return pltpu.roll(jnp.where(rows_of(x.shape) == SUB - 1, above, x), 1, 0)


def tile_at(index):
    if isinstance(index, int):
        return pl.ds(index * SUB, SUB)
    return pl.ds(pl.multiple_of(index * SUB, SUB), SUB)


def held(*arrays, space=pltpu.VMEM):
    return [pltpu.with_memory_space_constraint(x, space) for x in arrays]


def cost(micros):
    return pl.CostEstimate(flops=int(micros * 10**9), bytes_accessed=0, transcendentals=0)


def level_terms(params):
    return params[0, 0] - 1.0, 0.3 * params[0, 3]


def coefficients(bed, mask, kind, tide, flow_in):
    depth = mask.astype(jnp.float32) * (1.0 - 0.5 * jnp.tanh(bed))
    root = depth * lax.rsqrt(jnp.maximum(depth, 1e-12))
    relax = jnp.where(kind == 1, 0.5 * depth, 0.0)
    return root, 1.0 - relax, 0.3 * (relax * tide + jnp.where(kind == 2, flow_in * depth, 0.0))


def moving(stress, hydro):
    return [stress.at[0, k] for k in range(2)] + [hydro.at[0, k] for k in range(3)]


def pack_side_kernel(params_in, bed, mask, kind, stress, hydro, side, reals, ints, params, sems):
    rows, cols = bed.shape
    at_left = lax.axis_index("tx") == 0
    off = pl.multiple_of(jnp.where(at_left, cols - LANE, 0), LANE)
    strips = [reals.at[0], ints.at[0], ints.at[1]] + [reals.at[k] for k in range(1, 6)]
    copies = [
        pltpu.make_async_copy(src.at[:, pl.ds(off, LANE)], strip, sems.at[f])
        for f, (src, strip) in enumerate(zip([bed, mask, kind] + moving(stress, hydro), strips))
    ] + [pltpu.make_async_copy(params_in, params, sems.at[FIELDS])]
    for copy in copies:
        copy.start()
    for copy in copies:
        copy.wait()
    tide, flow_in = level_terms(params)
    lift = jnp.where(at_left, HALO, 0)
    lift_bed = jnp.where(at_left, 1, 0)
    lane = lanes_of((SUB, LANE))
    span = rows // FOLD // SUB
    beds = jnp.zeros((SUB, LANE), jnp.float32)
    for i in range(span):
        total = jnp.zeros((SUB, LANE), jnp.float32)
        for g in range(FOLD):
            at = tile_at(g * span + i)
            first = strips[0][at, :]
            fields = list(coefficients(first, strips[1][at, :], strips[2][at, :], tide, flow_in))
            fields += [strip[at, :] for strip in strips[3:]]
            for f, part in enumerate(fields):
                place = g * FIELDS + f
                total = jnp.where(lane // HALO == place, pltpu.roll(part, lift + place * HALO, 1), total)
            block = g * span + i
            beds = jnp.where(lane == block, pltpu.roll(first, lift_bed + block, 1), beds)
        side[tile_at(i), :] = total
    side[tile_at(span), :] = beds


def pack_side(params, *raw):
    rows, cols = raw[0].shape
    return pl.pallas_call(
        pack_side_kernel,
        name="pack_side",
        out_shape=pltpu.VMEM((rows // FOLD + SUB, LANE), jnp.float32),
        in_specs=[ANY] * 6,
        out_specs=VMEM,
        scratch_shapes=[
            pltpu.VMEM((6, rows, LANE), jnp.float32),
            pltpu.VMEM((2, rows, LANE), jnp.int32),
            pltpu.SMEM(params.shape, jnp.float32),
            pltpu.SemaphoreType.DMA((FIELDS + 1,)),
        ],
        compiler_params=pltpu.CompilerParams(vmem_limit_bytes=4 * MIB),
        cost_estimate=cost(2),
    )(*held(params, *raw, space=pltpu.HBM))


PARTS = 4


def prepare_kernel(
    params_in, bed, mask, kind, stress, hydro, bed_v, root, a, b, pay_a, pay_b,
    mask_v, kind_v, ends, params, load_sems, end_sems, params_sem,
):
    rows, cols = bed.shape
    lanes = cols // LANE
    chunk = rows // PARTS
    loads, copies = [], []
    for c in range(PARTS):
        at = pl.ds(c * chunk, chunk)
        loads.append([
            pltpu.make_async_copy(src.at[at], dst.at[at], load_sems.at[f, c])
            for f, (src, dst) in enumerate(((bed, bed_v), (mask, mask_v), (kind, kind_v)))
        ])
    for f, src in enumerate(moving(stress, hydro)):
        for end, start in enumerate((0, rows - SUB)):
            copies.append(pltpu.make_async_copy(src.at[pl.ds(start, SUB)], ends.at[end, f], end_sems.at[f, end]))
    loads[0].append(pltpu.make_async_copy(params_in, params, params_sem))
    for group in loads + [copies]:
        for copy in group:
            copy.start()
    for copy in loads[0]:
        copy.wait()
    tide, flow_in = level_terms(params)
    for c in range(PARTS):
        for copy in loads[c] if c else ():
            copy.wait()
        for i in range(c * chunk // SUB, (c + 1) * chunk // SUB):
            at = tile_at(i)
            root[at, :], a[at, :], b[at, :] = coefficients(bed_v[at, :], mask_v[at, :], kind_v[at, :], tide, flow_in)
    for copy in copies:
        copy.wait()
    low = rows_of((SUB, cols)) < HALO
    odd = lax.axis_index("ty") % 2 == 1

    def edge_rows(f, end):
        if f < 3:
            return (root, a, b)[f][tile_at(0 if end == 0 else rows // SUB - 1), :]
        return ends[end, f - 3]

    for p in range(FIELDS // 2):
        pairs = []
        for end in range(2):
            both = [edge_rows(f, end) for f in (2 * p, 2 * p + 1)]
            both[1 - end] = pltpu.roll(both[1 - end], HALO, 0)
            pairs.append(jnp.where(low, *both))
        for k in range(lanes):
            at, part = pl.ds(k * GROUP + p * SUB, SUB), slice(k * LANE, (k + 1) * LANE)
            top, bottom = pairs[0][:, part], pairs[1][:, part]
            pay_a[at, :] = jnp.where(odd, top, bottom)
            pay_b[at, :] = jnp.where(odd, bottom, top)
    top = fold_row(bed_v[tile_at(0), :])
    bottom = fold_row(pltpu.roll(bed_v[tile_at(rows // SUB - 1), :], 1, 0))
    at = pl.ds(lanes * GROUP + SUB, SUB)
    pay_a[at, :] = jnp.where(odd, top, bottom)
    pay_b[at, :] = jnp.where(odd, bottom, top)


def fold_row(x):
    row = rows_of((SUB, LANE))
    total = x[:, :LANE]
    for k in range(1, x.shape[1] // LANE):
        total = jnp.where(row == k, pltpu.roll(x[:, k * LANE : (k + 1) * LANE], k, 0), total)
    return total


def prepare(params, *raw):
    rows, cols = raw[0].shape
    tile = pltpu.VMEM((rows, cols), jnp.float32)
    return pl.pallas_call(
        prepare_kernel,
        name="prepare",
        out_shape=[tile] * 4 + [pltpu.VMEM((cols // LANE * GROUP + 2 * SUB, LANE), jnp.float32)] * 2,
        in_specs=[ANY] * 6,
        out_specs=[VMEM] * 6,
        scratch_shapes=[
            pltpu.VMEM((rows, cols), jnp.int32),
            pltpu.VMEM((rows, cols), jnp.int32),
            pltpu.VMEM((2, 5, SUB, cols), jnp.float32),
            pltpu.SMEM(params.shape, jnp.float32),
            pltpu.SemaphoreType.DMA((3, PARTS)),
            pltpu.SemaphoreType.DMA((5, 2)),
            pltpu.SemaphoreType.DMA,
        ],
        compiler_params=pltpu.CompilerParams(vmem_limit_bytes=5 * MIB),
        cost_estimate=cost(2),
    )(*held(params, *raw, space=pltpu.HBM))


def corner_kernel(side, in_a, in_b, pay_a, pay_b):
    at = pl.ds(pay_a.shape[0] - 2 * SUB, SUB)
    odd = lax.axis_index("ty") % 2 == 1
    top = side[pl.ds(0, SUB), :]
    bottom = side[pl.ds(side.shape[0] - 2 * SUB, SUB), :]
    pay_a[at, :] = jnp.where(odd, top, bottom)
    pay_b[at, :] = jnp.where(odd, bottom, top)


def add_corners(side, pay_a, pay_b):
    return pl.pallas_call(
        corner_kernel,
        name="add_corners",
        out_shape=[pltpu.VMEM(pay_a.shape, jnp.float32)] * 2,
        in_specs=[VMEM] * 3,
        out_specs=[VMEM] * 2,
        input_output_aliases={1: 0, 2: 1},
        compiler_params=pltpu.CompilerParams(vmem_limit_bytes=MIB),
        cost_estimate=cost(0.1),
    )(*held(side, pay_a, pay_b))


def side_lanes():
    at_left = lax.axis_index("tx") == 0
    drop = jnp.where(at_left, 0, HALO)
    lane = lanes_of((SUB, LANE))
    valid = jnp.where(at_left, lane, LANE - 1 - lane) < HALO
    return lambda strip: pltpu.roll(strip, LANE - drop, 1), valid


def unfold(strip, place):
    return pltpu.roll(strip, (LANE - place * HALO) % LANE, 1) if place else strip


def by_flag(flag, run):
    pl.when(flag)(lambda: run(True))
    pl.when(jnp.logical_not(flag))(lambda: run(False))


class Sweep:
    NAMES = (
        ["fc", "fr", "wc", "wr", "e1", "u1"]
        + ["v1", "e2", "u2", "v2", "qc1", "qr1", "qc2", "qr2"]
    )

    def __init__(self, count, wide, get, emit, weights, params, refs, trim_first, trim_last):
        self.count, self.wide, self.get, self.emit = count, wide, get, emit
        self.trim_first, self.trim_last = trim_first, trim_last
        self.__dict__.update(zip(self.NAMES + ["fr_last", "qr_last"], refs))
        cond = lax.axis_index("cond")
        self.slow = 1.0 - 0.2 * params[0, 1]
        total = weights[0]
        for k in range(1, weights.shape[0]):
            total = total + weights[k]
        ones = jnp.ones((SUB, LANE), jnp.float32)
        share = weights[cond].astype(jnp.float32) * ones / (total.astype(jnp.float32) * ones)
        self.scale = jnp.concatenate([-4.0 * params[0, 2] * share] * (wide // LANE), axis=1)

    @classmethod
    def scratch(cls, count, wide):
        block = pltpu.VMEM(((count + 1) * SUB, wide), jnp.float32)
        return [block] * len(cls.NAMES) + [
            pltpu.VMEM((STEPS, SUB, wide), jnp.float32),
            pltpu.VMEM((SUB, wide), jnp.float32),
        ]

    def speed_r(self, i, level, lower, v, wr):
        return (self.slow * v - (south(level, lower) - level) + self.get(4, i)) * wr

    def move(self, n, i, level, lower, u, v, faces, rest):
        right, down = east(level), south(level, lower)
        yield
        fc, fr, wc, wr = faces()
        u = (self.slow * u() - (right - level) + self.get(3, i)) * wc
        v = (self.slow * v() - (down - level) + self.get(4, i)) * wr
        flux_c = fc * u
        flux_r = fr * v
        left, up = west(flux_c), north(flux_r, self.fr_last[n])
        self.fr_last[n] = flux_r
        more = rest(u, v)
        yield
        out = self.get(1, i) * level + self.get(2, i) - (flux_c - left + flux_r - up)
        return out, more

    def step_one(self, i):
        at = tile_at(i)
        s = self.get(0, i)
        inside = i + 1 < self.count
        level = 0.3 * self.get(5, i)
        lower = 0.3 * self.get(5, i + 1) if inside else level
        right, down = east(s), south(s, self.get(0, i + 1) if inside else s)

        def faces():
            ratios = []
            for face in (s * right, s * down):
                base = face + 0.1
                inverse = pl.reciprocal(base, approx=True)
                ratios.append((0.3 * face, face * (inverse * (2.0 - base * inverse))))
            (fc, wc), (fr, wr) = ratios
            for ref, value in ((self.fc, fc), (self.fr, fr), (self.wc, wc), (self.wr, wr)):
                ref[at, :] = value
            return fc, fr, wc, wr

        def rest(u, v):
            self.u1[at, :] = u
            self.v1[at, :] = v
            self.qc1[at, :] = u * jnp.abs(u)
            self.qr1[at, :] = v * jnp.abs(v)

        out, _ = yield from self.move(
            0, i, level, lower, lambda: self.get(6, i), lambda: self.get(7, i), faces, rest
        )
        self.e1[at, :] = out

    def faces_at(self, at):
        return lambda: [ref[at, :] for ref in (self.fc, self.fr, self.wc, self.wr)]

    def step_two(self, i):
        at, after = tile_at(i), tile_at(i + 1)

        def rest(u, v):
            if not (self.trim_last and i == self.count - 1):
                self.u2[at, :] = u
                self.v2[at, :] = v
                self.qc2[at, :] = self.qc1[at, :] + u * jnp.abs(u)
                self.qr2[at, :] = self.qr1[at, :] + v * jnp.abs(v)

        out, _ = yield from self.move(
            1, i, self.e1[at, :], self.e1[after, :], lambda: self.u1[at, :], lambda: self.v1[at, :],
            self.faces_at(at), rest,
        )
        self.e2[at, :] = out

    def step_three(self, i):
        at, after = tile_at(i), tile_at(i + 1)
        if self.trim_last and i == self.count - 1:
            return
        if self.trim_first and i == 0:
            wr = self.wr[at, :]
            v = self.speed_r(i, self.e2[at, :], self.e2[after, :], self.v2[at, :], wr)
            self.fr_last[2] = self.fr[at, :] * v
            self.qr_last[...] = wr * (self.qr2[at, :] + v * jnp.abs(v))
            return

        def rest(u, v):
            qc = self.wc[at, :] * (self.qc2[at, :] + u * jnp.abs(u))
            qr = self.wr[at, :] * (self.qr2[at, :] + v * jnp.abs(v))
            left, up = west(qc), north(qr, self.qr_last[...])
            self.qr_last[...] = qr
            return u, v, qc, qr, left, up

        out, (u, v, qc, qr, left, up) = yield from self.move(
            2, i, self.e2[at, :], self.e2[after, :], lambda: self.u2[at, :], lambda: self.v2[at, :],
            self.faces_at(at), rest,
        )
        self.emit(i, out * (1.0 / 0.3), u, v, (qc - left + qr - up) * self.scale)

    def run(self):
        self.fr_last[...] = jnp.zeros_like(self.fr_last)
        self.qr_last[...] = jnp.zeros_like(self.qr_last)
        for ref in (self.e1, self.e2):
            ref[tile_at(self.count), :] = jnp.zeros((SUB, self.wide), jnp.float32)
        stages = (self.step_three, self.step_two, self.step_one)
        for t in range(self.count + LAG * (STEPS - 1)):
            turns = []
            for k, stage in enumerate(stages):
                i = t - LAG * (STEPS - 1 - k)
                if 0 <= i < self.count:
                    turns.append(stage(i))
            while turns:
                turns = [turn for turn in turns if next(turn, True) is None]


def reader(root, a, b, stress, hydro, side, side_x):
    rows = root.shape[0]
    span = rows // FOLD // SUB
    fields = [root, a, b] + moving(stress, hydro)
    turn, valid = side_lanes()
    for g in range(span):
        side_x[tile_at(g), :] = turn(side[tile_at(g), :])

    def read(f, block):
        part = unfold(side_x[tile_at(block % span), :], (block // span) * FIELDS + f)
        if f == 0:
            part = jnp.where(valid, part, 0.0)
        return jnp.concatenate([fields[f][tile_at(block), :], part], axis=1)

    return read


def quarter_writer(first, quarter, cols, hydro_out, pay):
    lane = lanes_of((SUB, LANE))
    lanes = cols // LANE
    rims = [jnp.zeros((SUB, LANE), jnp.float32)]

    def emit(i, e, u, v, change):
        at = tile_at(first + i)
        for k, value in enumerate((e, u, v)):
            hydro_out[0, k, at, :] = value[:, :cols]
        g = i - 1
        for k in range(lanes):
            pay[tile_at(k * quarter + g), :] = change[:, k * LANE : (k + 1) * LANE]
        rims[0] = jnp.where(lane // 2 == g, pltpu.roll(change[:, cols:], 1 + 2 * g, 1), rims[0])
        if g == quarter - 1:
            pay[tile_at(lanes * quarter), :] = rims[0]

    return emit


def middle_kernel(own, weights, params, root, a, b, stress, hydro, side, *refs):
    hydro_out, pay, side_x, *refs = refs[1:] if own else refs
    rows, cols = root.shape
    quarter = rows // SUB // 4
    read = reader(root, a, b, stress, hydro, side, side_x)

    def run(lower_half):
        first = (2 * quarter if lower_half else quarter) - 1
        emit = quarter_writer(first, quarter, cols, hydro_out, pay)
        get = lambda f, i: read(f, first + i)
        Sweep(quarter + 2, cols + LANE, get, emit, weights, params, refs, True, True).run()

    by_flag(lax.axis_index("cond") % 2 == (1 if own else 0), run)


def middle(own, weights, params, fields, side, hydro=None):
    rows, cols = fields[0].shape
    given = (hydro,) if own else ()
    return pl.pallas_call(
        functools.partial(middle_kernel, own),
        name="middle_own" if own else "middle_other",
        out_shape=[
            pltpu.VMEM(fields[4].shape, jnp.float32),
            pltpu.VMEM((cols // LANE * rows // 4 + SUB, LANE), jnp.float32),
        ],
        in_specs=[SMEM, SMEM] + [VMEM] * (6 + own),
        out_specs=[VMEM, VMEM],
        scratch_shapes=[pltpu.VMEM(side.shape, jnp.float32)] + Sweep.scratch(rows // SUB // 4 + 2, cols + LANE),
        input_output_aliases={8: 0} if own else {},
        compiler_params=pltpu.CompilerParams(vmem_limit_bytes=10 * MIB),
        cost_estimate=cost(4),
    )(weights, params, *held(*fields, side, *given))


def edge_kernel(
    own, weights, params, root, a, b, stress, hydro, side, far_a, far_b, hydro_in,
    hydro_out, pay, ends, side_x, *refs,
):
    rows, cols = root.shape
    blocks = rows // SUB
    quarter = blocks // 4
    lanes = cols // LANE
    read = reader(root, a, b, stress, hydro, side, side_x)
    turn, valid = side_lanes()
    ty = lax.axis_index("ty")
    corners = pl.ds(lanes * GROUP, SUB)

    def run(top):
        from_a = ty % 2 == (1 if top else 0)
        first = -1 if top else blocks - quarter - 1
        outside_map = ty == (0 if top else lax.axis_size("ty") - 1)
        inner = quarter if top else blocks - quarter - 1
        corner = turn(jnp.where(from_a, far_a[corners, :], far_b[corners, :]))
        for f in range(FIELDS):
            body = read(f, inner)
            parts = []
            for k in range(lanes):
                at = pl.ds(k * GROUP + f // 2 * SUB, SUB)
                part = jnp.where(from_a, far_a[at, :], far_b[at, :])
                parts.append(pltpu.roll(part, HALO, 0) if top == (f % 2 == 0) else part)
            end = unfold(corner, ((FOLD - 1) * FIELDS if top else 0) + f)
            if f == 0:
                end = jnp.where(valid, end, 0.0)
            outer = jnp.concatenate(parts + [end], axis=1)
            if f == 0:
                outer = jnp.where(outside_map, 0.0, outer)
            ends[0, f], ends[1, f] = (outer, body) if top else (body, outer)

        def get(f, i):
            if i == 0 or i == quarter + 1:
                return ends[0 if i == 0 else 1, f]
            return read(f, first + i)

        emit = quarter_writer(first, quarter, cols, hydro_out, pay)

        def finish(i, e, u, v, change):
            if 1 <= i <= quarter:
                emit(i, e, u, v, change)
            elif i == (0 if top else quarter + 1):
                rim = change[:, :cols]
                pay[tile_at(lanes * quarter + 1), :] = fold_row(pltpu.roll(rim, 1, 0) if top else rim)

        Sweep(
            quarter + 2, cols + LANE, get, finish, weights, params, refs, not top, top
        ).run()

    by_flag(lax.axis_index("cond") % 2 == (0 if own else 1), run)


def edge(own, weights, params, fields, side, far_a, far_b, hydro):
    rows, cols = fields[0].shape
    wide = cols + LANE
    return pl.pallas_call(
        functools.partial(edge_kernel, own),
        name="edge_own" if own else "edge_other",
        out_shape=[
            pltpu.VMEM(hydro.shape, jnp.float32),
            pltpu.VMEM((cols // LANE * rows // 4 + 2 * SUB, LANE), jnp.float32),
        ],
        in_specs=[SMEM, SMEM] + [VMEM] * 9,
        out_specs=[VMEM, VMEM],
        scratch_shapes=[pltpu.VMEM((2, FIELDS, SUB, wide), jnp.float32), pltpu.VMEM(side.shape, jnp.float32)]
        + Sweep.scratch(rows // SUB // 4 + 2, wide),
        input_output_aliases={10: 0},
        compiler_params=pltpu.CompilerParams(vmem_limit_bytes=12 * MIB),
        cost_estimate=cost(3),
    )(weights, params, *held(*fields, side, far_a, far_b, hydro))


class Update:
    def __init__(self, bed, side, far_a, far_b, own_m, got_m, own_e, got_e, change_v, next_v):
        self.bed, self.side, self.far_a, self.far_b = bed, side, far_a, far_b
        self.parts = {"m": (own_m, got_m), "e": (own_e, got_e)}
        self.change_v, self.next_v = change_v, next_v
        rows, self.cols = bed.shape
        self.blocks = rows // SUB
        self.quarter = self.blocks // 4
        self.lanes = self.cols // LANE
        self.wide = self.cols + LANE
        self.side_bed = side[pl.ds(side.shape[0] - SUB, SUB), :]
        self.drop_bed = jnp.where(lax.axis_index("tx") == 0, 0, 1)
        self.mine = lax.axis_index("cond") % 2
        self.odd = lax.axis_index("ty") % 2 == 1
        col = lanes_of((SUB, self.wide))
        last_c = lax.axis_index("tx") == lax.axis_size("tx") - 1
        first_c = lax.axis_index("tx") == 0
        self.shut_c = (last_c & (col == self.cols - 1)) | (first_c & (col == self.wide - 1))
        self.last_row = rows_of((SUB, self.wide)) == SUB - 1
        self.rims = {}

    def merged(self, q, block):
        own, got = self.parts["e" if q in (0, 3) else "m"]
        at = tile_at(block)
        return jnp.where(self.mine == q // 2, own[at, :], got[at, :])

    def outside(self, q):
        at = pl.ds(self.lanes * GROUP + SUB, SUB)
        a, b = self.far_a[at, :], self.far_b[at, :]
        bed = jnp.where(self.odd, a, b) if q == 0 else jnp.where(self.odd, b, a)
        z = bed + self.merged(q, self.lanes * self.quarter + 1)
        target = SUB - 1 if q == 0 else 0
        parts = [pltpu.roll(z, (SUB + target - k) % SUB, 0) if (target - k) % SUB else z for k in range(self.lanes)]
        return jnp.concatenate(parts + [jnp.zeros((SUB, LANE), jnp.float32)], axis=1)

    def level(self, b, keep):
        if b == -1:
            return self.outside(0)
        if b == self.blocks:
            return self.outside(3)
        q, g = divmod(b, self.quarter)
        change = jnp.concatenate([self.merged(q, k * self.quarter + g) for k in range(self.lanes)], axis=1)
        if keep:
            self.change_v[tile_at(b), :] = change
        if q not in self.rims:
            self.rims[q] = self.merged(q, self.lanes * self.quarter)
        cols_bed = pltpu.roll(self.side_bed, 2 * LANE - self.drop_bed - b, 1)
        cols_change = pltpu.roll(self.rims[q], LANE - 1 - 2 * g, 1)
        return jnp.concatenate([self.bed[tile_at(b), :] + change, cols_bed + cols_change], axis=1)

    def spill(self, slope):
        return 0.25 * (slope - jnp.clip(slope, -1.0, 1.0))

    def south_face(self, z, lower, b):
        out = self.spill(south(z, lower) - z)
        if b == -1:
            return jnp.where((lax.axis_index("ty") == 0) & self.last_row, 0.0, out)
        if b == self.blocks - 1:
            return jnp.where((lax.axis_index("ty") == lax.axis_size("ty") - 1) & self.last_row, 0.0, out)
        return out

    def run(self, first, stop, keep, after=lambda b: None):
        z = self.level(first - 1, keep)
        lower = self.level(first, keep)
        gr = self.south_face(z, lower, first - 1)
        for b in range(first, stop):
            z, lower = lower, self.level(b + 1, keep)
            gr_above, gr = gr, self.south_face(z, lower, b)
            gc = jnp.where(self.shut_c, 0.0, self.spill(east(z) - z))
            out = z + gc - west(gc) + gr - north(gr, gr_above)
            self.next_v[tile_at(b), :] = out[:, : self.cols]
            after(b)


def bed_middle_kernel(
    bed, side, far_a, far_b, own_m, got_m, hydro, bed_next, bed_change, hydro_out, change_v, next_v, sems
):
    rows = bed.shape[0]
    quarter = rows // SUB // 4
    copies = [pltpu.make_async_copy(hydro, hydro_out, sems.at[0])]
    copies[0].start()
    update = Update(bed, side, far_a, far_b, own_m, got_m, None, None, change_v, next_v)
    update.run(quarter + 1, 3 * quarter - 1, True)
    for src, dst, low, high in (
        (change_v, bed_change, quarter, 3 * quarter),
        (next_v, bed_next, quarter + 1, 3 * quarter - 1),
    ):
        at = pl.ds(low * SUB, (high - low) * SUB)
        copies.append(pltpu.make_async_copy(src.at[at], dst.at[at], sems.at[len(copies)]))
        copies[-1].start()
    for copy in copies:
        copy.wait()


def bed_edge_kernel(
    own, bed, side, far_a, far_b, own_m, got_m, part_e, next_in, change_in, bed_next, bed_change,
    change_v, next_v, sems,
):
    blocks = bed.shape[0] // SUB
    quarter = blocks // 4
    update = Update(bed, side, far_a, far_b, own_m, got_m, part_e, part_e, change_v, next_v)

    def run(top):
        rows = (0, quarter + 1) if top else (blocks - quarter - 1, blocks)
        changes = (0, quarter) if top else (blocks - quarter, blocks)
        update.run(*rows, True)
        copies = []
        for n, (src, dst, (low, high)) in enumerate(((change_v, bed_change, changes), (next_v, bed_next, rows))):
            at = pl.ds(low * SUB, (high - low) * SUB)
            copies.append(pltpu.make_async_copy(src.at[at], dst.at[at], sems.at[n]))
            copies[-1].start()
        for copy in copies:
            copy.wait()

    by_flag(lax.axis_index("cond") % 2 == (0 if own else 1), run)


def bed_scratch(rows, cols):
    return [
        pltpu.VMEM((rows, cols), jnp.float32),
        pltpu.VMEM((rows, cols), jnp.float32),
        pltpu.SemaphoreType.DMA((4,)),
    ]


def bed_middle(bed, side, far_a, far_b, own_m, got_m, hydro):
    return pl.pallas_call(
        bed_middle_kernel,
        name="bed_middle",
        out_shape=[pltpu.HBM(x.shape, jnp.float32) for x in (bed, bed, hydro)],
        in_specs=[VMEM] * 7,
        out_specs=[ANY] * 3,
        scratch_shapes=bed_scratch(*bed.shape),
        compiler_params=pltpu.CompilerParams(vmem_limit_bytes=6 * MIB),
        cost_estimate=cost(4),
    )(*held(bed, side, far_a, far_b, own_m, got_m, hydro))


def bed_edge(own, bed, side, far_a, far_b, own_m, got_m, part_e, bed_next, bed_change):
    return pl.pallas_call(
        functools.partial(bed_edge_kernel, own),
        name="bed_own" if own else "bed_other",
        out_shape=[pltpu.HBM(bed.shape, jnp.float32)] * 2,
        in_specs=[VMEM] * 7 + [ANY] * 2,
        out_specs=[ANY] * 2,
        scratch_shapes=bed_scratch(*bed.shape),
        input_output_aliases={7: 0, 8: 1},
        compiler_params=pltpu.CompilerParams(vmem_limit_bytes=6 * MIB),
        cost_estimate=cost(3),
    )(
        *held(bed, side, far_a, far_b, own_m, got_m, part_e),
        *held(bed_next, bed_change, space=pltpu.HBM),
    )


def shards(bed, land_mask, cell_class, weights, cond_params, wave_stress, hydro_state):
    ny = lax.axis_size("ty")
    nc = lax.axis_size("cond")
    raw = (bed, land_mask, cell_class, wave_stress, hydro_state)
    swap = [(i, i ^ 1) for i in range(nc)]

    def pairs(first):
        partner = list(range(ny))
        for i in range(first, ny - 1, 2):
            partner[i], partner[i + 1] = i + 1, i
        return list(enumerate(partner))

    def over_chips(part, beside=()):
        reach = 2
        while reach < nc:
            got = lax.ppermute(part, "cond", [(i, i ^ reach) for i in range(nc)])
            got, beside = lax.optimization_barrier((got, beside))
            part = part + got
            reach = 2 * reach
        return part, beside

    side = lax.ppermute(pack_side(cond_params, *raw), "tx", [(0, 1), (1, 0)])
    bed, *terms, far_a, far_b = prepare(cond_params, *raw)
    fields = (*terms, wave_stress, hydro_state)
    far_a, far_b = add_corners(side, far_a, far_b)
    far_a = lax.ppermute(far_a, "ty", pairs(0))
    hydro, pay = middle(False, weights, cond_params, fields, side)
    hydro, far_a, far_b = lax.optimization_barrier((hydro, far_a, far_b))
    far_b = lax.ppermute(far_b, "ty", pairs(1))
    got = lax.ppermute(pay, "cond", swap)
    hydro, pay = middle(True, weights, cond_params, fields, side, hydro)
    part_m = pay + got
    hydro, part_m = lax.optimization_barrier((hydro, part_m))
    hydro, pay = edge(False, weights, cond_params, fields, side, far_a, far_b, hydro)
    got = lax.ppermute(pay, "cond", swap)
    hydro, pay = edge(True, weights, cond_params, fields, side, far_a, far_b, hydro)
    own_m, hydro = over_chips(part_m, hydro)
    part_e = pay + got
    own_m, _ = lax.optimization_barrier((own_m, part_e))
    got_m = lax.ppermute(own_m, "cond", swap)
    bed_next, bed_change, hydro = bed_middle(bed, side, far_a, far_b, own_m, got_m, hydro)
    own_e, (bed_next, bed_change) = over_chips(part_e, (bed_next, bed_change))
    got_e = lax.ppermute(own_e, "cond", swap)
    given = (bed, side, far_a, far_b, own_m, got_m)
    bed_next, bed_change = bed_edge(True, *given, own_e, bed_next, bed_change)
    bed_next, bed_change = bed_edge(False, *given, got_e, bed_next, bed_change)
    return bed_next, bed_change, hydro


def solution(mesh):
    in_specs = (
        P("ty", "tx"),
        P("ty", "tx"),
        P("ty", "tx"),
        P(),
        P("cond", None),
        P("cond", None, "ty", "tx"),
        P("cond", None, "ty", "tx"),
    )
    out_specs = (P("ty", "tx"), P("ty", "tx"), P("cond", None, "ty", "tx"))
    return jax.shard_map(shards, mesh=mesh, in_specs=in_specs, out_specs=out_specs, check_vma=False)
```
